32 devices in a mesh: dp: 4 (over x, core), context: 2 (over y), tensor: 4 (over z).
Axes of the slice: x: 2, y: 2, z: 4, core: 2. Of those that a mesh axis runs over, the one named last changes fastest.
Arguments:
- layer_input_hidden: bfloat16 [4, 2048, 2560], P('dp', 'context', 'tensor'), may hold values from -60 to 60
- cotangent: bfloat16 [4, 2048, 2560], P('dp', 'context', 'tensor'), may hold values from -6 to 6
- valid_mask: int32 [4, 2048], P('dp'), may hold values from 0 to 1, as said below
- span_starts: int32 [4, 2], P('dp'), may hold values from 769 to 1792, as said below
- gain_attn: float32 [2560], P('tensor'), may hold values from 0.5 to 1.5
- w_query: bfloat16 [2560, 2560], P(None, 'tensor'), may hold values from -0.125 to 0.125
- w_key: bfloat16 [2560, 640], P(None, 'tensor'), may hold values from -0.125 to 0.125
- w_value: bfloat16 [2560, 640], P(None, 'tensor'), may hold values from -0.125 to 0.125
- w_out: bfloat16 [2560, 2560], P('tensor'), may hold values from -0.75 to 0.75
- gain_mlp: float32 [2560], P('tensor'), may hold values from 0.5 to 1.5
- w_gate: bfloat16 [2560, 7168], P(None, 'tensor'), may hold values from -0.125 to 0.125
- w_up: bfloat16 [2560, 7168], P(None, 'tensor'), may hold values from -0.125 to 0.125
- w_down: bfloat16 [7168, 2560], P('tensor'), may hold values from -0.125 to 0.125
Outputs:
- layer_out: bfloat16 [4, 2048, 2560], P('dp', 'context', 'tensor')
- input_grad: bfloat16 [4, 2048, 2560], P('dp', 'context', 'tensor')
- attention_gain_gradient: float32 [2560], P('tensor')
- query_grad: float32 [2560, 2560], P(('dp', 'context'), 'tensor')
- key_grad: float32 [2560, 640], P(('dp', 'context'), 'tensor')
- value_grad: float32 [2560, 640], P(('dp', 'context'), 'tensor')
- out_grad: float32 [2560, 2560], P('tensor', ('dp', 'context'))
- gain_mlp_grad: float32 [2560], P('tensor')
- gate_grad: float32 [2560, 7168], P(('dp', 'context'), 'tensor')
- up_grad: float32 [2560, 7168], P(('dp', 'context'), 'tensor')
- down_grad: float32 [7168, 2560], P('tensor', ('dp', 'context'))
- stream_rms: float32 [], replicated
- attention_rms: float32 [], replicated
- feedforward_rms: float32 [], replicated
The draws below stay inside these ranges and needn't reach their ends.
Inputs may be any that keep to these rules, and one draw needn't show every extreme that they name: `valid_mask`: A sequence's valid tokens are its first ones, 1536 of them or more; one sequence, drawn from the seed, is valid throughout. `span_starts`: the first span of a sequence contains positions 1023 and 1024; the second begins at 1280 or later and ends inside the sequence.
All inputs are finite; a program needn't handle non-finite values.
Results may differ from the reference program's by a relative error of at most 0.025.
Values may be sent and summed in bfloat16 or wider, within the bound.
A program may use at most 320 MiB of HBM per device.

```python
import math
import jax
import jax.numpy as jnp
from jax import lax

D = 2560
H = 32
KV = 8
HD = 80
FF = 7168
LEN = 2048
PIC = 256
SEQS = 4


def draw_layer_input_hidden(key, part):
    key = jax.random.fold_in(key, 11)
    key_one = jax.random.fold_in(key, 0)
    seq_ramp = jnp.arange(SEQS, dtype=jnp.float32)[:, None, None] / SEQS
    pos_ramp = jnp.arange(LEN, dtype=jnp.float32)[None, :, None] / LEN
    ramp_scale = jnp.exp(math.log(3.0) * (seq_ramp + pos_ramp - 1.0))
    base_draw = jax.random.normal(key_one, (SEQS, LEN, D), jnp.float32)
    return (base_draw * ramp_scale).astype(jnp.bfloat16)


def draw_valid_mask(key, part):
    key = jax.random.fold_in(key, 5)
    key_one, second = jax.random.split(key)
    lengths = jax.random.randint(key_one, (SEQS,), 3 * LEN // 4, LEN + 1)
    full_seq = jax.random.randint(second, (), 0, SEQS)
    lengths = jnp.where(jnp.arange(SEQS) == full_seq, LEN, lengths)
    return (jnp.arange(LEN)[None, :] < lengths[:, None]).astype(jnp.int32)


def draw_span_starts(key, part):
    key = jax.random.fold_in(key, 7)
    key_one, second, third, fourth = jax.random.split(key, 4)
    middle = jax.random.randint(key_one, (SEQS, 1), LEN // 2 - PIC + 1, LEN // 2)
    later_start = jax.random.randint(second, (SEQS, 1), LEN // 2 + PIC, LEN - PIC + 1)
    first_pick = jax.random.randint(third, (), 0, SEQS)
    second_pick = jax.random.randint(fourth, (), 0, SEQS)
    rows = jnp.arange(SEQS)[:, None]
    middle = jnp.where(rows == first_pick, LEN // 2 - PIC + 1, middle)
    later_start = jnp.where(rows == second_pick, LEN - PIC, later_start)
    return jnp.concatenate([middle, later_start], 1).astype(jnp.int32)


def shard_levels(stream_key, dims, shards, least, top_value):
    def one(position, parts):
        steps = jax.random.uniform(jax.random.fold_in(jax.random.fold_in(stream_key, 6), position), (parts,), jnp.float32, least / len(shards), top_value / len(shards))
        return jnp.repeat(jnp.exp(steps), dims[position] // parts).reshape((-1,) + (1,) * (len(dims) - position - 1))

    loudness = one(*shards[0])
    for cut in shards[1:]:
        loudness = loudness * one(*cut)
    return loudness


def centred(rng, extent, deviation, most, shards=(), kind=jnp.bfloat16):
    entries = deviation * jax.random.normal(rng, extent, jnp.float32)
    if shards:
        entries = entries * shard_levels(rng, extent, shards, -0.22, 0.18)
    return jnp.clip(entries, -most, most).astype(kind)


def setup_inputs(seed: int = 0) -> dict:
    key_of = jax.random.split(jax.random.key(seed), 14)
    return {
        "layer_input_hidden": draw_layer_input_hidden(jax.random.fold_in(key_of[13], 71), 0),
        "cotangent": centred(key_of[1], (SEQS, LEN, D), 1.0, 6.0, ((0, 4), (1, 2), (2, 4))),
        "valid_mask": draw_valid_mask(jax.random.fold_in(key_of[13], 71), 0),
        "span_starts": draw_span_starts(jax.random.fold_in(key_of[13], 71), 0),
        "gain_attn": jnp.clip(1.0 + 0.1 * jax.random.normal(key_of[4], (D,), jnp.float32), 0.5, 1.5),
        "w_query": centred(key_of[5], (D, H * HD), D ** -0.5, 0.125, ((1, 4),)),
        "w_key": centred(key_of[6], (D, KV * HD), D ** -0.5, 0.125, ((1, 4),)),
        "w_value": centred(key_of[7], (D, KV * HD), D ** -0.5, 0.125, ((1, 4),)),
        "w_out": centred(key_of[8], (H * HD, D), 64 ** -0.5, 0.75, ((0, 4),)),
        "gain_mlp": jnp.clip(1.0 + 0.1 * jax.random.normal(key_of[9], (D,), jnp.float32), 0.5, 1.5),
        "w_gate": centred(key_of[10], (D, FF), D ** -0.5, 0.125, ((1, 4),)),
        "w_up": centred(key_of[11], (D, FF), D ** -0.5, 0.125, ((1, 4),)),
        "w_down": centred(key_of[12], (FF, D), (FF // 4) ** -0.5, 0.125, ((0, 4),)),
    }


epsilon = 1e-05
rope_base = 1000000.0

@jax.custom_vjp
def low(v):
    return lax.optimization_barrier(v.astype(jnp.bfloat16)).astype(jnp.float32)

@jax.custom_vjp
def low_back(v):
    return v

def low_keep(v):
    return (low(v), None)

def low_pass(kept, grad):
    return (grad,)

def back_keep(v):
    return (v, None)

def back_low(kept, grad):
    return (low(grad),)
low.defvjp(low_keep, low_pass)
low_back.defvjp(back_keep, back_low)

def matmul(left_operand, right_operand):
    return jnp.einsum('tei,if->tef', left_operand, right_operand, precision=lax.Precision.HIGHEST)

def rope_tables():
    halves = jnp.arange(HD // 2, dtype=jnp.float32)
    inverse = rope_base ** (-2.0 * halves / HD)
    angles = jnp.arange(LEN, dtype=jnp.float32)[:, None] * inverse[None, :]
    return (jnp.cos(angles), jnp.sin(angles))

def rotate(vectors, cos_tab, sin_tab):
    lower_half = vectors[..., :HD // 2]
    upper_half = vectors[..., HD // 2:]
    cos_b = cos_tab[:, None, :]
    sin_b = sin_tab[:, None, :]
    return jnp.concatenate([lower_half * cos_b - upper_half * sin_b, upper_half * cos_b + lower_half * sin_b], -1)

def span_index(span_starts):
    positions = jnp.arange(LEN, dtype=jnp.int32)
    inside = (positions[None, None, :] >= span_starts[:, :, None]) & (positions[None, None, :] < span_starts[:, :, None] + PIC)
    labels = jnp.arange(1, span_starts.shape[1] + 1, dtype=jnp.int32)[None, :, None]
    return lax.optimization_barrier(jnp.sum(jnp.where(inside, labels, 0), axis=1)).astype(jnp.int32) - 1

def attend_sequence(queries, key_rot, value_seq, valid_row, span_row):
    group_size = H // KV
    block_rows = min(512, LEN)
    grouped = queries.reshape(LEN // block_rows, block_rows, KV, group_size, HD)
    row_positions = jnp.arange(LEN, dtype=jnp.int32).reshape(LEN // block_rows, block_rows)
    columns = jnp.arange(LEN, dtype=jnp.int32)
    score_scale = HD ** (-0.5)

    @jax.checkpoint
    def one_block(pieces):
        query_block, block_positions = pieces
        raw_scores = jnp.einsum('bkgd,jkd->kgbj', query_block, key_rot, precision=lax.Precision.HIGHEST)
        scores = low_back(raw_scores) * score_scale
        span_here = span_row[block_positions]
        same_span = (span_here[:, None] >= 0) & (span_here[:, None] == span_row[None, :])
        allowed = (valid_row[None, :] > 0) & ((columns[None, :] <= block_positions[:, None]) | same_span)
        scores = jnp.where(allowed[None, None], scores, -jnp.inf)
        row_max = lax.optimization_barrier(jnp.max(scores, -1, keepdims=True))
        shifted = jnp.exp(scores - row_max)
        attn_probs = low(shifted / lax.optimization_barrier(jnp.sum(shifted, -1, keepdims=True)))
        return jnp.einsum('kgbj,jkd->bkgd', attn_probs, value_seq, precision=lax.Precision.HIGHEST)
    mixed = lax.map(one_block, (grouped, row_positions))
    return mixed.reshape(LEN, H * HD)

def reference(layer_input_hidden, cotangent, valid_mask, span_starts, gain_attn, w_query, w_key, w_value, w_out, gain_mlp, w_gate, w_up, w_down):
    cos_tab, sin_tab = rope_tables()
    span_ids = span_index(span_starts)
    keep_mask = valid_mask.astype(jnp.float32)[:, :, None]
    seq_count = layer_input_hidden.shape[0]
    stream = layer_input_hidden.astype(jnp.float32)
    weights = tuple((weight_matrix.astype(jnp.float32) for weight_matrix in (w_query, w_key, w_value, w_out, w_gate, w_up, w_down)))

    def forward(inputs, gain_a, gain_m, query_w, key_w, value_w, out_w, gate_w, up_w, down_w):
        normed_a = low(inputs * lax.rsqrt(lax.optimization_barrier(jnp.mean(inputs * inputs, -1, keepdims=True)) + epsilon) * gain_a)
        query_pre = low_back(matmul(normed_a, query_w)).reshape(seq_count, LEN, H, HD)
        key_pre = low_back(matmul(normed_a, key_w)).reshape(seq_count, LEN, KV, HD)
        value_low = low(low_back(matmul(normed_a, value_w))).reshape(seq_count, LEN, KV, HD)
        query_rot = low(rotate(query_pre, cos_tab, sin_tab))
        key_rot = low(rotate(key_pre, cos_tab, sin_tab))
        mixed = lax.map(lambda pieces: attend_sequence(*pieces), (query_rot, key_rot, value_low, valid_mask, span_ids))
        attended = low(low_back(mixed))
        attn_out = keep_mask * low_back(matmul(attended, out_w))
        middle = inputs + attn_out
        normed_m = low(middle * lax.rsqrt(lax.optimization_barrier(jnp.mean(middle * middle, -1, keepdims=True)) + epsilon) * gain_m)
        gate_val = low_back(matmul(normed_m, gate_w))
        up_val = low_back(matmul(normed_m, up_w))
        activated = low(jax.nn.silu(gate_val) * up_val)
        ffn_out = keep_mask * low_back(matmul(activated, down_w))
        return (middle + ffn_out, (attn_out, ffn_out))
    output, pullback, extras = jax.vjp(forward, stream, gain_attn, gain_mlp, *weights, has_aux=True)
    gradients = pullback(cotangent.astype(jnp.float32))
    attn_out, ffn_out = extras
    token_count = jnp.sum(keep_mask)

    def root_mean(values_in):
        return jnp.sqrt(jnp.sum(keep_mask * values_in * values_in) / (token_count * D))
    return (output.astype(jnp.bfloat16), gradients[0].astype(jnp.bfloat16), gradients[1], gradients[3], gradients[4], gradients[5], gradients[6], gradients[2], gradients[7], gradients[8], gradients[9], root_mean(stream), root_mean(attn_out), root_mean(ffn_out))
```

```python
import functools
import math

import jax
import jax.numpy as jnp
from jax import lax
from jax.experimental import pallas as pl
from jax.experimental.pallas import tpu as pltpu
from jax.sharding import PartitionSpec as P

HD = 80
PIC = 256
F32 = jnp.float32
BF = jnp.bfloat16
SCALE = HD**-0.5
SCALE2 = SCALE * math.log2(math.e)
LOWEST = -1e30
GROUP_ROWS = 256
HOP_ROWS = 64
VMEM_LIMIT = 60 << 20
KEY_ROWS_FWD = 1024
KEY_ROWS_BWD = 512

epsilon = 1e-05
rope_base = 1000000.0


def dot(a, b):
    return jnp.dot(a, b, preferred_element_type=F32)


def dot_nt(a, b):
    return lax.dot_general(a, b, (((1,), (1,)), ((), ())), preferred_element_type=F32)


def ein(spec, a, b):
    return jnp.einsum(spec, a, b, preferred_element_type=F32)


def forward_kernel(
    group, key_rows, lim_ref, kend_ref, q_ref, k_ref, vt_ref, o_ref, lse_ref, acc, mx, sm
):
    rows = q_ref.shape[-1]
    acc[...] = jnp.zeros_like(acc)
    sm[...] = jnp.zeros_like(sm)
    mx[...] = jnp.full_like(mx, LOWEST)
    kend = kend_ref[...]

    def step(masked, i, _):
        at = pl.multiple_of(i * key_rows, key_rows)
        k_blk = k_ref[0, pl.ds(at, key_rows), :]
        v_blk = vt_ref[0, :, pl.ds(at, key_rows)]
        if masked:
            keep = (lax.broadcasted_iota(jnp.int32, (key_rows, rows), 0) + at) < kend
        for h in range(group):
            s = dot(k_blk, q_ref[h])
            if masked:
                s = jnp.where(keep, s, LOWEST)
            old = mx[h]
            new = jnp.maximum(old, jnp.max(s, 0, keepdims=True))
            p = jnp.exp2(s * SCALE2 - new * SCALE2)
            alpha = jnp.exp2((old - new) * SCALE2)
            mx[h] = new
            sm[h] = sm[h] * alpha + jnp.sum(p, 0, keepdims=True)
            acc[h] = acc[h] * alpha + dot(v_blk, p.astype(BF))
        return 0

    lax.fori_loop(0, lim_ref[pl.program_id(1), 0], functools.partial(step, False), 0)
    lax.fori_loop(lim_ref[pl.program_id(1), 0], lim_ref[pl.program_id(1), 1], functools.partial(step, True), 0)
    for h in range(group):
        o_ref[h] = (acc[h] / sm[h]).astype(BF)
        lse_ref[h] = mx[h] * SCALE2 + jnp.log2(sm[h])


def key_limits(kend, key_rows):
    by_group = kend.reshape(-1, GROUP_ROWS)
    return jnp.stack(
        [jnp.min(by_group, 1) // key_rows, -(-jnp.max(by_group, 1) // key_rows)], 1
    ).astype(jnp.int32)


def attend_forward(q, k, vt, kend):
    heads, _, total = q.shape
    rows = GROUP_ROWS
    kvs, keys, _ = k.shape
    group = heads // kvs
    key_rows = min(KEY_ROWS_FWD, keys)
    return pl.pallas_call(
        functools.partial(forward_kernel, group, key_rows),
        grid=(kvs, total // rows),
        in_specs=[
            pl.BlockSpec(memory_space=pltpu.SMEM),
            pl.BlockSpec((1, rows), lambda g, i: (0, i)),
            pl.BlockSpec((group, HD, rows), lambda g, i: (g, 0, i)),
            pl.BlockSpec((1, keys, HD), lambda g, i: (g, 0, 0)),
            pl.BlockSpec((1, HD, keys), lambda g, i: (g, 0, 0)),
        ],
        out_specs=[
            pl.BlockSpec((group, HD, rows), lambda g, i: (g, 0, i)),
            pl.BlockSpec((group, 1, rows), lambda g, i: (g, 0, i)),
        ],
        out_shape=[
            jax.ShapeDtypeStruct((heads, HD, total), BF),
            jax.ShapeDtypeStruct((heads, 1, total), F32),
        ],
        scratch_shapes=[
            pltpu.VMEM((group, HD, rows), F32),
            pltpu.VMEM((group, 1, rows), F32),
            pltpu.VMEM((group, 1, rows), F32),
        ],
        compiler_params=pltpu.CompilerParams(vmem_limit_bytes=32 << 20),
        cost_estimate=pl.CostEstimate(
            flops=10 * heads * total * keys * HD,
            bytes_accessed=8 << 20,
            transcendentals=heads * total * keys,
        ),
        name="attend_fwd",
    )(key_limits(kend, key_rows), kend, q, k, vt)


def backward_kernel(
    group, key_rows, lim_ref, kend_ref, q_ref, do_ref, o_ref, lse_ref, k_ref, kt_ref, v_ref,
    dq_ref, dk_ref, dv_ref, ds_all, p_all, q_all, do_all,
):
    @pl.when(pl.program_id(1) == 0)
    def _():
        dk_ref[...] = jnp.zeros_like(dk_ref)
        dv_ref[...] = jnp.zeros_like(dv_ref)

    rows = q_ref.shape[-1]
    dq_ref[...] = jnp.zeros_like(dq_ref)
    kend = kend_ref[...]
    delta = []
    for h in range(group):
        q_all[:, h * rows : (h + 1) * rows] = q_ref[h]
        do_all[:, h * rows : (h + 1) * rows] = do_ref[h]
        delta.append(jnp.sum(do_ref[h].astype(F32) * o_ref[h].astype(F32), 0, keepdims=True))

    def step(masked, i, _):
        at = pl.multiple_of(i * key_rows, key_rows)
        k_blk = k_ref[0, pl.ds(at, key_rows), :]
        v_blk = v_ref[0, pl.ds(at, key_rows), :]
        kt_blk = kt_ref[0, :, pl.ds(at, key_rows)]
        if masked:
            keep = (lax.broadcasted_iota(jnp.int32, (key_rows, rows), 0) + at) < kend
        for h in range(group):
            s = dot(k_blk, q_ref[h])
            p = jnp.exp2(s * SCALE2 - lse_ref[h])
            if masked:
                p = jnp.where(keep, p, 0.0)
            dp = dot(v_blk, do_ref[h])
            ds = (p * (dp - delta[h])).astype(BF)
            p_all[:, h * rows : (h + 1) * rows] = p.astype(BF)
            ds_all[:, h * rows : (h + 1) * rows] = ds
            dq_ref[h] += dot(kt_blk, ds)
        dk_ref[0, pl.ds(at, key_rows), :] += dot_nt(ds_all[...], q_all[...])
        dv_ref[0, pl.ds(at, key_rows), :] += dot_nt(p_all[...], do_all[...])
        return 0

    lax.fori_loop(0, lim_ref[pl.program_id(1), 0], functools.partial(step, False), 0)
    lax.fori_loop(lim_ref[pl.program_id(1), 0], lim_ref[pl.program_id(1), 1], functools.partial(step, True), 0)


def attend_backward(q, do, o, lse, k, kt, v, kend):
    heads, _, total = q.shape
    rows = GROUP_ROWS
    kvs, keys, _ = k.shape
    group = heads // kvs
    key_rows = min(KEY_ROWS_BWD, keys)
    by_head = pl.BlockSpec((group, HD, rows), lambda g, i: (g, 0, i))
    by_key = pl.BlockSpec((1, keys, HD), lambda g, i: (g, 0, 0))
    return pl.pallas_call(
        functools.partial(backward_kernel, group, key_rows),
        grid=(kvs, total // rows),
        in_specs=[
            pl.BlockSpec(memory_space=pltpu.SMEM),
            pl.BlockSpec((1, rows), lambda g, i: (0, i)),
            by_head,
            by_head,
            by_head,
            pl.BlockSpec((group, 1, rows), lambda g, i: (g, 0, i)),
            by_key,
            pl.BlockSpec((1, HD, keys), lambda g, i: (g, 0, 0)),
            by_key,
        ],
        out_specs=[by_head, by_key, by_key],
        out_shape=[
            jax.ShapeDtypeStruct((heads, HD, total), F32),
            jax.ShapeDtypeStruct(k.shape, F32),
            jax.ShapeDtypeStruct(k.shape, F32),
        ],
        scratch_shapes=[
            pltpu.VMEM((key_rows, group * rows), BF),
            pltpu.VMEM((key_rows, group * rows), BF),
            pltpu.VMEM((HD, group * rows), BF),
            pltpu.VMEM((HD, group * rows), BF),
        ],
        compiler_params=pltpu.CompilerParams(vmem_limit_bytes=40 << 20),
        cost_estimate=pl.CostEstimate(
            flops=16 * heads * total * keys * HD,
            bytes_accessed=16 << 20,
            transcendentals=heads * total * keys,
        ),
        name="attend_bwd",
    )(key_limits(kend, key_rows), kend, q, do, o, lse, k, kt, v)


MESH_ID = pl.DeviceIdType.MESH
RING = 8
SENT = 4


def add_low(a, b):
    return (a.astype(F32) + b.astype(F32)).astype(BF)


class Sums:
    def __init__(self, size, count, part, low, high, sent, sems):
        self.size, self.count, self.part = size, count, part
        self.low, self.high, self.sent = low, high, sent
        self.low_send, self.low_recv, self.high_send, self.high_recv = sems
        self.here = lax.axis_index("tensor")

    def barrier(self):
        here, size = self.here, self.size
        barrier = pltpu.get_barrier_semaphore()

        @pl.when(here > 0)
        def _():
            pl.semaphore_signal(
                barrier, inc=1, device_id={"tensor": here - 1}, device_id_type=MESH_ID
            )

        @pl.when(here < size - 1)
        def _():
            pl.semaphore_signal(
                barrier, inc=1, device_id={"tensor": here + 1}, device_id_type=MESH_ID
            )

        @pl.when((here > 0) & (here < size - 1))
        def _():
            pl.semaphore_wait(barrier, 2)

        @pl.when((here == 0) | (here == size - 1))
        def _():
            pl.semaphore_wait(barrier, 1)

    def up(self, c):
        slot = lax.rem(c, RING)
        return pltpu.make_async_remote_copy(
            src_ref=self.low.at[slot],
            dst_ref=self.low.at[slot],
            send_sem=self.low_send.at[slot],
            recv_sem=self.low_recv.at[slot],
            device_id={"tensor": self.here + 1},
            device_id_type=MESH_ID,
        )

    def down(self, c):
        slot, mine = lax.rem(c, RING), lax.rem(c, SENT)
        return pltpu.make_async_remote_copy(
            src_ref=self.sent.at[mine],
            dst_ref=self.high.at[slot],
            send_sem=self.high_send.at[mine],
            recv_sem=self.high_recv.at[slot],
            device_id={"tensor": self.here - 1},
            device_id_type=MESH_ID,
        )

    def tick(self, k):
        here, size, count = self.here, self.size, self.count
        bottom, top = here == 0, here == size - 1
        c = k - here

        @pl.when((c >= 0) & (c < count))
        def _():
            slot = lax.rem(c, RING)

            @pl.when(bottom)
            def _():
                self.low[slot] = self.part(c)

            @pl.when(jnp.logical_not(bottom))
            def _():
                self.up(c).wait_recv()
                self.low[slot] = add_low(self.low[slot], self.part(c))

            @pl.when(jnp.logical_not(top))
            def _():
                self.up(c).start()

        d = k - (size - 1 - here)

        @pl.when((d >= 0) & (d < count))
        def _():
            slot, mine = lax.rem(d, RING), lax.rem(d, SENT)

            @pl.when(top)
            def _():
                self.sent[mine] = self.part(d)

            @pl.when(jnp.logical_not(top))
            def _():
                self.down(d).wait_recv()

                @pl.when(jnp.logical_not(bottom))
                def _():
                    self.sent[mine] = add_low(self.high[slot], self.part(d))

            @pl.when(jnp.logical_not(bottom))
            def _():
                self.down(d).start()

        @pl.when((c >= 2) & (c < count + 2) & jnp.logical_not(top))
        def _():
            self.up(c - 2).wait_send()

        @pl.when((d >= 2) & (d < count + 2) & jnp.logical_not(bottom))
        def _():
            self.down(d - 2).wait_send()

    def total(self, c, then):
        slot = lax.rem(c, RING)
        top = self.here == self.size - 1

        @pl.when(top)
        def _():
            then(self.low[slot].astype(F32))

        @pl.when(jnp.logical_not(top))
        def _():
            then(self.low[slot].astype(F32) + self.high[slot].astype(F32))


def sum_scratch(hop, features):
    return [
        pltpu.VMEM((RING, hop, features), BF),
        pltpu.VMEM((RING, hop, features), BF),
        pltpu.VMEM((SENT, hop, features), BF),
        pltpu.SemaphoreType.DMA((RING,)),
        pltpu.SemaphoreType.DMA((RING,)),
        pltpu.SemaphoreType.DMA((SENT,)),
        pltpu.SemaphoreType.DMA((RING,)),
    ]


def tile_of(n, most):
    for tile in range(most, 0, -128):
        if n % tile == 0:
            return tile
    return n


def ffn_kernel(
    size, hop, chunk,
    mixed, keep, gain, w_out, w_gate, w_up, w_down, x, cot,
    normed_o, act_o, gg_o, gu_o, ffn_o, back_o, middle_o, square_o,
    low, high, sent, low_send, low_recv, high_send, high_recv,
    wo, wg, wu, wd, parts, normed, xs, cots, mids, act, gg, gu, ffn, back,
    w_sem, x_sem, cot_sem, normed_sem, mid_sem, act_sem, ffn_sem,
):
    rows, features = x.shape
    hidden = w_gate.shape[1]
    count, per, groups = rows // hop, chunk // hop, rows // chunk
    tile_f, tile_d = tile_of(hidden, 256), tile_of(features, 256)
    tiles_f, tiles_d = hidden // tile_f, features // tile_d
    half_f, half_d = -(-tiles_f // 2), -(-tiles_d // 2)
    lag = size - 1 + per - 1
    ticks = max(per * groups + lag, count + size)

    def part(c):
        return parts[lax.rem(lax.div(c, per), 2), pl.ds(pl.multiple_of(lax.rem(c, per) * hop, hop), hop), :]

    sums = Sums(size, count, part, low, high, sent, (low_send, low_recv, high_send, high_recv))
    loads = [
        pltpu.make_async_copy(a, b, w_sem.at[i])
        for i, (a, b) in enumerate(((w_out, wo), (w_gate, wg), (w_up, wu), (w_down, wd)))
    ]
    for load in loads:
        load.start()

    def load_x(c):
        slot = lax.rem(c, 2)
        return pltpu.make_async_copy(x.at[pl.ds(c * hop, hop)], xs.at[slot], x_sem.at[slot])

    def load_cot(g):
        return pltpu.make_async_copy(cot.at[pl.ds(g * chunk, chunk)], cots, cot_sem)

    def save_normed(c):
        at, q = lax.rem(lax.div(c, per), 2), lax.rem(c, per)
        return pltpu.make_async_copy(
            normed.at[at, pl.ds(q * hop, hop)], normed_o.at[pl.ds(c * hop, hop)], normed_sem.at[at, q]
        )

    def save_mid(c):
        slot = lax.rem(c, 2)
        return pltpu.make_async_copy(mids.at[slot], middle_o.at[pl.ds(c * hop, hop)], mid_sem.at[slot])

    def save_act(g):
        return [
            pltpu.make_async_copy(a, b.at[pl.ds(g * chunk, chunk)], act_sem.at[i])
            for i, (a, b) in enumerate(((act, act_o), (gg, gg_o), (gu, gu_o)))
        ]

    def save_ffn(g):
        return [
            pltpu.make_async_copy(a, b.at[pl.ds(g * chunk, chunk)], ffn_sem.at[i])
            for i, (a, b) in enumerate(((ffn, ffn_o), (back, back_o)))
        ]

    def project(g):
        at = lax.rem(g, 2)
        lhs = mixed[:, pl.ds(pl.multiple_of(g * chunk, chunk), chunk)]

        def one(j, _):
            cols = pl.ds(pl.multiple_of(j * tile_d, tile_d), tile_d)
            parts[at, :, cols] = lax.dot_general(
                lhs, wo[:, cols], (((0,), (0,)), ((), ())), preferred_element_type=F32
            ).astype(BF)
            return 0

        lax.fori_loop(0, tiles_d, one, 0)

    load_x(0).start()
    load_cot(0).start()
    square_o[...] = jnp.zeros_like(square_o)
    loads[0].wait()
    project(0)
    sums.barrier()

    def finish(c):
        slot = lax.rem(c, 2)
        load_x(c).wait()

        @pl.when(c + 1 < count)
        def _():
            load_x(c + 1).start()

        @pl.when(c >= 2)
        def _():
            save_mid(c - 2).wait()

        @pl.when(c >= 2 * per)
        def _():
            save_normed(c - 2 * per).wait()

        kept = keep[pl.ds(pl.multiple_of(c * hop, hop), hop), :]

        def then(total):
            out = kept * total
            square_o[...] += jnp.sum(out * out, 0, keepdims=True)
            mids[slot] = xs[slot].astype(F32) + out

        sums.total(c, then)
        mid = mids[slot]
        inv = lax.rsqrt(jnp.sum(mid * mid, 1, keepdims=True) / features + epsilon)
        at = lax.rem(lax.div(c, per), 2)
        normed[at, pl.ds(pl.multiple_of(lax.rem(c, per) * hop, hop), hop), :] = (
            mid * inv * gain[...]
        ).astype(BF)
        save_mid(c).start()
        save_normed(c).start()

    def inner(g, lo, hi):
        at = lax.rem(g, 2)
        kept = keep[pl.ds(pl.multiple_of(g * chunk, chunk), chunk), :]

        def one(j, _):
            cols = pl.ds(pl.multiple_of(j * tile_f, tile_f), tile_f)
            gate = dot(normed[at], wg[:, cols])
            up = dot(normed[at], wu[:, cols])
            grad = dot_nt(cots[...], wd[cols, :]) * kept
            sig = jax.nn.sigmoid(gate)
            silu = gate * sig
            act[:, cols] = (silu * up * kept).astype(BF)
            gg[:, cols] = (grad * up * (sig + silu * (1.0 - sig))).astype(BF)
            gu[:, cols] = (grad * silu).astype(BF)
            return 0

        lax.fori_loop(lo, hi, one, 0)

    def outer(g, lo, hi):
        def one(j, _):
            cols = pl.ds(pl.multiple_of(j * tile_d, tile_d), tile_d)
            ffn[:, cols] = dot(act[...], wd[:, cols]).astype(BF)
            back[:, cols] = (dot_nt(gg[...], wg[cols, :]) + dot_nt(gu[...], wu[cols, :])).astype(BF)
            return 0

        lax.fori_loop(lo, hi, one, 0)

    def tick(k, _):
        sums.tick(k)
        c = k - (size - 1)

        @pl.when((c >= 0) & (c < count))
        def _():
            finish(c)

        ahead = k + 2

        @pl.when((lax.rem(ahead, per) == 0) & (ahead < count))
        def _():
            project(lax.div(ahead, per))

        s = k - lag
        g, stage = lax.div(s, per), lax.rem(s, per)
        going = (s >= 0) & (g < groups)

        @pl.when(going & (stage == 0))
        def _():
            @pl.when(g == 0)
            def _():
                for load in loads[1:]:
                    load.wait()

            load_cot(g).wait()

            @pl.when(g > 0)
            def _():
                for copy in save_act(g - 1):
                    copy.wait()

            inner(g, 0, half_f)

        @pl.when(going & (stage == 1))
        def _():
            inner(g, half_f, tiles_f)
            for copy in save_act(g):
                copy.start()

            @pl.when(g + 1 < groups)
            def _():
                load_cot(g + 1).start()

        @pl.when(going & (stage == 2))
        def _():
            @pl.when(g > 0)
            def _():
                for copy in save_ffn(g - 1):
                    copy.wait()

            outer(g, 0, half_d)

        @pl.when(going & (stage == 3))
        def _():
            outer(g, half_d, tiles_d)
            for copy in save_ffn(g):
                copy.start()

        return 0

    lax.fori_loop(0, ticks, tick, 0)
    for copy in save_act(groups - 1) + save_ffn(groups - 1):
        copy.wait()
    for c in range(count - 2, count):
        save_mid(c).wait()
    for c in range(count - 2 * per, count):
        save_normed(c).wait()


def feed_forward(size, mixed, keep, gain, w_out, w_gate, w_up, w_down, x, cot, chunk, hop):
    rows, features = x.shape
    hidden = w_gate.shape[1]
    per = chunk // hop
    assert per == 4
    anywhere, vmem = pl.BlockSpec(memory_space=pl.ANY), pl.BlockSpec(memory_space=pltpu.VMEM)
    shape = jax.ShapeDtypeStruct
    return pl.pallas_call(
        functools.partial(ffn_kernel, size, hop, chunk),
        in_specs=[vmem] * 3 + [anywhere] * 6,
        out_specs=[anywhere] * 7 + [vmem],
        out_shape=[
            shape((rows, features), BF),
            shape((rows, hidden), BF),
            shape((rows, hidden), BF),
            shape((rows, hidden), BF),
            shape((rows, features), BF),
            shape((rows, features), BF),
            shape((rows, features), F32),
            shape((1, features), F32),
        ],
        scratch_shapes=sum_scratch(hop, features)
        + [
            pltpu.VMEM(w_out.shape, BF),
            pltpu.VMEM(w_gate.shape, BF),
            pltpu.VMEM(w_up.shape, BF),
            pltpu.VMEM(w_down.shape, BF),
            pltpu.VMEM((2, chunk, features), BF),
            pltpu.VMEM((2, chunk, features), BF),
            pltpu.VMEM((2, hop, features), BF),
            pltpu.VMEM((chunk, features), BF),
            pltpu.VMEM((2, hop, features), F32),
            pltpu.VMEM((chunk, hidden), BF),
            pltpu.VMEM((chunk, hidden), BF),
            pltpu.VMEM((chunk, hidden), BF),
            pltpu.VMEM((chunk, features), BF),
            pltpu.VMEM((chunk, features), BF),
            pltpu.SemaphoreType.DMA((4,)),
            pltpu.SemaphoreType.DMA((2,)),
            pltpu.SemaphoreType.DMA,
            pltpu.SemaphoreType.DMA((2, per)),
            pltpu.SemaphoreType.DMA((2,)),
            pltpu.SemaphoreType.DMA((3,)),
            pltpu.SemaphoreType.DMA((2,)),
        ],
        compiler_params=pltpu.CompilerParams(
            collective_id=1, has_side_effects=True, vmem_limit_bytes=VMEM_LIMIT
        ),
        cost_estimate=pl.CostEstimate(
            flops=2 * rows * features * (6 * hidden + w_out.shape[0]),
            bytes_accessed=80 << 20,
            transcendentals=rows * hidden,
        ),
        name="feed_forward",
    )(mixed, keep, gain, w_out, w_gate, w_up, w_down, x, cot)


def back_kernel(
    size, hop, chunk,
    parts, keep, gain, w_out, middle, cot,
    grad_o, grad_low_o, mixed_o, gain_o,
    low, high, sent, low_send, low_recv, high_send, high_recv,
    wo, mids, cots, grads, grads_low,
    w_sem, mid_sem, cot_sem, grad_sem, grad_low_sem,
):
    rows, features = middle.shape
    count, per, groups = rows // hop, chunk // hop, rows // chunk
    ticks = max(count + size, per * (groups - 1) + size - 1 + per)

    def part(c):
        return parts[pl.ds(pl.multiple_of(c * hop, hop), hop), :]

    sums = Sums(size, count, part, low, high, sent, (low_send, low_recv, high_send, high_recv))
    load_w = pltpu.make_async_copy(w_out, wo, w_sem)
    load_w.start()

    def load_row(c):
        slot = lax.rem(c, 2)
        return [
            pltpu.make_async_copy(middle.at[pl.ds(c * hop, hop)], mids.at[slot], mid_sem.at[slot]),
            pltpu.make_async_copy(cot.at[pl.ds(c * hop, hop)], cots.at[slot], cot_sem.at[slot]),
        ]

    def save_grad(c):
        slot = lax.rem(c, 2)
        return pltpu.make_async_copy(grads.at[slot], grad_o.at[pl.ds(c * hop, hop)], grad_sem.at[slot])

    def save_low(c):
        q = lax.rem(c, per)
        return pltpu.make_async_copy(
            grads_low.at[pl.ds(q * hop, hop)], grad_low_o.at[pl.ds(c * hop, hop)], grad_low_sem.at[q]
        )

    for copy in load_row(0):
        copy.start()
    gain_o[...] = jnp.zeros_like(gain_o)
    sums.barrier()

    def finish(c):
        slot = lax.rem(c, 2)
        for copy in load_row(c):
            copy.wait()

        @pl.when(c + 1 < count)
        def _():
            for copy in load_row(c + 1):
                copy.start()

        @pl.when(c >= 2)
        def _():
            save_grad(c - 2).wait()

        @pl.when(c >= per)
        def _():
            save_low(c - per).wait()

        kept = keep[pl.ds(pl.multiple_of(c * hop, hop), hop), :]
        mid = mids[slot]
        inv = lax.rsqrt(jnp.sum(mid * mid, 1, keepdims=True) / features + epsilon)
        hat = mid * inv

        def then(total):
            gain_o[...] += jnp.sum(total * hat, 0, keepdims=True)
            weighted = total * gain[...]
            mean = jnp.sum(weighted * hat, 1, keepdims=True) / features
            grads[slot] = cots[slot].astype(F32) + inv * (weighted - hat * mean)

        sums.total(c, then)
        grads_low[pl.ds(pl.multiple_of(lax.rem(c, per) * hop, hop), hop), :] = (
            kept * grads[slot]
        ).astype(BF)
        save_grad(c).start()
        save_low(c).start()

    def tick(k, _):
        sums.tick(k)
        c = k - (size - 1)

        @pl.when((c >= 0) & (c < count))
        def _():
            finish(c)

            @pl.when(lax.rem(c, per) == per - 1)
            def _():
                g = lax.div(c, per)

                @pl.when(g == 0)
                def _():
                    load_w.wait()

                mixed_o[:, pl.ds(pl.multiple_of(g * chunk, chunk), chunk)] = dot_nt(
                    wo[...], grads_low[...]
                ).astype(BF)

        return 0

    lax.fori_loop(0, ticks, tick, 0)
    for c in range(count - 2, count):
        save_grad(c).wait()
    for c in range(count - per, count):
        save_low(c).wait()


def norm_back(size, parts, keep, gain, w_out, middle, cot, chunk, hop):
    rows, features = middle.shape
    per = chunk // hop
    anywhere, vmem = pl.BlockSpec(memory_space=pl.ANY), pl.BlockSpec(memory_space=pltpu.VMEM)
    shape = jax.ShapeDtypeStruct
    return pl.pallas_call(
        functools.partial(back_kernel, size, hop, chunk),
        in_specs=[vmem] * 3 + [anywhere] * 3,
        out_specs=[anywhere] * 2 + [vmem] * 2,
        out_shape=[
            shape((rows, features), F32),
            shape((rows, features), BF),
            shape((w_out.shape[0], rows), BF),
            shape((1, features), F32),
        ],
        scratch_shapes=sum_scratch(hop, features)
        + [
            pltpu.VMEM(w_out.shape, BF),
            pltpu.VMEM((2, hop, features), F32),
            pltpu.VMEM((2, hop, features), BF),
            pltpu.VMEM((2, hop, features), F32),
            pltpu.VMEM((chunk, features), BF),
            pltpu.SemaphoreType.DMA,
            pltpu.SemaphoreType.DMA((2,)),
            pltpu.SemaphoreType.DMA((2,)),
            pltpu.SemaphoreType.DMA((2,)),
            pltpu.SemaphoreType.DMA((per,)),
        ],
        compiler_params=pltpu.CompilerParams(
            collective_id=2, has_side_effects=True, vmem_limit_bytes=VMEM_LIMIT
        ),
        cost_estimate=pl.CostEstimate(
            flops=2 * rows * features * w_out.shape[0],
            bytes_accessed=40 << 20,
            transcendentals=rows,
        ),
        name="norm_back",
    )(parts, keep, gain, w_out, middle, cot)


class Line:
    def __init__(self, size):
        self.size = size
        self.here = lax.axis_index("tensor")
        self.up = [(i, i + 1) for i in range(size - 1)]
        self.down = [(i + 1, i) for i in range(size - 1)]

    def gather(self, own):
        size, here, width = self.size, self.here, own.shape[1]
        full = jnp.zeros((own.shape[0], size * width), own.dtype)
        full = lax.dynamic_update_slice(full, own, (0, here * width))
        rising, falling = [], []
        a = b = own
        for _ in range(size - 1):
            a = lax.ppermute(a, "tensor", self.up)
            b = lax.ppermute(b, "tensor", self.down)
            rising.append(a)
            falling.append(b)
        for s in range(size - 1):
            slot = lax.rem(here - 1 - s + size, size)
            block = jnp.where(here > s, rising[s], falling[size - 2 - s])
            full = lax.dynamic_update_slice(full, block, (0, slot * width))
        return full

    def gather_small(self, own):
        size, here, width = self.size, self.here, own.shape[1]
        full = jnp.zeros((own.shape[0], size * width), own.dtype)
        full = lax.dynamic_update_slice(full, own, (0, here * width))
        for s in range(1, size):
            block = lax.ppermute(own, "tensor", [(i, (i + s) % size) for i in range(size)])
            slot = lax.rem(here - s + size, size)
            full = lax.dynamic_update_slice(full, block, (0, slot * width))
        return full

    def scatter(self, partial_value, width):
        size, here = self.size, self.here

        def block(index):
            start = jnp.clip(index, 0, size - 1) * width
            return lax.dynamic_slice_in_dim(partial_value, start, width, 1)

        a = b = None
        for s in range(size - 1):
            up = block(here + (size - 1 - s))
            down = block(here - (size - 1 - s))
            if s:
                up = (up.astype(F32) + a.astype(F32)).astype(BF)
                down = (down.astype(F32) + b.astype(F32)).astype(BF)
            a = lax.ppermute(up, "tensor", self.up)
            b = lax.ppermute(down, "tensor", self.down)
        return block(here).astype(F32) + a.astype(F32) + b.astype(F32)


def rotate(vectors, cos_tab, sin_tab):
    lower = vectors[:, : HD // 2]
    upper = vectors[:, HD // 2 :]
    return jnp.concatenate([lower * cos_tab - upper * sin_tab, upper * cos_tab + lower * sin_tab], 1)


def local(
    axes,
    layer_input_hidden,
    cotangent,
    valid_mask,
    span_starts,
    gain_attn,
    w_query,
    w_key,
    w_value,
    w_out,
    gain_mlp,
    w_gate,
    w_up,
    w_down,
):
    line = Line(axes["tensor"])
    here = line.here
    _, rows, width = layer_input_hidden.shape
    features = width * line.size
    kvs = w_key.shape[1] // HD
    heads = w_query.shape[1] // HD
    place = lax.axis_index("context")
    offset = place * rows
    own_columns = here * width

    def own(a):
        return lax.dynamic_slice_in_dim(a, own_columns, width, 1)

    position = offset + jnp.arange(rows, dtype=jnp.int32)
    length = jnp.sum(valid_mask[0])
    starts = span_starts[0]
    last = position
    for k in range(starts.shape[0]):
        inside = (position >= starts[k]) & (position < starts[k] + PIC)
        last = jnp.maximum(last, jnp.where(inside, starts[k] + PIC - 1, 0))
    kend = jnp.minimum(last + 1, length)[None, :]
    keep = (position < length).astype(F32)[:, None]
    inverse_freq = rope_base ** (-2.0 * jnp.arange(HD // 2, dtype=F32) / HD)
    angles = inverse_freq[:, None] * position.astype(F32)[None, :]
    cos_tab, sin_tab = jnp.cos(angles), jnp.sin(angles)

    gains = line.gather_small(jnp.stack([gain_attn, gain_mlp]))
    gain_a, gain_m = gains[:1], gains[1:]

    x_low = line.gather(layer_input_hidden[0])
    stream = x_low.astype(F32)
    square_a = jnp.sum(stream * stream, 1, keepdims=True)
    inv_a = lax.rsqrt(square_a / features + epsilon)
    normed_a = (stream * inv_a * gain_a).astype(BF)
    key_t = rotate(ein("sd,dx->xs", normed_a, w_key).reshape(kvs, HD, rows), cos_tab, sin_tab)
    value_t = ein("sd,dx->xs", normed_a, w_value).reshape(kvs, HD, rows)
    mine = jnp.concatenate([key_t, value_t]).astype(BF)
    if axes["context"] == 2:
        other = lax.ppermute(mine, "context", [(0, 1), (1, 0)])
        first = place == 0
        both = jnp.concatenate(
            [jnp.where(first, mine, other), jnp.where(first, other, mine)], axis=2
        )
    else:
        both = lax.all_gather(mine, "context", axis=2, tiled=True)
    kt_all, vt_all = both[:kvs], both[kvs:]
    k_all, v_all = jnp.swapaxes(kt_all, 1, 2), jnp.swapaxes(vt_all, 1, 2)
    query_t = rotate(
        ein("sd,dx->xs", normed_a, w_query).reshape(heads, HD, rows), cos_tab, sin_tab
    ).astype(BF)

    cot = line.gather(jnp.where(square_a[0, 0] >= 0.0, cotangent[0], 0.0))

    mixed, lse = attend_forward(query_t, k_all, vt_all, kend)
    mixed_t = mixed.reshape(heads * HD, rows)
    normed_m, act, gg, gu, down_part, back_part, middle, attn_square = feed_forward(
        line.size, mixed_t, keep, gain_m, w_out, w_gate, w_up, w_down, x_low, cot, GROUP_ROWS, HOP_ROWS
    )
    grad_middle, grad_attn, grad_mixed, gain_m_rows = norm_back(
        line.size, back_part, keep, gain_m, w_out, middle, cot, GROUP_ROWS, HOP_ROWS
    )
    middle_own, grad_middle_own = own(middle), own(grad_middle)
    grad_q, grad_k, grad_v = attend_backward(
        query_t, grad_mixed.reshape(heads, HD, rows), mixed, lse, k_all, kt_all, v_all, kend
    )

    def shard(grad, dim):
        return lax.psum_scatter(
            grad.astype(BF), ("dp", "context"), scatter_dimension=dim, tiled=True
        ).astype(F32)

    down_sum = shard(ein("sf,sd->fd", act, cot), 1)
    gate_sum = shard(ein("sd,sf->df", normed_m, gg), 0)
    up_sum = shard(ein("sd,sf->df", normed_m, gu), 0)
    out_sum = shard(ein("xs,sd->xd", mixed_t, grad_attn), 1)

    ffn_out = line.scatter(down_part, width)
    layer_out = (middle_own + ffn_out).astype(BF)

    def halves(a):
        return a.astype(BF).reshape(kvs, axes["context"], rows, HD)

    dkv = jnp.concatenate([halves(grad_k), halves(grad_v)])
    dkv_own = lax.dynamic_index_in_dim(dkv, place, 1, False).astype(F32)
    if axes["context"] == 2:
        sent = lax.ppermute(
            lax.dynamic_index_in_dim(dkv, 1 - place, 1, False), "context", [(0, 1), (1, 0)]
        )
        dkv_own = dkv_own + sent.astype(F32)
    else:
        dkv_own = lax.psum_scatter(dkv, "context", scatter_dimension=1, tiled=False).astype(F32)
    dkv_t = jnp.swapaxes(dkv_own, 1, 2)
    grad_query = (
        rotate(grad_q * SCALE, cos_tab, -sin_tab).astype(BF).reshape(-1, rows)
    )
    grad_key = rotate(dkv_t[:kvs] * SCALE, cos_tab, -sin_tab).astype(BF).reshape(-1, rows)
    grad_value = dkv_t[kvs:].astype(BF).reshape(-1, rows)

    query_sum = shard(ein("sd,xs->dx", normed_a, grad_query), 0)
    key_sum = shard(ein("sd,xs->dx", normed_a, grad_key), 0)
    value_sum = shard(ein("sd,xs->dx", normed_a, grad_value), 0)

    partial_a = (
        ein("xs,dx->sd", grad_query, w_query)
        + ein("xs,dx->sd", grad_key, w_key)
        + ein("xs,dx->sd", grad_value, w_value)
    )
    hat_a = x_low.astype(F32) * inv_a
    row_dot = lax.psum(jnp.sum(partial_a * (hat_a * gain_a), 1), "tensor")[:, None]
    gain_a_part = jnp.sum(partial_a * hat_a, 0)
    grad_a = line.scatter(partial_a.astype(BF), width)
    hat_own = layer_input_hidden[0].astype(F32) * inv_a
    through = inv_a * (grad_a * gain_attn[None, :] - hat_own * (row_dot / features))
    input_grad = (grad_middle_own + through).astype(BF)

    gain_m_part = lax.dynamic_update_slice(
        jnp.zeros((1, features), F32), own(gain_m_rows), (0, own_columns)
    )[0]
    numbers = jnp.stack(
        [
            jnp.sum(keep * square_a) / line.size,
            jnp.sum(attn_square) / line.size,
            jnp.sum(ffn_out * ffn_out),
            jnp.sum(keep) / line.size,
        ]
    )
    total = lax.psum(
        jnp.concatenate([gain_a_part, gain_m_part, numbers]), ("dp", "context", "tensor")
    )
    gain_a_sum = lax.dynamic_slice_in_dim(total, own_columns, width, 0)
    gain_m_sum = lax.dynamic_slice_in_dim(total, features + own_columns, width, 0)
    numbers = total[2 * features :]
    rms = jnp.sqrt(numbers[:3] / (numbers[3] * features))
    return (
        layer_out[None],
        input_grad[None],
        gain_a_sum,
        query_sum,
        key_sum,
        value_sum,
        out_sum,
        gain_m_sum,
        gate_sum,
        up_sum,
        down_sum,
        rms[0],
        rms[1],
        rms[2],
    )


def solution(mesh):
    token = P("dp", "context", "tensor")
    by_rows = P(("dp", "context"), "tensor")
    by_columns = P("tensor", ("dp", "context"))
    cols, rows, vec = P(None, "tensor"), P("tensor", None), P("tensor")
    return jax.shard_map(
        functools.partial(local, dict(mesh.shape)),
        mesh=mesh,
        in_specs=(
            token,
            token,
            P("dp", None),
            P("dp", None),
            vec,
            cols,
            cols,
            cols,
            rows,
            vec,
            cols,
            cols,
            rows,
        ),
        out_specs=(
            token,
            token,
            vec,
            by_rows,
            by_rows,
            by_rows,
            by_columns,
            vec,
            by_rows,
            by_rows,
            by_columns,
            P(),
            P(),
            P(),
        ),
        check_vma=False,
    )
```

```python
import functools
import math

import jax
import jax.numpy as jnp
from jax import lax
from jax.experimental import pallas as pl
from jax.experimental.pallas import tpu as pltpu
from jax.sharding import PartitionSpec as P

HD = 80
PIC = 256
F32 = jnp.float32
BF = jnp.bfloat16
SCALE = HD**-0.5
SCALE2 = SCALE * math.log2(math.e)
LOWEST = -1e30
GROUP_ROWS = 256
HOP_ROWS = 64
VMEM_LIMIT = 60 << 20
KEY_ROWS_FWD = 1024
KEY_ROWS_BWD = 512

epsilon = 1e-05
rope_base = 1000000.0


def dot(a, b):
    return jnp.dot(a, b, preferred_element_type=F32)


def dot_nt(a, b):
    return lax.dot_general(a, b, (((1,), (1,)), ((), ())), preferred_element_type=F32)


def ein(spec, a, b):
    return jnp.einsum(spec, a, b, preferred_element_type=F32)


def forward_kernel(
    group, key_rows, lim_ref, kend_ref, q_ref, k_ref, vt_ref, o_ref, lse_ref, acc, mx, sm
):
    rows = q_ref.shape[-1]
    acc[...] = jnp.zeros_like(acc)
    sm[...] = jnp.zeros_like(sm)
    mx[...] = jnp.full_like(mx, LOWEST)
    kend = kend_ref[...]

    def step(masked, i, _):
        at = pl.multiple_of(i * key_rows, key_rows)
        k_blk = k_ref[0, pl.ds(at, key_rows), :]
        v_blk = vt_ref[0, :, pl.ds(at, key_rows)]
        if masked:
            keep = (lax.broadcasted_iota(jnp.int32, (key_rows, rows), 0) + at) < kend
        for h in range(group):
            s = dot(k_blk, q_ref[h])
            if masked:
                s = jnp.where(keep, s, LOWEST)
            old = mx[h]
            new = jnp.maximum(old, jnp.max(s, 0, keepdims=True))
            p = jnp.exp2(s * SCALE2 - new * SCALE2)
            alpha = jnp.exp2((old - new) * SCALE2)
            mx[h] = new
            sm[h] = sm[h] * alpha + jnp.sum(p, 0, keepdims=True)
            acc[h] = acc[h] * alpha + dot(v_blk, p.astype(BF))
        return 0

    lax.fori_loop(0, lim_ref[pl.program_id(1), 0], functools.partial(step, False), 0)
    lax.fori_loop(lim_ref[pl.program_id(1), 0], lim_ref[pl.program_id(1), 1], functools.partial(step, True), 0)
    for h in range(group):
        o_ref[h] = (acc[h] / sm[h]).astype(BF)
        lse_ref[h] = mx[h] * SCALE2 + jnp.log2(sm[h])


def key_limits(kend, key_rows):
    by_group = kend.reshape(-1, GROUP_ROWS)
    return jnp.stack(
        [jnp.min(by_group, 1) // key_rows, -(-jnp.max(by_group, 1) // key_rows)], 1
    ).astype(jnp.int32)


def attend_forward(q, k, vt, kend):
    heads, _, total = q.shape
    rows = GROUP_ROWS
    kvs, keys, _ = k.shape
    group = heads // kvs
    key_rows = min(KEY_ROWS_FWD, keys)
    return pl.pallas_call(
        functools.partial(forward_kernel, group, key_rows),
        grid=(kvs, total // rows),
        in_specs=[
            pl.BlockSpec(memory_space=pltpu.SMEM),
            pl.BlockSpec((1, rows), lambda g, i: (0, i)),
            pl.BlockSpec((group, HD, rows), lambda g, i: (g, 0, i)),
            pl.BlockSpec((1, keys, HD), lambda g, i: (g, 0, 0)),
            pl.BlockSpec((1, HD, keys), lambda g, i: (g, 0, 0)),
        ],
        out_specs=[
            pl.BlockSpec((group, HD, rows), lambda g, i: (g, 0, i)),
            pl.BlockSpec((group, 1, rows), lambda g, i: (g, 0, i)),
        ],
        out_shape=[
            jax.ShapeDtypeStruct((heads, HD, total), BF),
            jax.ShapeDtypeStruct((heads, 1, total), F32),
        ],
        scratch_shapes=[
            pltpu.VMEM((group, HD, rows), F32),
            pltpu.VMEM((group, 1, rows), F32),
            pltpu.VMEM((group, 1, rows), F32),
        ],
        compiler_params=pltpu.CompilerParams(vmem_limit_bytes=32 << 20),
        cost_estimate=pl.CostEstimate(
            flops=10 * heads * total * keys * HD,
            bytes_accessed=8 << 20,
            transcendentals=heads * total * keys,
        ),
        name="attend_fwd",
    )(key_limits(kend, key_rows), kend, q, k, vt)


def backward_kernel(
    group, key_rows, lim_ref, kend_ref, q_ref, do_ref, o_ref, lse_ref, k_ref, kt_ref, v_ref,
    dq_ref, dk_ref, dv_ref, ds_all, p_all, q_all, do_all,
):
    @pl.when(pl.program_id(1) == 0)
    def _():
        dk_ref[...] = jnp.zeros_like(dk_ref)
        dv_ref[...] = jnp.zeros_like(dv_ref)

    rows = q_ref.shape[-1]
    dq_ref[...] = jnp.zeros_like(dq_ref)
    kend = kend_ref[...]
    delta = []
    for h in range(group):
        q_all[:, h * rows : (h + 1) * rows] = q_ref[h]
        do_all[:, h * rows : (h + 1) * rows] = do_ref[h]
        delta.append(jnp.sum(do_ref[h].astype(F32) * o_ref[h].astype(F32), 0, keepdims=True))

    def step(masked, i, _):
        at = pl.multiple_of(i * key_rows, key_rows)
        k_blk = k_ref[0, pl.ds(at, key_rows), :]
        v_blk = v_ref[0, pl.ds(at, key_rows), :]
        kt_blk = kt_ref[0, :, pl.ds(at, key_rows)]
        if masked:
            keep = (lax.broadcasted_iota(jnp.int32, (key_rows, rows), 0) + at) < kend
        for h in range(group):
            s = dot(k_blk, q_ref[h])
            p = jnp.exp2(s * SCALE2 - lse_ref[h])
            if masked:
                p = jnp.where(keep, p, 0.0)
            dp = dot(v_blk, do_ref[h])
            ds = (p * (dp - delta[h])).astype(BF)
            p_all[:, h * rows : (h + 1) * rows] = p.astype(BF)
            ds_all[:, h * rows : (h + 1) * rows] = ds
            dq_ref[h] += dot(kt_blk, ds)
        dk_ref[0, pl.ds(at, key_rows), :] += dot_nt(ds_all[...], q_all[...])
        dv_ref[0, pl.ds(at, key_rows), :] += dot_nt(p_all[...], do_all[...])
        return 0

    lax.fori_loop(0, lim_ref[pl.program_id(1), 0], functools.partial(step, False), 0)
    lax.fori_loop(lim_ref[pl.program_id(1), 0], lim_ref[pl.program_id(1), 1], functools.partial(step, True), 0)


def attend_backward(q, do, o, lse, k, kt, v, kend, after):
    heads, _, total = q.shape
    rows = GROUP_ROWS
    kvs, keys, _ = k.shape
    group = heads // kvs
    key_rows = min(KEY_ROWS_BWD, keys)
    by_head = pl.BlockSpec((group, HD, rows), lambda g, i: (g, 0, i))
    by_key = pl.BlockSpec((1, keys, HD), lambda g, i: (g, 0, 0))

    def kernel(*refs):
        backward_kernel(group, key_rows, *refs[:9], *refs[9 + len(after) :])

    return pl.pallas_call(
        kernel,
        grid=(kvs, total // rows),
        in_specs=[
            pl.BlockSpec(memory_space=pltpu.SMEM),
            pl.BlockSpec((1, rows), lambda g, i: (0, i)),
            by_head,
            by_head,
            by_head,
            pl.BlockSpec((group, 1, rows), lambda g, i: (g, 0, i)),
            by_key,
            pl.BlockSpec((1, HD, keys), lambda g, i: (g, 0, 0)),
            by_key,
        ]
        + [pl.BlockSpec(memory_space=pl.ANY)] * len(after),
        out_specs=[by_head, by_key, by_key],
        out_shape=[
            jax.ShapeDtypeStruct((heads, HD, total), F32),
            jax.ShapeDtypeStruct(k.shape, F32),
            jax.ShapeDtypeStruct(k.shape, F32),
        ],
        scratch_shapes=[
            pltpu.VMEM((key_rows, group * rows), BF),
            pltpu.VMEM((key_rows, group * rows), BF),
            pltpu.VMEM((HD, group * rows), BF),
            pltpu.VMEM((HD, group * rows), BF),
        ],
        compiler_params=pltpu.CompilerParams(vmem_limit_bytes=40 << 20),
        cost_estimate=pl.CostEstimate(
            flops=16 * heads * total * keys * HD,
            bytes_accessed=16 << 20,
            transcendentals=heads * total * keys,
        ),
        name="attend_bwd",
    )(key_limits(kend, key_rows), kend, q, do, o, lse, k, kt, v, *after)


MESH_ID = pl.DeviceIdType.MESH
RING = 8
SENT = 4


def add_low(a, b):
    return (a.astype(F32) + b.astype(F32)).astype(BF)


class Sums:
    def __init__(self, size, count, part, low, high, sent, sems):
        self.size, self.count, self.part = size, count, part
        self.low, self.high, self.sent = low, high, sent
        self.low_send, self.low_recv, self.high_send, self.high_recv = sems
        self.here = lax.axis_index("tensor")

    def barrier(self):
        here, size = self.here, self.size
        barrier = pltpu.get_barrier_semaphore()

        @pl.when(here > 0)
        def _():
            pl.semaphore_signal(
                barrier, inc=1, device_id={"tensor": here - 1}, device_id_type=MESH_ID
            )

        @pl.when(here < size - 1)
        def _():
            pl.semaphore_signal(
                barrier, inc=1, device_id={"tensor": here + 1}, device_id_type=MESH_ID
            )

        @pl.when((here > 0) & (here < size - 1))
        def _():
            pl.semaphore_wait(barrier, 2)

        @pl.when((here == 0) | (here == size - 1))
        def _():
            pl.semaphore_wait(barrier, 1)

    def up(self, c):
        slot = lax.rem(c, RING)
        return pltpu.make_async_remote_copy(
            src_ref=self.low.at[slot],
            dst_ref=self.low.at[slot],
            send_sem=self.low_send.at[slot],
            recv_sem=self.low_recv.at[slot],
            device_id={"tensor": self.here + 1},
            device_id_type=MESH_ID,
        )

    def down(self, c):
        slot, mine = lax.rem(c, RING), lax.rem(c, SENT)
        return pltpu.make_async_remote_copy(
            src_ref=self.sent.at[mine],
            dst_ref=self.high.at[slot],
            send_sem=self.high_send.at[mine],
            recv_sem=self.high_recv.at[slot],
            device_id={"tensor": self.here - 1},
            device_id_type=MESH_ID,
        )

    def tick(self, k):
        here, size, count = self.here, self.size, self.count
        bottom, top = here == 0, here == size - 1
        c = k - here

        @pl.when((c >= 0) & (c < count))
        def _():
            slot = lax.rem(c, RING)

            @pl.when(bottom)
            def _():
                self.low[slot] = self.part(c)

            @pl.when(jnp.logical_not(bottom))
            def _():
                self.up(c).wait_recv()
                self.low[slot] = add_low(self.low[slot], self.part(c))

            @pl.when(jnp.logical_not(top))
            def _():
                self.up(c).start()

        d = k - (size - 1 - here)

        @pl.when((d >= 0) & (d < count))
        def _():
            slot, mine = lax.rem(d, RING), lax.rem(d, SENT)

            @pl.when(top)
            def _():
                self.sent[mine] = self.part(d)

            @pl.when(jnp.logical_not(top))
            def _():
                self.down(d).wait_recv()

                @pl.when(jnp.logical_not(bottom))
                def _():
                    self.sent[mine] = add_low(self.high[slot], self.part(d))

            @pl.when(jnp.logical_not(bottom))
            def _():
                self.down(d).start()

        @pl.when((c >= 2) & (c < count + 2) & jnp.logical_not(top))
        def _():
            self.up(c - 2).wait_send()

        @pl.when((d >= 2) & (d < count + 2) & jnp.logical_not(bottom))
        def _():
            self.down(d - 2).wait_send()

    def total(self, c, then):
        slot = lax.rem(c, RING)
        top = self.here == self.size - 1

        @pl.when(top)
        def _():
            then(self.low[slot].astype(F32))

        @pl.when(jnp.logical_not(top))
        def _():
            then(self.low[slot].astype(F32) + self.high[slot].astype(F32))


def sum_scratch(hop, features):
    return [
        pltpu.VMEM((RING, hop, features), BF),
        pltpu.VMEM((RING, hop, features), BF),
        pltpu.VMEM((SENT, hop, features), BF),
        pltpu.SemaphoreType.DMA((RING,)),
        pltpu.SemaphoreType.DMA((RING,)),
        pltpu.SemaphoreType.DMA((SENT,)),
        pltpu.SemaphoreType.DMA((RING,)),
    ]


def tile_of(n, most):
    for tile in range(most, 0, -128):
        if n % tile == 0:
            return tile
    return n


def ffn_kernel(
    size, hop, chunk,
    mixed, keep, gain, w_out, w_gate, w_up, w_down, x, cot,
    normed_o, act_o, gg_o, gu_o, ffn_o, back_o, middle_o, square_o,
    low, high, sent, low_send, low_recv, high_send, high_recv,
    wo, wg, wu, wd, parts, normed, xs, cots, mids, act, gg, gu, ffn, back,
    w_sem, x_sem, cot_sem, normed_sem, mid_sem, act_sem, ffn_sem,
):
    rows, features = x.shape
    hidden = w_gate.shape[1]
    count, per, groups = rows // hop, chunk // hop, rows // chunk
    tile_f, tile_d = tile_of(hidden, 256), tile_of(features, 256)
    tiles_f, tiles_d = hidden // tile_f, features // tile_d
    half_f, half_d = -(-tiles_f // 2), -(-tiles_d // 2)
    lag = size - 1 + per - 1
    ticks = max(per * groups + lag, count + size)

    def part(c):
        return parts[lax.rem(lax.div(c, per), 2), pl.ds(pl.multiple_of(lax.rem(c, per) * hop, hop), hop), :]

    sums = Sums(size, count, part, low, high, sent, (low_send, low_recv, high_send, high_recv))
    loads = [
        pltpu.make_async_copy(a, b, w_sem.at[i])
        for i, (a, b) in enumerate(((w_out, wo), (w_gate, wg), (w_up, wu), (w_down, wd)))
    ]
    for load in loads:
        load.start()

    def load_x(c):
        slot = lax.rem(c, 2)
        return pltpu.make_async_copy(x.at[pl.ds(c * hop, hop)], xs.at[slot], x_sem.at[slot])

    def load_cot(g):
        return pltpu.make_async_copy(cot.at[pl.ds(g * chunk, chunk)], cots, cot_sem)

    def save_normed(c):
        at, q = lax.rem(lax.div(c, per), 2), lax.rem(c, per)
        return pltpu.make_async_copy(
            normed.at[at, pl.ds(q * hop, hop)], normed_o.at[pl.ds(c * hop, hop)], normed_sem.at[at, q]
        )

    def save_mid(c):
        slot = lax.rem(c, 2)
        return pltpu.make_async_copy(mids.at[slot], middle_o.at[pl.ds(c * hop, hop)], mid_sem.at[slot])

    def save_act(g):
        return [
            pltpu.make_async_copy(a, b.at[pl.ds(g * chunk, chunk)], act_sem.at[i])
            for i, (a, b) in enumerate(((act, act_o), (gg, gg_o), (gu, gu_o)))
        ]

    def save_ffn(g):
        return [
            pltpu.make_async_copy(a, b.at[pl.ds(g * chunk, chunk)], ffn_sem.at[i])
            for i, (a, b) in enumerate(((ffn, ffn_o), (back, back_o)))
        ]

    def project(g):
        at = lax.rem(g, 2)
        lhs = mixed[:, pl.ds(pl.multiple_of(g * chunk, chunk), chunk)]

        def one(j, _):
            cols = pl.ds(pl.multiple_of(j * tile_d, tile_d), tile_d)
            parts[at, :, cols] = lax.dot_general(
                lhs, wo[:, cols], (((0,), (0,)), ((), ())), preferred_element_type=F32
            ).astype(BF)
            return 0

        lax.fori_loop(0, tiles_d, one, 0)

    load_x(0).start()
    load_cot(0).start()
    square_o[...] = jnp.zeros_like(square_o)
    loads[0].wait()
    project(0)
    sums.barrier()

    def finish(c):
        slot = lax.rem(c, 2)
        load_x(c).wait()

        @pl.when(c + 1 < count)
        def _():
            load_x(c + 1).start()

        @pl.when(c >= 2)
        def _():
            save_mid(c - 2).wait()

        @pl.when(c >= 2 * per)
        def _():
            save_normed(c - 2 * per).wait()

        kept = keep[pl.ds(pl.multiple_of(c * hop, hop), hop), :]

        def then(total):
            out = kept * total
            square_o[...] += jnp.sum(out * out, 0, keepdims=True)
            mids[slot] = xs[slot].astype(F32) + out

        sums.total(c, then)
        mid = mids[slot]
        inv = lax.rsqrt(jnp.sum(mid * mid, 1, keepdims=True) / features + epsilon)
        at = lax.rem(lax.div(c, per), 2)
        normed[at, pl.ds(pl.multiple_of(lax.rem(c, per) * hop, hop), hop), :] = (
            mid * inv * gain[...]
        ).astype(BF)
        save_mid(c).start()
        save_normed(c).start()

    def inner(g, lo, hi):
        at = lax.rem(g, 2)
        kept = keep[pl.ds(pl.multiple_of(g * chunk, chunk), chunk), :]

        def one(j, _):
            cols = pl.ds(pl.multiple_of(j * tile_f, tile_f), tile_f)
            gate = dot(normed[at], wg[:, cols])
            up = dot(normed[at], wu[:, cols])
            grad = dot_nt(cots[...], wd[cols, :]) * kept
            sig = jax.nn.sigmoid(gate)
            silu = gate * sig
            act[:, cols] = (silu * up * kept).astype(BF)
            gg[:, cols] = (grad * up * (sig + silu * (1.0 - sig))).astype(BF)
            gu[:, cols] = (grad * silu).astype(BF)
            return 0

        lax.fori_loop(lo, hi, one, 0)

    def outer(g, lo, hi):
        def one(j, _):
            cols = pl.ds(pl.multiple_of(j * tile_d, tile_d), tile_d)
            ffn[:, cols] = dot(act[...], wd[:, cols]).astype(BF)
            back[:, cols] = (dot_nt(gg[...], wg[cols, :]) + dot_nt(gu[...], wu[cols, :])).astype(BF)
            return 0

        lax.fori_loop(lo, hi, one, 0)

    def tick(k, _):
        sums.tick(k)
        c = k - (size - 1)

        @pl.when((c >= 0) & (c < count))
        def _():
            finish(c)

        ahead = k + 2

        @pl.when((lax.rem(ahead, per) == 0) & (ahead < count))
        def _():
            project(lax.div(ahead, per))

        s = k - lag
        g, stage = lax.div(s, per), lax.rem(s, per)
        going = (s >= 0) & (g < groups)

        @pl.when(going & (stage == 0))
        def _():
            @pl.when(g == 0)
            def _():
                for load in loads[1:]:
                    load.wait()

            load_cot(g).wait()

            @pl.when(g > 0)
            def _():
                for copy in save_act(g - 1):
                    copy.wait()

            inner(g, 0, half_f)

        @pl.when(going & (stage == 1))
        def _():
            inner(g, half_f, tiles_f)
            for copy in save_act(g):
                copy.start()

            @pl.when(g + 1 < groups)
            def _():
                load_cot(g + 1).start()

        @pl.when(going & (stage == 2))
        def _():
            @pl.when(g > 0)
            def _():
                for copy in save_ffn(g - 1):
                    copy.wait()

            outer(g, 0, half_d)

        @pl.when(going & (stage == 3))
        def _():
            outer(g, half_d, tiles_d)
            for copy in save_ffn(g):
                copy.start()

        return 0

    lax.fori_loop(0, ticks, tick, 0)
    for copy in save_act(groups - 1) + save_ffn(groups - 1):
        copy.wait()
    for c in range(count - 2, count):
        save_mid(c).wait()
    for c in range(count - 2 * per, count):
        save_normed(c).wait()


def feed_forward(size, mixed, keep, gain, w_out, w_gate, w_up, w_down, x, cot, chunk, hop):
    rows, features = x.shape
    hidden = w_gate.shape[1]
    per = chunk // hop
    assert per == 4
    anywhere, vmem = pl.BlockSpec(memory_space=pl.ANY), pl.BlockSpec(memory_space=pltpu.VMEM)
    shape = jax.ShapeDtypeStruct
    return pl.pallas_call(
        functools.partial(ffn_kernel, size, hop, chunk),
        in_specs=[vmem] * 3 + [anywhere] * 6,
        out_specs=[anywhere] * 7 + [vmem],
        out_shape=[
            shape((rows, features), BF),
            shape((rows, hidden), BF),
            shape((rows, hidden), BF),
            shape((rows, hidden), BF),
            shape((rows, features), BF),
            shape((rows, features), BF),
            shape((rows, features), F32),
            shape((1, features), F32),
        ],
        scratch_shapes=sum_scratch(hop, features)
        + [
            pltpu.VMEM(w_out.shape, BF),
            pltpu.VMEM(w_gate.shape, BF),
            pltpu.VMEM(w_up.shape, BF),
            pltpu.VMEM(w_down.shape, BF),
            pltpu.VMEM((2, chunk, features), BF),
            pltpu.VMEM((2, chunk, features), BF),
            pltpu.VMEM((2, hop, features), BF),
            pltpu.VMEM((chunk, features), BF),
            pltpu.VMEM((2, hop, features), F32),
            pltpu.VMEM((chunk, hidden), BF),
            pltpu.VMEM((chunk, hidden), BF),
            pltpu.VMEM((chunk, hidden), BF),
            pltpu.VMEM((chunk, features), BF),
            pltpu.VMEM((chunk, features), BF),
            pltpu.SemaphoreType.DMA((4,)),
            pltpu.SemaphoreType.DMA((2,)),
            pltpu.SemaphoreType.DMA,
            pltpu.SemaphoreType.DMA((2, per)),
            pltpu.SemaphoreType.DMA((2,)),
            pltpu.SemaphoreType.DMA((3,)),
            pltpu.SemaphoreType.DMA((2,)),
        ],
        compiler_params=pltpu.CompilerParams(
            collective_id=1, has_side_effects=True, vmem_limit_bytes=VMEM_LIMIT
        ),
        cost_estimate=pl.CostEstimate(
            flops=2 * rows * features * (6 * hidden + w_out.shape[0]),
            bytes_accessed=80 << 20,
            transcendentals=rows * hidden,
        ),
        name="feed_forward",
    )(mixed, keep, gain, w_out, w_gate, w_up, w_down, x, cot)


def back_kernel(
    size, hop, chunk,
    parts, keep, gain, w_out, middle, cot,
    grad_o, grad_low_o, mixed_o, gain_o,
    low, high, sent, low_send, low_recv, high_send, high_recv,
    wo, mids, cots, grads, grads_low,
    w_sem, mid_sem, cot_sem, grad_sem, grad_low_sem,
):
    rows, features = middle.shape
    count, per, groups = rows // hop, chunk // hop, rows // chunk
    ticks = max(count + size, per * (groups - 1) + size - 1 + per)

    def part(c):
        return parts[pl.ds(pl.multiple_of(c * hop, hop), hop), :]

    sums = Sums(size, count, part, low, high, sent, (low_send, low_recv, high_send, high_recv))
    load_w = pltpu.make_async_copy(w_out, wo, w_sem)
    load_w.start()

    def load_row(c):
        slot = lax.rem(c, 2)
        return [
            pltpu.make_async_copy(middle.at[pl.ds(c * hop, hop)], mids.at[slot], mid_sem.at[slot]),
            pltpu.make_async_copy(cot.at[pl.ds(c * hop, hop)], cots.at[slot], cot_sem.at[slot]),
        ]

    def save_grad(c):
        slot = lax.rem(c, 2)
        return pltpu.make_async_copy(grads.at[slot], grad_o.at[pl.ds(c * hop, hop)], grad_sem.at[slot])

    def save_low(c):
        q = lax.rem(c, per)
        return pltpu.make_async_copy(
            grads_low.at[pl.ds(q * hop, hop)], grad_low_o.at[pl.ds(c * hop, hop)], grad_low_sem.at[q]
        )

    for copy in load_row(0):
        copy.start()
    gain_o[...] = jnp.zeros_like(gain_o)
    sums.barrier()

    def finish(c):
        slot = lax.rem(c, 2)
        for copy in load_row(c):
            copy.wait()

        @pl.when(c + 1 < count)
        def _():
            for copy in load_row(c + 1):
                copy.start()

        @pl.when(c >= 2)
        def _():
            save_grad(c - 2).wait()

        @pl.when(c >= per)
        def _():
            save_low(c - per).wait()

        kept = keep[pl.ds(pl.multiple_of(c * hop, hop), hop), :]
        mid = mids[slot]
        inv = lax.rsqrt(jnp.sum(mid * mid, 1, keepdims=True) / features + epsilon)
        hat = mid * inv

        def then(total):
            gain_o[...] += jnp.sum(total * hat, 0, keepdims=True)
            weighted = total * gain[...]
            mean = jnp.sum(weighted * hat, 1, keepdims=True) / features
            grads[slot] = cots[slot].astype(F32) + inv * (weighted - hat * mean)

        sums.total(c, then)
        grads_low[pl.ds(pl.multiple_of(lax.rem(c, per) * hop, hop), hop), :] = (
            kept * grads[slot]
        ).astype(BF)
        save_grad(c).start()
        save_low(c).start()

    def tick(k, _):
        sums.tick(k)
        c = k - (size - 1)

        @pl.when((c >= 0) & (c < count))
        def _():
            finish(c)

            @pl.when(lax.rem(c, per) == per - 1)
            def _():
                g = lax.div(c, per)

                @pl.when(g == 0)
                def _():
                    load_w.wait()

                mixed_o[:, pl.ds(pl.multiple_of(g * chunk, chunk), chunk)] = dot_nt(
                    wo[...], grads_low[...]
                ).astype(BF)

        return 0

    lax.fori_loop(0, ticks, tick, 0)
    for c in range(count - 2, count):
        save_grad(c).wait()
    for c in range(count - per, count):
        save_low(c).wait()


def norm_back(size, parts, keep, gain, w_out, middle, cot, chunk, hop, after):
    rows, features = middle.shape
    per = chunk // hop
    anywhere, vmem = pl.BlockSpec(memory_space=pl.ANY), pl.BlockSpec(memory_space=pltpu.VMEM)
    shape = jax.ShapeDtypeStruct

    def kernel(*refs):
        back_kernel(size, hop, chunk, *refs[:6], *refs[6 + len(after) :])

    return pl.pallas_call(
        kernel,
        in_specs=[vmem] * 3 + [anywhere] * (3 + len(after)),
        out_specs=[anywhere] * 2 + [vmem] * 2,
        out_shape=[
            shape((rows, features), F32),
            shape((rows, features), BF),
            shape((w_out.shape[0], rows), BF),
            shape((1, features), F32),
        ],
        scratch_shapes=sum_scratch(hop, features)
        + [
            pltpu.VMEM(w_out.shape, BF),
            pltpu.VMEM((2, hop, features), F32),
            pltpu.VMEM((2, hop, features), BF),
            pltpu.VMEM((2, hop, features), F32),
            pltpu.VMEM((chunk, features), BF),
            pltpu.SemaphoreType.DMA,
            pltpu.SemaphoreType.DMA((2,)),
            pltpu.SemaphoreType.DMA((2,)),
            pltpu.SemaphoreType.DMA((2,)),
            pltpu.SemaphoreType.DMA((per,)),
        ],
        compiler_params=pltpu.CompilerParams(
            collective_id=2, has_side_effects=True, vmem_limit_bytes=VMEM_LIMIT
        ),
        cost_estimate=pl.CostEstimate(
            flops=2 * rows * features * w_out.shape[0],
            bytes_accessed=40 << 20,
            transcendentals=rows,
        ),
        name="norm_back",
    )(parts, keep, gain, w_out, middle, cot, *after)


def greet(peers):
    barrier = pltpu.get_barrier_semaphore()
    for peer in peers:
        pl.semaphore_signal(barrier, inc=1, device_id=peer, device_id_type=MESH_ID)
    pl.semaphore_wait(barrier, len(peers))


def others(axis, size):
    here = lax.axis_index(axis)
    return [lax.rem(here + i, size) for i in range(1, size)]


def project_kernel(
    size, contexts, chunk,
    own, gain_own, cos_tab, sin_tab, w_query, w_key, w_value,
    x_o, normed_o, inv_o, gain_o, query_o, kv_o,
    xs, gains, full, normed, kv, wq, wk, wv,
    up_send, up_recv, down_send, down_recv, gain_send, gain_recv, kv_send, kv_recv,
    own_sem, w_sem, out_sem, kv_sem,
):
    here, place = lax.axis_index("tensor"), lax.axis_index("context")
    rows, width = own.shape
    features = size * width
    groups, steps = rows // chunk, size - 1
    heads, kvs = w_query.shape[1] // HD, w_key.shape[1] // HD
    bottom, top = here == 0, here == size - 1

    loads = [
        pltpu.make_async_copy(a, b, w_sem.at[i])
        for i, (a, b) in enumerate(((w_query, wq), (w_key, wk), (w_value, wv)))
    ]

    def load_own(g):
        part = pl.ds(g * chunk, chunk)
        return pltpu.make_async_copy(own.at[part], xs.at[here, part], own_sem.at[g])

    for g in range(groups):
        load_own(g).start()
    for load in loads:
        load.start()
    gains[here] = gain_own[...]

    def block(owner, g):
        return xs.at[owner, pl.ds(g * chunk, chunk)]

    def up(g, s):
        owner = jnp.clip(here - s, 0, size - 1)
        return pltpu.make_async_remote_copy(
            src_ref=block(owner, g),
            dst_ref=block(owner, g),
            send_sem=up_send.at[g, s],
            recv_sem=up_recv.at[g, s],
            device_id={"tensor": here + 1},
            device_id_type=MESH_ID,
        )

    def down(g, s):
        owner = jnp.clip(here + s, 0, size - 1)
        return pltpu.make_async_remote_copy(
            src_ref=block(owner, g),
            dst_ref=block(owner, g),
            send_sem=down_send.at[g, s],
            recv_sem=down_recv.at[g, s],
            device_id={"tensor": here - 1},
            device_id_type=MESH_ID,
        )

    def send(g, s):
        @pl.when((here >= s) & jnp.logical_not(top))
        def _():
            up(g, s).start()

        @pl.when((here + s < size) & jnp.logical_not(bottom))
        def _():
            down(g, s).start()

    def sent(g, s):
        @pl.when((here >= s) & jnp.logical_not(top))
        def _():
            up(g, s).wait_send()

        @pl.when((here + s < size) & jnp.logical_not(bottom))
        def _():
            down(g, s).wait_send()

    def receive(g, s):
        @pl.when(here - 1 - s >= 0)
        def _():
            up(g, s).wait_recv()

        @pl.when(here + 1 + s < size)
        def _():
            down(g, s).wait_recv()

    tensor_peers = [{"tensor": i} for i in others("tensor", size)]
    context_peers = [{"context": i} for i in others("context", contexts)]
    greet(tensor_peers + context_peers)

    def gain_copy(i):
        return pltpu.make_async_remote_copy(
            src_ref=gains.at[here],
            dst_ref=gains.at[here],
            send_sem=gain_send.at[i],
            recv_sem=gain_recv.at[i],
            device_id=tensor_peers[i],
            device_id_type=MESH_ID,
        )

    def kv_copy(g, i):
        part = kv.at[:, :, pl.ds(pl.multiple_of(place * rows + g * chunk, chunk), chunk)]
        return pltpu.make_async_remote_copy(
            src_ref=part,
            dst_ref=part,
            send_sem=kv_send.at[g, i],
            recv_sem=kv_recv.at[g, i],
            device_id=context_peers[i],
            device_id_type=MESH_ID,
        )

    load_own(0).wait()
    send(0, 0)
    for i in range(size - 1):
        gain_copy(i).start()

    def save(g):
        part = pl.ds(g * chunk, chunk)
        return [
            pltpu.make_async_copy(full, x_o.at[part], out_sem.at[0]),
            pltpu.make_async_copy(normed, normed_o.at[part], out_sem.at[1]),
        ]

    def turn(u, cos_t, sin_t):
        lower, upper = u[: HD // 2], u[HD // 2 :]
        return jnp.concatenate([lower * cos_t - upper * sin_t, upper * cos_t + lower * sin_t], 0)

    def compute(g):
        part = pl.ds(pl.multiple_of(g * chunk, chunk), chunk)

        @pl.when(g == 0)
        def _():
            for load in loads:
                load.wait()
            for i in range(size - 1):
                gain_copy(i).wait_recv()
            gain_o[...] = jnp.concatenate([gains[j] for j in range(size)], 1)

        @pl.when(g > 0)
        def _():
            for copy in save(g - 1):
                copy.wait()

        full[...] = jnp.concatenate([xs[j, part, :] for j in range(size)], 1)
        stream = full[...].astype(F32)
        inv = lax.rsqrt(jnp.sum(stream * stream, 1, keepdims=True) / features + epsilon)
        inv_o[part, :] = inv
        normed[...] = (stream * inv * gain_o[0:1, :]).astype(BF)
        for copy in save(g):
            copy.start()
        cos_t, sin_t = cos_tab[:, part], sin_tab[:, part]
        mine = pl.ds(pl.multiple_of(place * rows + g * chunk, chunk), chunk)
        key = dot(normed[...], wk[...]).T
        value = dot(normed[...], wv[...]).T
        for h in range(kvs):
            kv[h, :, mine] = turn(key[h * HD : (h + 1) * HD], cos_t, sin_t).astype(BF)
            kv[kvs + h, :, mine] = value[h * HD : (h + 1) * HD].astype(BF)
        for i in range(contexts - 1):
            kv_copy(g, i).start()
        query = dot(normed[...], wq[...]).T
        for h in range(heads):
            query_o[h, :, part] = turn(query[h * HD : (h + 1) * HD], cos_t, sin_t).astype(BF)

    def tick(k, _):
        g, s = lax.div(k, steps), lax.rem(k, steps)

        @pl.when(s > 0)
        def _():
            receive(g, s - 1)
            send(g, s)

        @pl.when((s == steps - 1) & (g + 1 < groups))
        def _():
            load_own(g + 1).wait()
            send(g + 1, 0)

        @pl.when((s == 0) & (g > 0))
        def _():
            receive(g - 1, steps - 1)
            compute(g - 1)

        return 0

    lax.fori_loop(0, groups * steps + 1, tick, 0)
    for copy in save(groups - 1):
        copy.wait()
    for i in range(size - 1):
        gain_copy(i).wait_send()
    for g in range(groups):
        for s in range(steps):
            sent(g, s)
        for i in range(contexts - 1):
            kv_copy(g, i).wait()
    out = pltpu.make_async_copy(kv, kv_o, kv_sem)
    out.start()
    out.wait()


def project(axes, own, gain_own, cos_tab, sin_tab, w_query, w_key, w_value, chunk):
    size, contexts = axes["tensor"], axes["context"]
    rows, width = own.shape
    features, groups = size * width, rows // chunk
    heads, kvs = w_query.shape[1] // HD, w_key.shape[1] // HD
    anywhere, vmem = pl.BlockSpec(memory_space=pl.ANY), pl.BlockSpec(memory_space=pltpu.VMEM)
    shape, dma = jax.ShapeDtypeStruct, pltpu.SemaphoreType.DMA
    return pl.pallas_call(
        functools.partial(project_kernel, size, contexts, chunk),
        in_specs=[anywhere] + [vmem] * 3 + [anywhere] * 3,
        out_specs=[anywhere] * 2 + [vmem] * 3 + [anywhere],
        out_shape=[
            shape((rows, features), BF),
            shape((rows, features), BF),
            shape((rows, 1), F32),
            shape((8, features), F32),
            shape((heads, HD, rows), BF),
            shape((2 * kvs, HD, contexts * rows), BF),
        ],
        scratch_shapes=[
            pltpu.VMEM((size, rows, width), BF),
            pltpu.VMEM((size, 8, width), F32),
            pltpu.VMEM((chunk, features), BF),
            pltpu.VMEM((chunk, features), BF),
            pltpu.VMEM((2 * kvs, HD, contexts * rows), BF),
            pltpu.VMEM(w_query.shape, BF),
            pltpu.VMEM(w_key.shape, BF),
            pltpu.VMEM(w_value.shape, BF),
            dma((groups, size - 1)),
            dma((groups, size - 1)),
            dma((groups, size - 1)),
            dma((groups, size - 1)),
            dma((size - 1,)),
            dma((size - 1,)),
            dma((groups, max(contexts - 1, 1))),
            dma((groups, max(contexts - 1, 1))),
            dma((groups,)),
            dma((3,)),
            dma((2,)),
            dma,
        ],
        compiler_params=pltpu.CompilerParams(
            collective_id=3, has_side_effects=True, vmem_limit_bytes=VMEM_LIMIT
        ),
        cost_estimate=pl.CostEstimate(
            flops=2 * rows * features * (heads + 2 * kvs) * HD,
            bytes_accessed=20 << 20,
            transcendentals=rows,
        ),
        name="project",
    )(own, gain_own, cos_tab, sin_tab, w_query, w_key, w_value)


def input_kernel(
    size, chunk,
    grads, inv, gain, w_query, w_key, w_value, x,
    out_o, dot_o, gain_o,
    parts, ups, downs, xs, wq, wk, wv, dots, cols,
    up_send, up_recv, down_send, down_recv, dot_send, dot_recv, col_send, col_recv, w_sem, x_sem,
):
    here = lax.axis_index("tensor")
    rows, features = x.shape
    width, groups = features // size, rows // chunk
    count = (size - 1) * groups
    bottom, top = here == 0, here == size - 1
    nq, nk = w_query.shape[1], w_key.shape[1]

    loads = [
        pltpu.make_async_copy(a, b, w_sem.at[i])
        for i, (a, b) in enumerate(((w_query, wq), (w_key, wk), (w_value, wv)))
    ]

    def load_x(c):
        slot = lax.rem(c, 2)
        return pltpu.make_async_copy(x.at[pl.ds(c * chunk, chunk)], xs.at[slot], x_sem.at[slot])

    for load in loads:
        load.start()
    load_x(0).start()
    peers = [{"tensor": i} for i in others("tensor", size)]
    greet(peers)
    for load in loads:
        load.wait()

    def compute(c):
        slot = lax.rem(c, 2)
        part = pl.ds(pl.multiple_of(c * chunk, chunk), chunk)
        load_x(c).wait()

        @pl.when(c + 1 < groups)
        def _():
            load_x(c + 1).start()

        g = grads[:, part].astype(F32).T.astype(BF)
        whole = (
            dot_nt(g[:, :nq], wq[...])
            + dot_nt(g[:, nq : nq + nk], wk[...])
            + dot_nt(g[:, nq + nk :], wv[...])
        )
        hat = xs[slot].astype(F32) * inv[part, :]
        moved = whole * hat
        rowsum = jnp.sum(moved * gain[0:1, :], 1, keepdims=True)
        dots[here, :, part] = jnp.broadcast_to(rowsum, (chunk, 128)).T[:8]
        colsum = jnp.sum(moved, 0, keepdims=True)
        low = whole.astype(BF)
        for j in range(size):
            parts[j, part, :] = low[:, j * width : (j + 1) * width]
            piece = jnp.broadcast_to(colsum[:, j * width : (j + 1) * width], (8, width))

            @pl.when(c == 0)
            def _():
                cols[j] = piece

            @pl.when(c > 0)
            def _():
                cols[j] += piece

    def rows_of(m):
        return pl.ds(pl.multiple_of(lax.rem(m, groups) * chunk, chunk), chunk)

    def up(m, first):
        owner = size - 1 - lax.div(m, groups)
        return pltpu.make_async_remote_copy(
            src_ref=parts.at[owner, rows_of(m)] if first else ups.at[m],
            dst_ref=ups.at[m],
            send_sem=up_send.at[m],
            recv_sem=up_recv.at[m],
            device_id={"tensor": here + 1},
            device_id_type=MESH_ID,
        )

    def down(m, first):
        owner = lax.div(m, groups)
        return pltpu.make_async_remote_copy(
            src_ref=parts.at[owner, rows_of(m)] if first else downs.at[m],
            dst_ref=downs.at[m],
            send_sem=down_send.at[m],
            recv_sem=down_recv.at[m],
            device_id={"tensor": here - 1},
            device_id_type=MESH_ID,
        )

    def dot_copy(i):
        return pltpu.make_async_remote_copy(
            src_ref=dots.at[here],
            dst_ref=dots.at[here],
            send_sem=dot_send.at[i],
            recv_sem=dot_recv.at[i],
            device_id=peers[i],
            device_id_type=MESH_ID,
        )

    def col_copy(i):
        return pltpu.make_async_remote_copy(
            src_ref=cols.at[peers[i]["tensor"]],
            dst_ref=cols.at[size + i],
            send_sem=col_send.at[i],
            recv_sem=col_recv.at[i],
            device_id=peers[i],
            device_id_type=MESH_ID,
        )

    def tick(k, _):
        @pl.when(k < groups)
        def _():
            compute(k)

        m = k - here
        owner = size - 1 - lax.div(m, groups)

        @pl.when((m >= 0) & (owner > here))
        def _():
            @pl.when(bottom)
            def _():
                up(m, True).start()

            @pl.when(jnp.logical_not(bottom))
            def _():
                up(m, False).wait_recv()
                ups[m] = add_low(ups[m], parts[owner, rows_of(m), :])
                up(m, False).start()

        n = k - (size - 1 - here)
        below = lax.div(n, groups)

        @pl.when((n >= 0) & (below < here))
        def _():
            @pl.when(top)
            def _():
                down(n, True).start()

            @pl.when(jnp.logical_not(top))
            def _():
                down(n, False).wait_recv()
                downs[n] = add_low(downs[n], parts[below, rows_of(n), :])
                down(n, False).start()

        @pl.when(k == groups)
        def _():
            for i in range(size - 1):
                dot_copy(i).start()
                col_copy(i).start()

        return 0

    lax.fori_loop(0, max(count, groups + 1), tick, 0)

    for i in range(size - 1):
        dot_copy(i).wait()
        col_copy(i).wait()
    total = dots[0]
    for j in range(1, size):
        total = total + dots[j]
    dot_o[...] = total
    column = cols[here]
    for j in range(size - 1):
        column = column + cols[size + j]
    gain_o[...] = column

    def last(c, _):
        part = pl.ds(pl.multiple_of(c * chunk, chunk), chunk)
        m, n = (size - 1 - here) * groups + c, here * groups + c
        out_o[part, :] = parts[here, part, :].astype(F32)

        @pl.when(jnp.logical_not(bottom))
        def _():
            up(m, False).wait_recv()
            out_o[part, :] += ups[m].astype(F32)

        @pl.when(jnp.logical_not(top))
        def _():
            down(n, False).wait_recv()
            out_o[part, :] += downs[n].astype(F32)

        return 0

    lax.fori_loop(0, groups, last, 0)

    def drain(m, _):
        @pl.when(size - 1 - lax.div(m, groups) > here)
        def _():
            up(m, False).wait_send()

        @pl.when(lax.div(m, groups) < here)
        def _():
            down(m, False).wait_send()

        return 0

    lax.fori_loop(0, count, drain, 0)


def input_gradient(size, grads, inv, gain, w_query, w_key, w_value, x, chunk, after):
    rows, features = x.shape
    width, groups = features // size, rows // chunk
    count = (size - 1) * groups
    anywhere, vmem = pl.BlockSpec(memory_space=pl.ANY), pl.BlockSpec(memory_space=pltpu.VMEM)
    shape, dma = jax.ShapeDtypeStruct, pltpu.SemaphoreType.DMA

    def kernel(*refs):
        input_kernel(size, chunk, *refs[:7], *refs[7 + len(after) :])

    return pl.pallas_call(
        kernel,
        in_specs=[vmem] * 3 + [anywhere] * (4 + len(after)),
        out_specs=[vmem] * 3,
        out_shape=[shape((rows, width), F32), shape((8, rows), F32), shape((8, width), F32)],
        scratch_shapes=[
            pltpu.VMEM((size, rows, width), BF),
            pltpu.VMEM((count, chunk, width), BF),
            pltpu.VMEM((count, chunk, width), BF),
            pltpu.VMEM((2, chunk, features), BF),
            pltpu.VMEM(w_query.shape, BF),
            pltpu.VMEM(w_key.shape, BF),
            pltpu.VMEM(w_value.shape, BF),
            pltpu.VMEM((size, 8, rows), F32),
            pltpu.VMEM((2 * size - 1, 8, width), F32),
            dma((count,)),
            dma((count,)),
            dma((count,)),
            dma((count,)),
            dma((size - 1,)),
            dma((size - 1,)),
            dma((size - 1,)),
            dma((size - 1,)),
            dma((3,)),
            dma((2,)),
        ],
        compiler_params=pltpu.CompilerParams(
            collective_id=4, has_side_effects=True, vmem_limit_bytes=VMEM_LIMIT
        ),
        cost_estimate=pl.CostEstimate(
            flops=2 * rows * features * grads.shape[0],
            bytes_accessed=20 << 20,
            transcendentals=rows,
        ),
        name="input_gradient",
    )(grads, inv, gain, w_query, w_key, w_value, x, *after)


class Line:
    def __init__(self, size):
        self.size = size
        self.here = lax.axis_index("tensor")
        self.up = [(i, i + 1) for i in range(size - 1)]
        self.down = [(i + 1, i) for i in range(size - 1)]

    def gather(self, own):
        size, here, width = self.size, self.here, own.shape[1]
        full = jnp.zeros((own.shape[0], size * width), own.dtype)
        full = lax.dynamic_update_slice(full, own, (0, here * width))
        rising, falling = [], []
        a = b = own
        for _ in range(size - 1):
            a = lax.ppermute(a, "tensor", self.up)
            b = lax.ppermute(b, "tensor", self.down)
            rising.append(a)
            falling.append(b)
        for s in range(size - 1):
            slot = lax.rem(here - 1 - s + size, size)
            block = jnp.where(here > s, rising[s], falling[size - 2 - s])
            full = lax.dynamic_update_slice(full, block, (0, slot * width))
        return full

    def scatter(self, partial_value, width):
        size, here = self.size, self.here

        def block(index):
            start = jnp.clip(index, 0, size - 1) * width
            return lax.dynamic_slice_in_dim(partial_value, start, width, 1)

        a = b = None
        for s in range(size - 1):
            up = block(here + (size - 1 - s))
            down = block(here - (size - 1 - s))
            if s:
                up = (up.astype(F32) + a.astype(F32)).astype(BF)
                down = (down.astype(F32) + b.astype(F32)).astype(BF)
            a = lax.ppermute(up, "tensor", self.up)
            b = lax.ppermute(down, "tensor", self.down)
        return block(here).astype(F32) + a.astype(F32) + b.astype(F32)


def rotate(vectors, cos_tab, sin_tab):
    lower = vectors[:, : HD // 2]
    upper = vectors[:, HD // 2 :]
    return jnp.concatenate([lower * cos_tab - upper * sin_tab, upper * cos_tab + lower * sin_tab], 1)


def local(
    axes,
    layer_input_hidden,
    cotangent,
    valid_mask,
    span_starts,
    gain_attn,
    w_query,
    w_key,
    w_value,
    w_out,
    gain_mlp,
    w_gate,
    w_up,
    w_down,
):
    line = Line(axes["tensor"])
    here = line.here
    _, rows, width = layer_input_hidden.shape
    features = width * line.size
    kvs = w_key.shape[1] // HD
    heads = w_query.shape[1] // HD
    place = lax.axis_index("context")
    offset = place * rows
    own_columns = here * width

    def own(a):
        return lax.dynamic_slice_in_dim(a, own_columns, width, 1)

    position = offset + jnp.arange(rows, dtype=jnp.int32)
    length = jnp.sum(valid_mask[0])
    starts = span_starts[0]
    last = position
    for k in range(starts.shape[0]):
        inside = (position >= starts[k]) & (position < starts[k] + PIC)
        last = jnp.maximum(last, jnp.where(inside, starts[k] + PIC - 1, 0))
    kend = jnp.minimum(last + 1, length)[None, :]
    keep = (position < length).astype(F32)[:, None]
    inverse_freq = rope_base ** (-2.0 * jnp.arange(HD // 2, dtype=F32) / HD)
    angles = inverse_freq[:, None] * position.astype(F32)[None, :]
    cos_tab, sin_tab = jnp.cos(angles), jnp.sin(angles)

    x_own = layer_input_hidden[0]
    gain_own = jnp.concatenate([gain_attn[None], gain_mlp[None], jnp.zeros((6, width), F32)])
    x_low, normed_a, inv_a, gains, query_t, both = project(
        axes, x_own, gain_own, cos_tab, sin_tab, w_query, w_key, w_value, GROUP_ROWS
    )
    gain_m = gains[1:2]
    kt_all, vt_all = both[:kvs], both[kvs:]
    k_all, v_all = jnp.swapaxes(kt_all, 1, 2), jnp.swapaxes(vt_all, 1, 2)
    cot = line.gather(jnp.where(inv_a[0, 0] >= 0.0, cotangent[0], 0.0))

    mixed, lse = attend_forward(query_t, k_all, vt_all, kend)
    mixed_t = mixed.reshape(heads * HD, rows)
    normed_m, act, gg, gu, down_part, back_part, middle, attn_square = feed_forward(
        line.size, mixed_t, keep, gain_m, w_out, w_gate, w_up, w_down, x_low, cot, GROUP_ROWS, HOP_ROWS
    )
    grad_down = ein("sf,sd->fd", act, cot).astype(BF)
    grad_gate = ein("sd,sf->df", normed_m, gg).astype(BF)
    grad_up = ein("sd,sf->df", normed_m, gu).astype(BF)
    grad_middle, grad_attn, grad_mixed, gain_m_rows = norm_back(
        line.size,
        back_part,
        keep,
        gain_m,
        w_out,
        middle,
        cot,
        GROUP_ROWS,
        HOP_ROWS,
        (grad_down, grad_gate, grad_up),
    )
    grad_out = ein("xs,sd->xd", mixed_t, grad_attn).astype(BF)
    grad_mixed = grad_mixed.reshape(heads, HD, rows)
    grad_q, grad_k, grad_v = attend_backward(
        query_t, grad_mixed, mixed, lse, k_all, kt_all, v_all, kend, (grad_out,)
    )
    middle_own, grad_middle_own = own(middle), own(grad_middle)

    ffn_out = line.scatter(down_part, width)
    layer_out = (middle_own + ffn_out).astype(BF)

    def halves(a):
        return a.astype(BF).reshape(kvs, axes["context"], rows, HD)

    dkv = jnp.concatenate([halves(grad_k), halves(grad_v)])
    dkv_own = lax.dynamic_index_in_dim(dkv, place, 1, False).astype(F32)
    if axes["context"] == 2:
        sent = lax.ppermute(
            lax.dynamic_index_in_dim(dkv, 1 - place, 1, False), "context", [(0, 1), (1, 0)]
        )
        dkv_own = dkv_own + sent.astype(F32)
    else:
        dkv_own = lax.psum_scatter(dkv, "context", scatter_dimension=1, tiled=False).astype(F32)
    dkv_t = jnp.swapaxes(dkv_own, 1, 2)
    grads = jnp.concatenate(
        [
            rotate(grad_q * SCALE, cos_tab, -sin_tab).astype(BF),
            rotate(dkv_t[:kvs] * SCALE, cos_tab, -sin_tab).astype(BF),
            dkv_t[kvs:].astype(BF),
        ]
    ).reshape(-1, rows)

    def shard(grad, dim):
        return lax.psum_scatter(grad, ("dp", "context"), scatter_dimension=dim, tiled=True)

    grad_project = ein("sd,xs->dx", normed_a, grads).astype(BF)
    down_sum = shard(grad_down, 1).astype(F32)
    gate_sum = shard(grad_gate, 0).astype(F32)
    up_sum = shard(grad_up, 0).astype(F32)
    out_sum = shard(grad_out, 1).astype(F32)
    project_sum = shard(grad_project, 0)
    cut = [heads * HD, (heads + kvs) * HD]
    query_sum, key_sum, value_sum = (a.astype(F32) for a in jnp.split(project_sum, cut, 1))

    grad_a, row_dot, gain_a_part = input_gradient(
        line.size,
        grads,
        inv_a,
        gains,
        w_query,
        w_key,
        w_value,
        x_low,
        GROUP_ROWS,
        (grad_project, ffn_out),
    )
    hat_own = x_own.astype(F32) * inv_a
    row_mean = row_dot[0][:, None] / features
    through = inv_a * (grad_a * gain_attn[None, :] - hat_own * row_mean)
    input_grad = (grad_middle_own + through).astype(BF)

    numbers = jnp.stack(
        [
            jnp.sum(keep * x_own.astype(F32) ** 2),
            jnp.sum(own(attn_square)),
            jnp.sum(ffn_out * ffn_out),
            jnp.sum(keep) / line.size,
        ]
    )
    numbers = lax.psum(numbers, ("dp", "context", "tensor"))
    gain_a_sum, gain_m_sum = lax.psum(
        (gain_a_part[0], own(gain_m_rows)[0]), ("dp", "context")
    )
    rms = jnp.sqrt(numbers[:3] / (numbers[3] * features))
    return (
        layer_out[None],
        input_grad[None],
        gain_a_sum,
        query_sum,
        key_sum,
        value_sum,
        out_sum,
        gain_m_sum,
        gate_sum,
        up_sum,
        down_sum,
        rms[0],
        rms[1],
        rms[2],
    )


def solution(mesh):
    token = P("dp", "context", "tensor")
    by_rows = P(("dp", "context"), "tensor")
    by_columns = P("tensor", ("dp", "context"))
    cols, rows, vec = P(None, "tensor"), P("tensor", None), P("tensor")
    return jax.shard_map(
        functools.partial(local, dict(mesh.shape)),
        mesh=mesh,
        in_specs=(
            token,
            token,
            P("dp", None),
            P("dp", None),
            vec,
            cols,
            cols,
            cols,
            rows,
            vec,
            cols,
            cols,
            rows,
        ),
        out_specs=(
            token,
            token,
            vec,
            by_rows,
            by_rows,
            by_rows,
            by_columns,
            vec,
            by_rows,
            by_rows,
            by_columns,
            P(),
            P(),
            P(),
        ),
        check_vma=False,
    )
```

```python
import functools
import math

import jax
import jax.numpy as jnp
from jax import lax
from jax.experimental import pallas as pl
from jax.experimental.pallas import tpu as pltpu
from jax.sharding import PartitionSpec as P

HD = 80
PIC = 256
LEAST_VALID = 1536
F32 = jnp.float32
BF = jnp.bfloat16
SCALE = HD**-0.5
SCALE2 = SCALE * math.log2(math.e)
LOWEST = -1e30
GROUP_ROWS = 256
HOP_ROWS = 64
VMEM_LIMIT = 60 << 20
KEY_ROWS_FWD = 1024
KEY_ROWS_BWD = 512

epsilon = 1e-05
rope_base = 1000000.0


def dot(a, b):
    return jnp.dot(a, b, preferred_element_type=F32)


def dot_nt(a, b):
    return lax.dot_general(a, b, (((1,), (1,)), ((), ())), preferred_element_type=F32)


def ein(spec, a, b):
    return jnp.einsum(spec, a, b, preferred_element_type=F32)


MESH_ID = pl.DeviceIdType.MESH
RING = 8
SENT = 4


def add_low(a, b):
    return (a.astype(F32) + b.astype(F32)).astype(BF)


class Sums:
    def __init__(self, size, count, part, low, high, sent, sems):
        self.size, self.count, self.part = size, count, part
        self.low, self.high, self.sent = low, high, sent
        self.low_send, self.low_recv, self.high_send, self.high_recv = sems
        self.here = lax.axis_index("tensor")

    def barrier(self):
        here, size = self.here, self.size
        barrier = pltpu.get_barrier_semaphore()

        @pl.when(here > 0)
        def _():
            pl.semaphore_signal(
                barrier, inc=1, device_id={"tensor": here - 1}, device_id_type=MESH_ID
            )

        @pl.when(here < size - 1)
        def _():
            pl.semaphore_signal(
                barrier, inc=1, device_id={"tensor": here + 1}, device_id_type=MESH_ID
            )

        @pl.when((here > 0) & (here < size - 1))
        def _():
            pl.semaphore_wait(barrier, 2)

        @pl.when((here == 0) | (here == size - 1))
        def _():
            pl.semaphore_wait(barrier, 1)

    def up(self, c):
        slot = lax.rem(c, RING)
        return pltpu.make_async_remote_copy(
            src_ref=self.low.at[slot],
            dst_ref=self.low.at[slot],
            send_sem=self.low_send.at[slot],
            recv_sem=self.low_recv.at[slot],
            device_id={"tensor": self.here + 1},
            device_id_type=MESH_ID,
        )

    def down(self, c):
        slot, mine = lax.rem(c, RING), lax.rem(c, SENT)
        return pltpu.make_async_remote_copy(
            src_ref=self.sent.at[mine],
            dst_ref=self.high.at[slot],
            send_sem=self.high_send.at[mine],
            recv_sem=self.high_recv.at[slot],
            device_id={"tensor": self.here - 1},
            device_id_type=MESH_ID,
        )

    def tick(self, k):
        here, size, count = self.here, self.size, self.count
        bottom, top = here == 0, here == size - 1
        c = k - here

        @pl.when((c >= 0) & (c < count))
        def _():
            slot = lax.rem(c, RING)

            @pl.when(bottom)
            def _():
                self.low[slot] = self.part(c)

            @pl.when(jnp.logical_not(bottom))
            def _():
                self.up(c).wait_recv()
                self.low[slot] = add_low(self.low[slot], self.part(c))

            @pl.when(jnp.logical_not(top))
            def _():
                self.up(c).start()

        d = k - (size - 1 - here)

        @pl.when((d >= 0) & (d < count))
        def _():
            slot, mine = lax.rem(d, RING), lax.rem(d, SENT)

            @pl.when(top)
            def _():
                self.sent[mine] = self.part(d)

            @pl.when(jnp.logical_not(top))
            def _():
                self.down(d).wait_recv()

                @pl.when(jnp.logical_not(bottom))
                def _():
                    self.sent[mine] = add_low(self.high[slot], self.part(d))

            @pl.when(jnp.logical_not(bottom))
            def _():
                self.down(d).start()

        @pl.when((c >= 2) & (c < count + 2) & jnp.logical_not(top))
        def _():
            self.up(c - 2).wait_send()

        @pl.when((d >= 2) & (d < count + 2) & jnp.logical_not(bottom))
        def _():
            self.down(d - 2).wait_send()

    def total(self, c, then):
        slot = lax.rem(c, RING)
        top = self.here == self.size - 1

        @pl.when(top)
        def _():
            then(self.low[slot].astype(F32))

        @pl.when(jnp.logical_not(top))
        def _():
            then(self.low[slot].astype(F32) + self.high[slot].astype(F32))


def sum_scratch(hop, features):
    return [
        pltpu.VMEM((RING, hop, features), BF),
        pltpu.VMEM((RING, hop, features), BF),
        pltpu.VMEM((SENT, hop, features), BF),
        pltpu.SemaphoreType.DMA((RING,)),
        pltpu.SemaphoreType.DMA((RING,)),
        pltpu.SemaphoreType.DMA((SENT,)),
        pltpu.SemaphoreType.DMA((RING,)),
    ]


def tile_of(n, most):
    for tile in range(most, 0, -128):
        if n % tile == 0:
            return tile
    return n


def ffn_kernel(
    size, hop, chunk,
    mixed, keep, gain, w_out, w_gate, w_up, w_down, x, cot,
    normed_o, act_o, gg_o, gu_o, ffn_o, back_o, middle_o, square_o,
    low, high, sent, low_send, low_recv, high_send, high_recv,
    wo, wg, wu, wd, parts, normed, xs, cots, mids, act, gg, gu, ffn, back, split,
    w_sem, x_sem, cot_sem, normed_sem, mid_sem, act_sem, ffn_sem,
):
    rows, features = x.shape
    hidden = w_gate.shape[1]
    count, per, groups = rows // hop, chunk // hop, rows // chunk
    tile_f, tile_d = tile_of(hidden, 256), tile_of(features, 256)
    tiles_f, tiles_d = hidden // tile_f, features // tile_d
    half_f, half_d = -(-tiles_f // 2), -(-tiles_d // 2)
    lag = size - 1 + per - 1
    ticks = max(per * groups + lag, count + size)

    def part(c):
        return parts[lax.rem(lax.div(c, per), 2), pl.ds(pl.multiple_of(lax.rem(c, per) * hop, hop), hop), :]

    sums = Sums(size, count, part, low, high, sent, (low_send, low_recv, high_send, high_recv))
    loads = [
        pltpu.make_async_copy(a, b, w_sem.at[i])
        for i, (a, b) in enumerate(((w_out, wo), (w_gate, wg), (w_up, wu), (w_down, wd)))
    ]
    for load in loads:
        load.start()

    def load_x(c):
        slot = lax.rem(c, 2)
        return pltpu.make_async_copy(x.at[pl.ds(c * hop, hop)], xs.at[slot], x_sem.at[slot])

    def load_cot(g):
        return pltpu.make_async_copy(cot.at[pl.ds(g * chunk, chunk)], cots, cot_sem)

    def save_normed(c):
        at, q = lax.rem(lax.div(c, per), 2), lax.rem(c, per)
        return pltpu.make_async_copy(
            normed.at[at, pl.ds(q * hop, hop)], normed_o.at[pl.ds(c * hop, hop)], normed_sem.at[at, q]
        )

    def save_mid(c):
        slot = lax.rem(c, 2)
        return pltpu.make_async_copy(mids.at[slot], middle_o.at[pl.ds(c * hop, hop)], mid_sem.at[slot])

    def save_act(g):
        return [
            pltpu.make_async_copy(a, b.at[pl.ds(g * chunk, chunk)], act_sem.at[i])
            for i, (a, b) in enumerate(((act, act_o), (gg, gg_o), (gu, gu_o)))
        ]

    def save_ffn(g):
        part = pl.ds(g * chunk, chunk)
        return [
            pltpu.make_async_copy(split, ffn_o.at[:, part], ffn_sem.at[0]),
            pltpu.make_async_copy(back, back_o.at[part], ffn_sem.at[1]),
        ]

    def project(g):
        at = lax.rem(g, 2)
        lhs = mixed[:, pl.ds(pl.multiple_of(g * chunk, chunk), chunk)]

        def one(j, _):
            cols = pl.ds(pl.multiple_of(j * tile_d, tile_d), tile_d)
            parts[at, :, cols] = lax.dot_general(
                lhs, wo[:, cols], (((0,), (0,)), ((), ())), preferred_element_type=F32
            ).astype(BF)
            return 0

        lax.fori_loop(0, tiles_d, one, 0)

    load_x(0).start()
    load_cot(0).start()
    square_o[...] = jnp.zeros_like(square_o)
    loads[0].wait()
    project(0)
    sums.barrier()

    def finish(c):
        slot = lax.rem(c, 2)
        load_x(c).wait()

        @pl.when(c + 1 < count)
        def _():
            load_x(c + 1).start()

        @pl.when(c >= 2)
        def _():
            save_mid(c - 2).wait()

        @pl.when(c >= 2 * per)
        def _():
            save_normed(c - 2 * per).wait()

        kept = keep[pl.ds(pl.multiple_of(c * hop, hop), hop), :]

        def then(total):
            out = kept * total
            square_o[...] += jnp.sum(out * out, 0, keepdims=True)
            mids[slot] = xs[slot].astype(F32) + out

        sums.total(c, then)
        mid = mids[slot]
        inv = lax.rsqrt(jnp.sum(mid * mid, 1, keepdims=True) / features + epsilon)
        at = lax.rem(lax.div(c, per), 2)
        normed[at, pl.ds(pl.multiple_of(lax.rem(c, per) * hop, hop), hop), :] = (
            mid * inv * gain[...]
        ).astype(BF)
        save_mid(c).start()
        save_normed(c).start()

    def inner(g, lo, hi):
        at = lax.rem(g, 2)
        kept = keep[pl.ds(pl.multiple_of(g * chunk, chunk), chunk), :]

        def one(j, _):
            cols = pl.ds(pl.multiple_of(j * tile_f, tile_f), tile_f)
            gate = dot(normed[at], wg[:, cols])
            up = dot(normed[at], wu[:, cols])
            grad = dot_nt(cots[...], wd[cols, :]) * kept
            sig = jax.nn.sigmoid(gate)
            silu = gate * sig
            act[:, cols] = (silu * up * kept).astype(BF)
            gg[:, cols] = (grad * up * (sig + silu * (1.0 - sig))).astype(BF)
            gu[:, cols] = (grad * silu).astype(BF)
            return 0

        lax.fori_loop(lo, hi, one, 0)

    def outer(g, lo, hi):
        def one(j, _):
            cols = pl.ds(pl.multiple_of(j * tile_d, tile_d), tile_d)
            ffn[:, cols] = dot(act[...], wd[:, cols]).astype(BF)
            back[:, cols] = (dot_nt(gg[...], wg[cols, :]) + dot_nt(gu[...], wu[cols, :])).astype(BF)
            return 0

        lax.fori_loop(lo, hi, one, 0)

    def tick(k, _):
        sums.tick(k)
        c = k - (size - 1)

        @pl.when((c >= 0) & (c < count))
        def _():
            finish(c)

        ahead = k + 2

        @pl.when((lax.rem(ahead, per) == 0) & (ahead < count))
        def _():
            project(lax.div(ahead, per))

        s = k - lag
        g, stage = lax.div(s, per), lax.rem(s, per)
        going = (s >= 0) & (g < groups)

        @pl.when(going & (stage == 0))
        def _():
            @pl.when(g == 0)
            def _():
                for load in loads[1:]:
                    load.wait()

            load_cot(g).wait()

            @pl.when(g > 0)
            def _():
                for copy in save_act(g - 1):
                    copy.wait()

            inner(g, 0, half_f)

        @pl.when(going & (stage == 1))
        def _():
            inner(g, half_f, tiles_f)
            for copy in save_act(g):
                copy.start()

            @pl.when(g + 1 < groups)
            def _():
                load_cot(g + 1).start()

        @pl.when(going & (stage == 2))
        def _():
            @pl.when(g > 0)
            def _():
                for copy in save_ffn(g - 1):
                    copy.wait()

            outer(g, 0, half_d)

        @pl.when(going & (stage == 3))
        def _():
            outer(g, half_d, tiles_d)
            for j in range(size):
                split[j] = ffn[:, j * (features // size) : (j + 1) * (features // size)]
            for copy in save_ffn(g):
                copy.start()

        return 0

    lax.fori_loop(0, ticks, tick, 0)
    for copy in save_act(groups - 1) + save_ffn(groups - 1):
        copy.wait()
    for c in range(count - 2, count):
        save_mid(c).wait()
    for c in range(count - 2 * per, count):
        save_normed(c).wait()


def feed_forward(size, mixed, keep, gain, w_out, w_gate, w_up, w_down, x, cot, chunk, hop):
    rows, features = x.shape
    hidden = w_gate.shape[1]
    per = chunk // hop
    assert per == 4
    anywhere, vmem = pl.BlockSpec(memory_space=pl.ANY), pl.BlockSpec(memory_space=pltpu.VMEM)
    shape = jax.ShapeDtypeStruct
    return pl.pallas_call(
        functools.partial(ffn_kernel, size, hop, chunk),
        in_specs=[vmem] * 3 + [anywhere] * 6,
        out_specs=[anywhere] * 7 + [vmem],
        out_shape=[
            shape((rows, features), BF),
            shape((rows, hidden), BF),
            shape((rows, hidden), BF),
            shape((rows, hidden), BF),
            shape((size, rows, features // size), BF),
            shape((rows, features), BF),
            shape((rows, features), F32),
            shape((1, features), F32),
        ],
        scratch_shapes=sum_scratch(hop, features)
        + [
            pltpu.VMEM(w_out.shape, BF),
            pltpu.VMEM(w_gate.shape, BF),
            pltpu.VMEM(w_up.shape, BF),
            pltpu.VMEM(w_down.shape, BF),
            pltpu.VMEM((2, chunk, features), BF),
            pltpu.VMEM((2, chunk, features), BF),
            pltpu.VMEM((2, hop, features), BF),
            pltpu.VMEM((chunk, features), BF),
            pltpu.VMEM((2, hop, features), F32),
            pltpu.VMEM((chunk, hidden), BF),
            pltpu.VMEM((chunk, hidden), BF),
            pltpu.VMEM((chunk, hidden), BF),
            pltpu.VMEM((chunk, features), BF),
            pltpu.VMEM((chunk, features), BF),
            pltpu.VMEM((size, chunk, features // size), BF),
            pltpu.SemaphoreType.DMA((4,)),
            pltpu.SemaphoreType.DMA((2,)),
            pltpu.SemaphoreType.DMA,
            pltpu.SemaphoreType.DMA((2, per)),
            pltpu.SemaphoreType.DMA((2,)),
            pltpu.SemaphoreType.DMA((3,)),
            pltpu.SemaphoreType.DMA((2,)),
        ],
        compiler_params=pltpu.CompilerParams(
            collective_id=1, has_side_effects=True, vmem_limit_bytes=VMEM_LIMIT
        ),
        cost_estimate=pl.CostEstimate(
            flops=2 * rows * features * (6 * hidden + w_out.shape[0]),
            bytes_accessed=80 << 20,
            transcendentals=rows * hidden,
        ),
        name="feed_forward",
    )(mixed, keep, gain, w_out, w_gate, w_up, w_down, x, cot)


def back_kernel(
    size, hop, chunk,
    parts, keep, gain, w_out, middle, cot,
    grad_o, grad_low_o, mixed_o, gain_o,
    low, high, sent, low_send, low_recv, high_send, high_recv,
    wo, mids, cots, grads, grads_low,
    w_sem, mid_sem, cot_sem, grad_sem, grad_low_sem,
):
    rows, features = middle.shape
    count, per, groups = rows // hop, chunk // hop, rows // chunk
    ticks = max(count + size, per * (groups - 1) + size - 1 + per)

    def part(c):
        return parts[pl.ds(pl.multiple_of(c * hop, hop), hop), :]

    sums = Sums(size, count, part, low, high, sent, (low_send, low_recv, high_send, high_recv))
    load_w = pltpu.make_async_copy(w_out, wo, w_sem)
    load_w.start()

    def load_row(c):
        slot = lax.rem(c, 2)
        return [
            pltpu.make_async_copy(middle.at[pl.ds(c * hop, hop)], mids.at[slot], mid_sem.at[slot]),
            pltpu.make_async_copy(cot.at[pl.ds(c * hop, hop)], cots.at[slot], cot_sem.at[slot]),
        ]

    def save_grad(c):
        slot = lax.rem(c, 2)
        return pltpu.make_async_copy(grads.at[slot], grad_o.at[pl.ds(c * hop, hop)], grad_sem.at[slot])

    def save_low(c):
        q = lax.rem(c, per)
        return pltpu.make_async_copy(
            grads_low.at[pl.ds(q * hop, hop)], grad_low_o.at[pl.ds(c * hop, hop)], grad_low_sem.at[q]
        )

    for copy in load_row(0):
        copy.start()
    gain_o[...] = jnp.zeros_like(gain_o)
    sums.barrier()

    def finish(c):
        slot = lax.rem(c, 2)
        for copy in load_row(c):
            copy.wait()

        @pl.when(c + 1 < count)
        def _():
            for copy in load_row(c + 1):
                copy.start()

        @pl.when(c >= 2)
        def _():
            save_grad(c - 2).wait()

        @pl.when(c >= per)
        def _():
            save_low(c - per).wait()

        kept = keep[pl.ds(pl.multiple_of(c * hop, hop), hop), :]
        mid = mids[slot]
        inv = lax.rsqrt(jnp.sum(mid * mid, 1, keepdims=True) / features + epsilon)
        hat = mid * inv

        def then(total):
            gain_o[...] += jnp.sum(total * hat, 0, keepdims=True)
            weighted = total * gain[...]
            mean = jnp.sum(weighted * hat, 1, keepdims=True) / features
            grads[slot] = cots[slot].astype(F32) + inv * (weighted - hat * mean)

        sums.total(c, then)
        grads_low[pl.ds(pl.multiple_of(lax.rem(c, per) * hop, hop), hop), :] = (
            kept * grads[slot]
        ).astype(BF)
        save_grad(c).start()
        save_low(c).start()

    def tick(k, _):
        sums.tick(k)
        c = k - (size - 1)

        @pl.when((c >= 0) & (c < count))
        def _():
            finish(c)

            @pl.when(lax.rem(c, per) == per - 1)
            def _():
                g = lax.div(c, per)

                @pl.when(g == 0)
                def _():
                    load_w.wait()

                mixed_o[:, pl.ds(pl.multiple_of(g * chunk, chunk), chunk)] = dot_nt(
                    wo[...], grads_low[...]
                ).astype(BF)

        return 0

    lax.fori_loop(0, ticks, tick, 0)
    for c in range(count - 2, count):
        save_grad(c).wait()
    for c in range(count - per, count):
        save_low(c).wait()


def norm_back(size, parts, keep, gain, w_out, middle, cot, chunk, hop, after):
    rows, features = middle.shape
    per = chunk // hop
    anywhere, vmem = pl.BlockSpec(memory_space=pl.ANY), pl.BlockSpec(memory_space=pltpu.VMEM)
    shape = jax.ShapeDtypeStruct

    def kernel(*refs):
        back_kernel(size, hop, chunk, *refs[:6], *refs[6 + len(after) :])

    return pl.pallas_call(
        kernel,
        in_specs=[vmem] * 3 + [anywhere] * (3 + len(after)),
        out_specs=[anywhere] * 2 + [vmem] * 2,
        out_shape=[
            shape((rows, features), F32),
            shape((rows, features), BF),
            shape((w_out.shape[0], rows), BF),
            shape((1, features), F32),
        ],
        scratch_shapes=sum_scratch(hop, features)
        + [
            pltpu.VMEM(w_out.shape, BF),
            pltpu.VMEM((2, hop, features), F32),
            pltpu.VMEM((2, hop, features), BF),
            pltpu.VMEM((2, hop, features), F32),
            pltpu.VMEM((chunk, features), BF),
            pltpu.SemaphoreType.DMA,
            pltpu.SemaphoreType.DMA((2,)),
            pltpu.SemaphoreType.DMA((2,)),
            pltpu.SemaphoreType.DMA((2,)),
            pltpu.SemaphoreType.DMA((per,)),
        ],
        compiler_params=pltpu.CompilerParams(
            collective_id=2, has_side_effects=True, vmem_limit_bytes=VMEM_LIMIT
        ),
        cost_estimate=pl.CostEstimate(
            flops=2 * rows * features * w_out.shape[0],
            bytes_accessed=40 << 20,
            transcendentals=rows,
        ),
        name="norm_back",
    )(parts, keep, gain, w_out, middle, cot, *after)


def greet(peers):
    barrier = pltpu.get_barrier_semaphore()
    for peer in peers:
        pl.semaphore_signal(barrier, inc=1, device_id=peer, device_id_type=MESH_ID)
    pl.semaphore_wait(barrier, len(peers))


def others(axis, size):
    here = lax.axis_index(axis)
    return [{axis: lax.rem(here + i, size)} for i in range(1, size)]


class Gather:
    def __init__(self, size, groups, chunk, own, blocks, sems):
        self.size, self.groups, self.chunk = size, groups, chunk
        self.own, self.blocks = own, blocks
        self.up_send, self.up_recv, self.down_send, self.down_recv, self.own_sem = sems
        self.steps = size - 1
        self.ticks = groups * self.steps + 1
        self.here = lax.axis_index("tensor")

    def load(self, g):
        part = pl.ds(g * self.chunk, self.chunk)
        return pltpu.make_async_copy(
            self.own.at[part], self.blocks.at[self.here, part], self.own_sem.at[g]
        )

    def load_all(self):
        for g in range(self.groups):
            self.load(g).start()

    def move(self, g, s, owner, peer, send, recv):
        block = self.blocks.at[jnp.clip(owner, 0, self.size - 1), pl.ds(g * self.chunk, self.chunk)]
        return pltpu.make_async_remote_copy(
            src_ref=block,
            dst_ref=block,
            send_sem=send.at[g, s],
            recv_sem=recv.at[g, s],
            device_id={"tensor": peer},
            device_id_type=MESH_ID,
        )

    def up(self, g, s):
        return self.move(g, s, self.here - s, self.here + 1, self.up_send, self.up_recv)

    def down(self, g, s):
        return self.move(g, s, self.here + s, self.here - 1, self.down_send, self.down_recv)

    def each(self, g, s, act):
        @pl.when((self.here >= s) & (self.here < self.size - 1))
        def _():
            act(self.up(g, s))

        @pl.when((self.here + s < self.size) & (self.here > 0))
        def _():
            act(self.down(g, s))

    def send(self, g, s):
        self.each(g, s, lambda copy: copy.start())

    def receive(self, g, s):
        @pl.when(self.here - 1 - s >= 0)
        def _():
            self.up(g, s).wait_recv()

        @pl.when(self.here + 1 + s < self.size)
        def _():
            self.down(g, s).wait_recv()

    def begin(self):
        self.load(0).wait()
        self.send(0, 0)

    def tick(self, k, then):
        g, s = lax.div(k, self.steps), lax.rem(k, self.steps)

        @pl.when((s > 0) & (g < self.groups))
        def _():
            self.receive(g, s - 1)
            self.send(g, s)

        @pl.when((s == self.steps - 1) & (g + 1 < self.groups))
        def _():
            self.load(g + 1).wait()
            self.send(g + 1, 0)

        @pl.when((s == 0) & (g > 0) & (g <= self.groups))
        def _():
            self.receive(g - 1, self.steps - 1)
            then(g - 1)

    def drain(self):
        for g in range(self.groups):
            for s in range(self.steps):
                self.each(g, s, lambda copy: copy.wait_send())


def gather_scratch(size, rows, width, chunk):
    dma, groups = pltpu.SemaphoreType.DMA, rows // chunk
    return [pltpu.VMEM((size, rows, width), BF)] + [dma((groups, size - 1))] * 4 + [dma((groups,))]


class Scatter:
    def __init__(self, size, groups, chunk, parts, ups, downs, sems):
        self.size, self.groups, self.chunk = size, groups, chunk
        self.parts, self.ups, self.downs = parts, ups, downs
        self.up_send, self.up_recv, self.down_send, self.down_recv = sems
        self.count = (size - 1) * groups
        self.here = lax.axis_index("tensor")

    def rows(self, m):
        return pl.ds(pl.multiple_of(lax.rem(m, self.groups) * self.chunk, self.chunk), self.chunk)

    def up(self, m, first):
        owner = self.size - 1 - lax.div(m, self.groups)
        return pltpu.make_async_remote_copy(
            src_ref=self.parts.at[owner, self.rows(m)] if first else self.ups.at[m],
            dst_ref=self.ups.at[m],
            send_sem=self.up_send.at[m],
            recv_sem=self.up_recv.at[m],
            device_id={"tensor": self.here + 1},
            device_id_type=MESH_ID,
        )

    def down(self, m, first):
        owner = lax.div(m, self.groups)
        return pltpu.make_async_remote_copy(
            src_ref=self.parts.at[owner, self.rows(m)] if first else self.downs.at[m],
            dst_ref=self.downs.at[m],
            send_sem=self.down_send.at[m],
            recv_sem=self.down_recv.at[m],
            device_id={"tensor": self.here - 1},
            device_id_type=MESH_ID,
        )

    def tick(self, k):
        bottom, top = self.here == 0, self.here == self.size - 1
        m = k - self.here
        owner = self.size - 1 - lax.div(m, self.groups)

        @pl.when((m >= 0) & (owner > self.here))
        def _():
            @pl.when(bottom)
            def _():
                self.up(m, True).start()

            @pl.when(jnp.logical_not(bottom))
            def _():
                self.up(m, False).wait_recv()
                self.ups[m] = add_low(self.ups[m], self.parts[owner, self.rows(m), :])
                self.up(m, False).start()

        n = k - (self.size - 1 - self.here)
        below = lax.div(n, self.groups)

        @pl.when((n >= 0) & (below < self.here))
        def _():
            @pl.when(top)
            def _():
                self.down(n, True).start()

            @pl.when(jnp.logical_not(top))
            def _():
                self.down(n, False).wait_recv()
                self.downs[n] = add_low(self.downs[n], self.parts[below, self.rows(n), :])
                self.down(n, False).start()

    def finish(self, out):
        here = self.here

        def last(c, _):
            part = self.rows(c)
            m, n = (self.size - 1 - here) * self.groups + c, here * self.groups + c
            out[part, :] = self.parts[here, part, :].astype(F32)

            @pl.when(here > 0)
            def _():
                self.up(m, False).wait_recv()
                out[part, :] += self.ups[m].astype(F32)

            @pl.when(here < self.size - 1)
            def _():
                self.down(n, False).wait_recv()
                out[part, :] += self.downs[n].astype(F32)

            return 0

        lax.fori_loop(0, self.groups, last, 0)

        def drain(m, _):
            @pl.when(self.size - 1 - lax.div(m, self.groups) > here)
            def _():
                self.up(m, False).wait_send()

            @pl.when(lax.div(m, self.groups) < here)
            def _():
                self.down(m, False).wait_send()

            return 0

        lax.fori_loop(0, self.count, drain, 0)


def scatter_scratch(size, rows, width, chunk):
    count = (size - 1) * (rows // chunk)
    return [
        pltpu.VMEM((size, rows, width), BF),
        pltpu.VMEM((count, chunk, width), BF),
        pltpu.VMEM((count, chunk, width), BF),
    ] + [pltpu.SemaphoreType.DMA((count,))] * 4


def turn(u, cos_t, sin_t):
    lower, upper = u[: HD // 2], u[HD // 2 :]
    return jnp.concatenate([lower * cos_t - upper * sin_t, upper * cos_t + lower * sin_t], 0)


def flip(a):
    return a.astype(F32).T


def key_blocks(g, chunk, rows, keys, key_rows):
    start = lax.axis_index("context") * rows + g * chunk
    free = jnp.minimum(start + 1, min(LEAST_VALID, keys))
    last = jnp.minimum(start + chunk + PIC - 1, keys)
    return lax.div(free, key_rows), lax.div(last + key_rows - 1, key_rows)


def project_kernel(
    size, contexts, chunk,
    own, gain_own, cos_tab, sin_tab, w_query, w_key, w_value,
    x_o, normed_o, inv_o, gain_o, query_o, kv_o,
    xs, up_send, up_recv, down_send, down_recv, own_sem,
    gains, full, normed, kv, wq, wk, wv,
    gain_send, gain_recv, kv_send, kv_recv, w_sem, out_sem, kv_sem,
):
    here, place = lax.axis_index("tensor"), lax.axis_index("context")
    rows, width = own.shape
    features = size * width
    groups = rows // chunk
    heads, kvs = w_query.shape[1] // HD, w_key.shape[1] // HD
    line = Gather(
        size, groups, chunk, own, xs, (up_send, up_recv, down_send, down_recv, own_sem)
    )
    loads = [
        pltpu.make_async_copy(a, b, w_sem.at[i])
        for i, (a, b) in enumerate(((w_query, wq), (w_key, wk), (w_value, wv)))
    ]
    line.load_all()
    for load in loads:
        load.start()
    gains[here] = gain_own[...]
    tensor_peers, context_peers = others("tensor", size), others("context", contexts)
    greet(tensor_peers + context_peers)

    def gain_copy(i):
        return pltpu.make_async_remote_copy(
            src_ref=gains.at[here],
            dst_ref=gains.at[here],
            send_sem=gain_send.at[i],
            recv_sem=gain_recv.at[i],
            device_id=tensor_peers[i],
            device_id_type=MESH_ID,
        )

    def kv_copy(g, i):
        part = kv.at[:, :, pl.ds(pl.multiple_of(place * rows + g * chunk, chunk), chunk)]
        return pltpu.make_async_remote_copy(
            src_ref=part,
            dst_ref=part,
            send_sem=kv_send.at[g, i],
            recv_sem=kv_recv.at[g, i],
            device_id=context_peers[i],
            device_id_type=MESH_ID,
        )

    line.begin()
    for i in range(size - 1):
        gain_copy(i).start()

    def save(g):
        part = pl.ds(g * chunk, chunk)
        return [
            pltpu.make_async_copy(full, x_o.at[part], out_sem.at[0]),
            pltpu.make_async_copy(normed, normed_o.at[part], out_sem.at[1]),
        ]

    def compute(g):
        part = pl.ds(pl.multiple_of(g * chunk, chunk), chunk)

        @pl.when(g == 0)
        def _():
            for load in loads:
                load.wait()
            for i in range(size - 1):
                gain_copy(i).wait_recv()
            gain_o[...] = jnp.concatenate([gains[j] for j in range(size)], 1)

        @pl.when(g > 0)
        def _():
            for copy in save(g - 1):
                copy.wait()

        full[...] = jnp.concatenate([xs[j, part, :] for j in range(size)], 1)
        stream = full[...].astype(F32)
        inv = lax.rsqrt(jnp.sum(stream * stream, 1, keepdims=True) / features + epsilon)
        inv_o[part, :] = inv
        normed[...] = (stream * inv * gain_o[0:1, :]).astype(BF)
        for copy in save(g):
            copy.start()
        cos_t, sin_t = cos_tab[:, part], sin_tab[:, part]
        mine = pl.ds(pl.multiple_of(place * rows + g * chunk, chunk), chunk)
        key = dot(normed[...], wk[...]).T
        value = dot(normed[...], wv[...]).T
        for h in range(kvs):
            kv[h, :, mine] = turn(key[h * HD : (h + 1) * HD], cos_t, sin_t).astype(BF)
            kv[kvs + h, :, mine] = value[h * HD : (h + 1) * HD].astype(BF)
        for i in range(contexts - 1):
            kv_copy(g, i).start()
        query = dot(normed[...], wq[...]).T
        for h in range(heads):
            query_o[h, :, part] = turn(query[h * HD : (h + 1) * HD], cos_t, sin_t).astype(BF)

    def tick(k, _):
        line.tick(k, compute)
        return 0

    lax.fori_loop(0, line.ticks, tick, 0)
    for copy in save(groups - 1):
        copy.wait()
    for i in range(size - 1):
        gain_copy(i).wait_send()
    line.drain()
    for g in range(groups):
        for i in range(contexts - 1):
            kv_copy(g, i).wait()
    out = pltpu.make_async_copy(kv, kv_o, kv_sem)
    out.start()
    out.wait()


def project(axes, own, gain_own, cos_tab, sin_tab, w_query, w_key, w_value, chunk, after):
    size, contexts = axes["tensor"], axes["context"]
    rows, width = own.shape
    features, groups = size * width, rows // chunk
    heads, kvs = w_query.shape[1] // HD, w_key.shape[1] // HD
    anywhere, vmem = pl.BlockSpec(memory_space=pl.ANY), pl.BlockSpec(memory_space=pltpu.VMEM)
    shape, dma = jax.ShapeDtypeStruct, pltpu.SemaphoreType.DMA

    def kernel(*refs):
        project_kernel(size, contexts, chunk, *refs[:7], *refs[7 + len(after) :])

    return pl.pallas_call(
        kernel,
        in_specs=[anywhere] + [vmem] * 3 + [anywhere] * (3 + len(after)),
        out_specs=[anywhere] * 2 + [vmem] * 3 + [anywhere],
        out_shape=[
            shape((rows, features), BF),
            shape((rows, features), BF),
            shape((rows, 1), F32),
            shape((8, features), F32),
            shape((heads, HD, rows), BF),
            shape((2 * kvs, HD, contexts * rows), BF),
        ],
        scratch_shapes=gather_scratch(size, rows, width, chunk)
        + [
            pltpu.VMEM((size, 8, width), F32),
            pltpu.VMEM((chunk, features), BF),
            pltpu.VMEM((chunk, features), BF),
            pltpu.VMEM((2 * kvs, HD, contexts * rows), BF),
            pltpu.VMEM(w_query.shape, BF),
            pltpu.VMEM(w_key.shape, BF),
            pltpu.VMEM(w_value.shape, BF),
            dma((size - 1,)),
            dma((size - 1,)),
            dma((groups, max(contexts - 1, 1))),
            dma((groups, max(contexts - 1, 1))),
            dma((3,)),
            dma((2,)),
            dma,
        ],
        compiler_params=pltpu.CompilerParams(
            collective_id=3, has_side_effects=True, vmem_limit_bytes=VMEM_LIMIT
        ),
        cost_estimate=pl.CostEstimate(
            flops=2 * rows * features * (heads + 2 * kvs) * HD,
            bytes_accessed=20 << 20,
            transcendentals=rows,
        ),
        name="project",
    )(own, gain_own, cos_tab, sin_tab, w_query, w_key, w_value, *after)


def attend_kernel(
    size, chunk, key_rows,
    own, q, kv, kend,
    cot_o, mixed_o, lse_o,
    blocks, up_send, up_recv, down_send, down_recv, own_sem,
    full, keys_in_rows, acc, mx, sm, out_sem,
):
    rows, _ = own.shape
    heads, kvs, keys = q.shape[0], kv.shape[0] // 2, kv.shape[2]
    groups, group = rows // chunk, heads // kvs
    units = kvs * groups
    line = Gather(
        size, groups, chunk, own, blocks, (up_send, up_recv, down_send, down_recv, own_sem)
    )
    line.load_all()
    greet(others("tensor", size))
    line.begin()
    for h in range(kvs):
        keys_in_rows[h] = flip(kv[h]).astype(BF)

    def save(g):
        return pltpu.make_async_copy(full, cot_o.at[pl.ds(g * chunk, chunk)], out_sem)

    def join(g):
        @pl.when(g > 0)
        def _():
            save(g - 1).wait()

        part = pl.ds(pl.multiple_of(g * chunk, chunk), chunk)
        full[...] = jnp.concatenate([blocks[j, part, :] for j in range(size)], 1)
        save(g).start()

    def unit(u):
        pair, g = lax.div(u, groups), lax.rem(u, groups)
        part = pl.ds(pl.multiple_of(g * chunk, chunk), chunk)
        free, last = key_blocks(g, chunk, rows, keys, key_rows)
        acc[...] = jnp.zeros_like(acc)
        sm[...] = jnp.zeros_like(sm)
        mx[...] = jnp.full_like(mx, LOWEST)
        limit = kend[:, part]

        def step(masked, i, _):
            at = pl.multiple_of(i * key_rows, key_rows)
            k_blk = keys_in_rows[pair, pl.ds(at, key_rows), :]
            v_blk = kv[kvs + pair, :, pl.ds(at, key_rows)]
            if masked:
                keep = (lax.broadcasted_iota(jnp.int32, (key_rows, chunk), 0) + at) < limit
            for h in range(group):
                s = dot(k_blk, q[pair * group + h, :, part])
                if masked:
                    s = jnp.where(keep, s, LOWEST)
                old = mx[h]
                new = jnp.maximum(old, jnp.max(s, 0, keepdims=True))
                p = jnp.exp2(s * SCALE2 - new * SCALE2)
                alpha = jnp.exp2((old - new) * SCALE2)
                mx[h] = new
                sm[h] = sm[h] * alpha + jnp.sum(p, 0, keepdims=True)
                acc[h] = acc[h] * alpha + dot(v_blk, p.astype(BF))
            return 0

        lax.fori_loop(0, free, functools.partial(step, False), 0)
        lax.fori_loop(free, last, functools.partial(step, True), 0)
        for h in range(group):
            mixed_o[pair * group + h, :, part] = (acc[h] / sm[h]).astype(BF)
            lse_o[pair * group + h, :, part] = mx[h] * SCALE2 + jnp.log2(sm[h])

    def tick(k, _):
        line.tick(k, join)

        @pl.when(k < units)
        def _():
            unit(k)

        return 0

    lax.fori_loop(0, max(line.ticks, units), tick, 0)
    save(groups - 1).wait()
    line.drain()


def attend_forward(size, own, q, kv, kend, chunk):
    heads, _, rows = q.shape
    kvs, keys = kv.shape[0] // 2, kv.shape[2]
    group, width = heads // kvs, own.shape[1]
    key_rows = min(KEY_ROWS_FWD, keys)
    anywhere, vmem = pl.BlockSpec(memory_space=pl.ANY), pl.BlockSpec(memory_space=pltpu.VMEM)
    shape = jax.ShapeDtypeStruct
    return pl.pallas_call(
        functools.partial(attend_kernel, size, chunk, key_rows),
        in_specs=[anywhere] + [vmem] * 3,
        out_specs=[anywhere] + [vmem] * 2,
        out_shape=[
            shape((rows, size * width), BF),
            shape((heads, HD, rows), BF),
            shape((heads, 1, rows), F32),
        ],
        scratch_shapes=gather_scratch(size, rows, width, chunk)
        + [
            pltpu.VMEM((chunk, size * width), BF),
            pltpu.VMEM((kvs, keys, HD), BF),
            pltpu.VMEM((group, HD, chunk), F32),
            pltpu.VMEM((group, 1, chunk), F32),
            pltpu.VMEM((group, 1, chunk), F32),
            pltpu.SemaphoreType.DMA,
        ],
        compiler_params=pltpu.CompilerParams(
            collective_id=5, has_side_effects=True, vmem_limit_bytes=VMEM_LIMIT
        ),
        cost_estimate=pl.CostEstimate(
            flops=10 * heads * rows * keys * HD,
            bytes_accessed=16 << 20,
            transcendentals=heads * rows * keys,
        ),
        name="attend_forward",
    )(own, q, kv, kend)


def attend_back_kernel(
    size, contexts, chunk, key_rows,
    ffn, q, kv, kend, do, o, lse, cos_tab, sin_tab,
    grads_o, ffn_o,
    parts, ups, downs, up_send, up_recv, down_send, down_recv,
    keys_in_rows, values_in_rows, dq, dk, dv, ds_all, p_all, q_all, do_all, mine, out_kv, in_kv,
    kv_send, kv_recv, part_sem,
):
    heads, _, rows = q.shape
    kvs, keys = kv.shape[0] // 2, kv.shape[2]
    groups, group = rows // chunk, heads // kvs
    units = kvs * groups
    place = lax.axis_index("context")
    line = Scatter(
        size, groups, chunk, parts, ups, downs, (up_send, up_recv, down_send, down_recv)
    )
    load = pltpu.make_async_copy(ffn, parts, part_sem)
    load.start()
    peers = others("context", contexts)
    greet(others("tensor", size) + peers)
    for h in range(kvs):
        keys_in_rows[h] = flip(kv[h]).astype(BF)
        values_in_rows[h] = flip(kv[kvs + h]).astype(BF)
    load.wait()

    def half(of):
        at = pl.ds(pl.multiple_of(of * rows, rows), rows)
        return dk[at, :].T, dv[at, :].T

    def kv_copy(pair, i):
        return pltpu.make_async_remote_copy(
            src_ref=out_kv.at[pair, i],
            dst_ref=in_kv.at[pair, i],
            send_sem=kv_send.at[pair, i],
            recv_sem=kv_recv.at[pair, i],
            device_id=peers[i],
            device_id_type=MESH_ID,
        )

    def unit(u):
        pair, g = lax.div(u, groups), lax.rem(u, groups)
        part = pl.ds(pl.multiple_of(g * chunk, chunk), chunk)
        free, last = key_blocks(g, chunk, rows, keys, key_rows)
        limit = kend[:, part]

        @pl.when(g == 0)
        def _():
            dk[...] = jnp.zeros_like(dk)
            dv[...] = jnp.zeros_like(dv)

        dq[...] = jnp.zeros_like(dq)
        delta = []
        for h in range(group):
            head = pair * group + h
            cols = slice(h * chunk, (h + 1) * chunk)
            q_all[:, cols] = q[head, :, part]
            do_all[:, cols] = do[head, :, part]
            delta.append(
                jnp.sum(do_all[:, cols].astype(F32) * o[head, :, part].astype(F32), 0, keepdims=True)
            )

        def step(masked, i, _):
            at = pl.multiple_of(i * key_rows, key_rows)
            k_blk = keys_in_rows[pair, pl.ds(at, key_rows), :]
            v_blk = values_in_rows[pair, pl.ds(at, key_rows), :]
            kt_blk = kv[pair, :, pl.ds(at, key_rows)]
            if masked:
                keep = (lax.broadcasted_iota(jnp.int32, (key_rows, chunk), 0) + at) < limit
            for h in range(group):
                cols = slice(h * chunk, (h + 1) * chunk)
                s = dot(k_blk, q_all[:, cols])
                p = jnp.exp2(s * SCALE2 - lse[pair * group + h, :, part])
                if masked:
                    p = jnp.where(keep, p, 0.0)
                dp = dot(v_blk, do_all[:, cols])
                ds = (p * (dp - delta[h])).astype(BF)
                p_all[:, cols] = p.astype(BF)
                ds_all[:, cols] = ds
                dq[h] += dot(kt_blk, ds)
            dk[pl.ds(at, key_rows), :] += dot_nt(ds_all[...], q_all[...])
            dv[pl.ds(at, key_rows), :] += dot_nt(p_all[...], do_all[...])
            return 0

        lax.fori_loop(0, free, functools.partial(step, False), 0)
        lax.fori_loop(free, last, functools.partial(step, True), 0)
        for h in range(group):
            grads_o[pair * group + h, :, part] = turn(
                dq[h] * SCALE, cos_tab[:, part], -sin_tab[:, part]
            ).astype(BF)

        @pl.when(g == groups - 1)
        def _():
            for i in range(contexts - 1):
                key, value = half(peers[i]["context"])
                out_kv[pair, i, 0] = key.astype(BF)
                out_kv[pair, i, 1] = value.astype(BF)
                kv_copy(pair, i).start()
            mine[pair, 0], mine[pair, 1] = half(place)

    def tick(k, _):
        line.tick(k)

        @pl.when(k < units)
        def _():
            unit(k)

        return 0

    lax.fori_loop(0, max(line.count, units), tick, 0)
    for pair in range(kvs):
        key, value = mine[pair, 0], mine[pair, 1]
        for i in range(contexts - 1):
            kv_copy(pair, i).wait()
            key = key + in_kv[pair, i, 0].astype(F32)
            value = value + in_kv[pair, i, 1].astype(F32)
        grads_o[heads + pair] = turn(key * SCALE, cos_tab[...], -sin_tab[...]).astype(BF)
        grads_o[heads + kvs + pair] = value.astype(BF)
    line.finish(ffn_o)


def attend_backward(axes, ffn, q, kv, kend, do, o, lse, cos_tab, sin_tab, chunk, after):
    size, contexts = axes["tensor"], axes["context"]
    heads, _, rows = q.shape
    kvs, keys = kv.shape[0] // 2, kv.shape[2]
    group, width = heads // kvs, ffn.shape[2]
    key_rows = min(KEY_ROWS_BWD, keys)
    anywhere, vmem = pl.BlockSpec(memory_space=pl.ANY), pl.BlockSpec(memory_space=pltpu.VMEM)
    shape, dma = jax.ShapeDtypeStruct, pltpu.SemaphoreType.DMA
    slots = max(contexts - 1, 1)

    def kernel(*refs):
        attend_back_kernel(size, contexts, chunk, key_rows, *refs[:9], *refs[9 + len(after) :])

    return pl.pallas_call(
        kernel,
        in_specs=[anywhere] + [vmem] * 8 + [anywhere] * len(after),
        out_specs=[vmem] * 2,
        out_shape=[shape((heads + 2 * kvs, HD, rows), BF), shape((rows, width), F32)],
        scratch_shapes=scatter_scratch(size, rows, width, chunk)
        + [
            pltpu.VMEM((kvs, keys, HD), BF),
            pltpu.VMEM((kvs, keys, HD), BF),
            pltpu.VMEM((group, HD, chunk), F32),
            pltpu.VMEM((keys, HD), F32),
            pltpu.VMEM((keys, HD), F32),
            pltpu.VMEM((key_rows, group * chunk), BF),
            pltpu.VMEM((key_rows, group * chunk), BF),
            pltpu.VMEM((HD, group * chunk), BF),
            pltpu.VMEM((HD, group * chunk), BF),
            pltpu.VMEM((kvs, 2, HD, rows), F32),
            pltpu.VMEM((kvs, slots, 2, HD, rows), BF),
            pltpu.VMEM((kvs, slots, 2, HD, rows), BF),
            dma((kvs, slots)),
            dma((kvs, slots)),
            dma,
        ],
        compiler_params=pltpu.CompilerParams(
            collective_id=6, has_side_effects=True, vmem_limit_bytes=VMEM_LIMIT
        ),
        cost_estimate=pl.CostEstimate(
            flops=16 * heads * rows * keys * HD,
            bytes_accessed=16 << 20,
            transcendentals=heads * rows * keys,
        ),
        name="attend_backward",
    )(ffn, q, kv, kend, do, o, lse, cos_tab, sin_tab, *after)


def input_kernel(
    axes, chunk,
    grads, inv, gain, extra, w_query, w_key, w_value, x,
    out_o, dot_o, sum_o,
    parts, ups, downs, up_send, up_recv, down_send, down_recv,
    xs, wq, wk, wv, dots, cols, cols_in, world,
    dot_send, dot_recv, col_send, col_recv, world_send, world_recv, w_sem, x_sem,
):
    size = axes["tensor"]
    here = lax.axis_index("tensor")
    rows, features = x.shape
    width, groups = features // size, rows // chunk
    nq, nk = w_query.shape[1], w_key.shape[1]
    line = Scatter(
        size, groups, chunk, parts, ups, downs, (up_send, up_recv, down_send, down_recv)
    )
    loads = [
        pltpu.make_async_copy(a, b, w_sem.at[i])
        for i, (a, b) in enumerate(((w_query, wq), (w_key, wk), (w_value, wv)))
    ]

    def load_x(c):
        slot = lax.rem(c, 2)
        return pltpu.make_async_copy(x.at[pl.ds(c * chunk, chunk)], xs.at[slot], x_sem.at[slot])

    for load in loads:
        load.start()
    load_x(0).start()
    contexts, replicas = axes["context"], axes["dp"] * axes["context"]
    spot = lax.axis_index("dp") * contexts + lax.axis_index("context")
    peers = others("tensor", size)
    far = [lax.rem(spot + i, replicas) for i in range(1, replicas)]
    far = [{"dp": lax.div(i, contexts), "context": lax.rem(i, contexts)} for i in far]
    greet(peers + far)
    for load in loads:
        load.wait()
    top_row = lax.broadcasted_iota(jnp.int32, (8, width), 0) == 0

    def compute(c):
        slot = lax.rem(c, 2)
        part = pl.ds(pl.multiple_of(c * chunk, chunk), chunk)
        load_x(c).wait()

        @pl.when(c + 1 < groups)
        def _():
            load_x(c + 1).start()

        g = flip(grads[:, part]).astype(BF)
        whole = (
            dot_nt(g[:, :nq], wq[...])
            + dot_nt(g[:, nq : nq + nk], wk[...])
            + dot_nt(g[:, nq + nk :], wv[...])
        )
        hat = xs[slot].astype(F32) * inv[part, :]
        moved = whole * hat
        rowsum = jnp.sum(moved * gain[0:1, :], 1, keepdims=True)
        dots[here, :, part] = jnp.broadcast_to(rowsum, (chunk, 128)).T[:8]
        colsum = jnp.sum(moved, 0, keepdims=True)
        low = whole.astype(BF)
        for j in range(size):
            parts[j, part, :] = low[:, j * width : (j + 1) * width]
            piece = jnp.where(top_row, colsum[:, j * width : (j + 1) * width], 0.0)

            @pl.when(c == 0)
            def _():
                cols[j] = piece + extra[0]

            @pl.when(c > 0)
            def _():
                cols[j] += piece

    def copy_to(src, dst, send, recv, peer):
        return pltpu.make_async_remote_copy(
            src_ref=src,
            dst_ref=dst,
            send_sem=send,
            recv_sem=recv,
            device_id=peer,
            device_id_type=MESH_ID,
        )

    def dot_copy(i):
        mine = dots.at[here]
        return copy_to(mine, mine, dot_send.at[i], dot_recv.at[i], peers[i])

    def col_copy(i):
        src = cols.at[peers[i]["tensor"]]
        return copy_to(src, cols_in.at[here], col_send.at[i], col_recv.at[i], peers[i])

    def world_copy(i):
        mine = world.at[spot]
        return copy_to(mine, mine, world_send.at[i], world_recv.at[i], far[i])

    def tick(k, _):
        @pl.when(k < groups)
        def _():
            compute(k)

        line.tick(k)

        @pl.when(k == groups)
        def _():
            cols_in[here] = cols[here]
            for i in range(size - 1):
                dot_copy(i).start()
                col_copy(i).start()

        @pl.when(k == groups + 3)
        def _():
            for i in range(size - 1):
                dot_copy(i).wait()
                col_copy(i).wait()
            total, column = dots[0], cols_in[0]
            for j in range(1, size):
                total = total + dots[j]
                column = column + cols_in[j]
            dot_o[...] = total
            world[spot] = column + extra[1]
            for i in range(replicas - 1):
                world_copy(i).start()

        return 0

    lax.fori_loop(0, max(line.count, groups + 4), tick, 0)
    line.finish(out_o)
    for i in range(replicas - 1):
        world_copy(i).wait()
    total = world[0]
    for j in range(1, replicas):
        total = total + world[j]
    sum_o[...] = total


def input_gradient(axes, grads, inv, gain, extra, w_query, w_key, w_value, x, chunk, after):
    size, replicas = axes["tensor"], axes["dp"] * axes["context"]
    rows, features = x.shape
    width = features // size
    anywhere, vmem = pl.BlockSpec(memory_space=pl.ANY), pl.BlockSpec(memory_space=pltpu.VMEM)
    shape, dma = jax.ShapeDtypeStruct, pltpu.SemaphoreType.DMA

    def kernel(*refs):
        input_kernel(axes, chunk, *refs[:8], *refs[8 + len(after) :])

    return pl.pallas_call(
        kernel,
        in_specs=[vmem] * 4 + [anywhere] * (4 + len(after)),
        out_specs=[vmem] * 3,
        out_shape=[shape((rows, width), F32), shape((8, rows), F32), shape((8, width), F32)],
        scratch_shapes=scatter_scratch(size, rows, width, chunk)
        + [
            pltpu.VMEM((2, chunk, features), BF),
            pltpu.VMEM(w_query.shape, BF),
            pltpu.VMEM(w_key.shape, BF),
            pltpu.VMEM(w_value.shape, BF),
            pltpu.VMEM((size, 8, rows), F32),
            pltpu.VMEM((size, 8, width), F32),
            pltpu.VMEM((size, 8, width), F32),
            pltpu.VMEM((replicas, 8, width), F32),
            dma((size - 1,)),
            dma((size - 1,)),
            dma((size - 1,)),
            dma((size - 1,)),
            dma((replicas - 1,)),
            dma((replicas - 1,)),
            dma((3,)),
            dma((2,)),
        ],
        compiler_params=pltpu.CompilerParams(
            collective_id=4, has_side_effects=True, vmem_limit_bytes=VMEM_LIMIT
        ),
        cost_estimate=pl.CostEstimate(
            flops=2 * rows * features * grads.shape[0],
            bytes_accessed=20 << 20,
            transcendentals=rows,
        ),
        name="input_gradient",
    )(grads, inv, gain, extra, w_query, w_key, w_value, x, *after)


def local(
    axes,
    layer_input_hidden,
    cotangent,
    valid_mask,
    span_starts,
    gain_attn,
    w_query,
    w_key,
    w_value,
    w_out,
    gain_mlp,
    w_gate,
    w_up,
    w_down,
):
    here = lax.axis_index("tensor")
    _, rows, width = layer_input_hidden.shape
    size = axes["tensor"]
    features = width * size
    kvs = w_key.shape[1] // HD
    heads = w_query.shape[1] // HD
    place = lax.axis_index("context")
    offset = place * rows
    own_columns = here * width

    def own(a):
        return lax.dynamic_slice_in_dim(a, own_columns, width, 1)

    position = offset + jnp.arange(rows, dtype=jnp.int32)
    length = jnp.sum(valid_mask[0])
    starts = span_starts[0]
    last = position
    for k in range(starts.shape[0]):
        inside = (position >= starts[k]) & (position < starts[k] + PIC)
        last = jnp.maximum(last, jnp.where(inside, starts[k] + PIC - 1, 0))
    kend = jnp.minimum(last + 1, length)[None, :]
    keep = (position < length).astype(F32)[:, None]
    inverse_freq = rope_base ** (-2.0 * jnp.arange(HD // 2, dtype=F32) / HD)
    angles = inverse_freq[:, None] * position.astype(F32)[None, :]
    cos_tab, sin_tab = jnp.cos(angles), jnp.sin(angles)

    x_own = layer_input_hidden[0]
    gain_own = jnp.concatenate([gain_attn[None], gain_mlp[None], jnp.zeros((6, width), F32)])
    x_low, normed_a, inv_a, gains, query_t, both = project(
        axes, x_own, gain_own, cos_tab, sin_tab, w_query, w_key, w_value, GROUP_ROWS, (kend, keep)
    )
    gain_m = gains[1:2]

    cot, mixed, lse = attend_forward(size, cotangent[0], query_t, both, kend, GROUP_ROWS)
    mixed_t = mixed.reshape(heads * HD, rows)
    normed_m, act, gg, gu, down_part, back_part, middle, attn_square = feed_forward(
        size, mixed_t, keep, gain_m, w_out, w_gate, w_up, w_down, x_low, cot, GROUP_ROWS, HOP_ROWS
    )

    def shard(grad, dim):
        return lax.psum_scatter(grad, ("dp", "context"), scatter_dimension=dim, tiled=True)

    grad_down = ein("sf,sd->fd", act, cot).astype(BF)
    grad_gate = ein("sd,sf->df", normed_m, gg).astype(BF)
    grad_up = ein("sd,sf->df", normed_m, gu).astype(BF)
    down_sum, gate_sum, up_sum = shard(grad_down, 1), shard(grad_gate, 0), shard(grad_up, 0)
    grad_middle, grad_attn, grad_mixed, gain_m_rows = norm_back(
        size,
        back_part,
        keep,
        gain_m,
        w_out,
        middle,
        cot,
        GROUP_ROWS,
        HOP_ROWS,
        (grad_down, grad_gate, grad_up),
    )
    grad_out = ein("xs,sd->xd", mixed_t, grad_attn).astype(BF)
    out_sum = shard(grad_out, 1)
    grads, ffn_out = attend_backward(
        axes,
        down_part,
        query_t,
        both,
        kend,
        grad_mixed.reshape(heads, HD, rows),
        mixed,
        lse,
        cos_tab,
        sin_tab,
        GROUP_ROWS,
        (grad_out, down_sum, gate_sum),
    )
    grads = grads.reshape(-1, rows)
    grad_project = ein("sd,xs->dx", normed_a, grads).astype(BF)
    project_sum = shard(grad_project, 0)
    layer_out = (own(middle) + ffn_out).astype(BF)

    numbers = jnp.stack(
        [
            jnp.sum(keep * x_own.astype(F32) ** 2),
            jnp.sum(own(attn_square)),
            jnp.sum(ffn_out * ffn_out),
            jnp.sum(keep) / size,
        ]
    )
    numbers = jnp.pad(numbers[None], ((1, 6), (0, width - 4)))
    extra = jnp.stack([numbers, jnp.pad(own(gain_m_rows), ((2, 5), (0, 0)))])
    grad_a, row_dot, sums = input_gradient(
        axes,
        grads,
        inv_a,
        gains,
        extra,
        w_query,
        w_key,
        w_value,
        x_low,
        GROUP_ROWS,
        (grad_project, up_sum, out_sum),
    )
    hat_own = x_own.astype(F32) * inv_a
    row_mean = row_dot[0][:, None] / features
    through = inv_a * (grad_a * gain_attn[None, :] - hat_own * row_mean)
    input_grad = (own(grad_middle) + through).astype(BF)
    gain_a_sum, gain_m_sum, numbers = sums[0], sums[2], sums[1, :4]
    down_sum, gate_sum, up_sum, out_sum, project_sum = (
        a.astype(F32) for a in (down_sum, gate_sum, up_sum, out_sum, project_sum)
    )
    cut = [heads * HD, (heads + kvs) * HD]
    query_sum, key_sum, value_sum = jnp.split(project_sum, cut, 1)
    rms = jnp.sqrt(numbers[:3] / (numbers[3] * features))
    return (
        layer_out[None],
        input_grad[None],
        gain_a_sum,
        query_sum,
        key_sum,
        value_sum,
        out_sum,
        gain_m_sum,
        gate_sum,
        up_sum,
        down_sum,
        rms[0],
        rms[1],
        rms[2],
    )


def solution(mesh):
    token = P("dp", "context", "tensor")
    by_rows = P(("dp", "context"), "tensor")
    by_columns = P("tensor", ("dp", "context"))
    cols, rows, vec = P(None, "tensor"), P("tensor", None), P("tensor")
    return jax.shard_map(
        functools.partial(local, dict(mesh.shape)),
        mesh=mesh,
        in_specs=(
            token,
            token,
            P("dp", None),
            P("dp", None),
            vec,
            cols,
            cols,
            cols,
            rows,
            vec,
            cols,
            cols,
            rows,
        ),
        out_specs=(
            token,
            token,
            vec,
            by_rows,
            by_rows,
            by_rows,
            by_columns,
            vec,
            by_rows,
            by_rows,
            by_columns,
            P(),
            P(),
            P(),
        ),
        check_vma=False,
    )
```

```python
import functools
import math

import jax
import jax.numpy as jnp
from jax import lax
from jax.experimental import pallas as pl
from jax.experimental.pallas import tpu as pltpu
from jax.sharding import PartitionSpec as P

HD = 80
PIC = 256
LEAST_VALID = 1536
F32 = jnp.float32
BF = jnp.bfloat16
SCALE = HD**-0.5
SCALE2 = SCALE * math.log2(math.e)
LOWEST = -1e30
GROUP_ROWS = 256
HOP_ROWS = 64
VMEM_LIMIT = 60 << 20
KEY_ROWS_FWD = 1024
KEY_ROWS_BWD = 512

epsilon = 1e-05
rope_base = 1000000.0


def dot(a, b):
    return jnp.dot(a, b, preferred_element_type=F32)


def dot_nt(a, b):
    return lax.dot_general(a, b, (((1,), (1,)), ((), ())), preferred_element_type=F32)


def ein(spec, a, b):
    return jnp.einsum(spec, a, b, preferred_element_type=F32)


MESH_ID = pl.DeviceIdType.MESH
RING = 8
SENT = 4


def add_low(a, b):
    return (a.astype(F32) + b.astype(F32)).astype(BF)


class Sums:
    def __init__(self, size, count, part, low, high, sent, sems):
        self.size, self.count, self.part = size, count, part
        self.low, self.high, self.sent = low, high, sent
        self.low_send, self.low_recv, self.high_send, self.high_recv = sems
        self.here = lax.axis_index("tensor")

    def barrier(self):
        here, size = self.here, self.size
        barrier = pltpu.get_barrier_semaphore()

        @pl.when(here > 0)
        def _():
            pl.semaphore_signal(
                barrier, inc=1, device_id={"tensor": here - 1}, device_id_type=MESH_ID
            )

        @pl.when(here < size - 1)
        def _():
            pl.semaphore_signal(
                barrier, inc=1, device_id={"tensor": here + 1}, device_id_type=MESH_ID
            )

        @pl.when((here > 0) & (here < size - 1))
        def _():
            pl.semaphore_wait(barrier, 2)

        @pl.when((here == 0) | (here == size - 1))
        def _():
            pl.semaphore_wait(barrier, 1)

    def up(self, c):
        slot = lax.rem(c, RING)
        return pltpu.make_async_remote_copy(
            src_ref=self.low.at[slot],
            dst_ref=self.low.at[slot],
            send_sem=self.low_send.at[slot],
            recv_sem=self.low_recv.at[slot],
            device_id={"tensor": self.here + 1},
            device_id_type=MESH_ID,
        )

    def down(self, c):
        slot, mine = lax.rem(c, RING), lax.rem(c, SENT)
        return pltpu.make_async_remote_copy(
            src_ref=self.sent.at[mine],
            dst_ref=self.high.at[slot],
            send_sem=self.high_send.at[mine],
            recv_sem=self.high_recv.at[slot],
            device_id={"tensor": self.here - 1},
            device_id_type=MESH_ID,
        )

    def tick(self, k):
        here, size, count = self.here, self.size, self.count
        bottom, top = here == 0, here == size - 1
        c = k - here

        @pl.when((c >= 0) & (c < count))
        def _():
            slot = lax.rem(c, RING)

            @pl.when(bottom)
            def _():
                self.low[slot] = self.part(c)

            @pl.when(jnp.logical_not(bottom))
            def _():
                self.up(c).wait_recv()
                self.low[slot] = add_low(self.low[slot], self.part(c))

            @pl.when(jnp.logical_not(top))
            def _():
                self.up(c).start()

        d = k - (size - 1 - here)

        @pl.when((d >= 0) & (d < count))
        def _():
            slot, mine = lax.rem(d, RING), lax.rem(d, SENT)

            @pl.when(top)
            def _():
                self.sent[mine] = self.part(d)

            @pl.when(jnp.logical_not(top))
            def _():
                self.down(d).wait_recv()

                @pl.when(jnp.logical_not(bottom))
                def _():
                    self.sent[mine] = add_low(self.high[slot], self.part(d))

            @pl.when(jnp.logical_not(bottom))
            def _():
                self.down(d).start()

        @pl.when((c >= 2) & (c < count + 2) & jnp.logical_not(top))
        def _():
            self.up(c - 2).wait_send()

        @pl.when((d >= 2) & (d < count + 2) & jnp.logical_not(bottom))
        def _():
            self.down(d - 2).wait_send()

    def total(self, c, then):
        slot = lax.rem(c, RING)
        top = self.here == self.size - 1

        @pl.when(top)
        def _():
            then(self.low[slot].astype(F32))

        @pl.when(jnp.logical_not(top))
        def _():
            then(self.low[slot].astype(F32) + self.high[slot].astype(F32))


def sum_scratch(hop, features):
    return [
        pltpu.VMEM((RING, hop, features), BF),
        pltpu.VMEM((RING, hop, features), BF),
        pltpu.VMEM((SENT, hop, features), BF),
        pltpu.SemaphoreType.DMA((RING,)),
        pltpu.SemaphoreType.DMA((RING,)),
        pltpu.SemaphoreType.DMA((SENT,)),
        pltpu.SemaphoreType.DMA((RING,)),
    ]


def own_columns(size, a, then):
    width = a.shape[1] // size
    for j in range(size):

        @pl.when(lax.axis_index("tensor") == j)
        def _():
            then(a[:, j * width : (j + 1) * width])


def tile_of(n, most):
    for tile in range(most, 0, -128):
        if n % tile == 0:
            return tile
    return n


def ffn_kernel(
    size, hop, chunk,
    mixed, keep, gain, w_out, w_gate, w_up, w_down, x, cot,
    normed_o, act_o, ggu_o, ffn_o, back_o, middle_o, own_o, square_o,
    low, high, sent, low_send, low_recv, high_send, high_recv,
    wo, wg, wu, wd, parts, normed, xs, cots, mids, owns, act, ggu, ffn, back, split,
    w_sem, x_sem, cot_sem, normed_sem, mid_sem, own_sem, act_sem, ffn_sem,
):
    rows, features = x.shape
    hidden = w_gate.shape[1]
    count, per, groups = rows // hop, chunk // hop, rows // chunk
    tile_f, tile_d = tile_of(hidden, 256), tile_of(features, 256)
    tiles_f, tiles_d = hidden // tile_f, features // tile_d
    half_f, half_d = -(-tiles_f // 2), -(-tiles_d // 2)
    lag = size - 1 + per - 1
    ticks = max(per * groups + lag, count + size)

    def part(c):
        return parts[lax.rem(lax.div(c, per), 2), pl.ds(pl.multiple_of(lax.rem(c, per) * hop, hop), hop), :]

    sums = Sums(size, count, part, low, high, sent, (low_send, low_recv, high_send, high_recv))
    loads = [
        pltpu.make_async_copy(a, b, w_sem.at[i])
        for i, (a, b) in enumerate(((w_out, wo), (w_gate, wg), (w_up, wu), (w_down, wd)))
    ]
    for load in loads:
        load.start()

    def load_x(c):
        slot = lax.rem(c, 2)
        return pltpu.make_async_copy(x.at[pl.ds(c * hop, hop)], xs.at[slot], x_sem.at[slot])

    def load_cot(g):
        return pltpu.make_async_copy(cot.at[pl.ds(g * chunk, chunk)], cots, cot_sem)

    def save_normed(c):
        at, q = lax.rem(lax.div(c, per), 2), lax.rem(c, per)
        return pltpu.make_async_copy(
            normed.at[at, pl.ds(q * hop, hop)], normed_o.at[pl.ds(c * hop, hop)], normed_sem.at[at, q]
        )

    def save_mid(c):
        slot = lax.rem(c, 2)
        return pltpu.make_async_copy(mids.at[slot], middle_o.at[pl.ds(c * hop, hop)], mid_sem.at[slot])

    def save_own(c):
        slot = lax.rem(c, 2)
        return pltpu.make_async_copy(owns.at[slot], own_o.at[pl.ds(c * hop, hop)], own_sem.at[slot])

    def save_act(g):
        return [
            pltpu.make_async_copy(a, b.at[pl.ds(g * chunk, chunk)], act_sem.at[i])
            for i, (a, b) in enumerate(((act, act_o), (ggu, ggu_o)))
        ]

    def save_ffn(g):
        part = pl.ds(g * chunk, chunk)
        return [
            pltpu.make_async_copy(split, ffn_o.at[:, part], ffn_sem.at[0]),
            pltpu.make_async_copy(back, back_o.at[part], ffn_sem.at[1]),
        ]

    def project(g):
        at = lax.rem(g, 2)
        lhs = mixed[:, pl.ds(pl.multiple_of(g * chunk, chunk), chunk)]

        def one(j, _):
            cols = pl.ds(pl.multiple_of(j * tile_d, tile_d), tile_d)
            parts[at, :, cols] = lax.dot_general(
                lhs, wo[:, cols], (((0,), (0,)), ((), ())), preferred_element_type=F32
            ).astype(BF)
            return 0

        lax.fori_loop(0, tiles_d, one, 0)

    load_x(0).start()
    load_cot(0).start()
    square_o[...] = jnp.zeros_like(square_o)
    loads[0].wait()
    project(0)
    sums.barrier()

    def finish(c):
        slot = lax.rem(c, 2)
        load_x(c).wait()

        @pl.when(c + 1 < count)
        def _():
            load_x(c + 1).start()

        @pl.when(c >= 2)
        def _():
            save_mid(c - 2).wait()
            save_own(c - 2).wait()

        @pl.when(c >= 2 * per)
        def _():
            save_normed(c - 2 * per).wait()

        kept = keep[pl.ds(pl.multiple_of(c * hop, hop), hop), :]

        def then(total):
            out = kept * total
            square_o[...] += jnp.sum(out * out, 0, keepdims=True)
            mids[slot] = xs[slot].astype(F32) + out

        sums.total(c, then)
        mid = mids[slot]
        own_columns(size, mid, lambda piece: owns.__setitem__(slot, piece))
        save_own(c).start()
        inv = lax.rsqrt(jnp.sum(mid * mid, 1, keepdims=True) / features + epsilon)
        at = lax.rem(lax.div(c, per), 2)
        normed[at, pl.ds(pl.multiple_of(lax.rem(c, per) * hop, hop), hop), :] = (
            mid * inv * gain[1:2, :]
        ).astype(BF)
        save_mid(c).start()
        save_normed(c).start()

    def inner(g, lo, hi):
        at = lax.rem(g, 2)
        kept = keep[pl.ds(pl.multiple_of(g * chunk, chunk), chunk), :]

        def one(j, _):
            cols = pl.ds(pl.multiple_of(j * tile_f, tile_f), tile_f)
            gate = dot(normed[at], wg[:, cols])
            up = dot(normed[at], wu[:, cols])
            grad = dot_nt(cots[...], wd[cols, :]) * kept
            sig = jax.nn.sigmoid(gate)
            silu = gate * sig
            act[:, cols] = (silu * up * kept).astype(BF)
            ggu[:, cols] = (grad * up * (sig + silu * (1.0 - sig))).astype(BF)
            cols = pl.ds(pl.multiple_of(hidden + j * tile_f, tile_f), tile_f)
            ggu[:, cols] = (grad * silu).astype(BF)
            return 0

        lax.fori_loop(lo, hi, one, 0)

    def outer(g, lo, hi):
        def one(j, _):
            cols = pl.ds(pl.multiple_of(j * tile_d, tile_d), tile_d)
            ffn[:, cols] = dot(act[...], wd[:, cols]).astype(BF)
            back[:, cols] = (
                dot_nt(ggu[:, :hidden], wg[cols, :]) + dot_nt(ggu[:, hidden:], wu[cols, :])
            ).astype(BF)
            return 0

        lax.fori_loop(lo, hi, one, 0)

    def tick(k, _):
        sums.tick(k)
        c = k - (size - 1)

        @pl.when((c >= 0) & (c < count))
        def _():
            finish(c)

        ahead = k + 2

        @pl.when((lax.rem(ahead, per) == 0) & (ahead < count))
        def _():
            project(lax.div(ahead, per))

        s = k - lag
        g, stage = lax.div(s, per), lax.rem(s, per)
        going = (s >= 0) & (g < groups)

        @pl.when(going & (stage == 0))
        def _():
            @pl.when(g == 0)
            def _():
                for load in loads[1:]:
                    load.wait()

            load_cot(g).wait()

            @pl.when(g > 0)
            def _():
                for copy in save_act(g - 1):
                    copy.wait()

            inner(g, 0, half_f)

        @pl.when(going & (stage == 1))
        def _():
            inner(g, half_f, tiles_f)
            for copy in save_act(g):
                copy.start()

            @pl.when(g + 1 < groups)
            def _():
                load_cot(g + 1).start()

        @pl.when(going & (stage == 2))
        def _():
            @pl.when(g > 0)
            def _():
                for copy in save_ffn(g - 1):
                    copy.wait()

            outer(g, 0, half_d)

        @pl.when(going & (stage == 3))
        def _():
            outer(g, half_d, tiles_d)
            for j in range(size):
                split[j] = ffn[:, j * (features // size) : (j + 1) * (features // size)]
            for copy in save_ffn(g):
                copy.start()

        return 0

    lax.fori_loop(0, ticks, tick, 0)
    for copy in save_act(groups - 1) + save_ffn(groups - 1):
        copy.wait()
    for c in range(count - 2, count):
        save_mid(c).wait()
        save_own(c).wait()
    for c in range(count - 2 * per, count):
        save_normed(c).wait()


def feed_forward(size, mixed, keep, gain, w_out, w_gate, w_up, w_down, x, cot, chunk, hop):
    rows, features = x.shape
    hidden = w_gate.shape[1]
    per = chunk // hop
    assert per == 4
    anywhere, vmem = pl.BlockSpec(memory_space=pl.ANY), pl.BlockSpec(memory_space=pltpu.VMEM)
    shape = jax.ShapeDtypeStruct
    return pl.pallas_call(
        functools.partial(ffn_kernel, size, hop, chunk),
        in_specs=[vmem] * 3 + [anywhere] * 6,
        out_specs=[anywhere] * 7 + [vmem],
        out_shape=[
            shape((rows, features), BF),
            shape((rows, hidden), BF),
            shape((rows, 2 * hidden), BF),
            shape((size, rows, features // size), BF),
            shape((rows, features), BF),
            shape((rows, features), F32),
            shape((rows, features // size), F32),
            shape((1, features), F32),
        ],
        scratch_shapes=sum_scratch(hop, features)
        + [
            pltpu.VMEM(w_out.shape, BF),
            pltpu.VMEM(w_gate.shape, BF),
            pltpu.VMEM(w_up.shape, BF),
            pltpu.VMEM(w_down.shape, BF),
            pltpu.VMEM((2, chunk, features), BF),
            pltpu.VMEM((2, chunk, features), BF),
            pltpu.VMEM((2, hop, features), BF),
            pltpu.VMEM((chunk, features), BF),
            pltpu.VMEM((2, hop, features), F32),
            pltpu.VMEM((2, hop, features // size), F32),
            pltpu.VMEM((chunk, hidden), BF),
            pltpu.VMEM((chunk, 2 * hidden), BF),
            pltpu.VMEM((chunk, features), BF),
            pltpu.VMEM((chunk, features), BF),
            pltpu.VMEM((size, chunk, features // size), BF),
            pltpu.SemaphoreType.DMA((4,)),
            pltpu.SemaphoreType.DMA((2,)),
            pltpu.SemaphoreType.DMA,
            pltpu.SemaphoreType.DMA((2, per)),
            pltpu.SemaphoreType.DMA((2,)),
            pltpu.SemaphoreType.DMA((2,)),
            pltpu.SemaphoreType.DMA((2,)),
            pltpu.SemaphoreType.DMA((2,)),
        ],
        compiler_params=pltpu.CompilerParams(
            collective_id=1, has_side_effects=True, vmem_limit_bytes=VMEM_LIMIT
        ),
        cost_estimate=pl.CostEstimate(
            flops=2 * rows * features * (6 * hidden + w_out.shape[0]),
            bytes_accessed=80 << 20,
            transcendentals=rows * hidden,
        ),
        name="feed_forward",
    )(mixed, keep, gain, w_out, w_gate, w_up, w_down, x, cot)


def back_kernel(
    size, hop, chunk,
    parts, keep, gain, w_out, middle, cot, act,
    own_o, grad_low_o, mixed_o, gain_o, down_o,
    low, high, sent, low_send, low_recv, high_send, high_recv,
    wo, mids, cots, acts, owns, grads_low, tiles,
    load_sem, mid_sem, own_sem, grad_low_sem, tile_sem,
):
    rows, features = middle.shape
    count, per, groups = rows // hop, chunk // hop, rows // chunk
    tile = tile_of(features, 256)
    tile_count = features // tile
    ticks = max(count + size, per * (groups - 1) + size - 1 + per, tile_count + 1)

    def part(c):
        return parts[pl.ds(pl.multiple_of(c * hop, hop), hop), :]

    sums = Sums(size, count, part, low, high, sent, (low_send, low_recv, high_send, high_recv))
    loads = [
        pltpu.make_async_copy(a, b, load_sem.at[i])
        for i, (a, b) in enumerate(((cot, cots), (w_out, wo), (act, acts)))
    ]

    def load_mid(c):
        slot = lax.rem(c, 2)
        return pltpu.make_async_copy(
            middle.at[pl.ds(c * hop, hop)], mids.at[slot], mid_sem.at[slot]
        )

    def save_own(c):
        slot = lax.rem(c, 2)
        return pltpu.make_async_copy(owns.at[slot], own_o.at[pl.ds(c * hop, hop)], own_sem.at[slot])

    def save_low(c):
        q = lax.rem(c, per)
        return pltpu.make_async_copy(
            grads_low.at[pl.ds(q * hop, hop)], grad_low_o.at[pl.ds(c * hop, hop)], grad_low_sem.at[q]
        )

    def save_tile(j):
        slot = lax.rem(j, 2)
        return pltpu.make_async_copy(
            tiles.at[slot], down_o.at[pl.ds(j * tile, tile)], tile_sem.at[slot]
        )

    load_mid(0).start()
    for load in loads:
        load.start()
    gain_o[...] = jnp.zeros_like(gain_o)
    sums.barrier()

    def finish(c):
        slot = lax.rem(c, 2)
        load_mid(c).wait()

        @pl.when(c + 1 < count)
        def _():
            load_mid(c + 1).start()

        @pl.when(c >= 2)
        def _():
            save_own(c - 2).wait()

        @pl.when(c >= per)
        def _():
            save_low(c - per).wait()

        chunk_rows = pl.ds(pl.multiple_of(c * hop, hop), hop)
        kept = keep[chunk_rows, :]
        mid = mids[slot]
        inv = lax.rsqrt(jnp.sum(mid * mid, 1, keepdims=True) / features + epsilon)
        hat = mid * inv

        def then(total):
            gain_o[...] += jnp.sum(total * hat, 0, keepdims=True)
            weighted = total * gain[1:2, :]
            mean = jnp.sum(weighted * hat, 1, keepdims=True) / features
            mids[slot] = cots[chunk_rows, :].astype(F32) + inv * (weighted - hat * mean)

        sums.total(c, then)
        grad = mids[slot]
        own_columns(size, grad, lambda piece: owns.__setitem__(slot, piece))
        grads_low[pl.ds(pl.multiple_of(lax.rem(c, per) * hop, hop), hop), :] = (kept * grad).astype(
            BF
        )
        save_own(c).start()
        save_low(c).start()

    def weight_tile(j):
        slot = lax.rem(j, 2)

        @pl.when(j >= 2)
        def _():
            save_tile(j - 2).wait()

        cols = pl.ds(pl.multiple_of(j * tile, tile), tile)
        tiles[slot] = dot(flip(cots[:, cols]).astype(BF), acts[...]).astype(BF)
        save_tile(j).start()

    def tick(k, _):
        sums.tick(k)
        c = k - (size - 1)

        @pl.when(k == 1)
        def _():
            for load in loads:
                load.wait()

        @pl.when((c >= 0) & (c < count))
        def _():
            finish(c)

            @pl.when(lax.rem(c, per) == per - 1)
            def _():
                g = lax.div(c, per)
                mixed_o[:, pl.ds(pl.multiple_of(g * chunk, chunk), chunk)] = dot_nt(
                    wo[...], grads_low[...]
                ).astype(BF)

        @pl.when((k >= 1) & (k <= tile_count))
        def _():
            weight_tile(k - 1)

        return 0

    lax.fori_loop(0, ticks, tick, 0)
    for c in range(count - 2, count):
        save_own(c).wait()
    for c in range(count - per, count):
        save_low(c).wait()
    for j in range(max(tile_count - 2, 0), tile_count):
        save_tile(j).wait()


def norm_back(size, parts, keep, gain, w_out, middle, cot, act, chunk, hop, after):
    rows, features = middle.shape
    per = chunk // hop
    anywhere, vmem = pl.BlockSpec(memory_space=pl.ANY), pl.BlockSpec(memory_space=pltpu.VMEM)
    shape, dma = jax.ShapeDtypeStruct, pltpu.SemaphoreType.DMA

    def kernel(*refs):
        back_kernel(size, hop, chunk, *refs[:7], *refs[7 + len(after) :])

    return pl.pallas_call(
        kernel,
        in_specs=[vmem] * 3 + [anywhere] * (4 + len(after)),
        out_specs=[anywhere] * 2 + [vmem] * 2 + [anywhere],
        out_shape=[
            shape((rows, features // size), F32),
            shape((rows, features), BF),
            shape((w_out.shape[0], rows), BF),
            shape((1, features), F32),
            shape((features, act.shape[1]), BF),
        ],
        scratch_shapes=sum_scratch(hop, features)
        + [
            pltpu.VMEM(w_out.shape, BF),
            pltpu.VMEM((2, hop, features), F32),
            pltpu.VMEM(cot.shape, BF),
            pltpu.VMEM(act.shape, BF),
            pltpu.VMEM((2, hop, features // size), F32),
            pltpu.VMEM((chunk, features), BF),
            pltpu.VMEM((2, tile_of(features, 256), act.shape[1]), BF),
            dma((3,)),
            dma((2,)),
            dma((2,)),
            dma((per,)),
            dma((2,)),
        ],
        compiler_params=pltpu.CompilerParams(
            collective_id=2, has_side_effects=True, vmem_limit_bytes=VMEM_LIMIT
        ),
        cost_estimate=pl.CostEstimate(
            flops=2 * rows * features * (w_out.shape[0] + act.shape[1]),
            bytes_accessed=40 << 20,
            transcendentals=rows,
        ),
        name="norm_back",
    )(parts, keep, gain, w_out, middle, cot, act, *after)


def greet(peers):
    barrier = pltpu.get_barrier_semaphore()
    for peer in peers:
        pl.semaphore_signal(barrier, inc=1, device_id=peer, device_id_type=MESH_ID)
    pl.semaphore_wait(barrier, len(peers))


def others(axis, size):
    here = lax.axis_index(axis)
    return [{axis: lax.rem(here + i, size)} for i in range(1, size)]


class Gather:
    def __init__(self, size, groups, chunk, own, blocks, sems):
        self.size, self.groups, self.chunk = size, groups, chunk
        self.own, self.blocks = own, blocks
        self.up_send, self.up_recv, self.down_send, self.down_recv, self.own_sem = sems
        self.steps = size - 1
        self.ticks = groups * self.steps + 1
        self.here = lax.axis_index("tensor")

    def load(self, g):
        part = pl.ds(g * self.chunk, self.chunk)
        return pltpu.make_async_copy(
            self.own.at[part], self.blocks.at[self.here, part], self.own_sem.at[g]
        )

    def load_all(self):
        for g in range(self.groups):
            self.load(g).start()

    def move(self, g, s, owner, peer, send, recv):
        block = self.blocks.at[jnp.clip(owner, 0, self.size - 1), pl.ds(g * self.chunk, self.chunk)]
        return pltpu.make_async_remote_copy(
            src_ref=block,
            dst_ref=block,
            send_sem=send.at[g, s],
            recv_sem=recv.at[g, s],
            device_id={"tensor": peer},
            device_id_type=MESH_ID,
        )

    def up(self, g, s):
        return self.move(g, s, self.here - s, self.here + 1, self.up_send, self.up_recv)

    def down(self, g, s):
        return self.move(g, s, self.here + s, self.here - 1, self.down_send, self.down_recv)

    def each(self, g, s, act):
        @pl.when((self.here >= s) & (self.here < self.size - 1))
        def _():
            act(self.up(g, s))

        @pl.when((self.here + s < self.size) & (self.here > 0))
        def _():
            act(self.down(g, s))

    def send(self, g, s):
        self.each(g, s, lambda copy: copy.start())

    def receive(self, g, s):
        @pl.when(self.here - 1 - s >= 0)
        def _():
            self.up(g, s).wait_recv()

        @pl.when(self.here + 1 + s < self.size)
        def _():
            self.down(g, s).wait_recv()

    def begin(self):
        self.load(0).wait()
        self.send(0, 0)

    def tick(self, k, then):
        g, s = lax.div(k, self.steps), lax.rem(k, self.steps)

        @pl.when((s > 0) & (g < self.groups))
        def _():
            self.receive(g, s - 1)
            self.send(g, s)

        @pl.when((s == self.steps - 1) & (g + 1 < self.groups))
        def _():
            self.load(g + 1).wait()
            self.send(g + 1, 0)

        @pl.when((s == 0) & (g > 0) & (g <= self.groups))
        def _():
            self.receive(g - 1, self.steps - 1)
            then(g - 1)

    def drain(self):
        for g in range(self.groups):
            for s in range(self.steps):
                self.each(g, s, lambda copy: copy.wait_send())


def gather_scratch(size, rows, width, chunk):
    dma, groups = pltpu.SemaphoreType.DMA, rows // chunk
    return [pltpu.VMEM((size, rows, width), BF)] + [dma((groups, size - 1))] * 4 + [dma((groups,))]


class Scatter:
    def __init__(self, size, groups, chunk, parts, ups, downs, sems):
        self.size, self.groups, self.chunk = size, groups, chunk
        self.parts, self.ups, self.downs = parts, ups, downs
        self.up_send, self.up_recv, self.down_send, self.down_recv = sems
        self.count = (size - 1) * groups
        self.here = lax.axis_index("tensor")

    def rows(self, m):
        return pl.ds(pl.multiple_of(lax.rem(m, self.groups) * self.chunk, self.chunk), self.chunk)

    def up(self, m, first):
        owner = self.size - 1 - lax.div(m, self.groups)
        return pltpu.make_async_remote_copy(
            src_ref=self.parts.at[owner, self.rows(m)] if first else self.ups.at[m],
            dst_ref=self.ups.at[m],
            send_sem=self.up_send.at[m],
            recv_sem=self.up_recv.at[m],
            device_id={"tensor": self.here + 1},
            device_id_type=MESH_ID,
        )

    def down(self, m, first):
        owner = lax.div(m, self.groups)
        return pltpu.make_async_remote_copy(
            src_ref=self.parts.at[owner, self.rows(m)] if first else self.downs.at[m],
            dst_ref=self.downs.at[m],
            send_sem=self.down_send.at[m],
            recv_sem=self.down_recv.at[m],
            device_id={"tensor": self.here - 1},
            device_id_type=MESH_ID,
        )

    def tick(self, k):
        bottom, top = self.here == 0, self.here == self.size - 1
        m = k - self.here
        owner = self.size - 1 - lax.div(m, self.groups)

        @pl.when((m >= 0) & (owner > self.here))
        def _():
            @pl.when(bottom)
            def _():
                self.up(m, True).start()

            @pl.when(jnp.logical_not(bottom))
            def _():
                self.up(m, False).wait_recv()
                self.ups[m] = add_low(self.ups[m], self.parts[owner, self.rows(m), :])
                self.up(m, False).start()

        n = k - (self.size - 1 - self.here)
        below = lax.div(n, self.groups)

        @pl.when((n >= 0) & (below < self.here))
        def _():
            @pl.when(top)
            def _():
                self.down(n, True).start()

            @pl.when(jnp.logical_not(top))
            def _():
                self.down(n, False).wait_recv()
                self.downs[n] = add_low(self.downs[n], self.parts[below, self.rows(n), :])
                self.down(n, False).start()

    def finish(self, total, then):
        here = self.here

        def last(c, _):
            part = self.rows(c)
            m, n = (self.size - 1 - here) * self.groups + c, here * self.groups + c
            total[...] = self.parts[here, part, :].astype(F32)

            @pl.when(here > 0)
            def _():
                self.up(m, False).wait_recv()
                total[...] += self.ups[m].astype(F32)

            @pl.when(here < self.size - 1)
            def _():
                self.down(n, False).wait_recv()
                total[...] += self.downs[n].astype(F32)

            then(part, total[...])
            return 0

        lax.fori_loop(0, self.groups, last, 0)

        def drain(m, _):
            @pl.when(self.size - 1 - lax.div(m, self.groups) > here)
            def _():
                self.up(m, False).wait_send()

            @pl.when(lax.div(m, self.groups) < here)
            def _():
                self.down(m, False).wait_send()

            return 0

        lax.fori_loop(0, self.count, drain, 0)


def scatter_scratch(size, rows, width, chunk):
    count = (size - 1) * (rows // chunk)
    return [
        pltpu.VMEM((size, rows, width), BF),
        pltpu.VMEM((count, chunk, width), BF),
        pltpu.VMEM((count, chunk, width), BF),
        pltpu.VMEM((chunk, width), F32),
    ] + [pltpu.SemaphoreType.DMA((count,))] * 4


def turn(u, cos_t, sin_t):
    lower, upper = u[: HD // 2], u[HD // 2 :]
    return jnp.concatenate([lower * cos_t - upper * sin_t, upper * cos_t + lower * sin_t], 0)


def flip(a):
    return a.astype(F32).T


def key_blocks(g, chunk, rows, keys, key_rows):
    start = lax.axis_index("context") * rows + g * chunk
    free = jnp.minimum(start + 1, min(LEAST_VALID, keys))
    last = jnp.minimum(start + chunk + PIC - 1, keys)
    return lax.div(free, key_rows), lax.div(last + key_rows - 1, key_rows)


def project_kernel(
    size, contexts, chunk,
    own, gain_attn, gain_mlp, cos_tab, sin_tab, mask, starts, w_query, w_key_t, w_value_t,
    x_o, normed_o, inv_o, gain_o, query_o, kv_o, kend_o, keep_o,
    xs, up_send, up_recv, down_send, down_recv, own_sem,
    gains, full, normed, kv, wq, wk, wv,
    gain_send, gain_recv, kv_send, kv_recv, w_sem, out_sem, kv_sem,
):
    here, place = lax.axis_index("tensor"), lax.axis_index("context")
    rows, width = own.shape
    features = size * width
    groups = rows // chunk
    heads, kvs = w_query.shape[1] // HD, w_key_t.shape[0] // HD
    line = Gather(
        size, groups, chunk, own, xs, (up_send, up_recv, down_send, down_recv, own_sem)
    )
    loads = [
        pltpu.make_async_copy(a, b, w_sem.at[i])
        for i, (a, b) in enumerate(((w_query, wq), (w_key_t, wk), (w_value_t, wv)))
    ]
    line.load_all()
    for load in loads:
        load.start()
    gains[here] = jnp.zeros_like(gains[here])
    gains[here, 0:1] = gain_attn[...]
    gains[here, 1:2] = gain_mlp[...]
    tensor_peers, context_peers = others("tensor", size), others("context", contexts)
    greet(tensor_peers + context_peers)

    def gain_copy(i):
        return pltpu.make_async_remote_copy(
            src_ref=gains.at[here],
            dst_ref=gains.at[here],
            send_sem=gain_send.at[i],
            recv_sem=gain_recv.at[i],
            device_id=tensor_peers[i],
            device_id_type=MESH_ID,
        )

    def kv_copy(g, i):
        part = kv.at[:, :, pl.ds(pl.multiple_of(place * rows + g * chunk, chunk), chunk)]
        return pltpu.make_async_remote_copy(
            src_ref=part,
            dst_ref=part,
            send_sem=kv_send.at[g, i],
            recv_sem=kv_recv.at[g, i],
            device_id=context_peers[i],
            device_id_type=MESH_ID,
        )

    line.begin()
    for i in range(size - 1):
        gain_copy(i).start()

    length = jnp.sum(mask[...].astype(F32), 1, keepdims=True).astype(jnp.int32)
    position = lax.broadcasted_iota(jnp.int32, (1, rows), 1) + place * rows
    last = position
    for k in range(starts.shape[1]):
        start = starts[:, k : k + 1]
        inside = (position >= start) & (position < start + PIC)
        last = jnp.maximum(last, jnp.where(inside, start + PIC - 1, 0))
    kend_o[...] = jnp.minimum(last + 1, length)
    down_rows = lax.broadcasted_iota(jnp.int32, (rows, 1), 0) + place * rows
    keep_o[...] = jnp.where(down_rows < length, 1.0, 0.0)

    def save(g):
        part = pl.ds(g * chunk, chunk)
        return [
            pltpu.make_async_copy(full, x_o.at[part], out_sem.at[0]),
            pltpu.make_async_copy(normed, normed_o.at[part], out_sem.at[1]),
        ]

    def compute(g):
        part = pl.ds(pl.multiple_of(g * chunk, chunk), chunk)

        @pl.when(g == 0)
        def _():
            for load in loads:
                load.wait()
            for i in range(size - 1):
                gain_copy(i).wait_recv()
            gain_o[...] = jnp.concatenate([gains[j] for j in range(size)], 1)

        @pl.when(g > 0)
        def _():
            for copy in save(g - 1):
                copy.wait()

        full[...] = jnp.concatenate([xs[j, part, :] for j in range(size)], 1)
        stream = full[...].astype(F32)
        inv = lax.rsqrt(jnp.sum(stream * stream, 1, keepdims=True) / features + epsilon)
        inv_o[part, :] = inv
        normed[...] = (stream * inv * gain_o[0:1, :]).astype(BF)
        for copy in save(g):
            copy.start()
        cos_t, sin_t = cos_tab[:, part], sin_tab[:, part]
        mine = pl.ds(pl.multiple_of(place * rows + g * chunk, chunk), chunk)
        key = dot_nt(wk[...], normed[...])
        value = dot_nt(wv[...], normed[...])
        for h in range(kvs):
            kv[h, :, mine] = turn(key[h * HD : (h + 1) * HD], cos_t, sin_t).astype(BF)
            kv[kvs + h, :, mine] = value[h * HD : (h + 1) * HD].astype(BF)
        for i in range(contexts - 1):
            kv_copy(g, i).start()
        query = dot(normed[...], wq[...]).T
        for h in range(heads):
            query_o[h, :, part] = turn(query[h * HD : (h + 1) * HD], cos_t, sin_t).astype(BF)

    def tick(k, _):
        line.tick(k, compute)
        return 0

    lax.fori_loop(0, line.ticks, tick, 0)
    for copy in save(groups - 1):
        copy.wait()
    for i in range(size - 1):
        gain_copy(i).wait_send()
    line.drain()
    for g in range(groups):
        for i in range(contexts - 1):
            kv_copy(g, i).wait()
    out = pltpu.make_async_copy(kv, kv_o, kv_sem)
    out.start()
    out.wait()


def project(
    axes, own, gain_attn, gain_mlp, cos_tab, sin_tab, mask, starts, w_query, w_key_t, w_value_t, chunk
):
    size, contexts = axes["tensor"], axes["context"]
    rows, width = own.shape
    features, groups = size * width, rows // chunk
    heads, kvs = w_query.shape[1] // HD, w_key_t.shape[0] // HD
    anywhere, vmem = pl.BlockSpec(memory_space=pl.ANY), pl.BlockSpec(memory_space=pltpu.VMEM)
    shape, dma = jax.ShapeDtypeStruct, pltpu.SemaphoreType.DMA
    return pl.pallas_call(
        functools.partial(project_kernel, size, contexts, chunk),
        in_specs=[anywhere] + [vmem] * 6 + [anywhere] * 3,
        out_specs=[anywhere] * 2 + [vmem] * 3 + [anywhere] + [vmem] * 2,
        out_shape=[
            shape((rows, features), BF),
            shape((rows, features), BF),
            shape((rows, 1), F32),
            shape((8, features), F32),
            shape((heads, HD, rows), BF),
            shape((2 * kvs, HD, contexts * rows), BF),
            shape((1, rows), jnp.int32),
            shape((rows, 1), F32),
        ],
        scratch_shapes=gather_scratch(size, rows, width, chunk)
        + [
            pltpu.VMEM((size, 8, width), F32),
            pltpu.VMEM((chunk, features), BF),
            pltpu.VMEM((chunk, features), BF),
            pltpu.VMEM((2 * kvs, HD, contexts * rows), BF),
            pltpu.VMEM(w_query.shape, BF),
            pltpu.VMEM(w_key_t.shape, BF),
            pltpu.VMEM(w_value_t.shape, BF),
            dma((size - 1,)),
            dma((size - 1,)),
            dma((groups, max(contexts - 1, 1))),
            dma((groups, max(contexts - 1, 1))),
            dma((3,)),
            dma((2,)),
            dma,
        ],
        compiler_params=pltpu.CompilerParams(
            collective_id=3, has_side_effects=True, vmem_limit_bytes=VMEM_LIMIT
        ),
        cost_estimate=pl.CostEstimate(
            flops=2 * rows * features * (heads + 2 * kvs) * HD,
            bytes_accessed=20 << 20,
            transcendentals=rows,
        ),
        name="project",
    )(own, gain_attn, gain_mlp, cos_tab, sin_tab, mask, starts, w_query, w_key_t, w_value_t)


def attend_kernel(
    size, chunk, key_rows,
    own, q, kv, kend,
    cot_o, mixed_o, lse_o,
    blocks, up_send, up_recv, down_send, down_recv, own_sem,
    full, keys_in_rows, acc, mx, sm, out_sem,
):
    rows, _ = own.shape
    heads, kvs, keys = q.shape[0], kv.shape[0] // 2, kv.shape[2]
    groups, group = rows // chunk, heads // kvs
    units = kvs * groups
    line = Gather(
        size, groups, chunk, own, blocks, (up_send, up_recv, down_send, down_recv, own_sem)
    )
    line.load_all()
    greet(others("tensor", size))
    line.begin()
    for h in range(kvs):
        keys_in_rows[h] = flip(kv[h]).astype(BF)

    def save(g):
        return pltpu.make_async_copy(full, cot_o.at[pl.ds(g * chunk, chunk)], out_sem)

    def join(g):
        @pl.when(g > 0)
        def _():
            save(g - 1).wait()

        part = pl.ds(pl.multiple_of(g * chunk, chunk), chunk)
        full[...] = jnp.concatenate([blocks[j, part, :] for j in range(size)], 1)
        save(g).start()

    def unit(u):
        pair, g = lax.div(u, groups), lax.rem(u, groups)
        part = pl.ds(pl.multiple_of(g * chunk, chunk), chunk)
        free, last = key_blocks(g, chunk, rows, keys, key_rows)
        acc[...] = jnp.zeros_like(acc)
        sm[...] = jnp.zeros_like(sm)
        mx[...] = jnp.full_like(mx, LOWEST)
        limit = kend[:, part]

        def step(masked, i, _):
            at = pl.multiple_of(i * key_rows, key_rows)
            k_blk = keys_in_rows[pair, pl.ds(at, key_rows), :]
            v_blk = kv[kvs + pair, :, pl.ds(at, key_rows)]
            if masked:
                keep = (lax.broadcasted_iota(jnp.int32, (key_rows, chunk), 0) + at) < limit
            for h in range(group):
                s = dot(k_blk, q[pair * group + h, :, part])
                if masked:
                    s = jnp.where(keep, s, LOWEST)
                old = mx[h]
                new = jnp.maximum(old, jnp.max(s, 0, keepdims=True))
                p = jnp.exp2(s * SCALE2 - new * SCALE2)
                alpha = jnp.exp2((old - new) * SCALE2)
                mx[h] = new
                sm[h] = sm[h] * alpha + jnp.sum(p, 0, keepdims=True)
                acc[h] = acc[h] * alpha + dot(v_blk, p.astype(BF))
            return 0

        lax.fori_loop(0, free, functools.partial(step, False), 0)
        lax.fori_loop(free, last, functools.partial(step, True), 0)
        for h in range(group):
            mixed_o[pair * group + h, :, part] = (acc[h] / sm[h]).astype(BF)
            lse_o[pair * group + h, :, part] = mx[h] * SCALE2 + jnp.log2(sm[h])

    def tick(k, _):
        line.tick(k, join)

        @pl.when(k < units)
        def _():
            unit(k)

        return 0

    lax.fori_loop(0, max(line.ticks, units), tick, 0)
    save(groups - 1).wait()
    line.drain()


def attend_forward(size, own, q, kv, kend, chunk):
    heads, _, rows = q.shape
    kvs, keys = kv.shape[0] // 2, kv.shape[2]
    group, width = heads // kvs, own.shape[1]
    key_rows = min(KEY_ROWS_FWD, keys)
    anywhere, vmem = pl.BlockSpec(memory_space=pl.ANY), pl.BlockSpec(memory_space=pltpu.VMEM)
    shape = jax.ShapeDtypeStruct
    return pl.pallas_call(
        functools.partial(attend_kernel, size, chunk, key_rows),
        in_specs=[anywhere] + [vmem] * 3,
        out_specs=[anywhere] + [vmem] * 2,
        out_shape=[
            shape((rows, size * width), BF),
            shape((heads, HD, rows), BF),
            shape((heads, 1, rows), F32),
        ],
        scratch_shapes=gather_scratch(size, rows, width, chunk)
        + [
            pltpu.VMEM((chunk, size * width), BF),
            pltpu.VMEM((kvs, keys, HD), BF),
            pltpu.VMEM((group, HD, chunk), F32),
            pltpu.VMEM((group, 1, chunk), F32),
            pltpu.VMEM((group, 1, chunk), F32),
            pltpu.SemaphoreType.DMA,
        ],
        compiler_params=pltpu.CompilerParams(
            collective_id=5, has_side_effects=True, vmem_limit_bytes=VMEM_LIMIT
        ),
        cost_estimate=pl.CostEstimate(
            flops=10 * heads * rows * keys * HD,
            bytes_accessed=16 << 20,
            transcendentals=heads * rows * keys,
        ),
        name="attend_forward",
    )(own, q, kv, kend)


def attend_back_kernel(
    size, contexts, chunk, key_rows,
    ffn, q, kv, kend, do, o, lse, cos_tab, sin_tab, middle, grad_attn, normed,
    grads_o, layer_o, square_o, weights_o,
    parts, ups, downs, total, up_send, up_recv, down_send, down_recv,
    keys_in_rows, values_in_rows, dq, dk, dv, ds_all, p_all, q_all, do_all, mine, out_kv, in_kv,
    grads_in, normed_in, tiles,
    kv_send, kv_recv, part_sem, tile_sem,
):
    heads, _, rows = q.shape
    kvs, keys = kv.shape[0] // 2, kv.shape[2]
    groups, group = rows // chunk, heads // kvs
    units = kvs * groups
    place = lax.axis_index("context")
    line = Scatter(
        size, groups, chunk, parts, ups, downs, (up_send, up_recv, down_send, down_recv)
    )
    loads = [
        pltpu.make_async_copy(a, b, part_sem.at[i])
        for i, (a, b) in enumerate(((ffn, parts), (grad_attn, grads_in), (normed, normed_in)))
    ]
    for load in loads:
        load.start()
    square_o[...] = jnp.zeros_like(square_o)
    peers = others("context", contexts)
    greet(others("tensor", size) + peers)
    for h in range(kvs):
        keys_in_rows[h] = flip(kv[h]).astype(BF)
        values_in_rows[h] = flip(kv[kvs + h]).astype(BF)
    loads[0].wait()

    def half(of):
        at = pl.ds(pl.multiple_of(of * rows, rows), rows)
        return dk[at, :].T, dv[at, :].T

    def kv_copy(pair, i):
        return pltpu.make_async_remote_copy(
            src_ref=out_kv.at[pair, i],
            dst_ref=in_kv.at[pair, i],
            send_sem=kv_send.at[pair, i],
            recv_sem=kv_recv.at[pair, i],
            device_id=peers[i],
            device_id_type=MESH_ID,
        )

    def unit(u):
        pair, g = lax.div(u, groups), lax.rem(u, groups)
        part = pl.ds(pl.multiple_of(g * chunk, chunk), chunk)
        free, last = key_blocks(g, chunk, rows, keys, key_rows)
        limit = kend[:, part]

        @pl.when(g == 0)
        def _():
            dk[...] = jnp.zeros_like(dk)
            dv[...] = jnp.zeros_like(dv)

        dq[...] = jnp.zeros_like(dq)
        delta = []
        for h in range(group):
            head = pair * group + h
            cols = slice(h * chunk, (h + 1) * chunk)
            q_all[:, cols] = q[head, :, part]
            do_all[:, cols] = do[head, :, part]
            delta.append(
                jnp.sum(do_all[:, cols].astype(F32) * o[head, :, part].astype(F32), 0, keepdims=True)
            )

        def step(masked, i, _):
            at = pl.multiple_of(i * key_rows, key_rows)
            k_blk = keys_in_rows[pair, pl.ds(at, key_rows), :]
            v_blk = values_in_rows[pair, pl.ds(at, key_rows), :]
            kt_blk = kv[pair, :, pl.ds(at, key_rows)]
            if masked:
                keep = (lax.broadcasted_iota(jnp.int32, (key_rows, chunk), 0) + at) < limit
            for h in range(group):
                cols = slice(h * chunk, (h + 1) * chunk)
                s = dot(k_blk, q_all[:, cols])
                p = jnp.exp2(s * SCALE2 - lse[pair * group + h, :, part])
                if masked:
                    p = jnp.where(keep, p, 0.0)
                dp = dot(v_blk, do_all[:, cols])
                ds = (p * (dp - delta[h])).astype(BF)
                p_all[:, cols] = p.astype(BF)
                ds_all[:, cols] = ds
                dq[h] += dot(kt_blk, ds)
            dk[pl.ds(at, key_rows), :] += dot_nt(ds_all[...], q_all[...])
            dv[pl.ds(at, key_rows), :] += dot_nt(p_all[...], do_all[...])
            return 0

        lax.fori_loop(0, free, functools.partial(step, False), 0)
        lax.fori_loop(free, last, functools.partial(step, True), 0)
        for h in range(group):
            grads_o[pair * group + h, :, part] = turn(
                dq[h] * SCALE, cos_tab[:, part], -sin_tab[:, part]
            ).astype(BF)

        @pl.when(g == groups - 1)
        def _():
            for i in range(contexts - 1):
                key, value = half(peers[i]["context"])
                out_kv[pair, i, 0] = key.astype(BF)
                out_kv[pair, i, 1] = value.astype(BF)
                kv_copy(pair, i).start()
            mine[pair, 0], mine[pair, 1] = half(place)

    def join():
        for pair in range(kvs):
            key, value = mine[pair, 0], mine[pair, 1]
            for i in range(contexts - 1):
                kv_copy(pair, i).wait()
                key = key + in_kv[pair, i, 0].astype(F32)
                value = value + in_kv[pair, i, 1].astype(F32)
            grads_o[heads + pair] = turn(key * SCALE, cos_tab[...], -sin_tab[...]).astype(BF)
            grads_o[heads + kvs + pair] = value.astype(BF)

    features = normed.shape[1]
    tile = tile_of(features, 256)
    tile_count, each = features // tile, 4

    def save_tile(j):
        slot = lax.rem(j, 2)
        return pltpu.make_async_copy(
            tiles.at[slot], weights_o.at[pl.ds(j * tile, tile)], tile_sem.at[slot]
        )

    def weight_tile(j):
        slot = lax.rem(j, 2)

        @pl.when(j >= 2)
        def _():
            save_tile(j - 2).wait()

        cols = pl.ds(pl.multiple_of(j * tile, tile), tile)
        out = dot_nt(flip(grads_in[:, cols]).astype(BF), o[...].reshape(heads * HD, rows))
        into = dot_nt(
            flip(normed_in[:, cols]).astype(BF), grads_o[...].reshape((heads + 2 * kvs) * HD, rows)
        )
        tiles[slot] = jnp.concatenate([out, into], 1).astype(BF)
        save_tile(j).start()

    def tick(k, _):
        line.tick(k)

        @pl.when(k < units)
        def _():
            unit(k)

        @pl.when(k == units)
        def _():
            join()
            for load in loads[1:]:
                load.wait()

        first = (k - units - 1) * each
        for j in range(each):

            @pl.when((first >= 0) & (first + j < tile_count))
            def _():
                weight_tile(first + j)

        return 0

    lax.fori_loop(0, max(line.count, units + 1 + -(-tile_count // each)), tick, 0)

    def then(part, ffn_out):
        square_o[...] += jnp.sum(ffn_out * ffn_out, 0, keepdims=True)
        layer_o[part, :] = (middle[part, :] + ffn_out).astype(BF)

    line.finish(total, then)
    for j in range(max(tile_count - 2, 0), tile_count):
        save_tile(j).wait()


def attend_backward(
    axes, ffn, q, kv, kend, do, o, lse, cos_tab, sin_tab, middle, grad_attn, normed, chunk, after
):
    size, contexts = axes["tensor"], axes["context"]
    heads, _, rows = q.shape
    kvs, keys = kv.shape[0] // 2, kv.shape[2]
    group, width = heads // kvs, ffn.shape[2]
    key_rows = min(KEY_ROWS_BWD, keys)
    anywhere, vmem = pl.BlockSpec(memory_space=pl.ANY), pl.BlockSpec(memory_space=pltpu.VMEM)
    shape, dma = jax.ShapeDtypeStruct, pltpu.SemaphoreType.DMA
    slots = max(contexts - 1, 1)

    def kernel(*refs):
        attend_back_kernel(size, contexts, chunk, key_rows, *refs[:12], *refs[12 + len(after) :])

    return pl.pallas_call(
        kernel,
        in_specs=[anywhere] + [vmem] * 9 + [anywhere] * (2 + len(after)),
        out_specs=[vmem] * 3 + [anywhere],
        out_shape=[
            shape((heads + 2 * kvs, HD, rows), BF),
            shape((rows, width), BF),
            shape((1, width), F32),
            shape((size * width, (2 * heads + 2 * kvs) * HD), BF),
        ],
        scratch_shapes=scatter_scratch(size, rows, width, chunk)
        + [
            pltpu.VMEM((kvs, keys, HD), BF),
            pltpu.VMEM((kvs, keys, HD), BF),
            pltpu.VMEM((group, HD, chunk), F32),
            pltpu.VMEM((keys, HD), F32),
            pltpu.VMEM((keys, HD), F32),
            pltpu.VMEM((key_rows, group * chunk), BF),
            pltpu.VMEM((key_rows, group * chunk), BF),
            pltpu.VMEM((HD, group * chunk), BF),
            pltpu.VMEM((HD, group * chunk), BF),
            pltpu.VMEM((kvs, 2, HD, rows), F32),
            pltpu.VMEM((kvs, slots, 2, HD, rows), BF),
            pltpu.VMEM((kvs, slots, 2, HD, rows), BF),
            pltpu.VMEM(grad_attn.shape, BF),
            pltpu.VMEM(normed.shape, BF),
            pltpu.VMEM((2, tile_of(size * width, 256), (2 * heads + 2 * kvs) * HD), BF),
            dma((kvs, slots)),
            dma((kvs, slots)),
            dma((3,)),
            dma((2,)),
        ],
        compiler_params=pltpu.CompilerParams(
            collective_id=6, has_side_effects=True, vmem_limit_bytes=VMEM_LIMIT
        ),
        cost_estimate=pl.CostEstimate(
            flops=16 * heads * rows * keys * HD,
            bytes_accessed=16 << 20,
            transcendentals=heads * rows * keys,
        ),
        name="attend_backward",
    )(ffn, q, kv, kend, do, o, lse, cos_tab, sin_tab, middle, grad_attn, normed, *after)


def input_kernel(
    axes, chunk,
    grads, inv, gain, keep, attn_square, gain_rows, ffn_square, gain_own, x_own, grad_own,
    w_query, w_key_t, w_value_t, x, ggu_sum, down_sum,
    out_o, sum_o, gate_o, up_o, down_o,
    parts, ups, downs, total, up_send, up_recv, down_send, down_recv,
    xs, wq, wk, wv, dots, dot_sum, cols, cols_in, world, square, ggu, downw, gate_f, up_f, down_f,
    dot_send, dot_recv, col_send, col_recv, world_send, world_recv, w_sem, x_sem, out_sem,
):
    size = axes["tensor"]
    here = lax.axis_index("tensor")
    rows, features = x.shape
    width, groups = features // size, rows // chunk
    nq, nk = w_query.shape[1], w_key_t.shape[0]
    hidden = down_sum.shape[1]
    line = Scatter(
        size, groups, chunk, parts, ups, downs, (up_send, up_recv, down_send, down_recv)
    )
    loads = [
        pltpu.make_async_copy(a, b, w_sem.at[i])
        for i, (a, b) in enumerate(
            ((w_query, wq), (w_key_t, wk), (w_value_t, wv), (ggu_sum, ggu), (down_sum, downw))
        )
    ]

    def load_x(c):
        slot = lax.rem(c, 2)
        return pltpu.make_async_copy(x.at[pl.ds(c * chunk, chunk)], xs.at[slot], x_sem.at[slot])

    for load in loads:
        load.start()
    load_x(0).start()
    contexts, replicas = axes["context"], axes["dp"] * axes["context"]
    spot = lax.axis_index("dp") * contexts + lax.axis_index("context")
    peers = others("tensor", size)
    far = [lax.rem(spot + i, replicas) for i in range(1, replicas)]
    far = [{"dp": lax.div(i, contexts), "context": lax.rem(i, contexts)} for i in far]
    greet(peers + far)
    for load in loads[:3]:
        load.wait()
    square[...] = jnp.zeros_like(square)
    row = lax.broadcasted_iota(jnp.int32, (8, width), 0)
    lane = lax.broadcasted_iota(jnp.int32, (8, width), 1)

    def compute(c):
        slot = lax.rem(c, 2)
        part = pl.ds(pl.multiple_of(c * chunk, chunk), chunk)
        load_x(c).wait()

        @pl.when(c + 1 < groups)
        def _():
            load_x(c + 1).start()

        g = flip(grads[:, part]).astype(BF)
        whole = (
            dot_nt(g[:, :nq], wq[...])
            + dot(g[:, nq : nq + nk], wk[...])
            + dot(g[:, nq + nk :], wv[...])
        )
        stream = xs[slot].astype(F32)
        square[...] += jnp.sum(stream * stream * keep[part, :], 0, keepdims=True)
        moved = whole * (stream * inv[part, :])
        rowsum = jnp.sum(moved * gain[0:1, :], 1, keepdims=True)
        dots[here, :, part] = jnp.broadcast_to(rowsum, (chunk, 128)).T[:8]
        colsum = jnp.sum(moved, 0, keepdims=True)
        low = whole.astype(BF)
        for j in range(size):
            parts[j, part, :] = low[:, j * width : (j + 1) * width]
            piece = jnp.where(row == 0, colsum[:, j * width : (j + 1) * width], 0.0)

            @pl.when(c == 0)
            def _():
                cols[j] = piece

            @pl.when(c > 0)
            def _():
                cols[j] += piece

    def copy_to(src, dst, send, recv, peer):
        return pltpu.make_async_remote_copy(
            src_ref=src,
            dst_ref=dst,
            send_sem=send,
            recv_sem=recv,
            device_id=peer,
            device_id_type=MESH_ID,
        )

    def dot_copy(i):
        mine = dots.at[here]
        return copy_to(mine, mine, dot_send.at[i], dot_recv.at[i], peers[i])

    def col_copy(i):
        src = cols.at[peers[i]["tensor"]]
        return copy_to(src, cols_in.at[here], col_send.at[i], col_recv.at[i], peers[i])

    def world_copy(i):
        mine = world.at[spot]
        return copy_to(mine, mine, world_send.at[i], world_recv.at[i], far[i])

    saves = [
        pltpu.make_async_copy(a, b, out_sem.at[i])
        for i, (a, b) in enumerate(((gate_f, gate_o), (up_f, up_o), (down_f, down_o)))
    ]

    def exchange():
        numbers = jnp.zeros((8, width), F32)
        for i, a in enumerate((square[...], attn_square[...], ffn_square[...], keep[...])):
            a = jnp.sum(jnp.sum(a, 0, keepdims=True), 1, keepdims=True)
            share = 1.0 if i == 2 else 1.0 / size
            numbers += jnp.where((row == 1) & (lane == i), a * share, 0.0)
        for j in range(size):
            cols[j] += numbers
        cols_in[here] = cols[here]
        for i in range(size - 1):
            dot_copy(i).start()
            col_copy(i).start()

    def spread():
        for i in range(size - 1):
            dot_copy(i).wait()
            col_copy(i).wait()
        dot_total, column = dots[0], cols_in[0]
        for j in range(1, size):
            dot_total = dot_total + dots[j]
            column = column + cols_in[j]
        dot_sum[...] = dot_total
        world[spot] = column

        def put(piece):
            world[spot, 2:3] = piece

        own_columns(size, gain_rows[...], put)
        for i in range(replicas - 1):
            world_copy(i).start()

    def tick(k, _):
        @pl.when(k < groups)
        def _():
            compute(k)

        line.tick(k)

        @pl.when(k == groups)
        def _():
            exchange()

        @pl.when(k == groups + 1)
        def _():
            for load in loads[3:]:
                load.wait()
            gate_f[...] = ggu[:, :hidden].astype(F32)
            saves[0].start()

        @pl.when(k == groups + 2)
        def _():
            up_f[...] = ggu[:, hidden:].astype(F32)
            saves[1].start()

        @pl.when(k == groups + 3)
        def _():
            spread()

        @pl.when(k == groups + 4)
        def _():
            down_f[...] = flip(downw[...])
            saves[2].start()

        return 0

    lax.fori_loop(0, max(line.count, groups + 5), tick, 0)

    def then(part, grad):
        through = grad * gain_own[...] - x_own[part, :].astype(F32) * inv[part, :] * (
            dot_sum[:, part].T[:, :1] / features
        )
        out_o[part, :] = (grad_own[part, :] + inv[part, :] * through).astype(BF)

    line.finish(total, then)
    for i in range(replicas - 1):
        world_copy(i).wait()
    everything = world[0]
    for j in range(1, replicas):
        everything = everything + world[j]
    sum_o[...] = everything
    for save in saves:
        save.wait()


def input_gradient(
    axes, grads, inv, gain, keep, attn_square, gain_rows, ffn_square, gain_own, x_own, grad_own,
    w_query, w_key_t, w_value_t, x, ggu_sum, down_sum, chunk, after,
):
    size, replicas = axes["tensor"], axes["dp"] * axes["context"]
    rows, features = x.shape
    width = features // size
    share, hidden = down_sum.shape
    anywhere, vmem = pl.BlockSpec(memory_space=pl.ANY), pl.BlockSpec(memory_space=pltpu.VMEM)
    shape, dma = jax.ShapeDtypeStruct, pltpu.SemaphoreType.DMA

    def kernel(*refs):
        input_kernel(axes, chunk, *refs[:16], *refs[16 + len(after) :])

    return pl.pallas_call(
        kernel,
        in_specs=[vmem] * 10 + [anywhere] * (6 + len(after)),
        out_specs=[vmem] * 2 + [anywhere] * 3,
        out_shape=[
            shape((rows, width), BF),
            shape((8, width), F32),
            shape((share, hidden), F32),
            shape((share, hidden), F32),
            shape((hidden, share), F32),
        ],
        scratch_shapes=scatter_scratch(size, rows, width, chunk)
        + [
            pltpu.VMEM((2, chunk, features), BF),
            pltpu.VMEM(w_query.shape, BF),
            pltpu.VMEM(w_key_t.shape, BF),
            pltpu.VMEM(w_value_t.shape, BF),
            pltpu.VMEM((size, 8, rows), F32),
            pltpu.VMEM((8, rows), F32),
            pltpu.VMEM((size, 8, width), F32),
            pltpu.VMEM((size, 8, width), F32),
            pltpu.VMEM((replicas, 8, width), F32),
            pltpu.VMEM((1, features), F32),
            pltpu.VMEM(ggu_sum.shape, BF),
            pltpu.VMEM(down_sum.shape, BF),
            pltpu.VMEM((share, hidden), F32),
            pltpu.VMEM((share, hidden), F32),
            pltpu.VMEM((hidden, share), F32),
            dma((size - 1,)),
            dma((size - 1,)),
            dma((size - 1,)),
            dma((size - 1,)),
            dma((replicas - 1,)),
            dma((replicas - 1,)),
            dma((5,)),
            dma((2,)),
            dma((3,)),
        ],
        compiler_params=pltpu.CompilerParams(
            collective_id=4, has_side_effects=True, vmem_limit_bytes=VMEM_LIMIT
        ),
        cost_estimate=pl.CostEstimate(
            flops=2 * rows * features * grads.shape[0],
            bytes_accessed=20 << 20,
            transcendentals=rows,
        ),
        name="input_gradient",
    )(
        grads, inv, gain, keep, attn_square, gain_rows, ffn_square, gain_own, x_own, grad_own,
        w_query, w_key_t, w_value_t, x, ggu_sum, down_sum, *after,
    )


def local(
    axes,
    layer_input_hidden,
    cotangent,
    valid_mask,
    span_starts,
    gain_attn,
    w_query,
    w_key,
    w_value,
    w_out,
    gain_mlp,
    w_gate,
    w_up,
    w_down,
):
    _, rows, width = layer_input_hidden.shape
    size = axes["tensor"]
    features = width * size
    kvs = w_key.shape[1] // HD
    heads = w_query.shape[1] // HD
    position = lax.axis_index("context") * rows + jnp.arange(rows, dtype=jnp.int32)
    inverse_freq = rope_base ** (-2.0 * jnp.arange(HD // 2, dtype=F32) / HD)
    angles = inverse_freq[:, None] * position.astype(F32)[None, :]
    cos_tab, sin_tab = jnp.cos(angles), jnp.sin(angles)
    x_own = layer_input_hidden[0]
    w_key_t, w_value_t = w_key.T, w_value.T

    def shard(grad):
        return lax.psum_scatter(grad, ("dp", "context"), scatter_dimension=0, tiled=True)

    x_low, normed_a, inv_a, gains, query_t, both, kend, keep = project(
        axes,
        x_own,
        gain_attn[None],
        gain_mlp[None],
        cos_tab,
        sin_tab,
        valid_mask,
        span_starts,
        w_query,
        w_key_t,
        w_value_t,
        GROUP_ROWS,
    )
    cot, mixed, lse = attend_forward(size, cotangent[0], query_t, both, kend, GROUP_ROWS)
    normed_m, act, ggu, down_part, back_part, middle, middle_own, attn_square = feed_forward(
        size,
        mixed.reshape(heads * HD, rows),
        keep,
        gains,
        w_out,
        w_gate,
        w_up,
        w_down,
        x_low,
        cot,
        GROUP_ROWS,
        HOP_ROWS,
    )
    grad_ggu = ein("sd,sf->df", normed_m, ggu).astype(BF)
    ggu_sum = shard(grad_ggu)

    grad_own, grad_attn, grad_mixed, gain_m_rows, grad_down = norm_back(
        size, back_part, keep, gains, w_out, middle, cot, act, GROUP_ROWS, HOP_ROWS, (grad_ggu,)
    )
    down_sum = shard(grad_down)
    grads, layer_out, ffn_square, grad_rest = attend_backward(
        axes,
        down_part,
        query_t,
        both,
        kend,
        grad_mixed.reshape(heads, HD, rows),
        mixed,
        lse,
        cos_tab,
        sin_tab,
        middle_own,
        grad_attn,
        normed_a,
        GROUP_ROWS,
        (grad_down,),
    )
    rest_sum = shard(grad_rest)

    input_grad, sums, gate_sum, up_sum, down_sum = input_gradient(
        axes,
        grads.reshape(-1, rows),
        inv_a,
        gains,
        keep,
        attn_square,
        gain_m_rows,
        ffn_square,
        gain_attn[None],
        x_own,
        grad_own,
        w_query,
        w_key_t,
        w_value_t,
        x_low,
        ggu_sum,
        down_sum,
        GROUP_ROWS,
        (grad_rest,),
    )
    rest_sum = rest_sum.astype(F32)
    cut = [heads * HD, 2 * heads * HD, (2 * heads + kvs) * HD]
    out_sum, query_sum, key_sum, value_sum = jnp.split(rest_sum, cut, 1)
    rms = jnp.sqrt(sums[1, :3] / (sums[1, 3] * features))
    return (
        layer_out[None],
        input_grad[None],
        sums[0],
        query_sum,
        key_sum,
        value_sum,
        out_sum.T,
        sums[2],
        gate_sum,
        up_sum,
        down_sum,
        rms[0],
        rms[1],
        rms[2],
    )


def solution(mesh):
    token = P("dp", "context", "tensor")
    by_rows = P(("dp", "context"), "tensor")
    by_columns = P("tensor", ("dp", "context"))
    cols, rows, vec = P(None, "tensor"), P("tensor", None), P("tensor")
    return jax.shard_map(
        functools.partial(local, dict(mesh.shape)),
        mesh=mesh,
        in_specs=(
            token,
            token,
            P("dp", None),
            P("dp", None),
            vec,
            cols,
            cols,
            cols,
            rows,
            vec,
            cols,
            cols,
            rows,
        ),
        out_specs=(
            token,
            token,
            vec,
            by_rows,
            by_rows,
            by_rows,
            by_columns,
            vec,
            by_rows,
            by_rows,
            by_columns,
            P(),
            P(),
            P(),
        ),
        check_vma=False,
    )
```

```python
import functools
import math

import jax
import jax.numpy as jnp
from jax import lax
from jax.experimental import pallas as pl
from jax.experimental.pallas import tpu as pltpu
from jax.sharding import PartitionSpec as P

HD = 80
PIC = 256
LEAST_VALID = 1536
F32 = jnp.float32
BF = jnp.bfloat16
SCALE = HD**-0.5
SCALE2 = SCALE * math.log2(math.e)
LOWEST = -1e30
GROUP_ROWS = 256
HOP_ROWS = 64
VMEM_LIMIT = 60 << 20
KEY_ROWS_FWD = 1024
KEY_ROWS_BWD = 512

epsilon = 1e-05
rope_base = 1000000.0


def dot(a, b):
    return jnp.dot(a, b, preferred_element_type=F32)


def dot_nt(a, b):
    return lax.dot_general(a, b, (((1,), (1,)), ((), ())), preferred_element_type=F32)


def ein(spec, a, b):
    return jnp.einsum(spec, a, b, preferred_element_type=F32)


MESH_ID = pl.DeviceIdType.MESH
RING = 8
SENT = 4


def add_low(a, b):
    return (a.astype(F32) + b.astype(F32)).astype(BF)


class Sums:
    def __init__(self, size, count, part, low, high, sent, sems):
        self.size, self.count, self.part = size, count, part
        self.low, self.high, self.sent = low, high, sent
        self.low_send, self.low_recv, self.high_send, self.high_recv = sems
        self.here = lax.axis_index("tensor")

    def barrier(self):
        here, size = self.here, self.size
        barrier = pltpu.get_barrier_semaphore()

        @pl.when(here > 0)
        def _():
            pl.semaphore_signal(
                barrier, inc=1, device_id={"tensor": here - 1}, device_id_type=MESH_ID
            )

        @pl.when(here < size - 1)
        def _():
            pl.semaphore_signal(
                barrier, inc=1, device_id={"tensor": here + 1}, device_id_type=MESH_ID
            )

        @pl.when((here > 0) & (here < size - 1))
        def _():
            pl.semaphore_wait(barrier, 2)

        @pl.when((here == 0) | (here == size - 1))
        def _():
            pl.semaphore_wait(barrier, 1)

    def up(self, c):
        slot = lax.rem(c, RING)
        return pltpu.make_async_remote_copy(
            src_ref=self.low.at[slot],
            dst_ref=self.low.at[slot],
            send_sem=self.low_send.at[slot],
            recv_sem=self.low_recv.at[slot],
            device_id={"tensor": self.here + 1},
            device_id_type=MESH_ID,
        )

    def down(self, c):
        slot, mine = lax.rem(c, RING), lax.rem(c, SENT)
        return pltpu.make_async_remote_copy(
            src_ref=self.sent.at[mine],
            dst_ref=self.high.at[slot],
            send_sem=self.high_send.at[mine],
            recv_sem=self.high_recv.at[slot],
            device_id={"tensor": self.here - 1},
            device_id_type=MESH_ID,
        )

    def tick(self, k):
        here, size, count = self.here, self.size, self.count
        bottom, top = here == 0, here == size - 1
        c = k - here

        @pl.when((c >= 0) & (c < count))
        def _():
            slot = lax.rem(c, RING)

            @pl.when(bottom)
            def _():
                self.low[slot] = self.part(c)

            @pl.when(jnp.logical_not(bottom))
            def _():
                self.up(c).wait_recv()
                self.low[slot] = add_low(self.low[slot], self.part(c))

            @pl.when(jnp.logical_not(top))
            def _():
                self.up(c).start()

        d = k - (size - 1 - here)

        @pl.when((d >= 0) & (d < count))
        def _():
            slot, mine = lax.rem(d, RING), lax.rem(d, SENT)

            @pl.when(top)
            def _():
                self.sent[mine] = self.part(d)

            @pl.when(jnp.logical_not(top))
            def _():
                self.down(d).wait_recv()

                @pl.when(jnp.logical_not(bottom))
                def _():
                    self.sent[mine] = add_low(self.high[slot], self.part(d))

            @pl.when(jnp.logical_not(bottom))
            def _():
                self.down(d).start()

        @pl.when((c >= 2) & (c < count + 2) & jnp.logical_not(top))
        def _():
            self.up(c - 2).wait_send()

        @pl.when((d >= 2) & (d < count + 2) & jnp.logical_not(bottom))
        def _():
            self.down(d - 2).wait_send()

    def total(self, c, then):
        slot = lax.rem(c, RING)
        top = self.here == self.size - 1

        @pl.when(top)
        def _():
            then(self.low[slot].astype(F32))

        @pl.when(jnp.logical_not(top))
        def _():
            then(self.low[slot].astype(F32) + self.high[slot].astype(F32))


def sum_scratch(hop, features):
    return [
        pltpu.VMEM((RING, hop, features), BF),
        pltpu.VMEM((RING, hop, features), BF),
        pltpu.VMEM((SENT, hop, features), BF),
        pltpu.SemaphoreType.DMA((RING,)),
        pltpu.SemaphoreType.DMA((RING,)),
        pltpu.SemaphoreType.DMA((SENT,)),
        pltpu.SemaphoreType.DMA((RING,)),
    ]


def own_columns(size, a, then):
    width = a.shape[1] // size
    for j in range(size):

        @pl.when(lax.axis_index("tensor") == j)
        def _():
            then(a[:, j * width : (j + 1) * width])


def tile_of(n, most):
    for tile in range(most, 0, -128):
        if n % tile == 0:
            return tile
    return n


def ffn_kernel(
    size, hop, chunk,
    mixed, keep, gain, w_out, w_gate, w_up, w_down, x, cot,
    normed_o, act_o, ggu_o, ffn_o, back_o, middle_o, own_o, square_o,
    low, high, sent, low_send, low_recv, high_send, high_recv,
    wo, wg, wu, wd, parts, normed, xs, cots, mids, owns, act, ggu, ffn, back, split,
    w_sem, x_sem, cot_sem, normed_sem, mid_sem, own_sem, act_sem, ffn_sem,
):
    rows, features = x.shape
    hidden = w_gate.shape[1]
    count, per, groups = rows // hop, chunk // hop, rows // chunk
    tile_f, tile_d = tile_of(hidden, 256), tile_of(features, 256)
    tiles_f, tiles_d = hidden // tile_f, features // tile_d
    half_f, half_d = -(-tiles_f // 2), -(-tiles_d // 2)
    lag = size - 1 + per - 1
    ticks = max(per * groups + lag, count + size)

    def part(c):
        return parts[lax.rem(lax.div(c, per), 2), pl.ds(pl.multiple_of(lax.rem(c, per) * hop, hop), hop), :]

    sums = Sums(size, count, part, low, high, sent, (low_send, low_recv, high_send, high_recv))
    loads = [
        pltpu.make_async_copy(a, b, w_sem.at[i])
        for i, (a, b) in enumerate(((w_out, wo), (w_gate, wg), (w_up, wu), (w_down, wd)))
    ]
    for load in loads:
        load.start()

    def load_x(c):
        slot = lax.rem(c, 2)
        return pltpu.make_async_copy(x.at[pl.ds(c * hop, hop)], xs.at[slot], x_sem.at[slot])

    def load_cot(g):
        return pltpu.make_async_copy(cot.at[pl.ds(g * chunk, chunk)], cots, cot_sem)

    def save_normed(c):
        at, q = lax.rem(lax.div(c, per), 2), lax.rem(c, per)
        return pltpu.make_async_copy(
            normed.at[at, pl.ds(q * hop, hop)], normed_o.at[pl.ds(c * hop, hop)], normed_sem.at[at, q]
        )

    def save_mid(c):
        slot = lax.rem(c, 2)
        return pltpu.make_async_copy(mids.at[slot], middle_o.at[pl.ds(c * hop, hop)], mid_sem.at[slot])

    def save_own(c):
        slot = lax.rem(c, 2)
        return pltpu.make_async_copy(owns.at[slot], own_o.at[pl.ds(c * hop, hop)], own_sem.at[slot])

    def save_act(g):
        return [
            pltpu.make_async_copy(a, b.at[pl.ds(g * chunk, chunk)], act_sem.at[i])
            for i, (a, b) in enumerate(((act, act_o), (ggu, ggu_o)))
        ]

    def save_ffn(g):
        part = pl.ds(g * chunk, chunk)
        return [
            pltpu.make_async_copy(split, ffn_o.at[:, part], ffn_sem.at[0]),
            pltpu.make_async_copy(back, back_o.at[part], ffn_sem.at[1]),
        ]

    def project(g):
        at = lax.rem(g, 2)
        lhs = mixed[:, pl.ds(pl.multiple_of(g * chunk, chunk), chunk)]

        def one(j, _):
            cols = pl.ds(pl.multiple_of(j * tile_d, tile_d), tile_d)
            parts[at, :, cols] = lax.dot_general(
                lhs, wo[:, cols], (((0,), (0,)), ((), ())), preferred_element_type=F32
            ).astype(BF)
            return 0

        lax.fori_loop(0, tiles_d, one, 0)

    load_x(0).start()
    load_cot(0).start()
    square_o[...] = jnp.zeros_like(square_o)
    loads[0].wait()
    project(0)
    sums.barrier()

    def finish(c):
        slot = lax.rem(c, 2)
        load_x(c).wait()

        @pl.when(c + 1 < count)
        def _():
            load_x(c + 1).start()

        @pl.when(c >= 2)
        def _():
            save_mid(c - 2).wait()
            save_own(c - 2).wait()

        @pl.when(c >= 2 * per)
        def _():
            save_normed(c - 2 * per).wait()

        kept = keep[pl.ds(pl.multiple_of(c * hop, hop), hop), :]

        def then(total):
            out = kept * total
            square_o[...] += jnp.sum(out * out, 0, keepdims=True)
            mids[slot] = xs[slot].astype(F32) + out

        sums.total(c, then)
        mid = mids[slot]
        own_columns(size, mid, lambda piece: owns.__setitem__(slot, piece))
        save_own(c).start()
        inv = lax.rsqrt(jnp.sum(mid * mid, 1, keepdims=True) / features + epsilon)
        at = lax.rem(lax.div(c, per), 2)
        normed[at, pl.ds(pl.multiple_of(lax.rem(c, per) * hop, hop), hop), :] = (
            mid * inv * gain[1:2, :]
        ).astype(BF)
        save_mid(c).start()
        save_normed(c).start()

    def inner(g, lo, hi):
        at = lax.rem(g, 2)
        kept = keep[pl.ds(pl.multiple_of(g * chunk, chunk), chunk), :]

        def one(j, _):
            cols = pl.ds(pl.multiple_of(j * tile_f, tile_f), tile_f)
            gate = dot(normed[at], wg[:, cols])
            up = dot(normed[at], wu[:, cols])
            grad = dot_nt(cots[...], wd[cols, :]) * kept
            sig = jax.nn.sigmoid(gate)
            silu = gate * sig
            act[:, cols] = (silu * up * kept).astype(BF)
            ggu[:, cols] = (grad * up * (sig + silu * (1.0 - sig))).astype(BF)
            cols = pl.ds(pl.multiple_of(hidden + j * tile_f, tile_f), tile_f)
            ggu[:, cols] = (grad * silu).astype(BF)
            return 0

        lax.fori_loop(lo, hi, one, 0)

    def outer(g, lo, hi):
        def one(j, _):
            cols = pl.ds(pl.multiple_of(j * tile_d, tile_d), tile_d)
            ffn[:, cols] = dot(act[...], wd[:, cols]).astype(BF)
            back[:, cols] = (
                dot_nt(ggu[:, :hidden], wg[cols, :]) + dot_nt(ggu[:, hidden:], wu[cols, :])
            ).astype(BF)
            return 0

        lax.fori_loop(lo, hi, one, 0)

    def tick(k, _):
        sums.tick(k)
        c = k - (size - 1)

        @pl.when((c >= 0) & (c < count))
        def _():
            finish(c)

        ahead = k + 2

        @pl.when((lax.rem(ahead, per) == 0) & (ahead < count))
        def _():
            project(lax.div(ahead, per))

        s = k - lag
        g, stage = lax.div(s, per), lax.rem(s, per)
        going = (s >= 0) & (g < groups)

        @pl.when(going & (stage == 0))
        def _():
            @pl.when(g == 0)
            def _():
                for load in loads[1:]:
                    load.wait()

            load_cot(g).wait()

            @pl.when(g > 0)
            def _():
                for copy in save_act(g - 1):
                    copy.wait()

            inner(g, 0, half_f)

        @pl.when(going & (stage == 1))
        def _():
            inner(g, half_f, tiles_f)
            for copy in save_act(g):
                copy.start()

            @pl.when(g + 1 < groups)
            def _():
                load_cot(g + 1).start()

        @pl.when(going & (stage == 2))
        def _():
            @pl.when(g > 0)
            def _():
                for copy in save_ffn(g - 1):
                    copy.wait()

            outer(g, 0, half_d)

        @pl.when(going & (stage == 3))
        def _():
            outer(g, half_d, tiles_d)
            for j in range(size):
                split[j] = ffn[:, j * (features // size) : (j + 1) * (features // size)]
            for copy in save_ffn(g):
                copy.start()

        return 0

    lax.fori_loop(0, ticks, tick, 0)
    for copy in save_act(groups - 1) + save_ffn(groups - 1):
        copy.wait()
    for c in range(count - 2, count):
        save_mid(c).wait()
        save_own(c).wait()
    for c in range(count - 2 * per, count):
        save_normed(c).wait()


def feed_forward(size, mixed, keep, gain, w_out, w_gate, w_up, w_down, x, cot, chunk, hop):
    rows, features = x.shape
    hidden = w_gate.shape[1]
    per = chunk // hop
    assert per == 4
    anywhere, vmem = pl.BlockSpec(memory_space=pl.ANY), pl.BlockSpec(memory_space=pltpu.VMEM)
    shape = jax.ShapeDtypeStruct
    return pl.pallas_call(
        functools.partial(ffn_kernel, size, hop, chunk),
        in_specs=[vmem] * 3 + [anywhere] * 6,
        out_specs=[anywhere] * 7 + [vmem],
        out_shape=[
            shape((rows, features), BF),
            shape((rows, hidden), BF),
            shape((rows, 2 * hidden), BF),
            shape((size, rows, features // size), BF),
            shape((rows, features), BF),
            shape((rows, features), F32),
            shape((rows, features // size), F32),
            shape((1, features), F32),
        ],
        scratch_shapes=sum_scratch(hop, features)
        + [
            pltpu.VMEM(w_out.shape, BF),
            pltpu.VMEM(w_gate.shape, BF),
            pltpu.VMEM(w_up.shape, BF),
            pltpu.VMEM(w_down.shape, BF),
            pltpu.VMEM((2, chunk, features), BF),
            pltpu.VMEM((2, chunk, features), BF),
            pltpu.VMEM((2, hop, features), BF),
            pltpu.VMEM((chunk, features), BF),
            pltpu.VMEM((2, hop, features), F32),
            pltpu.VMEM((2, hop, features // size), F32),
            pltpu.VMEM((chunk, hidden), BF),
            pltpu.VMEM((chunk, 2 * hidden), BF),
            pltpu.VMEM((chunk, features), BF),
            pltpu.VMEM((chunk, features), BF),
            pltpu.VMEM((size, chunk, features // size), BF),
            pltpu.SemaphoreType.DMA((4,)),
            pltpu.SemaphoreType.DMA((2,)),
            pltpu.SemaphoreType.DMA,
            pltpu.SemaphoreType.DMA((2, per)),
            pltpu.SemaphoreType.DMA((2,)),
            pltpu.SemaphoreType.DMA((2,)),
            pltpu.SemaphoreType.DMA((2,)),
            pltpu.SemaphoreType.DMA((2,)),
        ],
        compiler_params=pltpu.CompilerParams(
            collective_id=1, has_side_effects=True, vmem_limit_bytes=VMEM_LIMIT
        ),
        cost_estimate=pl.CostEstimate(
            flops=2 * rows * features * (6 * hidden + w_out.shape[0]),
            bytes_accessed=80 << 20,
            transcendentals=rows * hidden,
        ),
        name="feed_forward",
    )(mixed, keep, gain, w_out, w_gate, w_up, w_down, x, cot)


def back_kernel(
    size, hop, chunk,
    parts, keep, gain, w_out, middle, cot, act,
    own_o, grad_low_o, mixed_o, gain_o, down_o,
    low, high, sent, low_send, low_recv, high_send, high_recv,
    wo, mids, cots, acts, owns, grads_low, tiles,
    load_sem, mid_sem, own_sem, grad_low_sem, tile_sem,
):
    rows, features = middle.shape
    count, per, groups = rows // hop, chunk // hop, rows // chunk
    tile = tile_of(features, 256)
    tile_count = features // tile
    ticks = max(count + size, per * (groups - 1) + size - 1 + per, tile_count + 1)

    def part(c):
        return parts[pl.ds(pl.multiple_of(c * hop, hop), hop), :]

    sums = Sums(size, count, part, low, high, sent, (low_send, low_recv, high_send, high_recv))
    loads = [
        pltpu.make_async_copy(a, b, load_sem.at[i])
        for i, (a, b) in enumerate(((cot, cots), (w_out, wo), (act, acts)))
    ]

    def load_mid(c):
        slot = lax.rem(c, 2)
        return pltpu.make_async_copy(
            middle.at[pl.ds(c * hop, hop)], mids.at[slot], mid_sem.at[slot]
        )

    def save_own(c):
        slot = lax.rem(c, 2)
        return pltpu.make_async_copy(owns.at[slot], own_o.at[pl.ds(c * hop, hop)], own_sem.at[slot])

    def save_low(c):
        q = lax.rem(c, per)
        return pltpu.make_async_copy(
            grads_low.at[pl.ds(q * hop, hop)], grad_low_o.at[pl.ds(c * hop, hop)], grad_low_sem.at[q]
        )

    def save_tile(j):
        slot = lax.rem(j, 2)
        return pltpu.make_async_copy(
            tiles.at[slot], down_o.at[pl.ds(j * tile, tile)], tile_sem.at[slot]
        )

    load_mid(0).start()
    for load in loads:
        load.start()
    gain_o[...] = jnp.zeros_like(gain_o)
    sums.barrier()

    def finish(c):
        slot = lax.rem(c, 2)
        load_mid(c).wait()

        @pl.when(c + 1 < count)
        def _():
            load_mid(c + 1).start()

        @pl.when(c >= 2)
        def _():
            save_own(c - 2).wait()

        @pl.when(c >= per)
        def _():
            save_low(c - per).wait()

        chunk_rows = pl.ds(pl.multiple_of(c * hop, hop), hop)
        kept = keep[chunk_rows, :]
        mid = mids[slot]
        inv = lax.rsqrt(jnp.sum(mid * mid, 1, keepdims=True) / features + epsilon)
        hat = mid * inv

        def then(total):
            gain_o[...] += jnp.sum(total * hat, 0, keepdims=True)
            weighted = total * gain[1:2, :]
            mean = jnp.sum(weighted * hat, 1, keepdims=True) / features
            mids[slot] = cots[chunk_rows, :].astype(F32) + inv * (weighted - hat * mean)

        sums.total(c, then)
        grad = mids[slot]
        own_columns(size, grad, lambda piece: owns.__setitem__(slot, piece))
        grads_low[pl.ds(pl.multiple_of(lax.rem(c, per) * hop, hop), hop), :] = (kept * grad).astype(
            BF
        )
        save_own(c).start()
        save_low(c).start()

    def weight_tile(j):
        slot = lax.rem(j, 2)

        @pl.when(j >= 2)
        def _():
            save_tile(j - 2).wait()

        cols = pl.ds(pl.multiple_of(j * tile, tile), tile)
        tiles[slot] = dot(flip(cots[:, cols]).astype(BF), acts[...]).astype(BF)
        save_tile(j).start()

    def tick(k, _):
        sums.tick(k)
        c = k - (size - 1)

        @pl.when(k == 1)
        def _():
            for load in loads:
                load.wait()

        @pl.when((c >= 0) & (c < count))
        def _():
            finish(c)

            @pl.when(lax.rem(c, per) == per - 1)
            def _():
                g = lax.div(c, per)
                mixed_o[:, pl.ds(pl.multiple_of(g * chunk, chunk), chunk)] = dot_nt(
                    wo[...], grads_low[...]
                ).astype(BF)

        @pl.when((k >= 1) & (k <= tile_count))
        def _():
            weight_tile(k - 1)

        return 0

    lax.fori_loop(0, ticks, tick, 0)
    for c in range(count - 2, count):
        save_own(c).wait()
    for c in range(count - per, count):
        save_low(c).wait()
    for j in range(max(tile_count - 2, 0), tile_count):
        save_tile(j).wait()


def norm_back(size, parts, keep, gain, w_out, middle, cot, act, chunk, hop, after):
    rows, features = middle.shape
    per = chunk // hop
    anywhere, vmem = pl.BlockSpec(memory_space=pl.ANY), pl.BlockSpec(memory_space=pltpu.VMEM)
    shape, dma = jax.ShapeDtypeStruct, pltpu.SemaphoreType.DMA

    def kernel(*refs):
        back_kernel(size, hop, chunk, *refs[:7], *refs[7 + len(after) :])

    return pl.pallas_call(
        kernel,
        in_specs=[vmem] * 3 + [anywhere] * (4 + len(after)),
        out_specs=[anywhere] * 2 + [vmem] * 2 + [anywhere],
        out_shape=[
            shape((rows, features // size), F32),
            shape((rows, features), BF),
            shape((w_out.shape[0], rows), BF),
            shape((1, features), F32),
            shape((features, act.shape[1]), BF),
        ],
        scratch_shapes=sum_scratch(hop, features)
        + [
            pltpu.VMEM(w_out.shape, BF),
            pltpu.VMEM((2, hop, features), F32),
            pltpu.VMEM(cot.shape, BF),
            pltpu.VMEM(act.shape, BF),
            pltpu.VMEM((2, hop, features // size), F32),
            pltpu.VMEM((chunk, features), BF),
            pltpu.VMEM((2, tile_of(features, 256), act.shape[1]), BF),
            dma((3,)),
            dma((2,)),
            dma((2,)),
            dma((per,)),
            dma((2,)),
        ],
        compiler_params=pltpu.CompilerParams(
            collective_id=2, has_side_effects=True, vmem_limit_bytes=VMEM_LIMIT
        ),
        cost_estimate=pl.CostEstimate(
            flops=2 * rows * features * (w_out.shape[0] + act.shape[1]),
            bytes_accessed=40 << 20,
            transcendentals=rows,
        ),
        name="norm_back",
    )(parts, keep, gain, w_out, middle, cot, act, *after)


def greet(peers):
    barrier = pltpu.get_barrier_semaphore()
    for peer in peers:
        pl.semaphore_signal(barrier, inc=1, device_id=peer, device_id_type=MESH_ID)
    pl.semaphore_wait(barrier, len(peers))


def others(axis, size):
    here = lax.axis_index(axis)
    return [{axis: lax.rem(here + i, size)} for i in range(1, size)]


class Gather:
    def __init__(self, size, groups, chunk, own, blocks, sems):
        self.size, self.groups, self.chunk = size, groups, chunk
        self.own, self.blocks = own, blocks
        self.up_send, self.up_recv, self.down_send, self.down_recv, self.own_sem = sems
        self.steps = size - 1
        self.ticks = groups * self.steps + 1
        self.here = lax.axis_index("tensor")

    def load(self, g):
        part = pl.ds(g * self.chunk, self.chunk)
        return pltpu.make_async_copy(
            self.own.at[part], self.blocks.at[self.here, part], self.own_sem.at[g]
        )

    def load_all(self):
        for g in range(self.groups):
            self.load(g).start()

    def move(self, g, s, owner, peer, send, recv):
        block = self.blocks.at[jnp.clip(owner, 0, self.size - 1), pl.ds(g * self.chunk, self.chunk)]
        return pltpu.make_async_remote_copy(
            src_ref=block,
            dst_ref=block,
            send_sem=send.at[g, s],
            recv_sem=recv.at[g, s],
            device_id={"tensor": peer},
            device_id_type=MESH_ID,
        )

    def up(self, g, s):
        return self.move(g, s, self.here - s, self.here + 1, self.up_send, self.up_recv)

    def down(self, g, s):
        return self.move(g, s, self.here + s, self.here - 1, self.down_send, self.down_recv)

    def each(self, g, s, act):
        @pl.when((self.here >= s) & (self.here < self.size - 1))
        def _():
            act(self.up(g, s))

        @pl.when((self.here + s < self.size) & (self.here > 0))
        def _():
            act(self.down(g, s))

    def send(self, g, s):
        self.each(g, s, lambda copy: copy.start())

    def receive(self, g, s):
        @pl.when(self.here - 1 - s >= 0)
        def _():
            self.up(g, s).wait_recv()

        @pl.when(self.here + 1 + s < self.size)
        def _():
            self.down(g, s).wait_recv()

    def begin(self):
        self.load(0).wait()
        self.send(0, 0)

    def tick(self, k, then):
        g, s = lax.div(k, self.steps), lax.rem(k, self.steps)

        @pl.when((s > 0) & (g < self.groups))
        def _():
            self.receive(g, s - 1)
            self.send(g, s)

        @pl.when((s == self.steps - 1) & (g + 1 < self.groups))
        def _():
            self.load(g + 1).wait()
            self.send(g + 1, 0)

        @pl.when((s == 0) & (g > 0) & (g <= self.groups))
        def _():
            self.receive(g - 1, self.steps - 1)
            then(g - 1)

    def drain(self):
        for g in range(self.groups):
            for s in range(self.steps):
                self.each(g, s, lambda copy: copy.wait_send())


def gather_scratch(size, rows, width, chunk):
    dma, groups = pltpu.SemaphoreType.DMA, rows // chunk
    return [pltpu.VMEM((size, rows, width), BF)] + [dma((groups, size - 1))] * 4 + [dma((groups,))]


class Scatter:
    def __init__(self, size, groups, chunk, parts, ups, downs, sems):
        self.size, self.groups, self.chunk = size, groups, chunk
        self.parts, self.ups, self.downs = parts, ups, downs
        self.up_send, self.up_recv, self.down_send, self.down_recv = sems
        self.count = (size - 1) * groups
        self.here = lax.axis_index("tensor")

    def rows(self, m):
        return pl.ds(pl.multiple_of(lax.rem(m, self.groups) * self.chunk, self.chunk), self.chunk)

    def up(self, m, first):
        owner = self.size - 1 - lax.div(m, self.groups)
        return pltpu.make_async_remote_copy(
            src_ref=self.parts.at[owner, self.rows(m)] if first else self.ups.at[m],
            dst_ref=self.ups.at[m],
            send_sem=self.up_send.at[m],
            recv_sem=self.up_recv.at[m],
            device_id={"tensor": self.here + 1},
            device_id_type=MESH_ID,
        )

    def down(self, m, first):
        owner = lax.div(m, self.groups)
        return pltpu.make_async_remote_copy(
            src_ref=self.parts.at[owner, self.rows(m)] if first else self.downs.at[m],
            dst_ref=self.downs.at[m],
            send_sem=self.down_send.at[m],
            recv_sem=self.down_recv.at[m],
            device_id={"tensor": self.here - 1},
            device_id_type=MESH_ID,
        )

    def tick(self, k):
        bottom, top = self.here == 0, self.here == self.size - 1
        m = k - self.here
        owner = self.size - 1 - lax.div(m, self.groups)

        @pl.when((m >= 0) & (owner > self.here))
        def _():
            @pl.when(bottom)
            def _():
                self.up(m, True).start()

            @pl.when(jnp.logical_not(bottom))
            def _():
                self.up(m, False).wait_recv()
                self.ups[m] = add_low(self.ups[m], self.parts[owner, self.rows(m), :])
                self.up(m, False).start()

        n = k - (self.size - 1 - self.here)
        below = lax.div(n, self.groups)

        @pl.when((n >= 0) & (below < self.here))
        def _():
            @pl.when(top)
            def _():
                self.down(n, True).start()

            @pl.when(jnp.logical_not(top))
            def _():
                self.down(n, False).wait_recv()
                self.downs[n] = add_low(self.downs[n], self.parts[below, self.rows(n), :])
                self.down(n, False).start()

    def finish(self, total, then):
        here = self.here

        def last(c, _):
            part = self.rows(c)
            m, n = (self.size - 1 - here) * self.groups + c, here * self.groups + c
            total[...] = self.parts[here, part, :].astype(F32)

            @pl.when(here > 0)
            def _():
                self.up(m, False).wait_recv()
                total[...] += self.ups[m].astype(F32)

            @pl.when(here < self.size - 1)
            def _():
                self.down(n, False).wait_recv()
                total[...] += self.downs[n].astype(F32)

            then(part, total[...])
            return 0

        lax.fori_loop(0, self.groups, last, 0)

        def drain(m, _):
            @pl.when(self.size - 1 - lax.div(m, self.groups) > here)
            def _():
                self.up(m, False).wait_send()

            @pl.when(lax.div(m, self.groups) < here)
            def _():
                self.down(m, False).wait_send()

            return 0

        lax.fori_loop(0, self.count, drain, 0)


def scatter_scratch(size, rows, width, chunk):
    count = (size - 1) * (rows // chunk)
    return [
        pltpu.VMEM((size, rows, width), BF),
        pltpu.VMEM((count, chunk, width), BF),
        pltpu.VMEM((count, chunk, width), BF),
        pltpu.VMEM((chunk, width), F32),
    ] + [pltpu.SemaphoreType.DMA((count,))] * 4


def turn(u, cos_t, sin_t):
    lower, upper = u[: HD // 2], u[HD // 2 :]
    return jnp.concatenate([lower * cos_t - upper * sin_t, upper * cos_t + lower * sin_t], 0)


def flip(a):
    return a.astype(F32).T


def key_blocks(g, chunk, rows, keys, key_rows):
    start = lax.axis_index("context") * rows + g * chunk
    free = jnp.minimum(start + 1, min(LEAST_VALID, keys))
    last = jnp.minimum(start + chunk + PIC - 1, keys)
    return lax.div(free, key_rows), lax.div(last + key_rows - 1, key_rows)


def project_kernel(
    size, contexts, chunk,
    own, gain_attn, gain_mlp, cos_tab, sin_tab, mask, starts, w_query, w_key_t, w_value_t,
    x_o, normed_o, inv_o, gain_o, query_o, kv_o, kend_o, keep_o,
    xs, up_send, up_recv, down_send, down_recv, own_sem,
    gains, full, normed, kv, wq, wk, wv,
    gain_send, gain_recv, kv_send, kv_recv, w_sem, out_sem, kv_sem,
):
    here, place = lax.axis_index("tensor"), lax.axis_index("context")
    rows, width = own.shape
    features = size * width
    groups = rows // chunk
    heads, kvs = w_query.shape[1] // HD, w_key_t.shape[0] // HD
    line = Gather(
        size, groups, chunk, own, xs, (up_send, up_recv, down_send, down_recv, own_sem)
    )
    loads = [
        pltpu.make_async_copy(a, b, w_sem.at[i])
        for i, (a, b) in enumerate(((w_query, wq), (w_key_t, wk), (w_value_t, wv)))
    ]
    line.load_all()
    for load in loads:
        load.start()
    gains[here] = jnp.zeros_like(gains[here])
    gains[here, 0:1] = gain_attn[...]
    gains[here, 1:2] = gain_mlp[...]
    tensor_peers, context_peers = others("tensor", size), others("context", contexts)
    greet(tensor_peers + context_peers)

    def gain_copy(i):
        return pltpu.make_async_remote_copy(
            src_ref=gains.at[here],
            dst_ref=gains.at[here],
            send_sem=gain_send.at[i],
            recv_sem=gain_recv.at[i],
            device_id=tensor_peers[i],
            device_id_type=MESH_ID,
        )

    def kv_copy(g, i):
        part = kv.at[:, :, pl.ds(pl.multiple_of(place * rows + g * chunk, chunk), chunk)]
        return pltpu.make_async_remote_copy(
            src_ref=part,
            dst_ref=part,
            send_sem=kv_send.at[g, i],
            recv_sem=kv_recv.at[g, i],
            device_id=context_peers[i],
            device_id_type=MESH_ID,
        )

    line.begin()
    for i in range(size - 1):
        gain_copy(i).start()

    length = jnp.sum(mask[...].astype(F32), 1, keepdims=True).astype(jnp.int32)
    position = lax.broadcasted_iota(jnp.int32, (1, rows), 1) + place * rows
    last = position
    for k in range(starts.shape[1]):
        start = starts[:, k : k + 1]
        inside = (position >= start) & (position < start + PIC)
        last = jnp.maximum(last, jnp.where(inside, start + PIC - 1, 0))
    kend_o[...] = jnp.minimum(last + 1, length)
    down_rows = lax.broadcasted_iota(jnp.int32, (rows, 1), 0) + place * rows
    keep_o[...] = jnp.where(down_rows < length, 1.0, 0.0)

    def save(g):
        part = pl.ds(g * chunk, chunk)
        return [
            pltpu.make_async_copy(full, x_o.at[part], out_sem.at[0]),
            pltpu.make_async_copy(normed, normed_o.at[part], out_sem.at[1]),
        ]

    def compute(g):
        part = pl.ds(pl.multiple_of(g * chunk, chunk), chunk)

        @pl.when(g == 0)
        def _():
            for load in loads:
                load.wait()
            for i in range(size - 1):
                gain_copy(i).wait_recv()
            gain_o[...] = jnp.concatenate([gains[j] for j in range(size)], 1)

        @pl.when(g > 0)
        def _():
            for copy in save(g - 1):
                copy.wait()

        full[...] = jnp.concatenate([xs[j, part, :] for j in range(size)], 1)
        stream = full[...].astype(F32)
        inv = lax.rsqrt(jnp.sum(stream * stream, 1, keepdims=True) / features + epsilon)
        inv_o[part, :] = inv
        normed[...] = (stream * inv * gain_o[0:1, :]).astype(BF)
        for copy in save(g):
            copy.start()
        cos_t, sin_t = cos_tab[:, part], sin_tab[:, part]
        mine = pl.ds(pl.multiple_of(place * rows + g * chunk, chunk), chunk)
        key = dot_nt(wk[...], normed[...])
        value = dot_nt(wv[...], normed[...])
        for h in range(kvs):
            kv[h, :, mine] = turn(key[h * HD : (h + 1) * HD], cos_t, sin_t).astype(BF)
            kv[kvs + h, :, mine] = value[h * HD : (h + 1) * HD].astype(BF)
        for i in range(contexts - 1):
            kv_copy(g, i).start()
        query = dot(normed[...], wq[...]).T
        for h in range(heads):
            query_o[h, :, part] = turn(query[h * HD : (h + 1) * HD], cos_t, sin_t).astype(BF)

    def tick(k, _):
        line.tick(k, compute)
        return 0

    lax.fori_loop(0, line.ticks, tick, 0)
    for copy in save(groups - 1):
        copy.wait()
    for i in range(size - 1):
        gain_copy(i).wait_send()
    line.drain()
    for g in range(groups):
        for i in range(contexts - 1):
            kv_copy(g, i).wait()
    out = pltpu.make_async_copy(kv, kv_o, kv_sem)
    out.start()
    out.wait()


def project(
    axes, own, gain_attn, gain_mlp, cos_tab, sin_tab, mask, starts, w_query, w_key_t, w_value_t, chunk
):
    size, contexts = axes["tensor"], axes["context"]
    rows, width = own.shape
    features, groups = size * width, rows // chunk
    heads, kvs = w_query.shape[1] // HD, w_key_t.shape[0] // HD
    anywhere, vmem = pl.BlockSpec(memory_space=pl.ANY), pl.BlockSpec(memory_space=pltpu.VMEM)
    shape, dma = jax.ShapeDtypeStruct, pltpu.SemaphoreType.DMA
    return pl.pallas_call(
        functools.partial(project_kernel, size, contexts, chunk),
        in_specs=[anywhere] + [vmem] * 6 + [anywhere] * 3,
        out_specs=[anywhere] * 2 + [vmem] * 3 + [anywhere] + [vmem] * 2,
        out_shape=[
            shape((rows, features), BF),
            shape((rows, features), BF),
            shape((rows, 1), F32),
            shape((8, features), F32),
            shape((heads, HD, rows), BF),
            shape((2 * kvs, HD, contexts * rows), BF),
            shape((1, rows), jnp.int32),
            shape((rows, 1), F32),
        ],
        scratch_shapes=gather_scratch(size, rows, width, chunk)
        + [
            pltpu.VMEM((size, 8, width), F32),
            pltpu.VMEM((chunk, features), BF),
            pltpu.VMEM((chunk, features), BF),
            pltpu.VMEM((2 * kvs, HD, contexts * rows), BF),
            pltpu.VMEM(w_query.shape, BF),
            pltpu.VMEM(w_key_t.shape, BF),
            pltpu.VMEM(w_value_t.shape, BF),
            dma((size - 1,)),
            dma((size - 1,)),
            dma((groups, max(contexts - 1, 1))),
            dma((groups, max(contexts - 1, 1))),
            dma((3,)),
            dma((2,)),
            dma,
        ],
        compiler_params=pltpu.CompilerParams(
            collective_id=3, has_side_effects=True, vmem_limit_bytes=VMEM_LIMIT
        ),
        cost_estimate=pl.CostEstimate(
            flops=2 * rows * features * (heads + 2 * kvs) * HD,
            bytes_accessed=20 << 20,
            transcendentals=rows,
        ),
        name="project",
    )(own, gain_attn, gain_mlp, cos_tab, sin_tab, mask, starts, w_query, w_key_t, w_value_t)


def attend_kernel(
    size, chunk, key_rows,
    own, q, kv, kend,
    cot_o, mixed_o, lse_o,
    blocks, up_send, up_recv, down_send, down_recv, own_sem,
    full, keys_in_rows, acc, mx, sm, out_sem,
):
    rows, _ = own.shape
    heads, kvs, keys = q.shape[0], kv.shape[0] // 2, kv.shape[2]
    groups, group = rows // chunk, heads // kvs
    units = kvs * groups
    line = Gather(
        size, groups, chunk, own, blocks, (up_send, up_recv, down_send, down_recv, own_sem)
    )
    line.load_all()
    greet(others("tensor", size))
    line.begin()
    for h in range(kvs):
        keys_in_rows[h] = flip(kv[h]).astype(BF)

    def save(g):
        return pltpu.make_async_copy(full, cot_o.at[pl.ds(g * chunk, chunk)], out_sem)

    def join(g):
        @pl.when(g > 0)
        def _():
            save(g - 1).wait()

        part = pl.ds(pl.multiple_of(g * chunk, chunk), chunk)
        full[...] = jnp.concatenate([blocks[j, part, :] for j in range(size)], 1)
        save(g).start()

    def unit(u):
        pair, g = lax.div(u, groups), lax.rem(u, groups)
        part = pl.ds(pl.multiple_of(g * chunk, chunk), chunk)
        free, last = key_blocks(g, chunk, rows, keys, key_rows)
        acc[...] = jnp.zeros_like(acc)
        sm[...] = jnp.zeros_like(sm)
        mx[...] = jnp.full_like(mx, LOWEST)
        limit = kend[:, part]

        def step(masked, i, _):
            at = pl.multiple_of(i * key_rows, key_rows)
            k_blk = keys_in_rows[pair, pl.ds(at, key_rows), :]
            v_blk = kv[kvs + pair, :, pl.ds(at, key_rows)]
            if masked:
                keep = (lax.broadcasted_iota(jnp.int32, (key_rows, chunk), 0) + at) < limit
            for h in range(group):
                s = dot(k_blk, q[pair * group + h, :, part])
                if masked:
                    s = jnp.where(keep, s, LOWEST)
                old = mx[h]
                new = jnp.maximum(old, jnp.max(s, 0, keepdims=True))
                p = jnp.exp2(s * SCALE2 - new * SCALE2)
                alpha = jnp.exp2((old - new) * SCALE2)
                mx[h] = new
                sm[h] = sm[h] * alpha + jnp.sum(p, 0, keepdims=True)
                acc[h] = acc[h] * alpha + dot(v_blk, p.astype(BF))
            return 0

        lax.fori_loop(0, free, functools.partial(step, False), 0)
        lax.fori_loop(free, last, functools.partial(step, True), 0)
        for h in range(group):
            mixed_o[pair * group + h, :, part] = (acc[h] / sm[h]).astype(BF)
            lse_o[pair * group + h, :, part] = mx[h] * SCALE2 + jnp.log2(sm[h])

    def tick(k, _):
        line.tick(k, join)

        @pl.when(k < units)
        def _():
            unit(k)

        return 0

    lax.fori_loop(0, max(line.ticks, units), tick, 0)
    save(groups - 1).wait()
    line.drain()


def attend_forward(size, own, q, kv, kend, chunk):
    heads, _, rows = q.shape
    kvs, keys = kv.shape[0] // 2, kv.shape[2]
    group, width = heads // kvs, own.shape[1]
    key_rows = min(KEY_ROWS_FWD, keys)
    anywhere, vmem = pl.BlockSpec(memory_space=pl.ANY), pl.BlockSpec(memory_space=pltpu.VMEM)
    shape = jax.ShapeDtypeStruct
    return pl.pallas_call(
        functools.partial(attend_kernel, size, chunk, key_rows),
        in_specs=[anywhere] + [vmem] * 3,
        out_specs=[anywhere] + [vmem] * 2,
        out_shape=[
            shape((rows, size * width), BF),
            shape((heads, HD, rows), BF),
            shape((heads, 1, rows), F32),
        ],
        scratch_shapes=gather_scratch(size, rows, width, chunk)
        + [
            pltpu.VMEM((chunk, size * width), BF),
            pltpu.VMEM((kvs, keys, HD), BF),
            pltpu.VMEM((group, HD, chunk), F32),
            pltpu.VMEM((group, 1, chunk), F32),
            pltpu.VMEM((group, 1, chunk), F32),
            pltpu.SemaphoreType.DMA,
        ],
        compiler_params=pltpu.CompilerParams(
            collective_id=5, has_side_effects=True, vmem_limit_bytes=VMEM_LIMIT
        ),
        cost_estimate=pl.CostEstimate(
            flops=10 * heads * rows * keys * HD,
            bytes_accessed=16 << 20,
            transcendentals=heads * rows * keys,
        ),
        name="attend_forward",
    )(own, q, kv, kend)


def attend_back_kernel(
    size, contexts, chunk, key_rows,
    ffn, q, kv, kend, do, o, lse, cos_tab, sin_tab, middle, grad_attn, normed,
    grads_o, layer_o, square_o, weights_o,
    parts, ups, downs, total, up_send, up_recv, down_send, down_recv,
    keys_in_rows, values_in_rows, dq, dk, dv, ds_all, p_all, q_all, do_all, mine, out_kv, in_kv,
    grads_in, normed_in, tiles,
    kv_send, kv_recv, part_sem, tile_sem,
):
    heads, _, rows = q.shape
    kvs, keys = kv.shape[0] // 2, kv.shape[2]
    groups, group = rows // chunk, heads // kvs
    units = kvs * groups
    place = lax.axis_index("context")
    line = Scatter(
        size, groups, chunk, parts, ups, downs, (up_send, up_recv, down_send, down_recv)
    )
    loads = [
        pltpu.make_async_copy(a, b, part_sem.at[i])
        for i, (a, b) in enumerate(((ffn, parts), (grad_attn, grads_in), (normed, normed_in)))
    ]
    for load in loads:
        load.start()
    square_o[...] = jnp.zeros_like(square_o)
    peers = others("context", contexts)
    greet(others("tensor", size) + peers)
    for h in range(kvs):
        keys_in_rows[h] = flip(kv[h]).astype(BF)
        values_in_rows[h] = flip(kv[kvs + h]).astype(BF)
    loads[0].wait()

    def half(of):
        at = pl.ds(pl.multiple_of(of * rows, rows), rows)
        return dk[at, :].T, dv[at, :].T

    def kv_copy(pair, i):
        return pltpu.make_async_remote_copy(
            src_ref=out_kv.at[pair, i],
            dst_ref=in_kv.at[pair, i],
            send_sem=kv_send.at[pair, i],
            recv_sem=kv_recv.at[pair, i],
            device_id=peers[i],
            device_id_type=MESH_ID,
        )

    def unit(u):
        pair, g = lax.div(u, groups), lax.rem(u, groups)
        part = pl.ds(pl.multiple_of(g * chunk, chunk), chunk)
        free, last = key_blocks(g, chunk, rows, keys, key_rows)
        limit = kend[:, part]

        @pl.when(g == 0)
        def _():
            dk[...] = jnp.zeros_like(dk)
            dv[...] = jnp.zeros_like(dv)

        dq[...] = jnp.zeros_like(dq)
        delta = []
        for h in range(group):
            head = pair * group + h
            cols = slice(h * chunk, (h + 1) * chunk)
            q_all[:, cols] = q[head, :, part]
            do_all[:, cols] = do[head, :, part]
            delta.append(
                jnp.sum(do_all[:, cols].astype(F32) * o[head, :, part].astype(F32), 0, keepdims=True)
            )

        def step(masked, i, _):
            at = pl.multiple_of(i * key_rows, key_rows)
            k_blk = keys_in_rows[pair, pl.ds(at, key_rows), :]
            v_blk = values_in_rows[pair, pl.ds(at, key_rows), :]
            kt_blk = kv[pair, :, pl.ds(at, key_rows)]
            if masked:
                keep = (lax.broadcasted_iota(jnp.int32, (key_rows, chunk), 0) + at) < limit
            for h in range(group):
                cols = slice(h * chunk, (h + 1) * chunk)
                s = dot(k_blk, q_all[:, cols])
                p = jnp.exp2(s * SCALE2 - lse[pair * group + h, :, part])
                if masked:
                    p = jnp.where(keep, p, 0.0)
                dp = dot(v_blk, do_all[:, cols])
                ds = (p * (dp - delta[h])).astype(BF)
                p_all[:, cols] = p.astype(BF)
                ds_all[:, cols] = ds
                dq[h] += dot(kt_blk, ds)
            dk[pl.ds(at, key_rows), :] += dot_nt(ds_all[...], q_all[...])
            dv[pl.ds(at, key_rows), :] += dot_nt(p_all[...], do_all[...])
            return 0

        lax.fori_loop(0, free, functools.partial(step, False), 0)
        lax.fori_loop(free, last, functools.partial(step, True), 0)
        for h in range(group):
            grads_o[pair * group + h, :, part] = turn(
                dq[h] * SCALE, cos_tab[:, part], -sin_tab[:, part]
            ).astype(BF)

        @pl.when(g == groups - 1)
        def _():
            for i in range(contexts - 1):
                key, value = half(peers[i]["context"])
                out_kv[pair, i, 0] = key.astype(BF)
                out_kv[pair, i, 1] = value.astype(BF)
                kv_copy(pair, i).start()
            mine[pair, 0], mine[pair, 1] = half(place)

    def join():
        for pair in range(kvs):
            key, value = mine[pair, 0], mine[pair, 1]
            for i in range(contexts - 1):
                kv_copy(pair, i).wait()
                key = key + in_kv[pair, i, 0].astype(F32)
                value = value + in_kv[pair, i, 1].astype(F32)
            grads_o[heads + pair] = turn(key * SCALE, cos_tab[...], -sin_tab[...]).astype(BF)
            grads_o[heads + kvs + pair] = value.astype(BF)

    features = normed.shape[1]
    tile = tile_of(features, 256)
    tile_count, each = features // tile, 4

    def save_tile(j):
        slot = lax.rem(j, 2)
        return pltpu.make_async_copy(
            tiles.at[slot], weights_o.at[pl.ds(j * tile, tile)], tile_sem.at[slot]
        )

    def weight_tile(j):
        slot = lax.rem(j, 2)

        @pl.when(j >= 2)
        def _():
            save_tile(j - 2).wait()

        cols = pl.ds(pl.multiple_of(j * tile, tile), tile)
        out = dot_nt(flip(grads_in[:, cols]).astype(BF), o[...].reshape(heads * HD, rows))
        into = dot_nt(
            flip(normed_in[:, cols]).astype(BF), grads_o[...].reshape((heads + 2 * kvs) * HD, rows)
        )
        tiles[slot] = jnp.concatenate([out, into], 1).astype(BF)
        save_tile(j).start()

    def tick(k, _):
        line.tick(k)

        @pl.when(k < units)
        def _():
            unit(k)

        @pl.when(k == units)
        def _():
            join()
            for load in loads[1:]:
                load.wait()

        first = (k - units - 1) * each
        for j in range(each):

            @pl.when((first >= 0) & (first + j < tile_count))
            def _():
                weight_tile(first + j)

        return 0

    lax.fori_loop(0, max(line.count, units + 1 + -(-tile_count // each)), tick, 0)

    def then(part, ffn_out):
        square_o[...] += jnp.sum(ffn_out * ffn_out, 0, keepdims=True)
        layer_o[part, :] = (middle[part, :] + ffn_out).astype(BF)

    line.finish(total, then)
    for j in range(max(tile_count - 2, 0), tile_count):
        save_tile(j).wait()


def attend_backward(
    axes, ffn, q, kv, kend, do, o, lse, cos_tab, sin_tab, middle, grad_attn, normed, chunk, after
):
    size, contexts = axes["tensor"], axes["context"]
    heads, _, rows = q.shape
    kvs, keys = kv.shape[0] // 2, kv.shape[2]
    group, width = heads // kvs, ffn.shape[2]
    key_rows = min(KEY_ROWS_BWD, keys)
    anywhere, vmem = pl.BlockSpec(memory_space=pl.ANY), pl.BlockSpec(memory_space=pltpu.VMEM)
    shape, dma = jax.ShapeDtypeStruct, pltpu.SemaphoreType.DMA
    slots = max(contexts - 1, 1)

    def kernel(*refs):
        attend_back_kernel(size, contexts, chunk, key_rows, *refs[:12], *refs[12 + len(after) :])

    return pl.pallas_call(
        kernel,
        in_specs=[anywhere] + [vmem] * 9 + [anywhere] * (2 + len(after)),
        out_specs=[vmem] * 3 + [anywhere],
        out_shape=[
            shape((heads + 2 * kvs, HD, rows), BF),
            shape((rows, width), BF),
            shape((1, width), F32),
            shape((size * width, (2 * heads + 2 * kvs) * HD), BF),
        ],
        scratch_shapes=scatter_scratch(size, rows, width, chunk)
        + [
            pltpu.VMEM((kvs, keys, HD), BF),
            pltpu.VMEM((kvs, keys, HD), BF),
            pltpu.VMEM((group, HD, chunk), F32),
            pltpu.VMEM((keys, HD), F32),
            pltpu.VMEM((keys, HD), F32),
            pltpu.VMEM((key_rows, group * chunk), BF),
            pltpu.VMEM((key_rows, group * chunk), BF),
            pltpu.VMEM((HD, group * chunk), BF),
            pltpu.VMEM((HD, group * chunk), BF),
            pltpu.VMEM((kvs, 2, HD, rows), F32),
            pltpu.VMEM((kvs, slots, 2, HD, rows), BF),
            pltpu.VMEM((kvs, slots, 2, HD, rows), BF),
            pltpu.VMEM(grad_attn.shape, BF),
            pltpu.VMEM(normed.shape, BF),
            pltpu.VMEM((2, tile_of(size * width, 256), (2 * heads + 2 * kvs) * HD), BF),
            dma((kvs, slots)),
            dma((kvs, slots)),
            dma((3,)),
            dma((2,)),
        ],
        compiler_params=pltpu.CompilerParams(
            collective_id=6, has_side_effects=True, vmem_limit_bytes=VMEM_LIMIT
        ),
        cost_estimate=pl.CostEstimate(
            flops=16 * heads * rows * keys * HD,
            bytes_accessed=16 << 20,
            transcendentals=heads * rows * keys,
        ),
        name="attend_backward",
    )(ffn, q, kv, kend, do, o, lse, cos_tab, sin_tab, middle, grad_attn, normed, *after)


def input_kernel(
    axes, chunk,
    grads, inv, gain, keep, attn_square, gain_rows, ffn_square, gain_own, x_own, grad_own,
    w_query, w_key_t, w_value_t, x,
    out_o, sum_o,
    parts, ups, downs, total, up_send, up_recv, down_send, down_recv,
    xs, wq, wk, wv, dots, dot_sum, cols, cols_in, world, square,
    dot_send, dot_recv, col_send, col_recv, world_send, world_recv, w_sem, x_sem,
):
    size = axes["tensor"]
    here = lax.axis_index("tensor")
    rows, features = x.shape
    width, groups = features // size, rows // chunk
    nq, nk = w_query.shape[1], w_key_t.shape[0]
    line = Scatter(
        size, groups, chunk, parts, ups, downs, (up_send, up_recv, down_send, down_recv)
    )
    loads = [
        pltpu.make_async_copy(a, b, w_sem.at[i])
        for i, (a, b) in enumerate(((w_query, wq), (w_key_t, wk), (w_value_t, wv)))
    ]

    def load_x(c):
        slot = lax.rem(c, 2)
        return pltpu.make_async_copy(x.at[pl.ds(c * chunk, chunk)], xs.at[slot], x_sem.at[slot])

    for load in loads:
        load.start()
    load_x(0).start()
    contexts, replicas = axes["context"], axes["dp"] * axes["context"]
    spot = lax.axis_index("dp") * contexts + lax.axis_index("context")
    peers = others("tensor", size)
    far = [lax.rem(spot + i, replicas) for i in range(1, replicas)]
    far = [{"dp": lax.div(i, contexts), "context": lax.rem(i, contexts)} for i in far]
    greet(peers + far)
    for load in loads:
        load.wait()
    square[...] = jnp.zeros_like(square)
    row = lax.broadcasted_iota(jnp.int32, (8, width), 0)
    lane = lax.broadcasted_iota(jnp.int32, (8, width), 1)

    def compute(c):
        slot = lax.rem(c, 2)
        part = pl.ds(pl.multiple_of(c * chunk, chunk), chunk)
        load_x(c).wait()

        @pl.when(c + 1 < groups)
        def _():
            load_x(c + 1).start()

        g = flip(grads[:, part]).astype(BF)
        whole = (
            dot_nt(g[:, :nq], wq[...])
            + dot(g[:, nq : nq + nk], wk[...])
            + dot(g[:, nq + nk :], wv[...])
        )
        stream = xs[slot].astype(F32)
        square[...] += jnp.sum(stream * stream * keep[part, :], 0, keepdims=True)
        moved = whole * (stream * inv[part, :])
        rowsum = jnp.sum(moved * gain[0:1, :], 1, keepdims=True)
        dots[here, :, part] = jnp.broadcast_to(rowsum, (chunk, 128)).T[:8]
        colsum = jnp.sum(moved, 0, keepdims=True)
        low = whole.astype(BF)
        for j in range(size):
            parts[j, part, :] = low[:, j * width : (j + 1) * width]
            piece = jnp.where(row == 0, colsum[:, j * width : (j + 1) * width], 0.0)

            @pl.when(c == 0)
            def _():
                cols[j] = piece

            @pl.when(c > 0)
            def _():
                cols[j] += piece

    def copy_to(src, dst, send, recv, peer):
        return pltpu.make_async_remote_copy(
            src_ref=src,
            dst_ref=dst,
            send_sem=send,
            recv_sem=recv,
            device_id=peer,
            device_id_type=MESH_ID,
        )

    def dot_copy(i):
        mine = dots.at[here]
        return copy_to(mine, mine, dot_send.at[i], dot_recv.at[i], peers[i])

    def col_copy(i):
        src = cols.at[peers[i]["tensor"]]
        return copy_to(src, cols_in.at[here], col_send.at[i], col_recv.at[i], peers[i])

    def world_copy(i):
        mine = world.at[spot]
        return copy_to(mine, mine, world_send.at[i], world_recv.at[i], far[i])

    def exchange():
        numbers = jnp.zeros((8, width), F32)
        for i, a in enumerate((square[...], attn_square[...], ffn_square[...], keep[...])):
            a = jnp.sum(jnp.sum(a, 0, keepdims=True), 1, keepdims=True)
            share = 1.0 if i == 2 else 1.0 / size
            numbers += jnp.where((row == 1) & (lane == i), a * share, 0.0)
        for j in range(size):
            cols[j] += numbers
        cols_in[here] = cols[here]
        for i in range(size - 1):
            dot_copy(i).start()
            col_copy(i).start()

    def spread():
        for i in range(size - 1):
            dot_copy(i).wait()
            col_copy(i).wait()
        dot_total, column = dots[0], cols_in[0]
        for j in range(1, size):
            dot_total = dot_total + dots[j]
            column = column + cols_in[j]
        dot_sum[...] = dot_total
        world[spot] = column

        def put(piece):
            world[spot, 2:3] = piece

        own_columns(size, gain_rows[...], put)
        for i in range(replicas - 1):
            world_copy(i).start()

    def tick(k, _):
        @pl.when(k < groups)
        def _():
            compute(k)

        line.tick(k)

        @pl.when(k == groups)
        def _():
            exchange()

        @pl.when(k == groups + 3)
        def _():
            spread()

        return 0

    lax.fori_loop(0, max(line.count, groups + 4), tick, 0)

    def then(part, grad):
        through = grad * gain_own[...] - x_own[part, :].astype(F32) * inv[part, :] * (
            dot_sum[:, part].T[:, :1] / features
        )
        out_o[part, :] = (grad_own[part, :] + inv[part, :] * through).astype(BF)

    line.finish(total, then)
    for i in range(replicas - 1):
        world_copy(i).wait()
    everything = world[0]
    for j in range(1, replicas):
        everything = everything + world[j]
    sum_o[...] = everything


def input_gradient(
    axes, grads, inv, gain, keep, attn_square, gain_rows, ffn_square, gain_own, x_own, grad_own,
    w_query, w_key_t, w_value_t, x, chunk, after,
):
    size, replicas = axes["tensor"], axes["dp"] * axes["context"]
    rows, features = x.shape
    width = features // size
    anywhere, vmem = pl.BlockSpec(memory_space=pl.ANY), pl.BlockSpec(memory_space=pltpu.VMEM)
    shape, dma = jax.ShapeDtypeStruct, pltpu.SemaphoreType.DMA

    def kernel(*refs):
        input_kernel(axes, chunk, *refs[:14], *refs[14 + len(after) :])

    return pl.pallas_call(
        kernel,
        in_specs=[vmem] * 10 + [anywhere] * (4 + len(after)),
        out_specs=[vmem] * 2,
        out_shape=[
            shape((rows, width), BF),
            shape((8, width), F32),
        ],
        scratch_shapes=scatter_scratch(size, rows, width, chunk)
        + [
            pltpu.VMEM((2, chunk, features), BF),
            pltpu.VMEM(w_query.shape, BF),
            pltpu.VMEM(w_key_t.shape, BF),
            pltpu.VMEM(w_value_t.shape, BF),
            pltpu.VMEM((size, 8, rows), F32),
            pltpu.VMEM((8, rows), F32),
            pltpu.VMEM((size, 8, width), F32),
            pltpu.VMEM((size, 8, width), F32),
            pltpu.VMEM((replicas, 8, width), F32),
            pltpu.VMEM((1, features), F32),
            dma((size - 1,)),
            dma((size - 1,)),
            dma((size - 1,)),
            dma((size - 1,)),
            dma((replicas - 1,)),
            dma((replicas - 1,)),
            dma((3,)),
            dma((2,)),
        ],
        compiler_params=pltpu.CompilerParams(
            collective_id=4, has_side_effects=True, vmem_limit_bytes=VMEM_LIMIT
        ),
        cost_estimate=pl.CostEstimate(
            flops=2 * rows * features * grads.shape[0],
            bytes_accessed=20 << 20,
            transcendentals=rows,
        ),
        name="input_gradient",
    )(
        grads, inv, gain, keep, attn_square, gain_rows, ffn_square, gain_own, x_own, grad_own,
        w_query, w_key_t, w_value_t, x, *after,
    )


def local(
    axes,
    layer_input_hidden,
    cotangent,
    valid_mask,
    span_starts,
    gain_attn,
    w_query,
    w_key,
    w_value,
    w_out,
    gain_mlp,
    w_gate,
    w_up,
    w_down,
):
    _, rows, width = layer_input_hidden.shape
    size = axes["tensor"]
    features = width * size
    kvs = w_key.shape[1] // HD
    heads = w_query.shape[1] // HD
    position = lax.axis_index("context") * rows + jnp.arange(rows, dtype=jnp.int32)
    inverse_freq = rope_base ** (-2.0 * jnp.arange(HD // 2, dtype=F32) / HD)
    angles = inverse_freq[:, None] * position.astype(F32)[None, :]
    cos_tab, sin_tab = jnp.cos(angles), jnp.sin(angles)
    x_own = layer_input_hidden[0]
    w_key_t, w_value_t = w_key.T, w_value.T

    def shard(grad):
        return lax.psum_scatter(grad, ("dp", "context"), scatter_dimension=0, tiled=True)

    x_low, normed_a, inv_a, gains, query_t, both, kend, keep = project(
        axes,
        x_own,
        gain_attn[None],
        gain_mlp[None],
        cos_tab,
        sin_tab,
        valid_mask,
        span_starts,
        w_query,
        w_key_t,
        w_value_t,
        GROUP_ROWS,
    )
    cot, mixed, lse = attend_forward(size, cotangent[0], query_t, both, kend, GROUP_ROWS)
    normed_m, act, ggu, down_part, back_part, middle, middle_own, attn_square = feed_forward(
        size,
        mixed.reshape(heads * HD, rows),
        keep,
        gains,
        w_out,
        w_gate,
        w_up,
        w_down,
        x_low,
        cot,
        GROUP_ROWS,
        HOP_ROWS,
    )
    grad_ggu = ein("sd,sf->df", normed_m, ggu).astype(BF)
    ggu_sum = shard(grad_ggu)

    grad_own, grad_attn, grad_mixed, gain_m_rows, grad_down = norm_back(
        size, back_part, keep, gains, w_out, middle, cot, act, GROUP_ROWS, HOP_ROWS, (grad_ggu,)
    )
    down_sum = shard(grad_down)
    grads, layer_out, ffn_square, grad_rest = attend_backward(
        axes,
        down_part,
        query_t,
        both,
        kend,
        grad_mixed.reshape(heads, HD, rows),
        mixed,
        lse,
        cos_tab,
        sin_tab,
        middle_own,
        grad_attn,
        normed_a,
        GROUP_ROWS,
        (ggu_sum,),
    )
    rest_sum = shard(grad_rest)

    input_grad, sums = input_gradient(
        axes,
        grads.reshape(-1, rows),
        inv_a,
        gains,
        keep,
        attn_square,
        gain_m_rows,
        ffn_square,
        gain_attn[None],
        x_own,
        grad_own,
        w_query,
        w_key_t,
        w_value_t,
        x_low,
        GROUP_ROWS,
        (grad_rest, down_sum),
    )
    rest_sum = jnp.where(sums[1, 3] >= 0.0, rest_sum.astype(F32), 0.0)
    gate_sum, up_sum = jnp.split(ggu_sum.astype(F32), 2, 1)
    down_sum = down_sum.astype(F32).T
    cut = [heads * HD, 2 * heads * HD, (2 * heads + kvs) * HD]
    out_sum, query_sum, key_sum, value_sum = jnp.split(rest_sum, cut, 1)
    rms = jnp.sqrt(sums[1, :3] / (sums[1, 3] * features))
    return (
        layer_out[None],
        input_grad[None],
        sums[0],
        query_sum,
        key_sum,
        value_sum,
        out_sum.T,
        sums[2],
        gate_sum,
        up_sum,
        down_sum,
        rms[0],
        rms[1],
        rms[2],
    )


def solution(mesh):
    token = P("dp", "context", "tensor")
    by_rows = P(("dp", "context"), "tensor")
    by_columns = P("tensor", ("dp", "context"))
    cols, rows, vec = P(None, "tensor"), P("tensor", None), P("tensor")
    return jax.shard_map(
        functools.partial(local, dict(mesh.shape)),
        mesh=mesh,
        in_specs=(
            token,
            token,
            P("dp", None),
            P("dp", None),
            vec,
            cols,
            cols,
            cols,
            rows,
            vec,
            cols,
            cols,
            rows,
        ),
        out_specs=(
            token,
            token,
            vec,
            by_rows,
            by_rows,
            by_rows,
            by_columns,
            vec,
            by_rows,
            by_rows,
            by_columns,
            P(),
            P(),
            P(),
        ),
        check_vma=False,
    )
```

```python
import functools
import math

import jax
import jax.numpy as jnp
from jax import lax
from jax.experimental import pallas as pl
from jax.experimental.pallas import tpu as pltpu
from jax.sharding import PartitionSpec as P

HD = 80
PIC = 256
LEAST_VALID = 1536
F32 = jnp.float32
BF = jnp.bfloat16
SCALE = HD**-0.5
SCALE2 = SCALE * math.log2(math.e)
LOWEST = -1e30
GROUP_ROWS = 256
HOP_ROWS = 64
VMEM_LIMIT = 60 << 20
KEY_ROWS_FWD = 1024
KEY_ROWS_BWD = 512

epsilon = 1e-05
rope_base = 1000000.0


def dot(a, b):
    return jnp.dot(a, b, preferred_element_type=F32)


def dot_nt(a, b):
    return lax.dot_general(a, b, (((1,), (1,)), ((), ())), preferred_element_type=F32)


def ein(spec, a, b):
    return jnp.einsum(spec, a, b, preferred_element_type=F32)


MESH_ID = pl.DeviceIdType.MESH
SENT = 4


def ring_of(size):
    return size + 4


def add_low(a, b):
    return (a.astype(F32) + b.astype(F32)).astype(BF)


class Sums:
    def __init__(self, size, count, part, low, high, sent, sems):
        self.size, self.count, self.part = size, count, part
        self.low, self.high, self.sent = low, high, sent
        self.low_send, self.low_recv, self.high_send, self.high_recv = sems
        self.here = lax.axis_index("tensor")

    def barrier(self):
        here, size = self.here, self.size
        barrier = pltpu.get_barrier_semaphore()

        @pl.when(here > 0)
        def _():
            pl.semaphore_signal(
                barrier, inc=1, device_id={"tensor": here - 1}, device_id_type=MESH_ID
            )

        @pl.when(here < size - 1)
        def _():
            pl.semaphore_signal(
                barrier, inc=1, device_id={"tensor": here + 1}, device_id_type=MESH_ID
            )

        @pl.when((here > 0) & (here < size - 1))
        def _():
            pl.semaphore_wait(barrier, 2)

        @pl.when((here == 0) | (here == size - 1))
        def _():
            pl.semaphore_wait(barrier, 1)

    def up(self, c):
        slot = lax.rem(c, ring_of(self.size))
        return pltpu.make_async_remote_copy(
            src_ref=self.low.at[slot],
            dst_ref=self.low.at[slot],
            send_sem=self.low_send.at[slot],
            recv_sem=self.low_recv.at[slot],
            device_id={"tensor": self.here + 1},
            device_id_type=MESH_ID,
        )

    def down(self, c):
        slot, mine = lax.rem(c, ring_of(self.size)), lax.rem(c, SENT)
        return pltpu.make_async_remote_copy(
            src_ref=self.sent.at[mine],
            dst_ref=self.high.at[slot],
            send_sem=self.high_send.at[mine],
            recv_sem=self.high_recv.at[slot],
            device_id={"tensor": self.here - 1},
            device_id_type=MESH_ID,
        )

    def tick(self, k):
        here, size, count = self.here, self.size, self.count
        bottom, top = here == 0, here == size - 1
        c = k - here

        @pl.when((c >= 0) & (c < count))
        def _():
            slot = lax.rem(c, ring_of(self.size))

            @pl.when(bottom)
            def _():
                self.low[slot] = self.part(c)

            @pl.when(jnp.logical_not(bottom))
            def _():
                self.up(c).wait_recv()
                self.low[slot] = add_low(self.low[slot], self.part(c))

            @pl.when(jnp.logical_not(top))
            def _():
                self.up(c).start()

        d = k - (size - 1 - here)

        @pl.when((d >= 0) & (d < count))
        def _():
            slot, mine = lax.rem(d, ring_of(self.size)), lax.rem(d, SENT)

            @pl.when(top)
            def _():
                self.sent[mine] = self.part(d)

            @pl.when(jnp.logical_not(top))
            def _():
                self.down(d).wait_recv()

                @pl.when(jnp.logical_not(bottom))
                def _():
                    self.sent[mine] = add_low(self.high[slot], self.part(d))

            @pl.when(jnp.logical_not(bottom))
            def _():
                self.down(d).start()

        @pl.when((c >= 2) & (c < count + 2) & jnp.logical_not(top))
        def _():
            self.up(c - 2).wait_send()

        @pl.when((d >= 2) & (d < count + 2) & jnp.logical_not(bottom))
        def _():
            self.down(d - 2).wait_send()

    def total(self, c, then):
        slot = lax.rem(c, ring_of(self.size))
        top = self.here == self.size - 1

        @pl.when(top)
        def _():
            then(self.low[slot].astype(F32))

        @pl.when(jnp.logical_not(top))
        def _():
            then(self.low[slot].astype(F32) + self.high[slot].astype(F32))


def sum_scratch(size, hop, features):
    ring, dma = ring_of(size), pltpu.SemaphoreType.DMA
    return [
        pltpu.VMEM((ring, hop, features), BF),
        pltpu.VMEM((ring, hop, features), BF),
        pltpu.VMEM((SENT, hop, features), BF),
        dma((ring,)),
        dma((ring,)),
        dma((SENT,)),
        dma((ring,)),
    ]


def own_columns(size, a, then):
    width = a.shape[1] // size
    for j in range(size):

        @pl.when(lax.axis_index("tensor") == j)
        def _():
            then(a[:, j * width : (j + 1) * width])


def tile_of(n, most):
    for tile in range(most, 0, -128):
        if n % tile == 0:
            return tile
    return n


def ffn_kernel(
    size, hop, chunk,
    mixed, keep, gain, w_out, w_gate, w_up, w_down, x, cot,
    normed_o, act_o, ggu_o, ffn_o, back_o, middle_o, own_o, square_o,
    low, high, sent, low_send, low_recv, high_send, high_recv,
    wo, wg, wu, wd, parts, normed, xs, cots, mids, owns, act, ggu, ffn, back, split,
    w_sem, x_sem, cot_sem, normed_sem, mid_sem, own_sem, act_sem, ffn_sem,
):
    rows, features = x.shape
    hidden = w_gate.shape[1]
    count, per, groups = rows // hop, chunk // hop, rows // chunk
    tile_f, tile_d = tile_of(hidden, 256), tile_of(features, 256)
    tiles_f, tiles_d = hidden // tile_f, features // tile_d
    half_f, half_d = -(-tiles_f // 2), -(-tiles_d // 2)
    lag = size - 1 + per - 1
    ahead, part_slots = per // 2, parts.shape[0]
    ticks = max(per * groups + lag, count + size)

    def part(c):
        slot = lax.rem(lax.div(c, per), part_slots)
        return parts[slot, pl.ds(pl.multiple_of(lax.rem(c, per) * hop, hop), hop), :]

    sums = Sums(size, count, part, low, high, sent, (low_send, low_recv, high_send, high_recv))
    loads = [
        pltpu.make_async_copy(a, b, w_sem.at[i])
        for i, (a, b) in enumerate(((w_out, wo), (w_gate, wg), (w_up, wu), (w_down, wd)))
    ]
    for load in loads:
        load.start()

    def load_x(c):
        slot = lax.rem(c, 2)
        return pltpu.make_async_copy(x.at[pl.ds(c * hop, hop)], xs.at[slot], x_sem.at[slot])

    def load_cot(g):
        return pltpu.make_async_copy(cot.at[pl.ds(g * chunk, chunk)], cots, cot_sem)

    def save_normed(c):
        at, q = lax.rem(lax.div(c, per), 2), lax.rem(c, per)
        return pltpu.make_async_copy(
            normed.at[at, pl.ds(q * hop, hop)], normed_o.at[pl.ds(c * hop, hop)], normed_sem.at[at, q]
        )

    def save_mid(c):
        slot = lax.rem(c, 2)
        return pltpu.make_async_copy(mids.at[slot], middle_o.at[pl.ds(c * hop, hop)], mid_sem.at[slot])

    def save_own(c):
        slot = lax.rem(c, 2)
        return pltpu.make_async_copy(owns.at[slot], own_o.at[pl.ds(c * hop, hop)], own_sem.at[slot])

    def save_act(g):
        return [
            pltpu.make_async_copy(a, b.at[pl.ds(g * chunk, chunk)], act_sem.at[i])
            for i, (a, b) in enumerate(((act, act_o), (ggu, ggu_o)))
        ]

    def save_ffn(g):
        part = pl.ds(g * chunk, chunk)
        return [
            pltpu.make_async_copy(split, ffn_o.at[:, part], ffn_sem.at[0]),
            pltpu.make_async_copy(back, back_o.at[part], ffn_sem.at[1]),
        ]

    def project(g):
        at = lax.rem(g, part_slots)
        lhs = mixed[:, pl.ds(pl.multiple_of(g * chunk, chunk), chunk)]

        def one(j, _):
            cols = pl.ds(pl.multiple_of(j * tile_d, tile_d), tile_d)
            parts[at, :, cols] = lax.dot_general(
                lhs, wo[:, cols], (((0,), (0,)), ((), ())), preferred_element_type=F32
            ).astype(BF)
            return 0

        lax.fori_loop(0, tiles_d, one, 0)

    load_x(0).start()
    load_cot(0).start()
    square_o[...] = jnp.zeros_like(square_o)
    loads[0].wait()
    project(0)
    sums.barrier()

    def finish(c):
        slot = lax.rem(c, 2)
        load_x(c).wait()

        @pl.when(c + 1 < count)
        def _():
            load_x(c + 1).start()

        @pl.when(c >= 2)
        def _():
            save_mid(c - 2).wait()
            save_own(c - 2).wait()

        @pl.when(c >= 2 * per)
        def _():
            save_normed(c - 2 * per).wait()

        kept = keep[pl.ds(pl.multiple_of(c * hop, hop), hop), :]

        def then(total):
            out = kept * total
            square_o[...] += jnp.sum(out * out, 0, keepdims=True)
            mids[slot] = xs[slot].astype(F32) + out

        sums.total(c, then)
        mid = mids[slot]
        own_columns(size, mid, lambda piece: owns.__setitem__(slot, piece))
        save_own(c).start()
        inv = lax.rsqrt(jnp.sum(mid * mid, 1, keepdims=True) / features + epsilon)
        at = lax.rem(lax.div(c, per), 2)
        normed[at, pl.ds(pl.multiple_of(lax.rem(c, per) * hop, hop), hop), :] = (
            mid * inv * gain[1:2, :]
        ).astype(BF)
        save_mid(c).start()
        save_normed(c).start()

    def inner(g, lo, hi):
        at = lax.rem(g, 2)
        kept = keep[pl.ds(pl.multiple_of(g * chunk, chunk), chunk), :]

        def one(j, _):
            cols = pl.ds(pl.multiple_of(j * tile_f, tile_f), tile_f)
            gate = dot(normed[at], wg[:, cols])
            up = dot(normed[at], wu[:, cols])
            grad = dot_nt(cots[...], wd[cols, :]) * kept
            sig = jax.nn.sigmoid(gate)
            silu = gate * sig
            act[:, cols] = (silu * up * kept).astype(BF)
            ggu[:, cols] = (grad * up * (sig + silu * (1.0 - sig))).astype(BF)
            cols = pl.ds(pl.multiple_of(hidden + j * tile_f, tile_f), tile_f)
            ggu[:, cols] = (grad * silu).astype(BF)
            return 0

        lax.fori_loop(lo, hi, one, 0)

    def outer(g, lo, hi):
        def one(j, _):
            cols = pl.ds(pl.multiple_of(j * tile_d, tile_d), tile_d)
            ffn[:, cols] = dot(act[...], wd[:, cols]).astype(BF)
            back[:, cols] = (
                dot_nt(ggu[:, :hidden], wg[cols, :]) + dot_nt(ggu[:, hidden:], wu[cols, :])
            ).astype(BF)
            return 0

        lax.fori_loop(lo, hi, one, 0)

    def tick(k, _):
        sums.tick(k)
        c = k - (size - 1)

        @pl.when((c >= 0) & (c < count))
        def _():
            finish(c)

        later = k + ahead

        @pl.when((lax.rem(later, per) == 0) & (later < count))
        def _():
            project(lax.div(later, per))

        s = k - lag
        g, stage = lax.div(s, per), lax.rem(s, per)
        going = (s >= 0) & (g < groups)

        @pl.when(going & (stage == 0 * per // 4))
        def _():
            @pl.when(g == 0)
            def _():
                for load in loads[1:]:
                    load.wait()

            load_cot(g).wait()

            @pl.when(g > 0)
            def _():
                for copy in save_act(g - 1):
                    copy.wait()

            inner(g, 0, half_f)

        @pl.when(going & (stage == 1 * per // 4))
        def _():
            inner(g, half_f, tiles_f)
            for copy in save_act(g):
                copy.start()

            @pl.when(g + 1 < groups)
            def _():
                load_cot(g + 1).start()

        @pl.when(going & (stage == 2 * per // 4))
        def _():
            @pl.when(g > 0)
            def _():
                for copy in save_ffn(g - 1):
                    copy.wait()

            outer(g, 0, half_d)

        @pl.when(going & (stage == 3 * per // 4))
        def _():
            outer(g, half_d, tiles_d)
            for j in range(size):
                split[j] = ffn[:, j * (features // size) : (j + 1) * (features // size)]
            for copy in save_ffn(g):
                copy.start()

        return 0

    lax.fori_loop(0, ticks, tick, 0)
    for copy in save_act(groups - 1) + save_ffn(groups - 1):
        copy.wait()
    for c in range(count - 2, count):
        save_mid(c).wait()
        save_own(c).wait()
    for c in range(count - 2 * per, count):
        save_normed(c).wait()


def feed_forward(size, mixed, keep, gain, w_out, w_gate, w_up, w_down, x, cot, chunk, hop):
    rows, features = x.shape
    hidden = w_gate.shape[1]
    per = chunk // hop
    anywhere, vmem = pl.BlockSpec(memory_space=pl.ANY), pl.BlockSpec(memory_space=pltpu.VMEM)
    shape = jax.ShapeDtypeStruct
    return pl.pallas_call(
        functools.partial(ffn_kernel, size, hop, chunk),
        in_specs=[vmem] * 3 + [anywhere] * 6,
        out_specs=[anywhere] * 7 + [vmem],
        out_shape=[
            shape((rows, features), BF),
            shape((rows, hidden), BF),
            shape((rows, 2 * hidden), BF),
            shape((size, rows, features // size), BF),
            shape((rows, features), BF),
            shape((rows, features), F32),
            shape((rows, features // size), F32),
            shape((1, features), F32),
        ],
        scratch_shapes=sum_scratch(size, hop, features)
        + [
            pltpu.VMEM(w_out.shape, BF),
            pltpu.VMEM(w_gate.shape, BF),
            pltpu.VMEM(w_up.shape, BF),
            pltpu.VMEM(w_down.shape, BF),
            pltpu.VMEM((-(-(per + size - 2 + per // 2) // per), chunk, features), BF),
            pltpu.VMEM((2, chunk, features), BF),
            pltpu.VMEM((2, hop, features), BF),
            pltpu.VMEM((chunk, features), BF),
            pltpu.VMEM((2, hop, features), F32),
            pltpu.VMEM((2, hop, features // size), F32),
            pltpu.VMEM((chunk, hidden), BF),
            pltpu.VMEM((chunk, 2 * hidden), BF),
            pltpu.VMEM((chunk, features), BF),
            pltpu.VMEM((chunk, features), BF),
            pltpu.VMEM((size, chunk, features // size), BF),
            pltpu.SemaphoreType.DMA((4,)),
            pltpu.SemaphoreType.DMA((2,)),
            pltpu.SemaphoreType.DMA,
            pltpu.SemaphoreType.DMA((2, per)),
            pltpu.SemaphoreType.DMA((2,)),
            pltpu.SemaphoreType.DMA((2,)),
            pltpu.SemaphoreType.DMA((2,)),
            pltpu.SemaphoreType.DMA((2,)),
        ],
        compiler_params=pltpu.CompilerParams(
            collective_id=1, has_side_effects=True, vmem_limit_bytes=VMEM_LIMIT
        ),
        cost_estimate=pl.CostEstimate(
            flops=2 * rows * features * (6 * hidden + w_out.shape[0]),
            bytes_accessed=80 << 20,
            transcendentals=rows * hidden,
        ),
        name="feed_forward",
    )(mixed, keep, gain, w_out, w_gate, w_up, w_down, x, cot)


def back_kernel(
    size, hop, chunk,
    parts, keep, gain, w_out, middle, cot, act,
    own_o, grad_low_o, mixed_o, gain_o, down_o,
    low, high, sent, low_send, low_recv, high_send, high_recv,
    wo, mids, cots, acts, owns, grads_low, tiles,
    load_sem, mid_sem, own_sem, grad_low_sem, tile_sem,
):
    rows, features = middle.shape
    count, per, groups = rows // hop, chunk // hop, rows // chunk
    tile = tile_of(features, 256)
    tile_count = features // tile
    ticks = max(count + size, per * (groups - 1) + size - 1 + per, tile_count + 1)

    def part(c):
        return parts[pl.ds(pl.multiple_of(c * hop, hop), hop), :]

    sums = Sums(size, count, part, low, high, sent, (low_send, low_recv, high_send, high_recv))
    loads = [
        pltpu.make_async_copy(a, b, load_sem.at[i])
        for i, (a, b) in enumerate(((cot, cots), (w_out, wo), (act, acts)))
    ]

    def load_mid(c):
        slot = lax.rem(c, 2)
        return pltpu.make_async_copy(
            middle.at[pl.ds(c * hop, hop)], mids.at[slot], mid_sem.at[slot]
        )

    def save_own(c):
        slot = lax.rem(c, 2)
        return pltpu.make_async_copy(owns.at[slot], own_o.at[pl.ds(c * hop, hop)], own_sem.at[slot])

    def save_low(c):
        q = lax.rem(c, per)
        return pltpu.make_async_copy(
            grads_low.at[pl.ds(q * hop, hop)], grad_low_o.at[pl.ds(c * hop, hop)], grad_low_sem.at[q]
        )

    def save_tile(j):
        slot = lax.rem(j, 2)
        return pltpu.make_async_copy(
            tiles.at[slot], down_o.at[pl.ds(j * tile, tile)], tile_sem.at[slot]
        )

    load_mid(0).start()
    for load in loads:
        load.start()
    gain_o[...] = jnp.zeros_like(gain_o)
    sums.barrier()

    def finish(c):
        slot = lax.rem(c, 2)
        load_mid(c).wait()

        @pl.when(c + 1 < count)
        def _():
            load_mid(c + 1).start()

        @pl.when(c >= 2)
        def _():
            save_own(c - 2).wait()

        @pl.when(c >= per)
        def _():
            save_low(c - per).wait()

        chunk_rows = pl.ds(pl.multiple_of(c * hop, hop), hop)
        kept = keep[chunk_rows, :]
        mid = mids[slot]
        inv = lax.rsqrt(jnp.sum(mid * mid, 1, keepdims=True) / features + epsilon)
        hat = mid * inv

        def then(total):
            gain_o[...] += jnp.sum(total * hat, 0, keepdims=True)
            weighted = total * gain[1:2, :]
            mean = jnp.sum(weighted * hat, 1, keepdims=True) / features
            mids[slot] = cots[chunk_rows, :].astype(F32) + inv * (weighted - hat * mean)

        sums.total(c, then)
        grad = mids[slot]
        own_columns(size, grad, lambda piece: owns.__setitem__(slot, piece))
        grads_low[pl.ds(pl.multiple_of(lax.rem(c, per) * hop, hop), hop), :] = (kept * grad).astype(
            BF
        )
        save_own(c).start()
        save_low(c).start()

    def weight_tile(j):
        slot = lax.rem(j, 2)

        @pl.when(j >= 2)
        def _():
            save_tile(j - 2).wait()

        cols = pl.ds(pl.multiple_of(j * tile, tile), tile)
        tiles[slot] = dot(flip(cots[:, cols]).astype(BF), acts[...]).astype(BF)
        save_tile(j).start()

    def tick(k, _):
        sums.tick(k)
        c = k - (size - 1)

        @pl.when(k == 1)
        def _():
            for load in loads:
                load.wait()

        @pl.when((c >= 0) & (c < count))
        def _():
            finish(c)

            @pl.when(lax.rem(c, per) == per - 1)
            def _():
                g = lax.div(c, per)
                mixed_o[:, pl.ds(pl.multiple_of(g * chunk, chunk), chunk)] = dot_nt(
                    wo[...], grads_low[...]
                ).astype(BF)

        @pl.when((k >= 1) & (k <= tile_count))
        def _():
            weight_tile(k - 1)

        return 0

    lax.fori_loop(0, ticks, tick, 0)
    for c in range(count - 2, count):
        save_own(c).wait()
    for c in range(count - per, count):
        save_low(c).wait()
    for j in range(max(tile_count - 2, 0), tile_count):
        save_tile(j).wait()


def norm_back(size, parts, keep, gain, w_out, middle, cot, act, chunk, hop, after):
    rows, features = middle.shape
    per = chunk // hop
    anywhere, vmem = pl.BlockSpec(memory_space=pl.ANY), pl.BlockSpec(memory_space=pltpu.VMEM)
    shape, dma = jax.ShapeDtypeStruct, pltpu.SemaphoreType.DMA

    def kernel(*refs):
        back_kernel(size, hop, chunk, *refs[:7], *refs[7 + len(after) :])

    return pl.pallas_call(
        kernel,
        in_specs=[vmem] * 3 + [anywhere] * (4 + len(after)),
        out_specs=[anywhere] * 2 + [vmem] * 2 + [anywhere],
        out_shape=[
            shape((rows, features // size), F32),
            shape((rows, features), BF),
            shape((w_out.shape[0], rows), BF),
            shape((1, features), F32),
            shape((features, act.shape[1]), BF),
        ],
        scratch_shapes=sum_scratch(size, hop, features)
        + [
            pltpu.VMEM(w_out.shape, BF),
            pltpu.VMEM((2, hop, features), F32),
            pltpu.VMEM(cot.shape, BF),
            pltpu.VMEM(act.shape, BF),
            pltpu.VMEM((2, hop, features // size), F32),
            pltpu.VMEM((chunk, features), BF),
            pltpu.VMEM((2, tile_of(features, 256), act.shape[1]), BF),
            dma((3,)),
            dma((2,)),
            dma((2,)),
            dma((per,)),
            dma((2,)),
        ],
        compiler_params=pltpu.CompilerParams(
            collective_id=2, has_side_effects=True, vmem_limit_bytes=VMEM_LIMIT
        ),
        cost_estimate=pl.CostEstimate(
            flops=2 * rows * features * (w_out.shape[0] + act.shape[1]),
            bytes_accessed=40 << 20,
            transcendentals=rows,
        ),
        name="norm_back",
    )(parts, keep, gain, w_out, middle, cot, act, *after)


def greet(peers):
    barrier = pltpu.get_barrier_semaphore()
    for peer in peers:
        pl.semaphore_signal(barrier, inc=1, device_id=peer, device_id_type=MESH_ID)
    pl.semaphore_wait(barrier, len(peers))


def others(axis, size):
    here = lax.axis_index(axis)
    return [{axis: lax.rem(here + i, size)} for i in range(1, size)]


class Gather:
    def __init__(self, size, groups, chunk, own, blocks, sems):
        self.size, self.groups, self.chunk = size, groups, chunk
        self.own, self.blocks = own, blocks
        self.up_send, self.up_recv, self.down_send, self.down_recv, self.own_sem = sems
        self.steps = size - 1
        self.ticks = groups * self.steps + 1
        self.here = lax.axis_index("tensor")

    def load(self, g):
        part = pl.ds(g * self.chunk, self.chunk)
        return pltpu.make_async_copy(
            self.own.at[part], self.blocks.at[self.here, part], self.own_sem.at[g]
        )

    def load_all(self):
        for g in range(self.groups):
            self.load(g).start()

    def move(self, g, s, owner, peer, send, recv):
        block = self.blocks.at[jnp.clip(owner, 0, self.size - 1), pl.ds(g * self.chunk, self.chunk)]
        return pltpu.make_async_remote_copy(
            src_ref=block,
            dst_ref=block,
            send_sem=send.at[g, s],
            recv_sem=recv.at[g, s],
            device_id={"tensor": peer},
            device_id_type=MESH_ID,
        )

    def up(self, g, s):
        return self.move(g, s, self.here - s, self.here + 1, self.up_send, self.up_recv)

    def down(self, g, s):
        return self.move(g, s, self.here + s, self.here - 1, self.down_send, self.down_recv)

    def each(self, g, s, act):
        @pl.when((self.here >= s) & (self.here < self.size - 1))
        def _():
            act(self.up(g, s))

        @pl.when((self.here + s < self.size) & (self.here > 0))
        def _():
            act(self.down(g, s))

    def send(self, g, s):
        self.each(g, s, lambda copy: copy.start())

    def receive(self, g, s):
        @pl.when(self.here - 1 - s >= 0)
        def _():
            self.up(g, s).wait_recv()

        @pl.when(self.here + 1 + s < self.size)
        def _():
            self.down(g, s).wait_recv()

    def begin(self):
        self.load(0).wait()
        self.send(0, 0)

    def tick(self, k, then):
        g, s = lax.div(k, self.steps), lax.rem(k, self.steps)

        @pl.when((s > 0) & (g < self.groups))
        def _():
            self.receive(g, s - 1)
            self.send(g, s)

        @pl.when((s == self.steps - 1) & (g + 1 < self.groups))
        def _():
            self.load(g + 1).wait()
            self.send(g + 1, 0)

        @pl.when((s == 0) & (g > 0) & (g <= self.groups))
        def _():
            self.receive(g - 1, self.steps - 1)
            then(g - 1)

    def drain(self):
        for g in range(self.groups):
            for s in range(self.steps):
                self.each(g, s, lambda copy: copy.wait_send())


def gather_scratch(size, rows, width, chunk):
    dma, groups = pltpu.SemaphoreType.DMA, rows // chunk
    return [pltpu.VMEM((size, rows, width), BF)] + [dma((groups, size - 1))] * 4 + [dma((groups,))]


class Scatter:
    def __init__(self, size, groups, chunk, parts, ups, downs, sems):
        self.size, self.groups, self.chunk = size, groups, chunk
        self.parts, self.ups, self.downs = parts, ups, downs
        self.up_send, self.up_recv, self.down_send, self.down_recv = sems
        self.count = (size - 1) * groups
        self.here = lax.axis_index("tensor")

    def rows(self, m):
        return pl.ds(pl.multiple_of(lax.rem(m, self.groups) * self.chunk, self.chunk), self.chunk)

    def up(self, m, first):
        owner = self.size - 1 - lax.div(m, self.groups)
        return pltpu.make_async_remote_copy(
            src_ref=self.parts.at[owner, self.rows(m)] if first else self.ups.at[m],
            dst_ref=self.ups.at[m],
            send_sem=self.up_send.at[m],
            recv_sem=self.up_recv.at[m],
            device_id={"tensor": self.here + 1},
            device_id_type=MESH_ID,
        )

    def down(self, m, first):
        owner = lax.div(m, self.groups)
        return pltpu.make_async_remote_copy(
            src_ref=self.parts.at[owner, self.rows(m)] if first else self.downs.at[m],
            dst_ref=self.downs.at[m],
            send_sem=self.down_send.at[m],
            recv_sem=self.down_recv.at[m],
            device_id={"tensor": self.here - 1},
            device_id_type=MESH_ID,
        )

    def tick(self, k):
        bottom, top = self.here == 0, self.here == self.size - 1
        m = k - self.here
        owner = self.size - 1 - lax.div(m, self.groups)

        @pl.when((m >= 0) & (owner > self.here))
        def _():
            @pl.when(bottom)
            def _():
                self.up(m, True).start()

            @pl.when(jnp.logical_not(bottom))
            def _():
                self.up(m, False).wait_recv()
                self.ups[m] = add_low(self.ups[m], self.parts[owner, self.rows(m), :])
                self.up(m, False).start()

        n = k - (self.size - 1 - self.here)
        below = lax.div(n, self.groups)

        @pl.when((n >= 0) & (below < self.here))
        def _():
            @pl.when(top)
            def _():
                self.down(n, True).start()

            @pl.when(jnp.logical_not(top))
            def _():
                self.down(n, False).wait_recv()
                self.downs[n] = add_low(self.downs[n], self.parts[below, self.rows(n), :])
                self.down(n, False).start()

    def finish(self, total, then):
        here = self.here

        def last(c, _):
            part = self.rows(c)
            m, n = (self.size - 1 - here) * self.groups + c, here * self.groups + c
            total[...] = self.parts[here, part, :].astype(F32)

            @pl.when(here > 0)
            def _():
                self.up(m, False).wait_recv()
                total[...] += self.ups[m].astype(F32)

            @pl.when(here < self.size - 1)
            def _():
                self.down(n, False).wait_recv()
                total[...] += self.downs[n].astype(F32)

            then(part, total[...])
            return 0

        lax.fori_loop(0, self.groups, last, 0)

        def drain(m, _):
            @pl.when(self.size - 1 - lax.div(m, self.groups) > here)
            def _():
                self.up(m, False).wait_send()

            @pl.when(lax.div(m, self.groups) < here)
            def _():
                self.down(m, False).wait_send()

            return 0

        lax.fori_loop(0, self.count, drain, 0)


def scatter_scratch(size, rows, width, chunk):
    count = (size - 1) * (rows // chunk)
    return [
        pltpu.VMEM((size, rows, width), BF),
        pltpu.VMEM((count, chunk, width), BF),
        pltpu.VMEM((count, chunk, width), BF),
        pltpu.VMEM((chunk, width), F32),
    ] + [pltpu.SemaphoreType.DMA((count,))] * 4


def turn(u, cos_t, sin_t):
    lower, upper = u[: HD // 2], u[HD // 2 :]
    return jnp.concatenate([lower * cos_t - upper * sin_t, upper * cos_t + lower * sin_t], 0)


def flip(a):
    return a.astype(F32).T


def key_blocks(g, chunk, rows, keys, key_rows):
    start = lax.axis_index("context") * rows + g * chunk
    free = jnp.minimum(start + 1, min(LEAST_VALID, keys))
    last = jnp.minimum(start + chunk + PIC - 1, keys)
    return lax.div(free, key_rows), lax.div(last + key_rows - 1, key_rows)


def attend_kernel(
    size, contexts, chunk, key_rows,
    own, own_cot, gain_pair, cos_tab, sin_tab, mask, starts, w_query, w_key_t, w_value_t,
    x_o, normed_o, inv_o, gain_o, q, kv_o, kend, keep_o, cot_o, mixed_o, lse_o,
    xs, up_send, up_recv, down_send, down_recv, own_sem,
    blocks, up_send_c, up_recv_c, down_send_c, down_recv_c, own_sem_c,
    gains, full, normed, full_c, kv, wq, wk, wv, keys_in_rows, acc, mx, sm,
    gain_send, gain_recv, kv_send, kv_recv, w_sem, out_sem, kv_sem, cot_sem,
):
    here, place = lax.axis_index("tensor"), lax.axis_index("context")
    rows, width = own.shape
    features = size * width
    groups = rows // chunk
    heads, kvs = w_query.shape[1] // HD, w_key_t.shape[0] // HD
    keys, group = contexts * rows, heads // kvs
    units = kvs * groups
    line = Gather(
        size, groups, chunk, own, xs, (up_send, up_recv, down_send, down_recv, own_sem)
    )
    line_c = Gather(
        size, groups, chunk, own_cot, blocks,
        (up_send_c, up_recv_c, down_send_c, down_recv_c, own_sem_c),
    )
    loads = [
        pltpu.make_async_copy(a, b, w_sem.at[i])
        for i, (a, b) in enumerate(((w_query, wq), (w_key_t, wk), (w_value_t, wv)))
    ]
    line.load_all()
    for load in loads:
        load.start()
    gains[here] = jnp.zeros_like(gains[here])
    gains[here, 0:2] = gain_pair[...]
    tensor_peers, context_peers = others("tensor", size), others("context", contexts)
    greet(tensor_peers + context_peers)

    def gain_copy(i):
        return pltpu.make_async_remote_copy(
            src_ref=gains.at[here],
            dst_ref=gains.at[here],
            send_sem=gain_send.at[i],
            recv_sem=gain_recv.at[i],
            device_id=tensor_peers[i],
            device_id_type=MESH_ID,
        )

    def kv_copy(g, i):
        part = kv.at[:, :, pl.ds(pl.multiple_of(place * rows + g * chunk, chunk), chunk)]
        return pltpu.make_async_remote_copy(
            src_ref=part,
            dst_ref=part,
            send_sem=kv_send.at[g, i],
            recv_sem=kv_recv.at[g, i],
            device_id=context_peers[i],
            device_id_type=MESH_ID,
        )

    line.begin()
    line_c.load_all()
    for i in range(size - 1):
        gain_copy(i).start()

    length = jnp.sum(mask[...].astype(F32), 1, keepdims=True).astype(jnp.int32)
    position = lax.broadcasted_iota(jnp.int32, (1, rows), 1) + place * rows
    last = position
    for k in range(starts.shape[1]):
        start = starts[:, k : k + 1]
        inside = (position >= start) & (position < start + PIC)
        last = jnp.maximum(last, jnp.where(inside, start + PIC - 1, 0))
    kend[...] = jnp.minimum(last + 1, length)
    down_rows = lax.broadcasted_iota(jnp.int32, (rows, 1), 0) + place * rows
    keep_o[...] = jnp.where(down_rows < length, 1.0, 0.0)

    def save(g):
        part = pl.ds(g * chunk, chunk)
        return [
            pltpu.make_async_copy(full, x_o.at[part], out_sem.at[0]),
            pltpu.make_async_copy(normed, normed_o.at[part], out_sem.at[1]),
        ]

    def project(g):
        part = pl.ds(pl.multiple_of(g * chunk, chunk), chunk)

        @pl.when(g == 0)
        def _():
            for load in loads:
                load.wait()
            for i in range(size - 1):
                gain_copy(i).wait_recv()
            gain_o[...] = jnp.concatenate([gains[j] for j in range(size)], 1)

        @pl.when(g > 0)
        def _():
            for copy in save(g - 1):
                copy.wait()

        full[...] = jnp.concatenate([xs[j, part, :] for j in range(size)], 1)
        stream = full[...].astype(F32)
        inv = lax.rsqrt(jnp.sum(stream * stream, 1, keepdims=True) / features + epsilon)
        inv_o[part, :] = inv
        normed[...] = (stream * inv * gain_o[0:1, :]).astype(BF)
        for copy in save(g):
            copy.start()
        cos_t, sin_t = cos_tab[:, part], sin_tab[:, part]
        mine = pl.ds(pl.multiple_of(place * rows + g * chunk, chunk), chunk)
        key = dot_nt(wk[...], normed[...])
        value = dot_nt(wv[...], normed[...])
        for h in range(kvs):
            kv[h, :, mine] = turn(key[h * HD : (h + 1) * HD], cos_t, sin_t).astype(BF)
            kv[kvs + h, :, mine] = value[h * HD : (h + 1) * HD].astype(BF)
        for i in range(contexts - 1):
            kv_copy(g, i).start()
        query = dot(normed[...], wq[...]).T
        for h in range(heads):
            q[h, :, part] = turn(query[h * HD : (h + 1) * HD], cos_t, sin_t).astype(BF)

    def save_cot(g):
        return pltpu.make_async_copy(full_c, cot_o.at[pl.ds(g * chunk, chunk)], cot_sem)

    def join(g):
        @pl.when(g > 0)
        def _():
            save_cot(g - 1).wait()

        part = pl.ds(pl.multiple_of(g * chunk, chunk), chunk)
        full_c[...] = jnp.concatenate([blocks[j, part, :] for j in range(size)], 1)
        save_cot(g).start()

    save_kv = pltpu.make_async_copy(kv, kv_o, kv_sem)

    def meet():
        for g in range(groups):
            for i in range(contexts - 1):
                kv_copy(g, i).wait_recv()
        save_kv.start()
        for h in range(kvs):
            keys_in_rows[h] = flip(kv[h]).astype(BF)

    def unit(u):
        pair, g = lax.div(u, groups), lax.rem(u, groups)
        part = pl.ds(pl.multiple_of(g * chunk, chunk), chunk)
        free, last = key_blocks(g, chunk, rows, keys, key_rows)
        acc[...] = jnp.zeros_like(acc)
        sm[...] = jnp.zeros_like(sm)
        mx[...] = jnp.full_like(mx, LOWEST)
        limit = kend[:, part]

        def step(masked, i, _):
            at = pl.multiple_of(i * key_rows, key_rows)
            k_blk = keys_in_rows[pair, pl.ds(at, key_rows), :]
            v_blk = kv[kvs + pair, :, pl.ds(at, key_rows)]
            if masked:
                keep = (lax.broadcasted_iota(jnp.int32, (key_rows, chunk), 0) + at) < limit
            for h in range(group):
                s = dot(k_blk, q[pair * group + h, :, part])
                if masked:
                    s = jnp.where(keep, s, LOWEST)
                old = mx[h]
                new = jnp.maximum(old, jnp.max(s, 0, keepdims=True))
                p = jnp.exp2(s * SCALE2 - new * SCALE2)
                alpha = jnp.exp2((old - new) * SCALE2)
                mx[h] = new
                sm[h] = sm[h] * alpha + jnp.sum(p, 0, keepdims=True)
                acc[h] = acc[h] * alpha + dot(v_blk, p.astype(BF))
            return 0

        lax.fori_loop(0, free, functools.partial(step, False), 0)
        lax.fori_loop(free, last, functools.partial(step, True), 0)
        for h in range(group):
            mixed_o[pair * group + h, :, part] = (acc[h] / sm[h]).astype(BF)
            lse_o[pair * group + h, :, part] = mx[h] * SCALE2 + jnp.log2(sm[h])

    turnover = line.ticks - 1

    def tick(k, _):
        @pl.when(k == turnover)
        def _():
            line_c.begin()

        line.tick(k, project)

        @pl.when(k >= turnover)
        def _():
            line_c.tick(k - turnover, join)

        u = k - line.ticks

        @pl.when(u == 0)
        def _():
            meet()

        @pl.when((u >= 0) & (u < units))
        def _():
            unit(u)

        return 0

    lax.fori_loop(0, max(turnover + line_c.ticks, line.ticks + units), tick, 0)
    for copy in [*save(groups - 1), save_cot(groups - 1), save_kv]:
        copy.wait()
    for i in range(size - 1):
        gain_copy(i).wait_send()
    line.drain()
    line_c.drain()
    for g in range(groups):
        for i in range(contexts - 1):
            kv_copy(g, i).wait_send()


def attend_forward(
    axes, own, own_cot, gain_pair, cos_tab, sin_tab, mask, starts, w_query, w_key_t, w_value_t, chunk
):
    size, contexts = axes["tensor"], axes["context"]
    rows, width = own.shape
    features, groups = size * width, rows // chunk
    heads, kvs = w_query.shape[1] // HD, w_key_t.shape[0] // HD
    keys, group = contexts * rows, heads // kvs
    key_rows = min(KEY_ROWS_FWD, keys)
    anywhere, vmem = pl.BlockSpec(memory_space=pl.ANY), pl.BlockSpec(memory_space=pltpu.VMEM)
    shape, dma = jax.ShapeDtypeStruct, pltpu.SemaphoreType.DMA
    return pl.pallas_call(
        functools.partial(attend_kernel, size, contexts, chunk, key_rows),
        in_specs=[anywhere] * 2 + [vmem] * 5 + [anywhere] * 3,
        out_specs=[anywhere] * 2 + [vmem] * 3 + [anywhere] + [vmem] * 2 + [anywhere] + [vmem] * 2,
        out_shape=[
            shape((rows, features), BF),
            shape((rows, features), BF),
            shape((rows, 1), F32),
            shape((8, features), F32),
            shape((heads, HD, rows), BF),
            shape((2 * kvs, HD, keys), BF),
            shape((1, rows), jnp.int32),
            shape((rows, 1), F32),
            shape((rows, features), BF),
            shape((heads, HD, rows), BF),
            shape((heads, 1, rows), F32),
        ],
        scratch_shapes=gather_scratch(size, rows, width, chunk)
        + gather_scratch(size, rows, width, chunk)
        + [
            pltpu.VMEM((size, 8, width), F32),
            pltpu.VMEM((chunk, features), BF),
            pltpu.VMEM((chunk, features), BF),
            pltpu.VMEM((chunk, features), BF),
            pltpu.VMEM((2 * kvs, HD, keys), BF),
            pltpu.VMEM(w_query.shape, BF),
            pltpu.VMEM(w_key_t.shape, BF),
            pltpu.VMEM(w_value_t.shape, BF),
            pltpu.VMEM((kvs, keys, HD), BF),
            pltpu.VMEM((group, HD, chunk), F32),
            pltpu.VMEM((group, 1, chunk), F32),
            pltpu.VMEM((group, 1, chunk), F32),
            dma((size - 1,)),
            dma((size - 1,)),
            dma((groups, max(contexts - 1, 1))),
            dma((groups, max(contexts - 1, 1))),
            dma((3,)),
            dma((2,)),
            dma,
            dma,
        ],
        compiler_params=pltpu.CompilerParams(
            collective_id=3, has_side_effects=True, vmem_limit_bytes=VMEM_LIMIT
        ),
        cost_estimate=pl.CostEstimate(
            flops=2 * rows * features * (heads + 2 * kvs) * HD + 10 * heads * rows * keys * HD,
            bytes_accessed=40 << 20,
            transcendentals=heads * rows * keys,
        ),
        name="attend_forward",
    )(own, own_cot, gain_pair, cos_tab, sin_tab, mask, starts, w_query, w_key_t, w_value_t)


def attend_back_kernel(
    size, contexts, chunk, key_rows,
    ffn, q, kv, kend, do, o, lse, cos_tab, sin_tab, middle, grad_attn, normed,
    grads_o, layer_o, square_o, weights_o,
    parts, ups, downs, total, up_send, up_recv, down_send, down_recv,
    keys_in_rows, values_in_rows, dq, dk, dv, ds_all, p_all, q_all, do_all, mine, out_kv, in_kv,
    grads_in, normed_in, tiles,
    kv_send, kv_recv, part_sem, tile_sem,
):
    heads, _, rows = q.shape
    kvs, keys = kv.shape[0] // 2, kv.shape[2]
    groups, group = rows // chunk, heads // kvs
    units = kvs * groups
    place = lax.axis_index("context")
    line = Scatter(
        size, groups, chunk, parts, ups, downs, (up_send, up_recv, down_send, down_recv)
    )
    loads = [
        pltpu.make_async_copy(a, b, part_sem.at[i])
        for i, (a, b) in enumerate(((ffn, parts), (grad_attn, grads_in), (normed, normed_in)))
    ]
    for load in loads:
        load.start()
    square_o[...] = jnp.zeros_like(square_o)
    peers = others("context", contexts)
    greet(others("tensor", size) + peers)
    loads[0].wait()

    def half(of):
        at = pl.ds(pl.multiple_of(of * rows, rows), rows)
        return dk[at, :].T, dv[at, :].T

    def kv_copy(pair, i):
        return pltpu.make_async_remote_copy(
            src_ref=out_kv.at[pair, i],
            dst_ref=in_kv.at[pair, i],
            send_sem=kv_send.at[pair, i],
            recv_sem=kv_recv.at[pair, i],
            device_id=peers[i],
            device_id_type=MESH_ID,
        )

    def unit(u):
        pair, g = lax.div(u, groups), lax.rem(u, groups)
        part = pl.ds(pl.multiple_of(g * chunk, chunk), chunk)
        free, last = key_blocks(g, chunk, rows, keys, key_rows)
        limit = kend[:, part]

        @pl.when(g == 0)
        def _():
            dk[...] = jnp.zeros_like(dk)
            dv[...] = jnp.zeros_like(dv)

        dq[...] = jnp.zeros_like(dq)
        delta = []
        for h in range(group):
            head = pair * group + h
            cols = slice(h * chunk, (h + 1) * chunk)
            q_all[:, cols] = q[head, :, part]
            do_all[:, cols] = do[head, :, part]
            delta.append(
                jnp.sum(do_all[:, cols].astype(F32) * o[head, :, part].astype(F32), 0, keepdims=True)
            )

        def step(masked, i, _):
            at = pl.multiple_of(i * key_rows, key_rows)
            k_blk = keys_in_rows[pair, pl.ds(at, key_rows), :]
            v_blk = values_in_rows[pair, pl.ds(at, key_rows), :]
            kt_blk = kv[pair, :, pl.ds(at, key_rows)]
            if masked:
                keep = (lax.broadcasted_iota(jnp.int32, (key_rows, chunk), 0) + at) < limit
            for h in range(group):
                cols = slice(h * chunk, (h + 1) * chunk)
                s = dot(k_blk, q_all[:, cols])
                p = jnp.exp2(s * SCALE2 - lse[pair * group + h, :, part])
                if masked:
                    p = jnp.where(keep, p, 0.0)
                dp = dot(v_blk, do_all[:, cols])
                ds = (p * (dp - delta[h])).astype(BF)
                p_all[:, cols] = p.astype(BF)
                ds_all[:, cols] = ds
                dq[h] += dot(kt_blk, ds)
            dk[pl.ds(at, key_rows), :] += dot_nt(ds_all[...], q_all[...])
            dv[pl.ds(at, key_rows), :] += dot_nt(p_all[...], do_all[...])
            return 0

        lax.fori_loop(0, free, functools.partial(step, False), 0)
        lax.fori_loop(free, last, functools.partial(step, True), 0)
        for h in range(group):
            grads_o[pair * group + h, :, part] = turn(
                dq[h] * SCALE, cos_tab[:, part], -sin_tab[:, part]
            ).astype(BF)

        @pl.when(g == groups - 1)
        def _():
            for i in range(contexts - 1):
                key, value = half(peers[i]["context"])
                out_kv[pair, i, 0] = key.astype(BF)
                out_kv[pair, i, 1] = value.astype(BF)
                kv_copy(pair, i).start()
            mine[pair, 0], mine[pair, 1] = half(place)

    def join():
        for pair in range(kvs):
            key, value = mine[pair, 0], mine[pair, 1]
            for i in range(contexts - 1):
                kv_copy(pair, i).wait()
                key = key + in_kv[pair, i, 0].astype(F32)
                value = value + in_kv[pair, i, 1].astype(F32)
            grads_o[heads + pair] = turn(key * SCALE, cos_tab[...], -sin_tab[...]).astype(BF)
            grads_o[heads + kvs + pair] = value.astype(BF)

    features = normed.shape[1]
    tile = tile_of(features, 256)
    tile_count, each = features // tile, 4

    def save_tile(j):
        slot = lax.rem(j, 2)
        return pltpu.make_async_copy(
            tiles.at[slot], weights_o.at[pl.ds(j * tile, tile)], tile_sem.at[slot]
        )

    def weight_tile(j):
        slot = lax.rem(j, 2)

        @pl.when(j >= 2)
        def _():
            save_tile(j - 2).wait()

        cols = pl.ds(pl.multiple_of(j * tile, tile), tile)
        out = dot_nt(flip(grads_in[:, cols]).astype(BF), o[...].reshape(heads * HD, rows))
        into = dot_nt(
            flip(normed_in[:, cols]).astype(BF), grads_o[...].reshape((heads + 2 * kvs) * HD, rows)
        )
        tiles[slot] = jnp.concatenate([out, into], 1).astype(BF)
        save_tile(j).start()

    def tick(k, _):
        line.tick(k)

        @pl.when(k == 0)
        def _():
            for h in range(kvs):
                keys_in_rows[h] = flip(kv[h]).astype(BF)
                values_in_rows[h] = flip(kv[kvs + h]).astype(BF)

        @pl.when(k < units)
        def _():
            unit(k)

        @pl.when(k == units)
        def _():
            join()
            for load in loads[1:]:
                load.wait()

        first = (k - units - 1) * each
        for j in range(each):

            @pl.when((first >= 0) & (first + j < tile_count))
            def _():
                weight_tile(first + j)

        return 0

    lax.fori_loop(0, max(line.count, units + 1 + -(-tile_count // each)), tick, 0)

    def then(part, ffn_out):
        square_o[...] += jnp.sum(ffn_out * ffn_out, 0, keepdims=True)
        layer_o[part, :] = (middle[part, :] + ffn_out).astype(BF)

    line.finish(total, then)
    for j in range(max(tile_count - 2, 0), tile_count):
        save_tile(j).wait()


def attend_backward(
    axes, ffn, q, kv, kend, do, o, lse, cos_tab, sin_tab, middle, grad_attn, normed, chunk, after
):
    size, contexts = axes["tensor"], axes["context"]
    heads, _, rows = q.shape
    kvs, keys = kv.shape[0] // 2, kv.shape[2]
    group, width = heads // kvs, ffn.shape[2]
    key_rows = min(KEY_ROWS_BWD, keys)
    anywhere, vmem = pl.BlockSpec(memory_space=pl.ANY), pl.BlockSpec(memory_space=pltpu.VMEM)
    shape, dma = jax.ShapeDtypeStruct, pltpu.SemaphoreType.DMA
    slots = max(contexts - 1, 1)

    def kernel(*refs):
        attend_back_kernel(size, contexts, chunk, key_rows, *refs[:12], *refs[12 + len(after) :])

    return pl.pallas_call(
        kernel,
        in_specs=[anywhere] + [vmem] * 9 + [anywhere] * (2 + len(after)),
        out_specs=[vmem] * 3 + [anywhere],
        out_shape=[
            shape((heads + 2 * kvs, HD, rows), BF),
            shape((rows, width), BF),
            shape((1, width), F32),
            shape((size * width, (2 * heads + 2 * kvs) * HD), BF),
        ],
        scratch_shapes=scatter_scratch(size, rows, width, chunk)
        + [
            pltpu.VMEM((kvs, keys, HD), BF),
            pltpu.VMEM((kvs, keys, HD), BF),
            pltpu.VMEM((group, HD, chunk), F32),
            pltpu.VMEM((keys, HD), F32),
            pltpu.VMEM((keys, HD), F32),
            pltpu.VMEM((key_rows, group * chunk), BF),
            pltpu.VMEM((key_rows, group * chunk), BF),
            pltpu.VMEM((HD, group * chunk), BF),
            pltpu.VMEM((HD, group * chunk), BF),
            pltpu.VMEM((kvs, 2, HD, rows), F32),
            pltpu.VMEM((kvs, slots, 2, HD, rows), BF),
            pltpu.VMEM((kvs, slots, 2, HD, rows), BF),
            pltpu.VMEM(grad_attn.shape, BF),
            pltpu.VMEM(normed.shape, BF),
            pltpu.VMEM((2, tile_of(size * width, 256), (2 * heads + 2 * kvs) * HD), BF),
            dma((kvs, slots)),
            dma((kvs, slots)),
            dma((3,)),
            dma((2,)),
        ],
        compiler_params=pltpu.CompilerParams(
            collective_id=6, has_side_effects=True, vmem_limit_bytes=VMEM_LIMIT
        ),
        cost_estimate=pl.CostEstimate(
            flops=16 * heads * rows * keys * HD,
            bytes_accessed=16 << 20,
            transcendentals=heads * rows * keys,
        ),
        name="attend_backward",
    )(ffn, q, kv, kend, do, o, lse, cos_tab, sin_tab, middle, grad_attn, normed, *after)


def input_kernel(
    axes, chunk,
    grads, inv, gain, keep, attn_square, gain_rows, ffn_square, gain_own, x_own, grad_own,
    w_query, w_key_t, w_value_t, x,
    out_o, sum_o,
    parts, ups, downs, total, up_send, up_recv, down_send, down_recv,
    xs, whole, wq, wk, wv, dots, dot_sum, cols, cols_in, world, square,
    dot_send, dot_recv, col_send, col_recv, world_send, world_recv, w_sem, x_sem,
):
    size = axes["tensor"]
    here = lax.axis_index("tensor")
    rows, features = x.shape
    width, groups = features // size, rows // chunk
    nq, nk = w_query.shape[1], w_key_t.shape[0]
    line = Scatter(
        size, groups, chunk, parts, ups, downs, (up_send, up_recv, down_send, down_recv)
    )
    loads = [
        pltpu.make_async_copy(a, b, w_sem.at[i])
        for i, (a, b) in enumerate(((w_query, wq), (w_key_t, wk), (w_value_t, wv)))
    ]

    def load_x(c):
        slot = lax.rem(c, 2)
        return pltpu.make_async_copy(x.at[pl.ds(c * chunk, chunk)], xs.at[slot], x_sem.at[slot])

    for load in loads:
        load.start()
    load_x(0).start()
    contexts, replicas = axes["context"], axes["dp"] * axes["context"]
    spot = lax.axis_index("dp") * contexts + lax.axis_index("context")
    peers = others("tensor", size)
    far = [lax.rem(spot + i, replicas) for i in range(1, replicas)]
    far = [{"dp": lax.div(i, contexts), "context": lax.rem(i, contexts)} for i in far]
    greet(peers + far)
    for load in loads:
        load.wait()
    square[...] = jnp.zeros_like(square)
    row = lax.broadcasted_iota(jnp.int32, (8, width), 0)
    lane = lax.broadcasted_iota(jnp.int32, (8, width), 1)

    def compute(c):
        slot = lax.rem(c, 2)
        part = pl.ds(pl.multiple_of(c * chunk, chunk), chunk)
        load_x(c).wait()

        @pl.when(c + 1 < groups)
        def _():
            load_x(c + 1).start()

        g = flip(grads[:, part]).astype(BF)
        whole[...] = (
            dot_nt(g[:, :nq], wq[...])
            + dot(g[:, nq : nq + nk], wk[...])
            + dot(g[:, nq + nk :], wv[...])
        )
        for j in range(size):
            parts[j, part, :] = whole[:, j * width : (j + 1) * width].astype(BF)

    def add_up(c):
        slot = lax.rem(c, 2)
        part = pl.ds(pl.multiple_of(c * chunk, chunk), chunk)
        stream = xs[slot].astype(F32)
        square[...] += jnp.sum(stream * stream * keep[part, :], 0, keepdims=True)
        moved = whole[...] * (stream * inv[part, :])
        rowsum = jnp.sum(moved * gain[0:1, :], 1, keepdims=True)
        dots[here, :, part] = jnp.broadcast_to(rowsum, (chunk, 128)).T[:8]
        colsum = jnp.sum(moved, 0, keepdims=True)
        for j in range(size):
            piece = jnp.where(row == 0, colsum[:, j * width : (j + 1) * width], 0.0)

            @pl.when(c == 0)
            def _():
                cols[j] = piece

            @pl.when(c > 0)
            def _():
                cols[j] += piece

    def copy_to(src, dst, send, recv, peer):
        return pltpu.make_async_remote_copy(
            src_ref=src,
            dst_ref=dst,
            send_sem=send,
            recv_sem=recv,
            device_id=peer,
            device_id_type=MESH_ID,
        )

    def dot_copy(i):
        mine = dots.at[here]
        return copy_to(mine, mine, dot_send.at[i], dot_recv.at[i], peers[i])

    def col_copy(i):
        src = cols.at[peers[i]["tensor"]]
        return copy_to(src, cols_in.at[here], col_send.at[i], col_recv.at[i], peers[i])

    def world_copy(i):
        mine = world.at[spot]
        return copy_to(mine, mine, world_send.at[i], world_recv.at[i], far[i])

    def exchange():
        numbers = jnp.zeros((8, width), F32)
        for i, a in enumerate((square[...], attn_square[...], ffn_square[...], keep[...])):
            a = jnp.sum(jnp.sum(a, 0, keepdims=True), 1, keepdims=True)
            share = 1.0 if i == 2 else 1.0 / size
            numbers += jnp.where((row == 1) & (lane == i), a * share, 0.0)
        for j in range(size):
            cols[j] += numbers
        cols_in[here] = cols[here]
        for i in range(size - 1):
            dot_copy(i).start()
            col_copy(i).start()

    def spread():
        for i in range(size - 1):
            dot_copy(i).wait()
            col_copy(i).wait()
        dot_total, column = dots[0], cols_in[0]
        for j in range(1, size):
            dot_total = dot_total + dots[j]
            column = column + cols_in[j]
        dot_sum[...] = dot_total
        world[spot] = column

        def put(piece):
            world[spot, 2:3] = piece

        own_columns(size, gain_rows[...], put)
        for i in range(replicas - 1):
            world_copy(i).start()

    def tick(k, _):
        @pl.when(k < groups)
        def _():
            compute(k)

        line.tick(k)

        @pl.when(k < groups)
        def _():
            add_up(k)

        @pl.when(k == groups)
        def _():
            exchange()

        @pl.when(k == groups + 3)
        def _():
            spread()

        return 0

    lax.fori_loop(0, max(line.count, groups + 4), tick, 0)

    def then(part, grad):
        through = grad * gain_own[...] - x_own[part, :].astype(F32) * inv[part, :] * (
            dot_sum[:, part].T[:, :1] / features
        )
        out_o[part, :] = (grad_own[part, :] + inv[part, :] * through).astype(BF)

    line.finish(total, then)
    for i in range(replicas - 1):
        world_copy(i).wait()
    everything = world[0]
    for j in range(1, replicas):
        everything = everything + world[j]
    sum_o[...] = everything


def input_gradient(
    axes, grads, inv, gain, keep, attn_square, gain_rows, ffn_square, gain_own, x_own, grad_own,
    w_query, w_key_t, w_value_t, x, chunk, after,
):
    size, replicas = axes["tensor"], axes["dp"] * axes["context"]
    rows, features = x.shape
    width = features // size
    anywhere, vmem = pl.BlockSpec(memory_space=pl.ANY), pl.BlockSpec(memory_space=pltpu.VMEM)
    shape, dma = jax.ShapeDtypeStruct, pltpu.SemaphoreType.DMA

    def kernel(*refs):
        input_kernel(axes, chunk, *refs[:14], *refs[14 + len(after) :])

    return pl.pallas_call(
        kernel,
        in_specs=[vmem] * 10 + [anywhere] * (4 + len(after)),
        out_specs=[vmem] * 2,
        out_shape=[
            shape((rows, width), BF),
            shape((8, width), F32),
        ],
        scratch_shapes=scatter_scratch(size, rows, width, chunk)
        + [
            pltpu.VMEM((2, chunk, features), BF),
            pltpu.VMEM((chunk, features), F32),
            pltpu.VMEM(w_query.shape, BF),
            pltpu.VMEM(w_key_t.shape, BF),
            pltpu.VMEM(w_value_t.shape, BF),
            pltpu.VMEM((size, 8, rows), F32),
            pltpu.VMEM((8, rows), F32),
            pltpu.VMEM((size, 8, width), F32),
            pltpu.VMEM((size, 8, width), F32),
            pltpu.VMEM((replicas, 8, width), F32),
            pltpu.VMEM((1, features), F32),
            dma((size - 1,)),
            dma((size - 1,)),
            dma((size - 1,)),
            dma((size - 1,)),
            dma((replicas - 1,)),
            dma((replicas - 1,)),
            dma((3,)),
            dma((2,)),
        ],
        compiler_params=pltpu.CompilerParams(
            collective_id=4, has_side_effects=True, vmem_limit_bytes=VMEM_LIMIT
        ),
        cost_estimate=pl.CostEstimate(
            flops=2 * rows * features * grads.shape[0],
            bytes_accessed=20 << 20,
            transcendentals=rows,
        ),
        name="input_gradient",
    )(
        grads, inv, gain, keep, attn_square, gain_rows, ffn_square, gain_own, x_own, grad_own,
        w_query, w_key_t, w_value_t, x, *after,
    )


def local(
    axes,
    layer_input_hidden,
    cotangent,
    valid_mask,
    span_starts,
    gain_attn,
    w_query,
    w_key,
    w_value,
    w_out,
    gain_mlp,
    w_gate,
    w_up,
    w_down,
):
    _, rows, width = layer_input_hidden.shape
    size = axes["tensor"]
    features = width * size
    kvs = w_key.shape[1] // HD
    heads = w_query.shape[1] // HD
    position = lax.axis_index("context") * rows + jnp.arange(rows, dtype=jnp.int32)
    inverse_freq = rope_base ** (-2.0 * jnp.arange(HD // 2, dtype=F32) / HD)
    angles = inverse_freq[:, None] * position.astype(F32)[None, :]
    cos_tab, sin_tab = jnp.cos(angles), jnp.sin(angles)
    x_own = layer_input_hidden[0]
    w_key_t, w_value_t = w_key.T, w_value.T

    def shard(grad):
        return lax.psum_scatter(grad, ("dp", "context"), scatter_dimension=0, tiled=True)

    (
        x_low,
        normed_a,
        inv_a,
        gains,
        query_t,
        both,
        kend,
        keep,
        cot,
        mixed,
        lse,
    ) = attend_forward(
        axes,
        x_own,
        cotangent[0],
        jnp.stack([gain_attn, gain_mlp]),
        cos_tab,
        sin_tab,
        valid_mask,
        span_starts,
        w_query,
        w_key_t,
        w_value_t,
        GROUP_ROWS,
    )
    normed_m, act, ggu, down_part, back_part, middle, middle_own, attn_square = feed_forward(
        size,
        mixed.reshape(heads * HD, rows),
        keep,
        gains,
        w_out,
        w_gate,
        w_up,
        w_down,
        x_low,
        cot,
        GROUP_ROWS,
        HOP_ROWS,
    )
    grad_ggu = ein("sd,sf->df", normed_m, ggu).astype(BF)
    ggu_sum = shard(grad_ggu)

    grad_own, grad_attn, grad_mixed, gain_m_rows, grad_down = norm_back(
        size, back_part, keep, gains, w_out, middle, cot, act, GROUP_ROWS, HOP_ROWS, (grad_ggu,)
    )
    down_sum = shard(grad_down)
    grads, layer_out, ffn_square, grad_rest = attend_backward(
        axes,
        down_part,
        query_t,
        both,
        kend,
        grad_mixed.reshape(heads, HD, rows),
        mixed,
        lse,
        cos_tab,
        sin_tab,
        middle_own,
        grad_attn,
        normed_a,
        GROUP_ROWS,
        (ggu_sum,),
    )
    rest_sum = shard(grad_rest)

    input_grad, sums = input_gradient(
        axes,
        grads.reshape(-1, rows),
        inv_a,
        gains,
        keep,
        attn_square,
        gain_m_rows,
        ffn_square,
        gain_attn[None],
        x_own,
        grad_own,
        w_query,
        w_key_t,
        w_value_t,
        x_low,
        GROUP_ROWS,
        (grad_rest, down_sum),
    )
    rest_sum = jnp.where(sums[1, 3] >= 0.0, rest_sum.astype(F32), 0.0)
    gate_sum, up_sum = jnp.split(ggu_sum.astype(F32), 2, 1)
    down_sum = down_sum.astype(F32).T
    cut = [heads * HD, 2 * heads * HD, (2 * heads + kvs) * HD]
    out_sum, query_sum, key_sum, value_sum = jnp.split(rest_sum, cut, 1)
    rms = jnp.sqrt(sums[1, :3] / (sums[1, 3] * features))
    return (
        layer_out[None],
        input_grad[None],
        sums[0],
        query_sum,
        key_sum,
        value_sum,
        out_sum.T,
        sums[2],
        gate_sum,
        up_sum,
        down_sum,
        rms[0],
        rms[1],
        rms[2],
    )


def solution(mesh):
    token = P("dp", "context", "tensor")
    by_rows = P(("dp", "context"), "tensor")
    by_columns = P("tensor", ("dp", "context"))
    cols, rows, vec = P(None, "tensor"), P("tensor", None), P("tensor")
    return jax.shard_map(
        functools.partial(local, dict(mesh.shape)),
        mesh=mesh,
        in_specs=(
            token,
            token,
            P("dp", None),
            P("dp", None),
            vec,
            cols,
            cols,
            cols,
            rows,
            vec,
            cols,
            cols,
            rows,
        ),
        out_specs=(
            token,
            token,
            vec,
            by_rows,
            by_rows,
            by_rows,
            by_columns,
            vec,
            by_rows,
            by_rows,
            by_columns,
            P(),
            P(),
            P(),
        ),
        check_vma=False,
    )
```

```python
import functools
import math

import jax
import jax.numpy as jnp
from jax import lax
from jax.experimental import pallas as pl
from jax.experimental.pallas import tpu as pltpu
from jax.sharding import PartitionSpec as P

HD = 80
PIC = 256
LEAST_VALID = 1536
F32 = jnp.float32
BF = jnp.bfloat16
SCALE = HD**-0.5
SCALE2 = SCALE * math.log2(math.e)
LOWEST = -1e30
GROUP_ROWS = 256
HOP_ROWS = 64
VMEM_LIMIT = 60 << 20
KEY_ROWS_FWD = 1024
KEY_ROWS_BWD = 512

epsilon = 1e-05
rope_base = 1000000.0


def dot(a, b):
    return jnp.dot(a, b, preferred_element_type=F32)


def dot_nt(a, b):
    return lax.dot_general(a, b, (((1,), (1,)), ((), ())), preferred_element_type=F32)


def ein(spec, a, b):
    return jnp.einsum(spec, a, b, preferred_element_type=F32)


MESH_ID = pl.DeviceIdType.MESH
SENT = 4


def ring_of(size):
    return size + 4


def add_low(a, b):
    return (a.astype(F32) + b.astype(F32)).astype(BF)


def partner(replicas):
    spot = lax.axis_index("dp")
    return [] if replicas % 2 else [{"dp": spot + 1 - 2 * lax.rem(spot, 2)}]


class Sums:
    def __init__(self, axes, count, part, low, high, sent, sems):
        self.size, self.count, self.part = axes["tensor"], count, part
        self.replicas = axes["dp"]
        self.low, self.high, self.sent = low, high, sent
        self.low_send, self.low_recv, self.high_send, self.high_recv = sems
        self.here = lax.axis_index("tensor")

    def barrier(self):
        here, size = self.here, self.size
        barrier = pltpu.get_barrier_semaphore()
        pair = partner(self.replicas)
        for peer in pair:
            pl.semaphore_signal(barrier, inc=1, device_id=peer, device_id_type=MESH_ID)

        @pl.when(here > 0)
        def _():
            pl.semaphore_signal(
                barrier, inc=1, device_id={"tensor": here - 1}, device_id_type=MESH_ID
            )

        @pl.when(here < size - 1)
        def _():
            pl.semaphore_signal(
                barrier, inc=1, device_id={"tensor": here + 1}, device_id_type=MESH_ID
            )

        @pl.when((here > 0) & (here < size - 1))
        def _():
            pl.semaphore_wait(barrier, 2 + len(pair))

        @pl.when((here == 0) | (here == size - 1))
        def _():
            pl.semaphore_wait(barrier, 1 + len(pair))

    def up(self, c):
        slot = lax.rem(c, ring_of(self.size))
        return pltpu.make_async_remote_copy(
            src_ref=self.low.at[slot],
            dst_ref=self.low.at[slot],
            send_sem=self.low_send.at[slot],
            recv_sem=self.low_recv.at[slot],
            device_id={"tensor": self.here + 1},
            device_id_type=MESH_ID,
        )

    def down(self, c):
        slot, mine = lax.rem(c, ring_of(self.size)), lax.rem(c, SENT)
        return pltpu.make_async_remote_copy(
            src_ref=self.sent.at[mine],
            dst_ref=self.high.at[slot],
            send_sem=self.high_send.at[mine],
            recv_sem=self.high_recv.at[slot],
            device_id={"tensor": self.here - 1},
            device_id_type=MESH_ID,
        )

    def tick(self, k):
        here, size, count = self.here, self.size, self.count
        bottom, top = here == 0, here == size - 1
        c = k - here

        @pl.when((c >= 0) & (c < count))
        def _():
            slot = lax.rem(c, ring_of(self.size))

            @pl.when(bottom)
            def _():
                self.low[slot] = self.part(c)

            @pl.when(jnp.logical_not(bottom))
            def _():
                self.up(c).wait_recv()
                self.low[slot] = add_low(self.low[slot], self.part(c))

            @pl.when(jnp.logical_not(top))
            def _():
                self.up(c).start()

        d = k - (size - 1 - here)

        @pl.when((d >= 0) & (d < count))
        def _():
            slot, mine = lax.rem(d, ring_of(self.size)), lax.rem(d, SENT)

            @pl.when(top)
            def _():
                self.sent[mine] = self.part(d)

            @pl.when(jnp.logical_not(top))
            def _():
                self.down(d).wait_recv()

                @pl.when(jnp.logical_not(bottom))
                def _():
                    self.sent[mine] = add_low(self.high[slot], self.part(d))

            @pl.when(jnp.logical_not(bottom))
            def _():
                self.down(d).start()

        @pl.when((c >= 2) & (c < count + 2) & jnp.logical_not(top))
        def _():
            self.up(c - 2).wait_send()

        @pl.when((d >= 2) & (d < count + 2) & jnp.logical_not(bottom))
        def _():
            self.down(d - 2).wait_send()

    def total(self, c, then):
        slot = lax.rem(c, ring_of(self.size))
        top = self.here == self.size - 1

        @pl.when(top)
        def _():
            then(self.low[slot].astype(F32))

        @pl.when(jnp.logical_not(top))
        def _():
            then(self.low[slot].astype(F32) + self.high[slot].astype(F32))


def sum_scratch(size, hop, features):
    ring, dma = ring_of(size), pltpu.SemaphoreType.DMA
    return [
        pltpu.VMEM((ring, hop, features), BF),
        pltpu.VMEM((ring, hop, features), BF),
        pltpu.VMEM((SENT, hop, features), BF),
        dma((ring,)),
        dma((ring,)),
        dma((SENT,)),
        dma((ring,)),
    ]


def own_columns(size, a, then):
    width = a.shape[1] // size
    for j in range(size):

        @pl.when(lax.axis_index("tensor") == j)
        def _():
            then(a[:, j * width : (j + 1) * width])


def tile_of(n, most):
    for tile in range(most, 0, -128):
        if n % tile == 0:
            return tile
    return n


def ffn_kernel(
    axes, hop, chunk,
    mixed, keep, gain, w_out, w_gate, w_up, w_down, x, cot,
    normed_o, act_o, ggu_o, ffn_o, back_o, middle_o, own_o, square_o,
    low, high, sent, low_send, low_recv, high_send, high_recv,
    wo, wg, wu, wd, parts, normed, xs, cots, mids, owns, act, ggu, ffn, back, split,
    w_sem, x_sem, cot_sem, normed_sem, mid_sem, own_sem, act_sem, ffn_sem,
):
    size = axes["tensor"]
    rows, features = x.shape
    hidden = w_gate.shape[1]
    count, per, groups = rows // hop, chunk // hop, rows // chunk
    tile_f, tile_d = tile_of(hidden, 256), tile_of(features, 256)
    tiles_f, tiles_d = hidden // tile_f, features // tile_d
    half_f, half_d = -(-tiles_f // 2), -(-tiles_d // 2)
    lag = size - 1 + per - 1
    ahead, part_slots = per // 2, parts.shape[0]
    ticks = max(per * groups + lag, count + size)

    def part(c):
        slot = lax.rem(lax.div(c, per), part_slots)
        return parts[slot, pl.ds(pl.multiple_of(lax.rem(c, per) * hop, hop), hop), :]

    sums = Sums(axes, count, part, low, high, sent, (low_send, low_recv, high_send, high_recv))
    loads = [
        pltpu.make_async_copy(a, b, w_sem.at[i])
        for i, (a, b) in enumerate(((w_out, wo), (w_gate, wg), (w_up, wu), (w_down, wd)))
    ]
    for load in loads:
        load.start()

    def load_x(c):
        slot = lax.rem(c, 2)
        return pltpu.make_async_copy(x.at[pl.ds(c * hop, hop)], xs.at[slot], x_sem.at[slot])

    def load_cot(g):
        return pltpu.make_async_copy(cot.at[pl.ds(g * chunk, chunk)], cots, cot_sem)

    def save_normed(c):
        at, q = lax.rem(lax.div(c, per), 2), lax.rem(c, per)
        return pltpu.make_async_copy(
            normed.at[at, pl.ds(q * hop, hop)], normed_o.at[pl.ds(c * hop, hop)], normed_sem.at[at, q]
        )

    def save_mid(c):
        slot = lax.rem(c, 2)
        return pltpu.make_async_copy(mids.at[slot], middle_o.at[pl.ds(c * hop, hop)], mid_sem.at[slot])

    def save_own(c):
        slot = lax.rem(c, 2)
        return pltpu.make_async_copy(owns.at[slot], own_o.at[pl.ds(c * hop, hop)], own_sem.at[slot])

    def save_act(g):
        return [
            pltpu.make_async_copy(a, b.at[pl.ds(g * chunk, chunk)], act_sem.at[i])
            for i, (a, b) in enumerate(((act, act_o), (ggu, ggu_o)))
        ]

    def save_ffn(g):
        part = pl.ds(g * chunk, chunk)
        return [
            pltpu.make_async_copy(split, ffn_o.at[:, part], ffn_sem.at[0]),
            pltpu.make_async_copy(back, back_o.at[part], ffn_sem.at[1]),
        ]

    def project(g):
        at = lax.rem(g, part_slots)
        lhs = mixed[:, pl.ds(pl.multiple_of(g * chunk, chunk), chunk)]

        def one(j, _):
            cols = pl.ds(pl.multiple_of(j * tile_d, tile_d), tile_d)
            parts[at, :, cols] = lax.dot_general(
                lhs, wo[:, cols], (((0,), (0,)), ((), ())), preferred_element_type=F32
            ).astype(BF)
            return 0

        lax.fori_loop(0, tiles_d, one, 0)

    load_x(0).start()
    load_cot(0).start()
    square_o[...] = jnp.zeros_like(square_o)
    loads[0].wait()
    project(0)
    sums.barrier()

    def finish(c):
        slot = lax.rem(c, 2)
        load_x(c).wait()

        @pl.when(c + 1 < count)
        def _():
            load_x(c + 1).start()

        @pl.when(c >= 2)
        def _():
            save_mid(c - 2).wait()
            save_own(c - 2).wait()

        @pl.when(c >= 2 * per)
        def _():
            save_normed(c - 2 * per).wait()

        kept = keep[pl.ds(pl.multiple_of(c * hop, hop), hop), :]

        def then(total):
            out = kept * total
            square_o[...] += jnp.sum(out * out, 0, keepdims=True)
            mids[slot] = xs[slot].astype(F32) + out

        sums.total(c, then)
        mid = mids[slot]
        own_columns(size, mid, lambda piece: owns.__setitem__(slot, piece))
        save_own(c).start()
        inv = lax.rsqrt(jnp.sum(mid * mid, 1, keepdims=True) / features + epsilon)
        at = lax.rem(lax.div(c, per), 2)
        normed[at, pl.ds(pl.multiple_of(lax.rem(c, per) * hop, hop), hop), :] = (
            mid * inv * gain[1:2, :]
        ).astype(BF)
        save_mid(c).start()
        save_normed(c).start()

    def inner(g, lo, hi):
        at = lax.rem(g, 2)
        kept = keep[pl.ds(pl.multiple_of(g * chunk, chunk), chunk), :]

        def one(j, _):
            cols = pl.ds(pl.multiple_of(j * tile_f, tile_f), tile_f)
            gate = dot(normed[at], wg[:, cols])
            up = dot(normed[at], wu[:, cols])
            grad = dot_nt(cots[...], wd[cols, :]) * kept
            sig = jax.nn.sigmoid(gate)
            silu = gate * sig
            act[:, cols] = (silu * up * kept).astype(BF)
            ggu[:, cols] = (grad * up * (sig + silu * (1.0 - sig))).astype(BF)
            cols = pl.ds(pl.multiple_of(hidden + j * tile_f, tile_f), tile_f)
            ggu[:, cols] = (grad * silu).astype(BF)
            return 0

        lax.fori_loop(lo, hi, one, 0)

    def outer(g, lo, hi):
        def one(j, _):
            cols = pl.ds(pl.multiple_of(j * tile_d, tile_d), tile_d)
            ffn[:, cols] = dot(act[...], wd[:, cols]).astype(BF)
            back[:, cols] = (
                dot_nt(ggu[:, :hidden], wg[cols, :]) + dot_nt(ggu[:, hidden:], wu[cols, :])
            ).astype(BF)
            return 0

        lax.fori_loop(lo, hi, one, 0)

    def tick(k, _):
        sums.tick(k)
        c = k - (size - 1)

        @pl.when((c >= 0) & (c < count))
        def _():
            finish(c)

        later = k + ahead

        @pl.when((lax.rem(later, per) == 0) & (later < count))
        def _():
            project(lax.div(later, per))

        s = k - lag
        g, stage = lax.div(s, per), lax.rem(s, per)
        going = (s >= 0) & (g < groups)

        @pl.when(going & (stage == 0 * per // 4))
        def _():
            @pl.when(g == 0)
            def _():
                for load in loads[1:]:
                    load.wait()

            load_cot(g).wait()

            @pl.when(g > 0)
            def _():
                for copy in save_act(g - 1):
                    copy.wait()

            inner(g, 0, half_f)

        @pl.when(going & (stage == 1 * per // 4))
        def _():
            inner(g, half_f, tiles_f)
            for copy in save_act(g):
                copy.start()

            @pl.when(g + 1 < groups)
            def _():
                load_cot(g + 1).start()

        @pl.when(going & (stage == 2 * per // 4))
        def _():
            @pl.when(g > 0)
            def _():
                for copy in save_ffn(g - 1):
                    copy.wait()

            outer(g, 0, half_d)

        @pl.when(going & (stage == 3 * per // 4))
        def _():
            outer(g, half_d, tiles_d)
            for j in range(size):
                split[j] = ffn[:, j * (features // size) : (j + 1) * (features // size)]
            for copy in save_ffn(g):
                copy.start()

        return 0

    lax.fori_loop(0, ticks, tick, 0)
    for copy in save_act(groups - 1) + save_ffn(groups - 1):
        copy.wait()
    for c in range(count - 2, count):
        save_mid(c).wait()
        save_own(c).wait()
    for c in range(count - 2 * per, count):
        save_normed(c).wait()


def feed_forward(axes, mixed, keep, gain, w_out, w_gate, w_up, w_down, x, cot, chunk, hop):
    size = axes["tensor"]
    rows, features = x.shape
    hidden = w_gate.shape[1]
    per = chunk // hop
    anywhere, vmem = pl.BlockSpec(memory_space=pl.ANY), pl.BlockSpec(memory_space=pltpu.VMEM)
    shape = jax.ShapeDtypeStruct
    return pl.pallas_call(
        functools.partial(ffn_kernel, axes, hop, chunk),
        in_specs=[vmem] * 3 + [anywhere] * 6,
        out_specs=[anywhere] * 7 + [vmem],
        out_shape=[
            shape((rows, features), BF),
            shape((rows, hidden), BF),
            shape((rows, 2 * hidden), BF),
            shape((size, rows, features // size), BF),
            shape((rows, features), BF),
            shape((rows, features), F32),
            shape((rows, features // size), F32),
            shape((1, features), F32),
        ],
        scratch_shapes=sum_scratch(size, hop, features)
        + [
            pltpu.VMEM(w_out.shape, BF),
            pltpu.VMEM(w_gate.shape, BF),
            pltpu.VMEM(w_up.shape, BF),
            pltpu.VMEM(w_down.shape, BF),
            pltpu.VMEM((-(-(per + size - 2 + per // 2) // per), chunk, features), BF),
            pltpu.VMEM((2, chunk, features), BF),
            pltpu.VMEM((2, hop, features), BF),
            pltpu.VMEM((chunk, features), BF),
            pltpu.VMEM((2, hop, features), F32),
            pltpu.VMEM((2, hop, features // size), F32),
            pltpu.VMEM((chunk, hidden), BF),
            pltpu.VMEM((chunk, 2 * hidden), BF),
            pltpu.VMEM((chunk, features), BF),
            pltpu.VMEM((chunk, features), BF),
            pltpu.VMEM((size, chunk, features // size), BF),
            pltpu.SemaphoreType.DMA((4,)),
            pltpu.SemaphoreType.DMA((2,)),
            pltpu.SemaphoreType.DMA,
            pltpu.SemaphoreType.DMA((2, per)),
            pltpu.SemaphoreType.DMA((2,)),
            pltpu.SemaphoreType.DMA((2,)),
            pltpu.SemaphoreType.DMA((2,)),
            pltpu.SemaphoreType.DMA((2,)),
        ],
        compiler_params=pltpu.CompilerParams(
            collective_id=1, has_side_effects=True, vmem_limit_bytes=VMEM_LIMIT
        ),
        cost_estimate=pl.CostEstimate(
            flops=2 * rows * features * (6 * hidden + w_out.shape[0]),
            bytes_accessed=80 << 20,
            transcendentals=rows * hidden,
        ),
        name="feed_forward",
    )(mixed, keep, gain, w_out, w_gate, w_up, w_down, x, cot)


def back_kernel(
    axes, hop, chunk,
    parts, keep, gain, w_out, middle, cot, act,
    own_o, grad_low_o, mixed_o, gain_o, down_o,
    low, high, sent, low_send, low_recv, high_send, high_recv,
    wo, mids, cots, acts, owns, grads_low, tiles,
    load_sem, mid_sem, own_sem, grad_low_sem, tile_sem,
):
    size = axes["tensor"]
    rows, features = middle.shape
    count, per, groups = rows // hop, chunk // hop, rows // chunk
    tile = tile_of(features, 256)
    tile_count = features // tile
    ticks = max(count + size, per * (groups - 1) + size - 1 + per, tile_count + 1)

    def part(c):
        return parts[pl.ds(pl.multiple_of(c * hop, hop), hop), :]

    sums = Sums(axes, count, part, low, high, sent, (low_send, low_recv, high_send, high_recv))
    loads = [
        pltpu.make_async_copy(a, b, load_sem.at[i])
        for i, (a, b) in enumerate(((cot, cots), (w_out, wo), (act, acts)))
    ]

    def load_mid(c):
        slot = lax.rem(c, 2)
        return pltpu.make_async_copy(
            middle.at[pl.ds(c * hop, hop)], mids.at[slot], mid_sem.at[slot]
        )

    def save_own(c):
        slot = lax.rem(c, 2)
        return pltpu.make_async_copy(owns.at[slot], own_o.at[pl.ds(c * hop, hop)], own_sem.at[slot])

    def save_low(c):
        q = lax.rem(c, per)
        return pltpu.make_async_copy(
            grads_low.at[pl.ds(q * hop, hop)], grad_low_o.at[pl.ds(c * hop, hop)], grad_low_sem.at[q]
        )

    def save_tile(j):
        slot = lax.rem(j, 2)
        return pltpu.make_async_copy(
            tiles.at[slot], down_o.at[pl.ds(j * tile, tile)], tile_sem.at[slot]
        )

    load_mid(0).start()
    for load in loads:
        load.start()
    gain_o[...] = jnp.zeros_like(gain_o)
    sums.barrier()

    def finish(c):
        slot = lax.rem(c, 2)
        load_mid(c).wait()

        @pl.when(c + 1 < count)
        def _():
            load_mid(c + 1).start()

        @pl.when(c >= 2)
        def _():
            save_own(c - 2).wait()

        @pl.when(c >= per)
        def _():
            save_low(c - per).wait()

        chunk_rows = pl.ds(pl.multiple_of(c * hop, hop), hop)
        kept = keep[chunk_rows, :]
        mid = mids[slot]
        inv = lax.rsqrt(jnp.sum(mid * mid, 1, keepdims=True) / features + epsilon)
        hat = mid * inv

        def then(total):
            gain_o[...] += jnp.sum(total * hat, 0, keepdims=True)
            weighted = total * gain[1:2, :]
            mean = jnp.sum(weighted * hat, 1, keepdims=True) / features
            mids[slot] = cots[chunk_rows, :].astype(F32) + inv * (weighted - hat * mean)

        sums.total(c, then)
        grad = mids[slot]
        own_columns(size, grad, lambda piece: owns.__setitem__(slot, piece))
        grads_low[pl.ds(pl.multiple_of(lax.rem(c, per) * hop, hop), hop), :] = (kept * grad).astype(
            BF
        )
        save_own(c).start()
        save_low(c).start()

    def weight_tile(j):
        slot = lax.rem(j, 2)

        @pl.when(j >= 2)
        def _():
            save_tile(j - 2).wait()

        cols = pl.ds(pl.multiple_of(j * tile, tile), tile)
        tiles[slot] = dot(flip(cots[:, cols]).astype(BF), acts[...]).astype(BF)
        save_tile(j).start()

    def tick(k, _):
        sums.tick(k)
        c = k - (size - 1)

        @pl.when(k == 1)
        def _():
            for load in loads:
                load.wait()

        @pl.when((c >= 0) & (c < count))
        def _():
            finish(c)

            @pl.when(lax.rem(c, per) == per - 1)
            def _():
                g = lax.div(c, per)
                mixed_o[:, pl.ds(pl.multiple_of(g * chunk, chunk), chunk)] = dot_nt(
                    wo[...], grads_low[...]
                ).astype(BF)

        @pl.when((k >= 1) & (k <= tile_count))
        def _():
            weight_tile(k - 1)

        return 0

    lax.fori_loop(0, ticks, tick, 0)
    for c in range(count - 2, count):
        save_own(c).wait()
    for c in range(count - per, count):
        save_low(c).wait()
    for j in range(max(tile_count - 2, 0), tile_count):
        save_tile(j).wait()


def norm_back(axes, parts, keep, gain, w_out, middle, cot, act, chunk, hop, after):
    size = axes["tensor"]
    rows, features = middle.shape
    per = chunk // hop
    anywhere, vmem = pl.BlockSpec(memory_space=pl.ANY), pl.BlockSpec(memory_space=pltpu.VMEM)
    shape, dma = jax.ShapeDtypeStruct, pltpu.SemaphoreType.DMA

    def kernel(*refs):
        back_kernel(axes, hop, chunk, *refs[:7], *refs[7 + len(after) :])

    return pl.pallas_call(
        kernel,
        in_specs=[vmem] * 3 + [anywhere] * (4 + len(after)),
        out_specs=[anywhere] * 2 + [vmem] * 2 + [anywhere],
        out_shape=[
            shape((rows, features // size), F32),
            shape((rows, features), BF),
            shape((w_out.shape[0], rows), BF),
            shape((1, features), F32),
            shape((features, act.shape[1]), BF),
        ],
        scratch_shapes=sum_scratch(size, hop, features)
        + [
            pltpu.VMEM(w_out.shape, BF),
            pltpu.VMEM((2, hop, features), F32),
            pltpu.VMEM(cot.shape, BF),
            pltpu.VMEM(act.shape, BF),
            pltpu.VMEM((2, hop, features // size), F32),
            pltpu.VMEM((chunk, features), BF),
            pltpu.VMEM((2, tile_of(features, 256), act.shape[1]), BF),
            dma((3,)),
            dma((2,)),
            dma((2,)),
            dma((per,)),
            dma((2,)),
        ],
        compiler_params=pltpu.CompilerParams(
            collective_id=2, has_side_effects=True, vmem_limit_bytes=VMEM_LIMIT
        ),
        cost_estimate=pl.CostEstimate(
            flops=2 * rows * features * (w_out.shape[0] + act.shape[1]),
            bytes_accessed=40 << 20,
            transcendentals=rows,
        ),
        name="norm_back",
    )(parts, keep, gain, w_out, middle, cot, act, *after)


def greet(peers):
    barrier = pltpu.get_barrier_semaphore()
    for peer in peers:
        pl.semaphore_signal(barrier, inc=1, device_id=peer, device_id_type=MESH_ID)
    pl.semaphore_wait(barrier, len(peers))


def others(axis, size):
    here = lax.axis_index(axis)
    return [{axis: lax.rem(here + i, size)} for i in range(1, size)]


class Gather:
    def __init__(self, size, groups, chunk, own, blocks, sems):
        self.size, self.groups, self.chunk = size, groups, chunk
        self.own, self.blocks = own, blocks
        self.up_send, self.up_recv, self.down_send, self.down_recv, self.own_sem = sems
        self.steps = size - 1
        self.ticks = groups * self.steps + 1
        self.here = lax.axis_index("tensor")

    def load(self, g):
        part = pl.ds(g * self.chunk, self.chunk)
        return pltpu.make_async_copy(
            self.own.at[part], self.blocks.at[self.here, part], self.own_sem.at[g]
        )

    def load_all(self):
        for g in range(self.groups):
            self.load(g).start()

    def move(self, g, s, owner, peer, send, recv):
        block = self.blocks.at[jnp.clip(owner, 0, self.size - 1), pl.ds(g * self.chunk, self.chunk)]
        return pltpu.make_async_remote_copy(
            src_ref=block,
            dst_ref=block,
            send_sem=send.at[g, s],
            recv_sem=recv.at[g, s],
            device_id={"tensor": peer},
            device_id_type=MESH_ID,
        )

    def up(self, g, s):
        return self.move(g, s, self.here - s, self.here + 1, self.up_send, self.up_recv)

    def down(self, g, s):
        return self.move(g, s, self.here + s, self.here - 1, self.down_send, self.down_recv)

    def each(self, g, s, act):
        @pl.when((self.here >= s) & (self.here < self.size - 1))
        def _():
            act(self.up(g, s))

        @pl.when((self.here + s < self.size) & (self.here > 0))
        def _():
            act(self.down(g, s))

    def send(self, g, s):
        self.each(g, s, lambda copy: copy.start())

    def receive(self, g, s):
        @pl.when(self.here - 1 - s >= 0)
        def _():
            self.up(g, s).wait_recv()

        @pl.when(self.here + 1 + s < self.size)
        def _():
            self.down(g, s).wait_recv()

    def begin(self):
        self.load(0).wait()
        self.send(0, 0)

    def tick(self, k, then):
        g, s = lax.div(k, self.steps), lax.rem(k, self.steps)

        @pl.when((s > 0) & (g < self.groups))
        def _():
            self.receive(g, s - 1)
            self.send(g, s)

        @pl.when((s == self.steps - 1) & (g + 1 < self.groups))
        def _():
            self.load(g + 1).wait()
            self.send(g + 1, 0)

        @pl.when((s == 0) & (g > 0) & (g <= self.groups))
        def _():
            self.receive(g - 1, self.steps - 1)
            then(g - 1)

    def drain(self):
        for g in range(self.groups):
            for s in range(self.steps):
                self.each(g, s, lambda copy: copy.wait_send())


def gather_scratch(size, rows, width, chunk):
    dma, groups = pltpu.SemaphoreType.DMA, rows // chunk
    return [pltpu.VMEM((size, rows, width), BF)] + [dma((groups, size - 1))] * 4 + [dma((groups,))]


class Scatter:
    def __init__(self, size, groups, chunk, parts, ups, downs, sems):
        self.size, self.groups, self.chunk = size, groups, chunk
        self.parts, self.ups, self.downs = parts, ups, downs
        self.up_send, self.up_recv, self.down_send, self.down_recv = sems
        self.count = (size - 1) * groups
        self.here = lax.axis_index("tensor")

    def rows(self, m):
        return pl.ds(pl.multiple_of(lax.rem(m, self.groups) * self.chunk, self.chunk), self.chunk)

    def up(self, m, first):
        owner = self.size - 1 - lax.div(m, self.groups)
        return pltpu.make_async_remote_copy(
            src_ref=self.parts.at[owner, self.rows(m)] if first else self.ups.at[m],
            dst_ref=self.ups.at[m],
            send_sem=self.up_send.at[m],
            recv_sem=self.up_recv.at[m],
            device_id={"tensor": self.here + 1},
            device_id_type=MESH_ID,
        )

    def down(self, m, first):
        owner = lax.div(m, self.groups)
        return pltpu.make_async_remote_copy(
            src_ref=self.parts.at[owner, self.rows(m)] if first else self.downs.at[m],
            dst_ref=self.downs.at[m],
            send_sem=self.down_send.at[m],
            recv_sem=self.down_recv.at[m],
            device_id={"tensor": self.here - 1},
            device_id_type=MESH_ID,
        )

    def tick(self, k):
        bottom, top = self.here == 0, self.here == self.size - 1
        m = k - self.here
        owner = self.size - 1 - lax.div(m, self.groups)

        @pl.when((m >= 0) & (owner > self.here))
        def _():
            @pl.when(bottom)
            def _():
                self.up(m, True).start()

            @pl.when(jnp.logical_not(bottom))
            def _():
                self.up(m, False).wait_recv()
                self.ups[m] = add_low(self.ups[m], self.parts[owner, self.rows(m), :])
                self.up(m, False).start()

        n = k - (self.size - 1 - self.here)
        below = lax.div(n, self.groups)

        @pl.when((n >= 0) & (below < self.here))
        def _():
            @pl.when(top)
            def _():
                self.down(n, True).start()

            @pl.when(jnp.logical_not(top))
            def _():
                self.down(n, False).wait_recv()
                self.downs[n] = add_low(self.downs[n], self.parts[below, self.rows(n), :])
                self.down(n, False).start()

    def close(self, c, total, then):
        here, part = self.here, self.rows(c)
        m, n = (self.size - 1 - here) * self.groups + c, here * self.groups + c
        total[...] = self.parts[here, part, :].astype(F32)

        @pl.when(here > 0)
        def _():
            self.up(m, False).wait_recv()
            total[...] += self.ups[m].astype(F32)

        @pl.when(here < self.size - 1)
        def _():
            self.down(n, False).wait_recv()
            total[...] += self.downs[n].astype(F32)

        then(part, total[...])

    def close_early(self, k, total, then):
        c = k - (self.count - self.groups + 2)

        @pl.when((c >= 0) & (c < self.groups) & (k < self.count))
        def _():
            self.close(c, total, then)

    def finish(self, ticks, total, then):
        done = min(max(min(ticks, self.count) - (self.count - self.groups + 2), 0), self.groups)

        def last(c, _):
            self.close(c, total, then)
            return 0

        lax.fori_loop(done, self.groups, last, 0)

        def drain(m, _):
            @pl.when(self.size - 1 - lax.div(m, self.groups) > self.here)
            def _():
                self.up(m, False).wait_send()

            @pl.when(lax.div(m, self.groups) < self.here)
            def _():
                self.down(m, False).wait_send()

            return 0

        lax.fori_loop(0, self.count, drain, 0)


def scatter_scratch(size, rows, width, chunk):
    count = (size - 1) * (rows // chunk)
    return [
        pltpu.VMEM((size, rows, width), BF),
        pltpu.VMEM((count, chunk, width), BF),
        pltpu.VMEM((count, chunk, width), BF),
        pltpu.VMEM((chunk, width), F32),
    ] + [pltpu.SemaphoreType.DMA((count,))] * 4


def turn(u, cos_t, sin_t):
    lower, upper = u[: HD // 2], u[HD // 2 :]
    return jnp.concatenate([lower * cos_t - upper * sin_t, upper * cos_t + lower * sin_t], 0)


def flip(a):
    return a.astype(F32).T


def key_blocks(g, chunk, rows, keys, key_rows):
    start = lax.axis_index("context") * rows + g * chunk
    free = jnp.minimum(start + 1, min(LEAST_VALID, keys))
    last = jnp.minimum(start + chunk + PIC - 1, keys)
    return lax.div(free, key_rows), lax.div(last + key_rows - 1, key_rows)


def attend_kernel(
    axes, chunk, key_rows,
    own, own_cot, gain_pair, cos_tab, sin_tab, mask, starts, w_query, w_key_t, w_value_t,
    x_o, normed_o, inv_o, gain_o, q, kv_o, kend, keep_o, cot_o, mixed_o, lse_o,
    xs, up_send, up_recv, down_send, down_recv, own_sem,
    blocks, up_send_c, up_recv_c, down_send_c, down_recv_c, own_sem_c,
    gains, full, normed, full_c, kv, wq, wk, wv, keys_in_rows, acc, mx, sm,
    gain_send, gain_recv, kv_send, kv_recv, w_sem, out_sem, kv_sem, cot_sem,
):
    size, contexts = axes["tensor"], axes["context"]
    here, place = lax.axis_index("tensor"), lax.axis_index("context")
    rows, width = own.shape
    features = size * width
    groups = rows // chunk
    heads, kvs = w_query.shape[1] // HD, w_key_t.shape[0] // HD
    keys, group = contexts * rows, heads // kvs
    units = kvs * groups
    line = Gather(
        size, groups, chunk, own, xs, (up_send, up_recv, down_send, down_recv, own_sem)
    )
    line_c = Gather(
        size, groups, chunk, own_cot, blocks,
        (up_send_c, up_recv_c, down_send_c, down_recv_c, own_sem_c),
    )
    loads = [
        pltpu.make_async_copy(a, b, w_sem.at[i])
        for i, (a, b) in enumerate(((w_query, wq), (w_key_t, wk), (w_value_t, wv)))
    ]
    line.load_all()
    for load in loads:
        load.start()
    gains[here] = jnp.zeros_like(gains[here])
    gains[here, 0:2] = gain_pair[...]
    tensor_peers, context_peers = others("tensor", size), others("context", contexts)
    greet(tensor_peers + context_peers + partner(axes["dp"]))

    def gain_copy(i):
        return pltpu.make_async_remote_copy(
            src_ref=gains.at[here],
            dst_ref=gains.at[here],
            send_sem=gain_send.at[i],
            recv_sem=gain_recv.at[i],
            device_id=tensor_peers[i],
            device_id_type=MESH_ID,
        )

    def kv_copy(g, i):
        part = kv.at[:, :, pl.ds(pl.multiple_of(place * rows + g * chunk, chunk), chunk)]
        return pltpu.make_async_remote_copy(
            src_ref=part,
            dst_ref=part,
            send_sem=kv_send.at[g, i],
            recv_sem=kv_recv.at[g, i],
            device_id=context_peers[i],
            device_id_type=MESH_ID,
        )

    line.begin()
    line_c.load_all()
    for i in range(size - 1):
        gain_copy(i).start()

    length = jnp.sum(mask[...].astype(F32), 1, keepdims=True).astype(jnp.int32)
    position = lax.broadcasted_iota(jnp.int32, (1, rows), 1) + place * rows
    last = position
    for k in range(starts.shape[1]):
        start = starts[:, k : k + 1]
        inside = (position >= start) & (position < start + PIC)
        last = jnp.maximum(last, jnp.where(inside, start + PIC - 1, 0))
    kend[...] = jnp.minimum(last + 1, length)
    down_rows = lax.broadcasted_iota(jnp.int32, (rows, 1), 0) + place * rows
    keep_o[...] = jnp.where(down_rows < length, 1.0, 0.0)

    def save(g):
        part = pl.ds(g * chunk, chunk)
        return [
            pltpu.make_async_copy(full, x_o.at[part], out_sem.at[0]),
            pltpu.make_async_copy(normed, normed_o.at[part], out_sem.at[1]),
        ]

    def project(g):
        part = pl.ds(pl.multiple_of(g * chunk, chunk), chunk)

        @pl.when(g == 0)
        def _():
            for load in loads:
                load.wait()
            for i in range(size - 1):
                gain_copy(i).wait_recv()
            gain_o[...] = jnp.concatenate([gains[j] for j in range(size)], 1)

        @pl.when(g > 0)
        def _():
            for copy in save(g - 1):
                copy.wait()

        full[...] = jnp.concatenate([xs[j, part, :] for j in range(size)], 1)
        stream = full[...].astype(F32)
        inv = lax.rsqrt(jnp.sum(stream * stream, 1, keepdims=True) / features + epsilon)
        inv_o[part, :] = inv
        normed[...] = (stream * inv * gain_o[0:1, :]).astype(BF)
        for copy in save(g):
            copy.start()
        cos_t, sin_t = cos_tab[:, part], sin_tab[:, part]
        mine = pl.ds(pl.multiple_of(place * rows + g * chunk, chunk), chunk)
        key = dot_nt(wk[...], normed[...])
        value = dot_nt(wv[...], normed[...])
        for h in range(kvs):
            kv[h, :, mine] = turn(key[h * HD : (h + 1) * HD], cos_t, sin_t).astype(BF)
            kv[kvs + h, :, mine] = value[h * HD : (h + 1) * HD].astype(BF)
        for i in range(contexts - 1):
            kv_copy(g, i).start()
        query = dot(normed[...], wq[...]).T
        for h in range(heads):
            q[h, :, part] = turn(query[h * HD : (h + 1) * HD], cos_t, sin_t).astype(BF)

    def save_cot(g):
        return pltpu.make_async_copy(full_c, cot_o.at[pl.ds(g * chunk, chunk)], cot_sem)

    def join(g):
        @pl.when(g > 0)
        def _():
            save_cot(g - 1).wait()

        part = pl.ds(pl.multiple_of(g * chunk, chunk), chunk)
        full_c[...] = jnp.concatenate([blocks[j, part, :] for j in range(size)], 1)
        save_cot(g).start()

    save_kv = pltpu.make_async_copy(kv, kv_o, kv_sem)

    def meet():
        for g in range(groups):
            for i in range(contexts - 1):
                kv_copy(g, i).wait_recv()
        save_kv.start()
        for h in range(kvs):
            keys_in_rows[h] = flip(kv[h]).astype(BF)

    def unit(u):
        pair, g = lax.div(u, groups), lax.rem(u, groups)
        part = pl.ds(pl.multiple_of(g * chunk, chunk), chunk)
        free, last = key_blocks(g, chunk, rows, keys, key_rows)
        acc[...] = jnp.zeros_like(acc)
        sm[...] = jnp.zeros_like(sm)
        mx[...] = jnp.full_like(mx, LOWEST)
        limit = kend[:, part]

        def step(masked, i, _):
            at = pl.multiple_of(i * key_rows, key_rows)
            k_blk = keys_in_rows[pair, pl.ds(at, key_rows), :]
            v_blk = kv[kvs + pair, :, pl.ds(at, key_rows)]
            if masked:
                keep = (lax.broadcasted_iota(jnp.int32, (key_rows, chunk), 0) + at) < limit
            for h in range(group):
                s = dot(k_blk, q[pair * group + h, :, part])
                if masked:
                    s = jnp.where(keep, s, LOWEST)
                old = mx[h]
                new = jnp.maximum(old, jnp.max(s, 0, keepdims=True))
                p = jnp.exp2(s * SCALE2 - new * SCALE2)
                alpha = jnp.exp2((old - new) * SCALE2)
                mx[h] = new
                sm[h] = sm[h] * alpha + jnp.sum(p, 0, keepdims=True)
                acc[h] = acc[h] * alpha + dot(v_blk, p.astype(BF))
            return 0

        lax.fori_loop(0, free, functools.partial(step, False), 0)
        lax.fori_loop(free, last, functools.partial(step, True), 0)
        for h in range(group):
            mixed_o[pair * group + h, :, part] = (acc[h] / sm[h]).astype(BF)
            lse_o[pair * group + h, :, part] = mx[h] * SCALE2 + jnp.log2(sm[h])

    turnover = line.ticks - 1

    def tick(k, _):
        @pl.when(k == turnover)
        def _():
            line_c.begin()

        line.tick(k, project)

        @pl.when(k >= turnover)
        def _():
            line_c.tick(k - turnover, join)

        u = k - line.ticks

        @pl.when(u == 0)
        def _():
            meet()

        @pl.when((u >= 0) & (u < units))
        def _():
            unit(u)

        return 0

    lax.fori_loop(0, max(turnover + line_c.ticks, line.ticks + units), tick, 0)
    for copy in [*save(groups - 1), save_cot(groups - 1), save_kv]:
        copy.wait()
    for i in range(size - 1):
        gain_copy(i).wait_send()
    line.drain()
    line_c.drain()
    for g in range(groups):
        for i in range(contexts - 1):
            kv_copy(g, i).wait_send()


def attend_forward(
    axes, own, own_cot, gain_pair, cos_tab, sin_tab, mask, starts, w_query, w_key_t, w_value_t, chunk
):
    size, contexts = axes["tensor"], axes["context"]
    rows, width = own.shape
    features, groups = size * width, rows // chunk
    heads, kvs = w_query.shape[1] // HD, w_key_t.shape[0] // HD
    keys, group = contexts * rows, heads // kvs
    key_rows = min(KEY_ROWS_FWD, keys)
    anywhere, vmem = pl.BlockSpec(memory_space=pl.ANY), pl.BlockSpec(memory_space=pltpu.VMEM)
    shape, dma = jax.ShapeDtypeStruct, pltpu.SemaphoreType.DMA
    return pl.pallas_call(
        functools.partial(attend_kernel, axes, chunk, key_rows),
        in_specs=[anywhere] * 2 + [vmem] * 5 + [anywhere] * 3,
        out_specs=[anywhere] * 2 + [vmem] * 3 + [anywhere] + [vmem] * 2 + [anywhere] + [vmem] * 2,
        out_shape=[
            shape((rows, features), BF),
            shape((rows, features), BF),
            shape((rows, 1), F32),
            shape((8, features), F32),
            shape((heads, HD, rows), BF),
            shape((2 * kvs, HD, keys), BF),
            shape((1, rows), jnp.int32),
            shape((rows, 1), F32),
            shape((rows, features), BF),
            shape((heads, HD, rows), BF),
            shape((heads, 1, rows), F32),
        ],
        scratch_shapes=gather_scratch(size, rows, width, chunk)
        + gather_scratch(size, rows, width, chunk)
        + [
            pltpu.VMEM((size, 8, width), F32),
            pltpu.VMEM((chunk, features), BF),
            pltpu.VMEM((chunk, features), BF),
            pltpu.VMEM((chunk, features), BF),
            pltpu.VMEM((2 * kvs, HD, keys), BF),
            pltpu.VMEM(w_query.shape, BF),
            pltpu.VMEM(w_key_t.shape, BF),
            pltpu.VMEM(w_value_t.shape, BF),
            pltpu.VMEM((kvs, keys, HD), BF),
            pltpu.VMEM((group, HD, chunk), F32),
            pltpu.VMEM((group, 1, chunk), F32),
            pltpu.VMEM((group, 1, chunk), F32),
            dma((size - 1,)),
            dma((size - 1,)),
            dma((groups, max(contexts - 1, 1))),
            dma((groups, max(contexts - 1, 1))),
            dma((3,)),
            dma((2,)),
            dma,
            dma,
        ],
        compiler_params=pltpu.CompilerParams(
            collective_id=3, has_side_effects=True, vmem_limit_bytes=VMEM_LIMIT
        ),
        cost_estimate=pl.CostEstimate(
            flops=2 * rows * features * (heads + 2 * kvs) * HD + 10 * heads * rows * keys * HD,
            bytes_accessed=40 << 20,
            transcendentals=heads * rows * keys,
        ),
        name="attend_forward",
    )(own, own_cot, gain_pair, cos_tab, sin_tab, mask, starts, w_query, w_key_t, w_value_t)


def attend_back_kernel(
    axes, chunk, key_rows,
    ffn, q, kv, kend, do, o, lse, cos_tab, sin_tab, middle, grad_attn, normed,
    grads_o, layer_o, square_o, weights_o,
    parts, ups, downs, total, up_send, up_recv, down_send, down_recv,
    keys_in_rows, values_in_rows, dq, dk, dv, ds_all, p_all, q_all, do_all, mine, out_kv, in_kv,
    grads_in, normed_in, tiles,
    kv_send, kv_recv, part_sem, tile_sem,
):
    size, contexts = axes["tensor"], axes["context"]
    heads, _, rows = q.shape
    kvs, keys = kv.shape[0] // 2, kv.shape[2]
    groups, group = rows // chunk, heads // kvs
    units = kvs * groups
    place = lax.axis_index("context")
    line = Scatter(
        size, groups, chunk, parts, ups, downs, (up_send, up_recv, down_send, down_recv)
    )
    loads = [
        pltpu.make_async_copy(a, b, part_sem.at[i])
        for i, (a, b) in enumerate(((ffn, parts), (grad_attn, grads_in), (normed, normed_in)))
    ]
    for load in loads:
        load.start()
    square_o[...] = jnp.zeros_like(square_o)
    peers = others("context", contexts)
    greet(others("tensor", size) + peers + partner(axes["dp"]))
    loads[0].wait()

    def half(of):
        at = pl.ds(pl.multiple_of(of * rows, rows), rows)
        return dk[at, :].T, dv[at, :].T

    def kv_copy(pair, i):
        return pltpu.make_async_remote_copy(
            src_ref=out_kv.at[pair, i],
            dst_ref=in_kv.at[pair, i],
            send_sem=kv_send.at[pair, i],
            recv_sem=kv_recv.at[pair, i],
            device_id=peers[i],
            device_id_type=MESH_ID,
        )

    def unit(u):
        pair, g = lax.div(u, groups), lax.rem(u, groups)
        part = pl.ds(pl.multiple_of(g * chunk, chunk), chunk)
        free, last = key_blocks(g, chunk, rows, keys, key_rows)
        limit = kend[:, part]

        @pl.when(g == 0)
        def _():
            dk[...] = jnp.zeros_like(dk)
            dv[...] = jnp.zeros_like(dv)

        dq[...] = jnp.zeros_like(dq)
        delta = []
        for h in range(group):
            head = pair * group + h
            cols = slice(h * chunk, (h + 1) * chunk)
            q_all[:, cols] = q[head, :, part]
            do_all[:, cols] = do[head, :, part]
            delta.append(
                jnp.sum(do_all[:, cols].astype(F32) * o[head, :, part].astype(F32), 0, keepdims=True)
            )

        def step(masked, i, _):
            at = pl.multiple_of(i * key_rows, key_rows)
            k_blk = keys_in_rows[pair, pl.ds(at, key_rows), :]
            v_blk = values_in_rows[pair, pl.ds(at, key_rows), :]
            kt_blk = kv[pair, :, pl.ds(at, key_rows)]
            if masked:
                keep = (lax.broadcasted_iota(jnp.int32, (key_rows, chunk), 0) + at) < limit
            for h in range(group):
                cols = slice(h * chunk, (h + 1) * chunk)
                s = dot(k_blk, q_all[:, cols])
                p = jnp.exp2(s * SCALE2 - lse[pair * group + h, :, part])
                if masked:
                    p = jnp.where(keep, p, 0.0)
                dp = dot(v_blk, do_all[:, cols])
                ds = (p * (dp - delta[h])).astype(BF)
                p_all[:, cols] = p.astype(BF)
                ds_all[:, cols] = ds
                dq[h] += dot(kt_blk, ds)
            dk[pl.ds(at, key_rows), :] += dot_nt(ds_all[...], q_all[...])
            dv[pl.ds(at, key_rows), :] += dot_nt(p_all[...], do_all[...])
            return 0

        lax.fori_loop(0, free, functools.partial(step, False), 0)
        lax.fori_loop(free, last, functools.partial(step, True), 0)
        for h in range(group):
            grads_o[pair * group + h, :, part] = turn(
                dq[h] * SCALE, cos_tab[:, part], -sin_tab[:, part]
            ).astype(BF)

        @pl.when(g == groups - 1)
        def _():
            for i in range(contexts - 1):
                key, value = half(peers[i]["context"])
                out_kv[pair, i, 0] = key.astype(BF)
                out_kv[pair, i, 1] = value.astype(BF)
                kv_copy(pair, i).start()
            mine[pair, 0], mine[pair, 1] = half(place)

    def join():
        for pair in range(kvs):
            key, value = mine[pair, 0], mine[pair, 1]
            for i in range(contexts - 1):
                kv_copy(pair, i).wait()
                key = key + in_kv[pair, i, 0].astype(F32)
                value = value + in_kv[pair, i, 1].astype(F32)
            grads_o[heads + pair] = turn(key * SCALE, cos_tab[...], -sin_tab[...]).astype(BF)
            grads_o[heads + kvs + pair] = value.astype(BF)

    features = normed.shape[1]
    tile = tile_of(features, 256)
    tile_count, each = features // tile, 4

    def save_tile(j):
        slot = lax.rem(j, 2)
        return pltpu.make_async_copy(
            tiles.at[slot], weights_o.at[pl.ds(j * tile, tile)], tile_sem.at[slot]
        )

    def weight_tile(j):
        slot = lax.rem(j, 2)

        @pl.when(j >= 2)
        def _():
            save_tile(j - 2).wait()

        cols = pl.ds(pl.multiple_of(j * tile, tile), tile)
        out = dot_nt(flip(grads_in[:, cols]).astype(BF), o[...].reshape(heads * HD, rows))
        into = dot_nt(
            flip(normed_in[:, cols]).astype(BF), grads_o[...].reshape((heads + 2 * kvs) * HD, rows)
        )
        tiles[slot] = jnp.concatenate([out, into], 1).astype(BF)
        save_tile(j).start()

    def then(part, ffn_out):
        square_o[...] += jnp.sum(ffn_out * ffn_out, 0, keepdims=True)
        layer_o[part, :] = (middle[part, :] + ffn_out).astype(BF)

    def tick(k, _):
        line.tick(k)

        @pl.when(k == 0)
        def _():
            for h in range(kvs):
                keys_in_rows[h] = flip(kv[h]).astype(BF)
                values_in_rows[h] = flip(kv[kvs + h]).astype(BF)

        @pl.when(k < units)
        def _():
            unit(k)

        @pl.when(k == units)
        def _():
            join()
            for load in loads[1:]:
                load.wait()

        first = (k - units - 1) * each
        for j in range(each):

            @pl.when((first >= 0) & (first + j < tile_count))
            def _():
                weight_tile(first + j)

        line.close_early(k, total, then)
        return 0

    ticks = max(line.count, units + 1 + -(-tile_count // each))
    lax.fori_loop(0, ticks, tick, 0)

    line.finish(ticks, total, then)
    for j in range(max(tile_count - 2, 0), tile_count):
        save_tile(j).wait()


def attend_backward(
    axes, ffn, q, kv, kend, do, o, lse, cos_tab, sin_tab, middle, grad_attn, normed, chunk, after
):
    size, contexts = axes["tensor"], axes["context"]
    heads, _, rows = q.shape
    kvs, keys = kv.shape[0] // 2, kv.shape[2]
    group, width = heads // kvs, ffn.shape[2]
    key_rows = min(KEY_ROWS_BWD, keys)
    anywhere, vmem = pl.BlockSpec(memory_space=pl.ANY), pl.BlockSpec(memory_space=pltpu.VMEM)
    shape, dma = jax.ShapeDtypeStruct, pltpu.SemaphoreType.DMA
    slots = max(contexts - 1, 1)

    def kernel(*refs):
        attend_back_kernel(axes, chunk, key_rows, *refs[:12], *refs[12 + len(after) :])

    return pl.pallas_call(
        kernel,
        in_specs=[anywhere] + [vmem] * 9 + [anywhere] * (2 + len(after)),
        out_specs=[vmem] * 3 + [anywhere],
        out_shape=[
            shape((heads + 2 * kvs, HD, rows), BF),
            shape((rows, width), BF),
            shape((1, width), F32),
            shape((size * width, (2 * heads + 2 * kvs) * HD), BF),
        ],
        scratch_shapes=scatter_scratch(size, rows, width, chunk)
        + [
            pltpu.VMEM((kvs, keys, HD), BF),
            pltpu.VMEM((kvs, keys, HD), BF),
            pltpu.VMEM((group, HD, chunk), F32),
            pltpu.VMEM((keys, HD), F32),
            pltpu.VMEM((keys, HD), F32),
            pltpu.VMEM((key_rows, group * chunk), BF),
            pltpu.VMEM((key_rows, group * chunk), BF),
            pltpu.VMEM((HD, group * chunk), BF),
            pltpu.VMEM((HD, group * chunk), BF),
            pltpu.VMEM((kvs, 2, HD, rows), F32),
            pltpu.VMEM((kvs, slots, 2, HD, rows), BF),
            pltpu.VMEM((kvs, slots, 2, HD, rows), BF),
            pltpu.VMEM(grad_attn.shape, BF),
            pltpu.VMEM(normed.shape, BF),
            pltpu.VMEM((2, tile_of(size * width, 256), (2 * heads + 2 * kvs) * HD), BF),
            dma((kvs, slots)),
            dma((kvs, slots)),
            dma((3,)),
            dma((2,)),
        ],
        compiler_params=pltpu.CompilerParams(
            collective_id=6, has_side_effects=True, vmem_limit_bytes=VMEM_LIMIT
        ),
        cost_estimate=pl.CostEstimate(
            flops=16 * heads * rows * keys * HD,
            bytes_accessed=16 << 20,
            transcendentals=heads * rows * keys,
        ),
        name="attend_backward",
    )(ffn, q, kv, kend, do, o, lse, cos_tab, sin_tab, middle, grad_attn, normed, *after)


def input_kernel(
    axes, chunk,
    grads, inv, gain, keep, attn_square, gain_rows, ffn_square, gain_own, x_own, grad_own,
    w_query, w_key_t, w_value_t, x,
    out_o, sum_o,
    parts, ups, downs, total, up_send, up_recv, down_send, down_recv,
    xs, whole, wq, wk, wv, dots, dot_sum, cols, cols_in, world, square,
    dot_send, dot_recv, col_send, col_recv, world_send, world_recv, w_sem, x_sem,
):
    size = axes["tensor"]
    here = lax.axis_index("tensor")
    rows, features = x.shape
    width, groups = features // size, rows // chunk
    nq, nk = w_query.shape[1], w_key_t.shape[0]
    line = Scatter(
        size, groups, chunk, parts, ups, downs, (up_send, up_recv, down_send, down_recv)
    )
    loads = [
        pltpu.make_async_copy(a, b, w_sem.at[i])
        for i, (a, b) in enumerate(((w_query, wq), (w_key_t, wk), (w_value_t, wv)))
    ]

    def load_x(c):
        slot = lax.rem(c, 2)
        return pltpu.make_async_copy(x.at[pl.ds(c * chunk, chunk)], xs.at[slot], x_sem.at[slot])

    for load in loads:
        load.start()
    load_x(0).start()
    contexts, replicas = axes["context"], axes["dp"] * axes["context"]
    spot = lax.axis_index("dp") * contexts + lax.axis_index("context")
    peers = others("tensor", size)
    far = [lax.rem(spot + i, replicas) for i in range(1, replicas)]
    far = [{"dp": lax.div(i, contexts), "context": lax.rem(i, contexts)} for i in far]
    greet(peers + far)
    for load in loads:
        load.wait()
    square[...] = jnp.zeros_like(square)
    row = lax.broadcasted_iota(jnp.int32, (8, width), 0)
    lane = lax.broadcasted_iota(jnp.int32, (8, width), 1)

    def compute(c):
        slot = lax.rem(c, 2)
        part = pl.ds(pl.multiple_of(c * chunk, chunk), chunk)
        load_x(c).wait()

        @pl.when(c + 1 < groups)
        def _():
            load_x(c + 1).start()

        g = flip(grads[:, part]).astype(BF)
        whole[...] = (
            dot_nt(g[:, :nq], wq[...])
            + dot(g[:, nq : nq + nk], wk[...])
            + dot(g[:, nq + nk :], wv[...])
        )
        for j in range(size):
            parts[j, part, :] = whole[:, j * width : (j + 1) * width].astype(BF)

    def add_up(c):
        slot = lax.rem(c, 2)
        part = pl.ds(pl.multiple_of(c * chunk, chunk), chunk)
        stream = xs[slot].astype(F32)
        square[...] += jnp.sum(stream * stream * keep[part, :], 0, keepdims=True)
        moved = whole[...] * (stream * inv[part, :])
        rowsum = jnp.sum(moved * gain[0:1, :], 1, keepdims=True)
        dots[here, :, part] = jnp.broadcast_to(rowsum, (chunk, 128)).T[:8]
        colsum = jnp.sum(moved, 0, keepdims=True)
        for j in range(size):
            piece = jnp.where(row == 0, colsum[:, j * width : (j + 1) * width], 0.0)

            @pl.when(c == 0)
            def _():
                cols[j] = piece

            @pl.when(c > 0)
            def _():
                cols[j] += piece

    def copy_to(src, dst, send, recv, peer):
        return pltpu.make_async_remote_copy(
            src_ref=src,
            dst_ref=dst,
            send_sem=send,
            recv_sem=recv,
            device_id=peer,
            device_id_type=MESH_ID,
        )

    def dot_copy(i):
        mine = dots.at[here]
        return copy_to(mine, mine, dot_send.at[i], dot_recv.at[i], peers[i])

    def col_copy(i):
        src = cols.at[peers[i]["tensor"]]
        return copy_to(src, cols_in.at[here], col_send.at[i], col_recv.at[i], peers[i])

    def world_copy(i):
        mine = world.at[spot]
        return copy_to(mine, mine, world_send.at[i], world_recv.at[i], far[i])

    def exchange():
        numbers = jnp.zeros((8, width), F32)
        for i, a in enumerate((square[...], attn_square[...], ffn_square[...], keep[...])):
            a = jnp.sum(jnp.sum(a, 0, keepdims=True), 1, keepdims=True)
            share = 1.0 if i == 2 else 1.0 / size
            numbers += jnp.where((row == 1) & (lane == i), a * share, 0.0)
        for j in range(size):
            cols[j] += numbers
        cols_in[here] = cols[here]
        for i in range(size - 1):
            dot_copy(i).start()
            col_copy(i).start()

    def spread():
        for i in range(size - 1):
            dot_copy(i).wait()
            col_copy(i).wait()
        dot_total, column = dots[0], cols_in[0]
        for j in range(1, size):
            dot_total = dot_total + dots[j]
            column = column + cols_in[j]
        dot_sum[...] = dot_total
        world[spot] = column

        def put(piece):
            world[spot, 2:3] = piece

        own_columns(size, gain_rows[...], put)
        for i in range(replicas - 1):
            world_copy(i).start()

    def then(part, grad):
        through = grad * gain_own[...] - x_own[part, :].astype(F32) * inv[part, :] * (
            dot_sum[:, part].T[:, :1] / features
        )
        out_o[part, :] = (grad_own[part, :] + inv[part, :] * through).astype(BF)

    def tick(k, _):
        @pl.when(k < groups)
        def _():
            compute(k)

        line.tick(k)

        @pl.when(k < groups)
        def _():
            add_up(k)

        @pl.when(k == groups)
        def _():
            exchange()

        @pl.when(k == groups + 3)
        def _():
            spread()

        line.close_early(k, total, then)
        return 0

    ticks = max(line.count, groups + 4)
    lax.fori_loop(0, ticks, tick, 0)

    line.finish(ticks, total, then)
    for i in range(replicas - 1):
        world_copy(i).wait()
    everything = world[0]
    for j in range(1, replicas):
        everything = everything + world[j]
    sum_o[...] = everything


def input_gradient(
    axes, grads, inv, gain, keep, attn_square, gain_rows, ffn_square, gain_own, x_own, grad_own,
    w_query, w_key_t, w_value_t, x, chunk, after,
):
    size, replicas = axes["tensor"], axes["dp"] * axes["context"]
    rows, features = x.shape
    width = features // size
    anywhere, vmem = pl.BlockSpec(memory_space=pl.ANY), pl.BlockSpec(memory_space=pltpu.VMEM)
    shape, dma = jax.ShapeDtypeStruct, pltpu.SemaphoreType.DMA

    def kernel(*refs):
        input_kernel(axes, chunk, *refs[:14], *refs[14 + len(after) :])

    return pl.pallas_call(
        kernel,
        in_specs=[vmem] * 10 + [anywhere] * (4 + len(after)),
        out_specs=[vmem] * 2,
        out_shape=[
            shape((rows, width), BF),
            shape((8, width), F32),
        ],
        scratch_shapes=scatter_scratch(size, rows, width, chunk)
        + [
            pltpu.VMEM((2, chunk, features), BF),
            pltpu.VMEM((chunk, features), F32),
            pltpu.VMEM(w_query.shape, BF),
            pltpu.VMEM(w_key_t.shape, BF),
            pltpu.VMEM(w_value_t.shape, BF),
            pltpu.VMEM((size, 8, rows), F32),
            pltpu.VMEM((8, rows), F32),
            pltpu.VMEM((size, 8, width), F32),
            pltpu.VMEM((size, 8, width), F32),
            pltpu.VMEM((replicas, 8, width), F32),
            pltpu.VMEM((1, features), F32),
            dma((size - 1,)),
            dma((size - 1,)),
            dma((size - 1,)),
            dma((size - 1,)),
            dma((replicas - 1,)),
            dma((replicas - 1,)),
            dma((3,)),
            dma((2,)),
        ],
        compiler_params=pltpu.CompilerParams(
            collective_id=4, has_side_effects=True, vmem_limit_bytes=VMEM_LIMIT
        ),
        cost_estimate=pl.CostEstimate(
            flops=2 * rows * features * grads.shape[0],
            bytes_accessed=20 << 20,
            transcendentals=rows,
        ),
        name="input_gradient",
    )(
        grads, inv, gain, keep, attn_square, gain_rows, ffn_square, gain_own, x_own, grad_own,
        w_query, w_key_t, w_value_t, x, *after,
    )


def local(
    axes,
    layer_input_hidden,
    cotangent,
    valid_mask,
    span_starts,
    gain_attn,
    w_query,
    w_key,
    w_value,
    w_out,
    gain_mlp,
    w_gate,
    w_up,
    w_down,
):
    _, rows, width = layer_input_hidden.shape
    size = axes["tensor"]
    features = width * size
    kvs = w_key.shape[1] // HD
    heads = w_query.shape[1] // HD
    position = lax.axis_index("context") * rows + jnp.arange(rows, dtype=jnp.int32)
    inverse_freq = rope_base ** (-2.0 * jnp.arange(HD // 2, dtype=F32) / HD)
    angles = inverse_freq[:, None] * position.astype(F32)[None, :]
    cos_tab, sin_tab = jnp.cos(angles), jnp.sin(angles)
    x_own = layer_input_hidden[0]
    w_key_t, w_value_t = w_key.T, w_value.T

    def shard(grad):
        return lax.psum_scatter(grad, ("dp", "context"), scatter_dimension=0, tiled=True)

    (
        x_low,
        normed_a,
        inv_a,
        gains,
        query_t,
        both,
        kend,
        keep,
        cot,
        mixed,
        lse,
    ) = attend_forward(
        axes,
        x_own,
        cotangent[0],
        jnp.stack([gain_attn, gain_mlp]),
        cos_tab,
        sin_tab,
        valid_mask,
        span_starts,
        w_query,
        w_key_t,
        w_value_t,
        GROUP_ROWS,
    )
    normed_m, act, ggu, down_part, back_part, middle, middle_own, attn_square = feed_forward(
        axes,
        mixed.reshape(heads * HD, rows),
        keep,
        gains,
        w_out,
        w_gate,
        w_up,
        w_down,
        x_low,
        cot,
        GROUP_ROWS,
        HOP_ROWS,
    )
    grad_ggu = ein("sd,sf->df", normed_m, ggu).astype(BF)
    ggu_sum = shard(grad_ggu)

    grad_own, grad_attn, grad_mixed, gain_m_rows, grad_down = norm_back(
        axes, back_part, keep, gains, w_out, middle, cot, act, GROUP_ROWS, HOP_ROWS, (grad_ggu,)
    )
    down_sum = shard(grad_down)
    grads, layer_out, ffn_square, grad_rest = attend_backward(
        axes,
        down_part,
        query_t,
        both,
        kend,
        grad_mixed.reshape(heads, HD, rows),
        mixed,
        lse,
        cos_tab,
        sin_tab,
        middle_own,
        grad_attn,
        normed_a,
        GROUP_ROWS,
        (ggu_sum,),
    )
    rest_sum = shard(grad_rest)

    input_grad, sums = input_gradient(
        axes,
        grads.reshape(-1, rows),
        inv_a,
        gains,
        keep,
        attn_square,
        gain_m_rows,
        ffn_square,
        gain_attn[None],
        x_own,
        grad_own,
        w_query,
        w_key_t,
        w_value_t,
        x_low,
        GROUP_ROWS,
        (grad_rest, down_sum),
    )
    rest_sum = jnp.where(sums[1, 3] >= 0.0, rest_sum.astype(F32), 0.0)
    gate_sum, up_sum = jnp.split(ggu_sum.astype(F32), 2, 1)
    down_sum = down_sum.astype(F32).T
    cut = [heads * HD, 2 * heads * HD, (2 * heads + kvs) * HD]
    out_sum, query_sum, key_sum, value_sum = jnp.split(rest_sum, cut, 1)
    rms = jnp.sqrt(sums[1, :3] / (sums[1, 3] * features))
    return (
        layer_out[None],
        input_grad[None],
        sums[0],
        query_sum,
        key_sum,
        value_sum,
        out_sum.T,
        sums[2],
        gate_sum,
        up_sum,
        down_sum,
        rms[0],
        rms[1],
        rms[2],
    )


def solution(mesh):
    token = P("dp", "context", "tensor")
    by_rows = P(("dp", "context"), "tensor")
    by_columns = P("tensor", ("dp", "context"))
    cols, rows, vec = P(None, "tensor"), P("tensor", None), P("tensor")
    return jax.shard_map(
        functools.partial(local, dict(mesh.shape)),
        mesh=mesh,
        in_specs=(
            token,
            token,
            P("dp", None),
            P("dp", None),
            vec,
            cols,
            cols,
            cols,
            rows,
            vec,
            cols,
            cols,
            rows,
        ),
        out_specs=(
            token,
            token,
            vec,
            by_rows,
            by_rows,
            by_rows,
            by_columns,
            vec,
            by_rows,
            by_rows,
            by_columns,
            P(),
            P(),
            P(),
        ),
        check_vma=False,
    )
```

```python
import functools
import math

import jax
import jax.numpy as jnp
from jax import lax
from jax.experimental import pallas as pl
from jax.experimental.pallas import tpu as pltpu
from jax.sharding import PartitionSpec as P

HD = 80
PIC = 256
LEAST_VALID = 1536
F32 = jnp.float32
BF = jnp.bfloat16
SCALE = HD**-0.5
SCALE2 = SCALE * math.log2(math.e)
LOWEST = -1e30
GROUP_ROWS = 256
HOP_ROWS = 64
VMEM_LIMIT = 60 << 20
KEY_ROWS_FWD = 512
KEY_ROWS_BWD = 512

epsilon = 1e-05
rope_base = 1000000.0


def dot(a, b):
    return jnp.dot(a, b, preferred_element_type=F32)


def dot_nt(a, b):
    return lax.dot_general(a, b, (((1,), (1,)), ((), ())), preferred_element_type=F32)


def ein(spec, a, b):
    return jnp.einsum(spec, a, b, preferred_element_type=F32)


MESH_ID = pl.DeviceIdType.MESH
SENT = 4


def ring_of(size):
    return size + 4


def add_low(a, b):
    return (a.astype(F32) + b.astype(F32)).astype(BF)


class Sums:
    def __init__(self, size, count, part, low, high, sent, sems):
        self.size, self.count, self.part = size, count, part
        self.low, self.high, self.sent = low, high, sent
        self.low_send, self.low_recv, self.high_send, self.high_recv = sems
        self.here = lax.axis_index("tensor")

    def barrier(self):
        here, size = self.here, self.size
        barrier = pltpu.get_barrier_semaphore()

        @pl.when(here > 0)
        def _():
            pl.semaphore_signal(
                barrier, inc=1, device_id={"tensor": here - 1}, device_id_type=MESH_ID
            )

        @pl.when(here < size - 1)
        def _():
            pl.semaphore_signal(
                barrier, inc=1, device_id={"tensor": here + 1}, device_id_type=MESH_ID
            )

        @pl.when((here > 0) & (here < size - 1))
        def _():
            pl.semaphore_wait(barrier, 2)

        @pl.when((here == 0) | (here == size - 1))
        def _():
            pl.semaphore_wait(barrier, 1)

    def up(self, c):
        slot = lax.rem(c, ring_of(self.size))
        return pltpu.make_async_remote_copy(
            src_ref=self.low.at[slot],
            dst_ref=self.low.at[slot],
            send_sem=self.low_send.at[slot],
            recv_sem=self.low_recv.at[slot],
            device_id={"tensor": self.here + 1},
            device_id_type=MESH_ID,
        )

    def down(self, c):
        slot, mine = lax.rem(c, ring_of(self.size)), lax.rem(c, SENT)
        return pltpu.make_async_remote_copy(
            src_ref=self.sent.at[mine],
            dst_ref=self.high.at[slot],
            send_sem=self.high_send.at[mine],
            recv_sem=self.high_recv.at[slot],
            device_id={"tensor": self.here - 1},
            device_id_type=MESH_ID,
        )

    def tick(self, k):
        here, size, count = self.here, self.size, self.count
        bottom, top = here == 0, here == size - 1
        c = k - here

        @pl.when((c >= 0) & (c < count))
        def _():
            slot = lax.rem(c, ring_of(self.size))

            @pl.when(bottom)
            def _():
                self.low[slot] = self.part(c)

            @pl.when(jnp.logical_not(bottom))
            def _():
                self.up(c).wait_recv()
                self.low[slot] = add_low(self.low[slot], self.part(c))

            @pl.when(jnp.logical_not(top))
            def _():
                self.up(c).start()

        d = k - (size - 1 - here)

        @pl.when((d >= 0) & (d < count))
        def _():
            slot, mine = lax.rem(d, ring_of(self.size)), lax.rem(d, SENT)

            @pl.when(top)
            def _():
                self.sent[mine] = self.part(d)

            @pl.when(jnp.logical_not(top))
            def _():
                self.down(d).wait_recv()

                @pl.when(jnp.logical_not(bottom))
                def _():
                    self.sent[mine] = add_low(self.high[slot], self.part(d))

            @pl.when(jnp.logical_not(bottom))
            def _():
                self.down(d).start()

        @pl.when((c >= 2) & (c < count + 2) & jnp.logical_not(top))
        def _():
            self.up(c - 2).wait_send()

        @pl.when((d >= 2) & (d < count + 2) & jnp.logical_not(bottom))
        def _():
            self.down(d - 2).wait_send()

    def total(self, c):
        slot = lax.rem(c, ring_of(self.size))
        high = jnp.where(self.here == self.size - 1, 0.0, self.high[slot].astype(F32))
        return self.low[slot].astype(F32) + high


def sum_scratch(size, hop, features):
    ring, dma = ring_of(size), pltpu.SemaphoreType.DMA
    return [
        pltpu.VMEM((ring, hop, features), BF),
        pltpu.VMEM((ring, hop, features), BF),
        pltpu.VMEM((SENT, hop, features), BF),
        dma((ring,)),
        dma((ring,)),
        dma((SENT,)),
        dma((ring,)),
    ]


def own_columns(size, a, then):
    width = a.shape[1] // size
    for j in range(size):

        @pl.when(lax.axis_index("tensor") == j)
        def _():
            then(a[:, j * width : (j + 1) * width])


def tile_of(n, most):
    for tile in range(most, 0, -128):
        if n % tile == 0:
            return tile
    return n


def ffn_kernel(
    size, hop, chunk,
    mixed, keep, gain, w_out, w_gate, w_up, w_down, x, cot,
    normed_o, act_o, ggu_o, ffn_o, back_o, middle_o, own_o, square_o,
    low, high, sent, low_send, low_recv, high_send, high_recv,
    wo, wg, wu, wd, parts, normed, xs, cots, mids, owns, act, ggu, ffn, back, split,
    w_sem, x_sem, cot_sem, normed_sem, mid_sem, own_sem, act_sem, ffn_sem,
):
    rows, features = x.shape
    hidden = w_gate.shape[1]
    count, per, groups = rows // hop, chunk // hop, rows // chunk
    tile_f, tile_d = tile_of(hidden, 256), tile_of(features, 256)
    tiles_f, tiles_d = hidden // tile_f, features // tile_d
    half_f, half_d = -(-tiles_f // 2), -(-tiles_d // 2)
    lag = size - 1 + per - 1
    ahead, part_slots = per // 2, parts.shape[0]
    ticks = max(per * groups + lag, count + size)

    def part(c):
        slot = lax.rem(lax.div(c, per), part_slots)
        return parts[slot, pl.ds(pl.multiple_of(lax.rem(c, per) * hop, hop), hop), :]

    sums = Sums(size, count, part, low, high, sent, (low_send, low_recv, high_send, high_recv))
    loads = [
        pltpu.make_async_copy(a, b, w_sem.at[i])
        for i, (a, b) in enumerate(((w_out, wo), (w_gate, wg), (w_up, wu), (w_down, wd)))
    ]
    for load in loads:
        load.start()

    def load_x(c):
        slot = lax.rem(c, 2)
        return pltpu.make_async_copy(x.at[pl.ds(c * hop, hop)], xs.at[slot], x_sem.at[slot])

    def load_cot(g):
        return pltpu.make_async_copy(cot.at[pl.ds(g * chunk, chunk)], cots, cot_sem)

    def save_normed(c):
        at, q = lax.rem(lax.div(c, per), 2), lax.rem(c, per)
        return pltpu.make_async_copy(
            normed.at[at, pl.ds(q * hop, hop)], normed_o.at[pl.ds(c * hop, hop)], normed_sem.at[at, q]
        )

    def save_mid(c):
        slot = lax.rem(c, 2)
        return pltpu.make_async_copy(mids.at[slot], middle_o.at[pl.ds(c * hop, hop)], mid_sem.at[slot])

    def save_own(c):
        slot = lax.rem(c, 2)
        return pltpu.make_async_copy(owns.at[slot], own_o.at[pl.ds(c * hop, hop)], own_sem.at[slot])

    def save_act(g):
        return [
            pltpu.make_async_copy(a, b.at[pl.ds(g * chunk, chunk)], act_sem.at[i])
            for i, (a, b) in enumerate(((act, act_o), (ggu, ggu_o)))
        ]

    def save_ffn(g):
        part = pl.ds(g * chunk, chunk)
        return [
            pltpu.make_async_copy(split, ffn_o.at[:, part], ffn_sem.at[0]),
            pltpu.make_async_copy(back, back_o.at[part], ffn_sem.at[1]),
        ]

    def project(g):
        at = lax.rem(g, part_slots)
        lhs = mixed[:, pl.ds(pl.multiple_of(g * chunk, chunk), chunk)]

        def one(j, _):
            cols = pl.ds(pl.multiple_of(j * tile_d, tile_d), tile_d)
            parts[at, :, cols] = lax.dot_general(
                lhs, wo[:, cols], (((0,), (0,)), ((), ())), preferred_element_type=F32
            ).astype(BF)
            return 0

        lax.fori_loop(0, tiles_d, one, 0)

    load_x(0).start()
    load_cot(0).start()
    square_o[...] = jnp.zeros_like(square_o)
    loads[0].wait()
    project(0)
    sums.barrier()

    def finish(c):
        slot = lax.rem(c, 2)
        load_x(c).wait()

        @pl.when(c + 1 < count)
        def _():
            load_x(c + 1).start()

        @pl.when(c >= 2)
        def _():
            save_mid(c - 2).wait()
            save_own(c - 2).wait()

        @pl.when(c >= 2 * per)
        def _():
            save_normed(c - 2 * per).wait()

        kept = keep[pl.ds(pl.multiple_of(c * hop, hop), hop), :]

        out = kept * sums.total(c)
        square_o[...] += jnp.sum(out * out, 0, keepdims=True)
        mids[slot] = xs[slot].astype(F32) + out
        mid = mids[slot]
        own_columns(size, mid, lambda piece: owns.__setitem__(slot, piece))
        save_own(c).start()
        inv = lax.rsqrt(jnp.sum(mid * mid, 1, keepdims=True) / features + epsilon)
        at = lax.rem(lax.div(c, per), 2)
        normed[at, pl.ds(pl.multiple_of(lax.rem(c, per) * hop, hop), hop), :] = (
            mid * inv * gain[1:2, :]
        ).astype(BF)
        save_mid(c).start()
        save_normed(c).start()

    def inner(g, lo, hi):
        at = lax.rem(g, 2)
        kept = keep[pl.ds(pl.multiple_of(g * chunk, chunk), chunk), :]

        def one(j, _):
            cols = pl.ds(pl.multiple_of(j * tile_f, tile_f), tile_f)
            gate = dot(normed[at], wg[:, cols])
            up = dot(normed[at], wu[:, cols])
            grad = dot_nt(cots[...], wd[cols, :]) * kept
            sig = jax.nn.sigmoid(gate)
            silu = gate * sig
            act[:, cols] = (silu * up * kept).astype(BF)
            ggu[:, cols] = (grad * up * (sig + silu * (1.0 - sig))).astype(BF)
            cols = pl.ds(pl.multiple_of(hidden + j * tile_f, tile_f), tile_f)
            ggu[:, cols] = (grad * silu).astype(BF)
            return 0

        lax.fori_loop(lo, hi, one, 0)

    def outer(g, lo, hi):
        def one(j, _):
            cols = pl.ds(pl.multiple_of(j * tile_d, tile_d), tile_d)
            ffn[:, cols] = dot(act[...], wd[:, cols]).astype(BF)
            back[:, cols] = (
                dot_nt(ggu[:, :hidden], wg[cols, :]) + dot_nt(ggu[:, hidden:], wu[cols, :])
            ).astype(BF)
            return 0

        lax.fori_loop(lo, hi, one, 0)

    def tick(k, _):
        sums.tick(k)
        c = k - (size - 1)

        @pl.when((c >= 0) & (c < count))
        def _():
            finish(c)

        later = k + ahead

        @pl.when((lax.rem(later, per) == 0) & (later < count))
        def _():
            project(lax.div(later, per))

        s = k - lag
        g, stage = lax.div(s, per), lax.rem(s, per)
        going = (s >= 0) & (g < groups)

        first, second, third, fourth = (stage == i * per // 4 for i in range(4))

        @pl.when(going & first)
        def _():
            @pl.when(g == 0)
            def _():
                for load in loads[1:]:
                    load.wait()

            load_cot(g).wait()

            @pl.when(g > 0)
            def _():
                for copy in save_act(g - 1):
                    copy.wait()

        @pl.when(going & (first | second))
        def _():
            inner(g, jnp.where(first, 0, half_f), jnp.where(first, half_f, tiles_f))

        @pl.when(going & second)
        def _():
            for copy in save_act(g):
                copy.start()

            @pl.when(g + 1 < groups)
            def _():
                load_cot(g + 1).start()

        @pl.when(going & third & (g > 0))
        def _():
            for copy in save_ffn(g - 1):
                copy.wait()

        @pl.when(going & (third | fourth))
        def _():
            outer(g, jnp.where(third, 0, half_d), jnp.where(third, half_d, tiles_d))

        @pl.when(going & fourth)
        def _():
            for j in range(size):
                split[j] = ffn[:, j * (features // size) : (j + 1) * (features // size)]
            for copy in save_ffn(g):
                copy.start()

        return 0

    lax.fori_loop(0, ticks, tick, 0)
    for copy in save_act(groups - 1) + save_ffn(groups - 1):
        copy.wait()
    for c in range(count - 2, count):
        save_mid(c).wait()
        save_own(c).wait()
    for c in range(count - 2 * per, count):
        save_normed(c).wait()


def feed_forward(size, mixed, keep, gain, w_out, w_gate, w_up, w_down, x, cot, chunk, hop):
    rows, features = x.shape
    hidden = w_gate.shape[1]
    per = chunk // hop
    anywhere, vmem = pl.BlockSpec(memory_space=pl.ANY), pl.BlockSpec(memory_space=pltpu.VMEM)
    shape = jax.ShapeDtypeStruct
    return pl.pallas_call(
        functools.partial(ffn_kernel, size, hop, chunk),
        in_specs=[vmem] * 3 + [anywhere] * 6,
        out_specs=[anywhere] * 7 + [vmem],
        out_shape=[
            shape((rows, features), BF),
            shape((rows, hidden), BF),
            shape((rows, 2 * hidden), BF),
            shape((size, rows, features // size), BF),
            shape((rows, features), BF),
            shape((rows, features), F32),
            shape((rows, features // size), F32),
            shape((1, features), F32),
        ],
        scratch_shapes=sum_scratch(size, hop, features)
        + [
            pltpu.VMEM(w_out.shape, BF),
            pltpu.VMEM(w_gate.shape, BF),
            pltpu.VMEM(w_up.shape, BF),
            pltpu.VMEM(w_down.shape, BF),
            pltpu.VMEM((-(-(per + size - 2 + per // 2) // per), chunk, features), BF),
            pltpu.VMEM((2, chunk, features), BF),
            pltpu.VMEM((2, hop, features), BF),
            pltpu.VMEM((chunk, features), BF),
            pltpu.VMEM((2, hop, features), F32),
            pltpu.VMEM((2, hop, features // size), F32),
            pltpu.VMEM((chunk, hidden), BF),
            pltpu.VMEM((chunk, 2 * hidden), BF),
            pltpu.VMEM((chunk, features), BF),
            pltpu.VMEM((chunk, features), BF),
            pltpu.VMEM((size, chunk, features // size), BF),
            pltpu.SemaphoreType.DMA((4,)),
            pltpu.SemaphoreType.DMA((2,)),
            pltpu.SemaphoreType.DMA,
            pltpu.SemaphoreType.DMA((2, per)),
            pltpu.SemaphoreType.DMA((2,)),
            pltpu.SemaphoreType.DMA((2,)),
            pltpu.SemaphoreType.DMA((2,)),
            pltpu.SemaphoreType.DMA((2,)),
        ],
        compiler_params=pltpu.CompilerParams(
            collective_id=1, has_side_effects=True, vmem_limit_bytes=VMEM_LIMIT
        ),
        cost_estimate=pl.CostEstimate(
            flops=2 * rows * features * (6 * hidden + w_out.shape[0]),
            bytes_accessed=80 << 20,
            transcendentals=rows * hidden,
        ),
        name="feed_forward",
    )(mixed, keep, gain, w_out, w_gate, w_up, w_down, x, cot)


def back_kernel(
    size, hop, chunk,
    parts, keep, gain, w_out, middle, cot, act,
    own_o, grad_low_o, mixed_o, gain_o, down_o,
    low, high, sent, low_send, low_recv, high_send, high_recv,
    wo, mids, cots, acts, owns, grads_low, tiles,
    load_sem, mid_sem, own_sem, grad_low_sem, tile_sem,
):
    rows, features = middle.shape
    count, per, groups = rows // hop, chunk // hop, rows // chunk
    tile = tile_of(features, 256)
    tile_count = features // tile
    ticks = max(count + size, per * (groups - 1) + size - 1 + per, tile_count + 1)

    def part(c):
        return parts[pl.ds(pl.multiple_of(c * hop, hop), hop), :]

    sums = Sums(size, count, part, low, high, sent, (low_send, low_recv, high_send, high_recv))
    loads = [
        pltpu.make_async_copy(a, b, load_sem.at[i])
        for i, (a, b) in enumerate(((cot, cots), (w_out, wo), (act, acts)))
    ]

    def load_mid(c):
        slot = lax.rem(c, 2)
        return pltpu.make_async_copy(
            middle.at[pl.ds(c * hop, hop)], mids.at[slot], mid_sem.at[slot]
        )

    def save_own(c):
        slot = lax.rem(c, 2)
        return pltpu.make_async_copy(owns.at[slot], own_o.at[pl.ds(c * hop, hop)], own_sem.at[slot])

    def save_low(c):
        q = lax.rem(c, per)
        return pltpu.make_async_copy(
            grads_low.at[pl.ds(q * hop, hop)], grad_low_o.at[pl.ds(c * hop, hop)], grad_low_sem.at[q]
        )

    def save_tile(j):
        slot = lax.rem(j, 2)
        return pltpu.make_async_copy(
            tiles.at[slot], down_o.at[pl.ds(j * tile, tile)], tile_sem.at[slot]
        )

    load_mid(0).start()
    for load in loads:
        load.start()
    gain_o[...] = jnp.zeros_like(gain_o)
    sums.barrier()

    def finish(c):
        slot = lax.rem(c, 2)
        load_mid(c).wait()

        @pl.when(c + 1 < count)
        def _():
            load_mid(c + 1).start()

        @pl.when(c >= 2)
        def _():
            save_own(c - 2).wait()

        @pl.when(c >= per)
        def _():
            save_low(c - per).wait()

        chunk_rows = pl.ds(pl.multiple_of(c * hop, hop), hop)
        kept = keep[chunk_rows, :]
        mid = mids[slot]
        inv = lax.rsqrt(jnp.sum(mid * mid, 1, keepdims=True) / features + epsilon)
        hat = mid * inv

        total = sums.total(c)
        gain_o[...] += jnp.sum(total * hat, 0, keepdims=True)
        weighted = total * gain[1:2, :]
        mean = jnp.sum(weighted * hat, 1, keepdims=True) / features
        mids[slot] = cots[chunk_rows, :].astype(F32) + inv * (weighted - hat * mean)
        grad = mids[slot]
        own_columns(size, grad, lambda piece: owns.__setitem__(slot, piece))
        grads_low[pl.ds(pl.multiple_of(lax.rem(c, per) * hop, hop), hop), :] = (kept * grad).astype(
            BF
        )
        save_own(c).start()
        save_low(c).start()

    def weight_tile(j):
        slot = lax.rem(j, 2)

        @pl.when(j >= 2)
        def _():
            save_tile(j - 2).wait()

        cols = pl.ds(pl.multiple_of(j * tile, tile), tile)
        tiles[slot] = dot(flip(cots[:, cols]).astype(BF), acts[...]).astype(BF)
        save_tile(j).start()

    def tick(k, _):
        sums.tick(k)
        c = k - (size - 1)

        @pl.when(k == 1)
        def _():
            for load in loads:
                load.wait()

        @pl.when((c >= 0) & (c < count))
        def _():
            finish(c)

            @pl.when(lax.rem(c, per) == per - 1)
            def _():
                g = lax.div(c, per)
                mixed_o[:, pl.ds(pl.multiple_of(g * chunk, chunk), chunk)] = dot_nt(
                    wo[...], grads_low[...]
                ).astype(BF)

        @pl.when((k >= 1) & (k <= tile_count))
        def _():
            weight_tile(k - 1)

        return 0

    lax.fori_loop(0, ticks, tick, 0)
    for c in range(count - 2, count):
        save_own(c).wait()
    for c in range(count - per, count):
        save_low(c).wait()
    for j in range(max(tile_count - 2, 0), tile_count):
        save_tile(j).wait()


def norm_back(size, parts, keep, gain, w_out, middle, cot, act, chunk, hop, after):
    rows, features = middle.shape
    per = chunk // hop
    anywhere, vmem = pl.BlockSpec(memory_space=pl.ANY), pl.BlockSpec(memory_space=pltpu.VMEM)
    shape, dma = jax.ShapeDtypeStruct, pltpu.SemaphoreType.DMA

    def kernel(*refs):
        back_kernel(size, hop, chunk, *refs[:7], *refs[7 + len(after) :])

    return pl.pallas_call(
        kernel,
        in_specs=[vmem] * 3 + [anywhere] * (4 + len(after)),
        out_specs=[anywhere] * 2 + [vmem] * 2 + [anywhere],
        out_shape=[
            shape((rows, features // size), F32),
            shape((rows, features), BF),
            shape((w_out.shape[0], rows), BF),
            shape((1, features), F32),
            shape((features, act.shape[1]), BF),
        ],
        scratch_shapes=sum_scratch(size, hop, features)
        + [
            pltpu.VMEM(w_out.shape, BF),
            pltpu.VMEM((2, hop, features), F32),
            pltpu.VMEM(cot.shape, BF),
            pltpu.VMEM(act.shape, BF),
            pltpu.VMEM((2, hop, features // size), F32),
            pltpu.VMEM((chunk, features), BF),
            pltpu.VMEM((2, tile_of(features, 256), act.shape[1]), BF),
            dma((3,)),
            dma((2,)),
            dma((2,)),
            dma((per,)),
            dma((2,)),
        ],
        compiler_params=pltpu.CompilerParams(
            collective_id=2, has_side_effects=True, vmem_limit_bytes=VMEM_LIMIT
        ),
        cost_estimate=pl.CostEstimate(
            flops=2 * rows * features * (w_out.shape[0] + act.shape[1]),
            bytes_accessed=40 << 20,
            transcendentals=rows,
        ),
        name="norm_back",
    )(parts, keep, gain, w_out, middle, cot, act, *after)


def greet(peers):
    barrier = pltpu.get_barrier_semaphore()
    for peer in peers:
        pl.semaphore_signal(barrier, inc=1, device_id=peer, device_id_type=MESH_ID)
    pl.semaphore_wait(barrier, len(peers))


def others(axis, size):
    here = lax.axis_index(axis)
    return [{axis: lax.rem(here + i, size)} for i in range(1, size)]


class Gather:
    def __init__(self, size, groups, chunk, own, blocks, sems):
        self.size, self.groups, self.chunk = size, groups, chunk
        self.own, self.blocks = own, blocks
        self.up_send, self.up_recv, self.down_send, self.down_recv, self.own_sem = sems
        self.steps = size - 1
        self.ticks = groups * self.steps + 1
        self.here = lax.axis_index("tensor")

    def load(self, g):
        part = pl.ds(g * self.chunk, self.chunk)
        return pltpu.make_async_copy(
            self.own.at[part], self.blocks.at[self.here, part], self.own_sem.at[g]
        )

    def load_all(self):
        for g in range(self.groups):
            self.load(g).start()

    def move(self, g, s, owner, peer, send, recv):
        block = self.blocks.at[jnp.clip(owner, 0, self.size - 1), pl.ds(g * self.chunk, self.chunk)]
        return pltpu.make_async_remote_copy(
            src_ref=block,
            dst_ref=block,
            send_sem=send.at[g, s],
            recv_sem=recv.at[g, s],
            device_id={"tensor": peer},
            device_id_type=MESH_ID,
        )

    def up(self, g, s):
        return self.move(g, s, self.here - s, self.here + 1, self.up_send, self.up_recv)

    def down(self, g, s):
        return self.move(g, s, self.here + s, self.here - 1, self.down_send, self.down_recv)

    def each(self, g, s, act):
        @pl.when((self.here >= s) & (self.here < self.size - 1))
        def _():
            act(self.up(g, s))

        @pl.when((self.here + s < self.size) & (self.here > 0))
        def _():
            act(self.down(g, s))

    def send(self, g, s):
        self.each(g, s, lambda copy: copy.start())

    def receive(self, g, s):
        @pl.when(self.here - 1 - s >= 0)
        def _():
            self.up(g, s).wait_recv()

        @pl.when(self.here + 1 + s < self.size)
        def _():
            self.down(g, s).wait_recv()

    def begin(self):
        self.load(0).wait()
        self.send(0, 0)

    def tick(self, k, then):
        g, s = lax.div(k, self.steps), lax.rem(k, self.steps)

        @pl.when((s > 0) & (g < self.groups))
        def _():
            self.receive(g, s - 1)
            self.send(g, s)

        @pl.when((s == self.steps - 1) & (g + 1 < self.groups))
        def _():
            self.load(g + 1).wait()
            self.send(g + 1, 0)

        @pl.when((s == 0) & (g > 0) & (g <= self.groups))
        def _():
            self.receive(g - 1, self.steps - 1)
            then(g - 1)

    def drain(self):
        for g in range(self.groups):
            for s in range(self.steps):
                self.each(g, s, lambda copy: copy.wait_send())


def gather_scratch(size, rows, width, chunk):
    dma, groups = pltpu.SemaphoreType.DMA, rows // chunk
    return [pltpu.VMEM((size, rows, width), BF)] + [dma((groups, size - 1))] * 4 + [dma((groups,))]


class Scatter:
    def __init__(self, size, groups, chunk, parts, ups, downs, sems):
        self.size, self.groups, self.chunk = size, groups, chunk
        self.parts, self.ups, self.downs = parts, ups, downs
        self.up_send, self.up_recv, self.down_send, self.down_recv = sems
        self.count = (size - 1) * groups
        self.here = lax.axis_index("tensor")

    def rows(self, m):
        return pl.ds(pl.multiple_of(lax.rem(m, self.groups) * self.chunk, self.chunk), self.chunk)

    def up(self, m, first):
        owner = self.size - 1 - lax.div(m, self.groups)
        return pltpu.make_async_remote_copy(
            src_ref=self.parts.at[owner, self.rows(m)] if first else self.ups.at[m],
            dst_ref=self.ups.at[m],
            send_sem=self.up_send.at[m],
            recv_sem=self.up_recv.at[m],
            device_id={"tensor": self.here + 1},
            device_id_type=MESH_ID,
        )

    def down(self, m, first):
        owner = lax.div(m, self.groups)
        return pltpu.make_async_remote_copy(
            src_ref=self.parts.at[owner, self.rows(m)] if first else self.downs.at[m],
            dst_ref=self.downs.at[m],
            send_sem=self.down_send.at[m],
            recv_sem=self.down_recv.at[m],
            device_id={"tensor": self.here - 1},
            device_id_type=MESH_ID,
        )

    def tick(self, k):
        bottom, top = self.here == 0, self.here == self.size - 1
        m = k - self.here
        owner = self.size - 1 - lax.div(m, self.groups)

        @pl.when((m >= 0) & (owner > self.here))
        def _():
            @pl.when(bottom)
            def _():
                self.up(m, True).start()

            @pl.when(jnp.logical_not(bottom))
            def _():
                self.up(m, False).wait_recv()
                self.ups[m] = add_low(self.ups[m], self.parts[owner, self.rows(m), :])
                self.up(m, False).start()

        n = k - (self.size - 1 - self.here)
        below = lax.div(n, self.groups)

        @pl.when((n >= 0) & (below < self.here))
        def _():
            @pl.when(top)
            def _():
                self.down(n, True).start()

            @pl.when(jnp.logical_not(top))
            def _():
                self.down(n, False).wait_recv()
                self.downs[n] = add_low(self.downs[n], self.parts[below, self.rows(n), :])
                self.down(n, False).start()

    def finish(self, total, then):
        here = self.here

        def last(c, _):
            part = self.rows(c)
            m, n = (self.size - 1 - here) * self.groups + c, here * self.groups + c
            total[...] = self.parts[here, part, :].astype(F32)

            @pl.when(here > 0)
            def _():
                self.up(m, False).wait_recv()
                total[...] += self.ups[m].astype(F32)

            @pl.when(here < self.size - 1)
            def _():
                self.down(n, False).wait_recv()
                total[...] += self.downs[n].astype(F32)

            then(part, total[...])
            return 0

        lax.fori_loop(0, self.groups, last, 0)

        def drain(m, _):
            @pl.when(self.size - 1 - lax.div(m, self.groups) > here)
            def _():
                self.up(m, False).wait_send()

            @pl.when(lax.div(m, self.groups) < here)
            def _():
                self.down(m, False).wait_send()

            return 0

        lax.fori_loop(0, self.count, drain, 0)


def scatter_scratch(size, rows, width, chunk):
    count = (size - 1) * (rows // chunk)
    return [
        pltpu.VMEM((size, rows, width), BF),
        pltpu.VMEM((count, chunk, width), BF),
        pltpu.VMEM((count, chunk, width), BF),
        pltpu.VMEM((chunk, width), F32),
    ] + [pltpu.SemaphoreType.DMA((count,))] * 4


def turn(u, cos_t, sin_t):
    lower, upper = u[: HD // 2], u[HD // 2 :]
    return jnp.concatenate([lower * cos_t - upper * sin_t, upper * cos_t + lower * sin_t], 0)


def flip(a):
    return a.astype(F32).T


def key_blocks(g, chunk, rows, keys, key_rows):
    start = lax.axis_index("context") * rows + g * chunk
    free = jnp.minimum(start + 1, min(LEAST_VALID, keys))
    last = jnp.minimum(start + chunk + PIC - 1, keys)
    return lax.div(free, key_rows), lax.div(last + key_rows - 1, key_rows)


def attend_kernel(
    size, contexts, chunk, key_rows,
    own, own_cot, gain_pair, cos_tab, sin_tab, mask, starts, w_query, w_key_t, w_value_t,
    x_o, normed_o, inv_o, gain_o, q, kv_o, kend, keep_o, cot_o, mixed_o, lse_o,
    xs, up_send, up_recv, down_send, down_recv, own_sem,
    blocks, up_send_c, up_recv_c, down_send_c, down_recv_c, own_sem_c,
    gains, full, normed, full_c, kv, wq, wk, wv, keys_in_rows, acc, mx, sm,
    gain_send, gain_recv, kv_send, kv_recv, w_sem, out_sem, kv_sem, cot_sem,
):
    here, place = lax.axis_index("tensor"), lax.axis_index("context")
    rows, width = own.shape
    features = size * width
    groups = rows // chunk
    heads, kvs = w_query.shape[1] // HD, w_key_t.shape[0] // HD
    keys, group = contexts * rows, heads // kvs
    units = kvs * groups
    line = Gather(
        size, groups, chunk, own, xs, (up_send, up_recv, down_send, down_recv, own_sem)
    )
    line_c = Gather(
        size, groups, chunk, own_cot, blocks,
        (up_send_c, up_recv_c, down_send_c, down_recv_c, own_sem_c),
    )
    loads = [
        pltpu.make_async_copy(a, b, w_sem.at[i])
        for i, (a, b) in enumerate(((w_query, wq), (w_key_t, wk), (w_value_t, wv)))
    ]
    line.load_all()
    for load in loads:
        load.start()
    gains[here] = jnp.zeros_like(gains[here])
    gains[here, 0:2] = gain_pair[...]
    tensor_peers, context_peers = others("tensor", size), others("context", contexts)
    greet(tensor_peers + context_peers)

    def gain_copy(i):
        return pltpu.make_async_remote_copy(
            src_ref=gains.at[here],
            dst_ref=gains.at[here],
            send_sem=gain_send.at[i],
            recv_sem=gain_recv.at[i],
            device_id=tensor_peers[i],
            device_id_type=MESH_ID,
        )

    def kv_copy(g, i):
        part = kv.at[:, :, pl.ds(pl.multiple_of(place * rows + g * chunk, chunk), chunk)]
        return pltpu.make_async_remote_copy(
            src_ref=part,
            dst_ref=part,
            send_sem=kv_send.at[g, i],
            recv_sem=kv_recv.at[g, i],
            device_id=context_peers[i],
            device_id_type=MESH_ID,
        )

    line.begin()
    line_c.load_all()
    for i in range(size - 1):
        gain_copy(i).start()

    length = jnp.sum(mask[...].astype(F32), 1, keepdims=True).astype(jnp.int32)
    position = lax.broadcasted_iota(jnp.int32, (1, rows), 1) + place * rows
    last = position
    for k in range(starts.shape[1]):
        start = starts[:, k : k + 1]
        inside = (position >= start) & (position < start + PIC)
        last = jnp.maximum(last, jnp.where(inside, start + PIC - 1, 0))
    kend[...] = jnp.minimum(last + 1, length)
    down_rows = lax.broadcasted_iota(jnp.int32, (rows, 1), 0) + place * rows
    keep_o[...] = jnp.where(down_rows < length, 1.0, 0.0)

    def save(g):
        part = pl.ds(g * chunk, chunk)
        return [
            pltpu.make_async_copy(full, x_o.at[part], out_sem.at[0]),
            pltpu.make_async_copy(normed, normed_o.at[part], out_sem.at[1]),
        ]

    def project(g):
        part = pl.ds(pl.multiple_of(g * chunk, chunk), chunk)

        @pl.when(g == 0)
        def _():
            for load in loads:
                load.wait()
            for i in range(size - 1):
                gain_copy(i).wait_recv()
            gain_o[...] = jnp.concatenate([gains[j] for j in range(size)], 1)

        @pl.when(g > 0)
        def _():
            for copy in save(g - 1):
                copy.wait()

        full[...] = jnp.concatenate([xs[j, part, :] for j in range(size)], 1)
        stream = full[...].astype(F32)
        inv = lax.rsqrt(jnp.sum(stream * stream, 1, keepdims=True) / features + epsilon)
        inv_o[part, :] = inv
        normed[...] = (stream * inv * gain_o[0:1, :]).astype(BF)
        for copy in save(g):
            copy.start()
        cos_t, sin_t = cos_tab[:, part], sin_tab[:, part]
        mine = pl.ds(pl.multiple_of(place * rows + g * chunk, chunk), chunk)
        key = dot_nt(wk[...], normed[...])
        value = dot_nt(wv[...], normed[...])
        for h in range(kvs):
            kv[h, :, mine] = turn(key[h * HD : (h + 1) * HD], cos_t, sin_t).astype(BF)
            kv[kvs + h, :, mine] = value[h * HD : (h + 1) * HD].astype(BF)
        for i in range(contexts - 1):
            kv_copy(g, i).start()
        query = dot(normed[...], wq[...]).T
        for h in range(heads):
            q[h, :, part] = turn(query[h * HD : (h + 1) * HD], cos_t, sin_t).astype(BF)

    def save_cot(g):
        return pltpu.make_async_copy(full_c, cot_o.at[pl.ds(g * chunk, chunk)], cot_sem)

    def join(g):
        @pl.when(g > 0)
        def _():
            save_cot(g - 1).wait()

        part = pl.ds(pl.multiple_of(g * chunk, chunk), chunk)
        full_c[...] = jnp.concatenate([blocks[j, part, :] for j in range(size)], 1)
        save_cot(g).start()

    save_kv = pltpu.make_async_copy(kv, kv_o, kv_sem)

    def meet():
        for g in range(groups):
            for i in range(contexts - 1):
                kv_copy(g, i).wait_recv()
        save_kv.start()
        for h in range(kvs):
            keys_in_rows[h] = flip(kv[h]).astype(BF)

    def unit(u):
        pair, g = lax.div(u, groups), lax.rem(u, groups)
        part = pl.ds(pl.multiple_of(g * chunk, chunk), chunk)
        free, last = key_blocks(g, chunk, rows, keys, key_rows)
        acc[...] = jnp.zeros_like(acc)
        sm[...] = jnp.zeros_like(sm)
        mx[...] = jnp.full_like(mx, LOWEST)
        limit = kend[:, part]

        def step(masked, i, _):
            at = pl.multiple_of(i * key_rows, key_rows)
            k_blk = keys_in_rows[pair, pl.ds(at, key_rows), :]
            v_blk = kv[kvs + pair, :, pl.ds(at, key_rows)]
            if masked:
                keep = (lax.broadcasted_iota(jnp.int32, (key_rows, chunk), 0) + at) < limit
            for h in range(group):
                s = dot(k_blk, q[pair * group + h, :, part])
                if masked:
                    s = jnp.where(keep, s, LOWEST)
                old = mx[h]
                new = jnp.maximum(old, jnp.max(s, 0, keepdims=True))
                p = jnp.exp2(s * SCALE2 - new * SCALE2)
                alpha = jnp.exp2((old - new) * SCALE2)
                mx[h] = new
                sm[h] = sm[h] * alpha + jnp.sum(p, 0, keepdims=True)
                acc[h] = acc[h] * alpha + dot(v_blk, p.astype(BF))
            return 0

        lax.fori_loop(0, free, functools.partial(step, False), 0)
        lax.fori_loop(free, last, functools.partial(step, True), 0)
        for h in range(group):
            mixed_o[pair * group + h, :, part] = (acc[h] / sm[h]).astype(BF)
            lse_o[pair * group + h, :, part] = mx[h] * SCALE2 + jnp.log2(sm[h])

    turnover = line.ticks - 1

    def tick(k, _):
        @pl.when(k == turnover)
        def _():
            line_c.begin()

        line.tick(k, project)

        @pl.when(k >= turnover)
        def _():
            line_c.tick(k - turnover, join)

        u = k - line.ticks

        @pl.when(u == 0)
        def _():
            meet()

        @pl.when((u >= 0) & (u < units))
        def _():
            unit(u)

        return 0

    lax.fori_loop(0, max(turnover + line_c.ticks, line.ticks + units), tick, 0)
    for copy in [*save(groups - 1), save_cot(groups - 1), save_kv]:
        copy.wait()
    for i in range(size - 1):
        gain_copy(i).wait_send()
    line.drain()
    line_c.drain()
    for g in range(groups):
        for i in range(contexts - 1):
            kv_copy(g, i).wait_send()


def attend_forward(
    axes, own, own_cot, gain_pair, cos_tab, sin_tab, mask, starts, w_query, w_key_t, w_value_t, chunk
):
    size, contexts = axes["tensor"], axes["context"]
    rows, width = own.shape
    features, groups = size * width, rows // chunk
    heads, kvs = w_query.shape[1] // HD, w_key_t.shape[0] // HD
    keys, group = contexts * rows, heads // kvs
    key_rows = min(KEY_ROWS_FWD, keys)
    anywhere, vmem = pl.BlockSpec(memory_space=pl.ANY), pl.BlockSpec(memory_space=pltpu.VMEM)
    shape, dma = jax.ShapeDtypeStruct, pltpu.SemaphoreType.DMA
    return pl.pallas_call(
        functools.partial(attend_kernel, size, contexts, chunk, key_rows),
        in_specs=[anywhere] * 2 + [vmem] * 5 + [anywhere] * 3,
        out_specs=[anywhere] * 2 + [vmem] * 3 + [anywhere] + [vmem] * 2 + [anywhere] + [vmem] * 2,
        out_shape=[
            shape((rows, features), BF),
            shape((rows, features), BF),
            shape((rows, 1), F32),
            shape((8, features), F32),
            shape((heads, HD, rows), BF),
            shape((2 * kvs, HD, keys), BF),
            shape((1, rows), jnp.int32),
            shape((rows, 1), F32),
            shape((rows, features), BF),
            shape((heads, HD, rows), BF),
            shape((heads, 1, rows), F32),
        ],
        scratch_shapes=gather_scratch(size, rows, width, chunk)
        + gather_scratch(size, rows, width, chunk)
        + [
            pltpu.VMEM((size, 8, width), F32),
            pltpu.VMEM((chunk, features), BF),
            pltpu.VMEM((chunk, features), BF),
            pltpu.VMEM((chunk, features), BF),
            pltpu.VMEM((2 * kvs, HD, keys), BF),
            pltpu.VMEM(w_query.shape, BF),
            pltpu.VMEM(w_key_t.shape, BF),
            pltpu.VMEM(w_value_t.shape, BF),
            pltpu.VMEM((kvs, keys, HD), BF),
            pltpu.VMEM((group, HD, chunk), F32),
            pltpu.VMEM((group, 1, chunk), F32),
            pltpu.VMEM((group, 1, chunk), F32),
            dma((size - 1,)),
            dma((size - 1,)),
            dma((groups, max(contexts - 1, 1))),
            dma((groups, max(contexts - 1, 1))),
            dma((3,)),
            dma((2,)),
            dma,
            dma,
        ],
        compiler_params=pltpu.CompilerParams(
            collective_id=3, has_side_effects=True, vmem_limit_bytes=VMEM_LIMIT
        ),
        cost_estimate=pl.CostEstimate(
            flops=2 * rows * features * (heads + 2 * kvs) * HD + 10 * heads * rows * keys * HD,
            bytes_accessed=40 << 20,
            transcendentals=heads * rows * keys,
        ),
        name="attend_forward",
    )(own, own_cot, gain_pair, cos_tab, sin_tab, mask, starts, w_query, w_key_t, w_value_t)


def attend_back_kernel(
    size, contexts, chunk, key_rows,
    ffn, q, kv, kend, do, o, lse, cos_tab, sin_tab, middle, grad_attn, normed,
    grads_o, layer_o, square_o, weights_o,
    parts, ups, downs, total, up_send, up_recv, down_send, down_recv,
    keys_in_rows, values_in_rows, dq, dk, dv, ds_all, p_all, q_all, do_all, mine, out_kv, in_kv,
    grads_in, normed_in, tiles,
    kv_send, kv_recv, part_sem, tile_sem,
):
    heads, _, rows = q.shape
    kvs, keys = kv.shape[0] // 2, kv.shape[2]
    groups, group = rows // chunk, heads // kvs
    units = kvs * groups
    place = lax.axis_index("context")
    line = Scatter(
        size, groups, chunk, parts, ups, downs, (up_send, up_recv, down_send, down_recv)
    )
    loads = [
        pltpu.make_async_copy(a, b, part_sem.at[i])
        for i, (a, b) in enumerate(((ffn, parts), (grad_attn, grads_in), (normed, normed_in)))
    ]
    for load in loads:
        load.start()
    square_o[...] = jnp.zeros_like(square_o)
    peers = others("context", contexts)
    greet(others("tensor", size) + peers)
    loads[0].wait()

    def half(of):
        at = pl.ds(pl.multiple_of(of * rows, rows), rows)
        return dk[at, :].T, dv[at, :].T

    def kv_copy(pair, i):
        return pltpu.make_async_remote_copy(
            src_ref=out_kv.at[pair, i],
            dst_ref=in_kv.at[pair, i],
            send_sem=kv_send.at[pair, i],
            recv_sem=kv_recv.at[pair, i],
            device_id=peers[i],
            device_id_type=MESH_ID,
        )

    def unit(u):
        pair, g = lax.div(u, groups), lax.rem(u, groups)
        part = pl.ds(pl.multiple_of(g * chunk, chunk), chunk)
        free, last = key_blocks(g, chunk, rows, keys, key_rows)
        limit = kend[:, part]

        @pl.when(g == 0)
        def _():
            dk[...] = jnp.zeros_like(dk)
            dv[...] = jnp.zeros_like(dv)

        dq[...] = jnp.zeros_like(dq)
        delta = []
        for h in range(group):
            head = pair * group + h
            cols = slice(h * chunk, (h + 1) * chunk)
            q_all[:, cols] = q[head, :, part]
            do_all[:, cols] = do[head, :, part]
            delta.append(
                jnp.sum(do_all[:, cols].astype(F32) * o[head, :, part].astype(F32), 0, keepdims=True)
            )

        def step(masked, i, _):
            at = pl.multiple_of(i * key_rows, key_rows)
            k_blk = keys_in_rows[pair, pl.ds(at, key_rows), :]
            v_blk = values_in_rows[pair, pl.ds(at, key_rows), :]
            kt_blk = kv[pair, :, pl.ds(at, key_rows)]
            if masked:
                keep = (lax.broadcasted_iota(jnp.int32, (key_rows, chunk), 0) + at) < limit
            for h in range(group):
                cols = slice(h * chunk, (h + 1) * chunk)
                s = dot(k_blk, q_all[:, cols])
                p = jnp.exp2(s * SCALE2 - lse[pair * group + h, :, part])
                if masked:
                    p = jnp.where(keep, p, 0.0)
                dp = dot(v_blk, do_all[:, cols])
                ds = (p * (dp - delta[h])).astype(BF)
                p_all[:, cols] = p.astype(BF)
                ds_all[:, cols] = ds
                dq[h] += dot(kt_blk, ds)
            dk[pl.ds(at, key_rows), :] += dot_nt(ds_all[...], q_all[...])
            dv[pl.ds(at, key_rows), :] += dot_nt(p_all[...], do_all[...])
            return 0

        lax.fori_loop(0, free, functools.partial(step, False), 0)
        lax.fori_loop(free, last, functools.partial(step, True), 0)
        for h in range(group):
            grads_o[pair * group + h, :, part] = turn(
                dq[h] * SCALE, cos_tab[:, part], -sin_tab[:, part]
            ).astype(BF)

        @pl.when(g == groups - 1)
        def _():
            for i in range(contexts - 1):
                key, value = half(peers[i]["context"])
                out_kv[pair, i, 0] = key.astype(BF)
                out_kv[pair, i, 1] = value.astype(BF)
                kv_copy(pair, i).start()
            mine[pair, 0], mine[pair, 1] = half(place)

    def join():
        for pair in range(kvs):
            key, value = mine[pair, 0], mine[pair, 1]
            for i in range(contexts - 1):
                kv_copy(pair, i).wait()
                key = key + in_kv[pair, i, 0].astype(F32)
                value = value + in_kv[pair, i, 1].astype(F32)
            grads_o[heads + pair] = turn(key * SCALE, cos_tab[...], -sin_tab[...]).astype(BF)
            grads_o[heads + kvs + pair] = value.astype(BF)

    features = normed.shape[1]
    tile = tile_of(features, 256)
    tile_count, each = features // tile, 4

    def save_tile(j):
        slot = lax.rem(j, 2)
        return pltpu.make_async_copy(
            tiles.at[slot], weights_o.at[pl.ds(j * tile, tile)], tile_sem.at[slot]
        )

    def weight_tile(j):
        slot = lax.rem(j, 2)

        @pl.when(j >= 2)
        def _():
            save_tile(j - 2).wait()

        cols = pl.ds(pl.multiple_of(j * tile, tile), tile)
        out = dot_nt(flip(grads_in[:, cols]).astype(BF), o[...].reshape(heads * HD, rows))
        into = dot_nt(
            flip(normed_in[:, cols]).astype(BF), grads_o[...].reshape((heads + 2 * kvs) * HD, rows)
        )
        tiles[slot] = jnp.concatenate([out, into], 1).astype(BF)
        save_tile(j).start()

    def tick(k, _):
        line.tick(k)

        @pl.when(k == 0)
        def _():
            for h in range(kvs):
                keys_in_rows[h] = flip(kv[h]).astype(BF)
                values_in_rows[h] = flip(kv[kvs + h]).astype(BF)

        @pl.when(k < units)
        def _():
            unit(k)

        @pl.when(k == units)
        def _():
            join()
            for load in loads[1:]:
                load.wait()

        first = (k - units - 1) * each
        for j in range(each):

            @pl.when((first >= 0) & (first + j < tile_count))
            def _():
                weight_tile(first + j)

        return 0

    lax.fori_loop(0, max(line.count, units + 1 + -(-tile_count // each)), tick, 0)

    def then(part, ffn_out):
        square_o[...] += jnp.sum(ffn_out * ffn_out, 0, keepdims=True)
        layer_o[part, :] = (middle[part, :] + ffn_out).astype(BF)

    line.finish(total, then)
    for j in range(max(tile_count - 2, 0), tile_count):
        save_tile(j).wait()


def attend_backward(
    axes, ffn, q, kv, kend, do, o, lse, cos_tab, sin_tab, middle, grad_attn, normed, chunk, after
):
    size, contexts = axes["tensor"], axes["context"]
    heads, _, rows = q.shape
    kvs, keys = kv.shape[0] // 2, kv.shape[2]
    group, width = heads // kvs, ffn.shape[2]
    key_rows = min(KEY_ROWS_BWD, keys)
    anywhere, vmem = pl.BlockSpec(memory_space=pl.ANY), pl.BlockSpec(memory_space=pltpu.VMEM)
    shape, dma = jax.ShapeDtypeStruct, pltpu.SemaphoreType.DMA
    slots = max(contexts - 1, 1)

    def kernel(*refs):
        attend_back_kernel(size, contexts, chunk, key_rows, *refs[:12], *refs[12 + len(after) :])

    return pl.pallas_call(
        kernel,
        in_specs=[anywhere] + [vmem] * 9 + [anywhere] * (2 + len(after)),
        out_specs=[vmem] * 3 + [anywhere],
        out_shape=[
            shape((heads + 2 * kvs, HD, rows), BF),
            shape((rows, width), BF),
            shape((1, width), F32),
            shape((size * width, (2 * heads + 2 * kvs) * HD), BF),
        ],
        scratch_shapes=scatter_scratch(size, rows, width, chunk)
        + [
            pltpu.VMEM((kvs, keys, HD), BF),
            pltpu.VMEM((kvs, keys, HD), BF),
            pltpu.VMEM((group, HD, chunk), F32),
            pltpu.VMEM((keys, HD), F32),
            pltpu.VMEM((keys, HD), F32),
            pltpu.VMEM((key_rows, group * chunk), BF),
            pltpu.VMEM((key_rows, group * chunk), BF),
            pltpu.VMEM((HD, group * chunk), BF),
            pltpu.VMEM((HD, group * chunk), BF),
            pltpu.VMEM((kvs, 2, HD, rows), F32),
            pltpu.VMEM((kvs, slots, 2, HD, rows), BF),
            pltpu.VMEM((kvs, slots, 2, HD, rows), BF),
            pltpu.VMEM(grad_attn.shape, BF),
            pltpu.VMEM(normed.shape, BF),
            pltpu.VMEM((2, tile_of(size * width, 256), (2 * heads + 2 * kvs) * HD), BF),
            dma((kvs, slots)),
            dma((kvs, slots)),
            dma((3,)),
            dma((2,)),
        ],
        compiler_params=pltpu.CompilerParams(
            collective_id=6, has_side_effects=True, vmem_limit_bytes=VMEM_LIMIT
        ),
        cost_estimate=pl.CostEstimate(
            flops=16 * heads * rows * keys * HD,
            bytes_accessed=16 << 20,
            transcendentals=heads * rows * keys,
        ),
        name="attend_backward",
    )(ffn, q, kv, kend, do, o, lse, cos_tab, sin_tab, middle, grad_attn, normed, *after)


def input_kernel(
    axes, chunk,
    grads, inv, gain, keep, attn_square, gain_rows, ffn_square, gain_own, x_own, grad_own,
    w_query, w_key_t, w_value_t, x,
    out_o, sum_o,
    parts, ups, downs, total, up_send, up_recv, down_send, down_recv,
    xs, whole, wq, wk, wv, dots, dot_sum, cols, cols_in, world, square,
    dot_send, dot_recv, col_send, col_recv, world_send, world_recv, w_sem, x_sem,
):
    size = axes["tensor"]
    here = lax.axis_index("tensor")
    rows, features = x.shape
    width, groups = features // size, rows // chunk
    nq, nk = w_query.shape[1], w_key_t.shape[0]
    line = Scatter(
        size, groups, chunk, parts, ups, downs, (up_send, up_recv, down_send, down_recv)
    )
    loads = [
        pltpu.make_async_copy(a, b, w_sem.at[i])
        for i, (a, b) in enumerate(((w_query, wq), (w_key_t, wk), (w_value_t, wv)))
    ]

    def load_x(c):
        slot = lax.rem(c, 2)
        return pltpu.make_async_copy(x.at[pl.ds(c * chunk, chunk)], xs.at[slot], x_sem.at[slot])

    for load in loads:
        load.start()
    load_x(0).start()
    contexts, replicas = axes["context"], axes["dp"] * axes["context"]
    spot = lax.axis_index("dp") * contexts + lax.axis_index("context")
    peers = others("tensor", size)
    far = [lax.rem(spot + i, replicas) for i in range(1, replicas)]
    far = [{"dp": lax.div(i, contexts), "context": lax.rem(i, contexts)} for i in far]
    greet(peers + far)
    for load in loads:
        load.wait()
    square[...] = jnp.zeros_like(square)
    row = lax.broadcasted_iota(jnp.int32, (8, width), 0)
    lane = lax.broadcasted_iota(jnp.int32, (8, width), 1)

    def compute(c):
        slot = lax.rem(c, 2)
        part = pl.ds(pl.multiple_of(c * chunk, chunk), chunk)
        load_x(c).wait()

        @pl.when(c + 1 < groups)
        def _():
            load_x(c + 1).start()

        g = flip(grads[:, part]).astype(BF)
        whole[...] = (
            dot_nt(g[:, :nq], wq[...])
            + dot(g[:, nq : nq + nk], wk[...])
            + dot(g[:, nq + nk :], wv[...])
        )
        for j in range(size):
            parts[j, part, :] = whole[:, j * width : (j + 1) * width].astype(BF)

    def add_up(c):
        slot = lax.rem(c, 2)
        part = pl.ds(pl.multiple_of(c * chunk, chunk), chunk)
        stream = xs[slot].astype(F32)
        square[...] += jnp.sum(stream * stream * keep[part, :], 0, keepdims=True)
        moved = whole[...] * (stream * inv[part, :])
        rowsum = jnp.sum(moved * gain[0:1, :], 1, keepdims=True)
        dots[here, :, part] = jnp.broadcast_to(rowsum, (chunk, 128)).T[:8]
        colsum = jnp.sum(moved, 0, keepdims=True)
        for j in range(size):
            piece = jnp.where(row == 0, colsum[:, j * width : (j + 1) * width], 0.0)

            @pl.when(c == 0)
            def _():
                cols[j] = piece

            @pl.when(c > 0)
            def _():
                cols[j] += piece

    def copy_to(src, dst, send, recv, peer):
        return pltpu.make_async_remote_copy(
            src_ref=src,
            dst_ref=dst,
            send_sem=send,
            recv_sem=recv,
            device_id=peer,
            device_id_type=MESH_ID,
        )

    def dot_copy(i):
        mine = dots.at[here]
        return copy_to(mine, mine, dot_send.at[i], dot_recv.at[i], peers[i])

    def col_copy(i):
        src = cols.at[peers[i]["tensor"]]
        return copy_to(src, cols_in.at[here], col_send.at[i], col_recv.at[i], peers[i])

    def world_copy(i):
        mine = world.at[spot]
        return copy_to(mine, mine, world_send.at[i], world_recv.at[i], far[i])

    def exchange():
        numbers = jnp.zeros((8, width), F32)
        for i, a in enumerate((square[...], attn_square[...], ffn_square[...], keep[...])):
            a = jnp.sum(jnp.sum(a, 0, keepdims=True), 1, keepdims=True)
            share = 1.0 if i == 2 else 1.0 / size
            numbers += jnp.where((row == 1) & (lane == i), a * share, 0.0)
        for j in range(size):
            cols[j] += numbers
        cols_in[here] = cols[here]
        for i in range(size - 1):
            dot_copy(i).start()
            col_copy(i).start()

    def spread():
        for i in range(size - 1):
            dot_copy(i).wait()
            col_copy(i).wait()
        dot_total, column = dots[0], cols_in[0]
        for j in range(1, size):
            dot_total = dot_total + dots[j]
            column = column + cols_in[j]
        dot_sum[...] = dot_total
        world[spot] = column

        def put(piece):
            world[spot, 2:3] = piece

        own_columns(size, gain_rows[...], put)
        for i in range(replicas - 1):
            world_copy(i).start()

    def tick(k, _):
        @pl.when(k < groups)
        def _():
            compute(k)

        line.tick(k)

        @pl.when(k < groups)
        def _():
            add_up(k)

        @pl.when(k == groups)
        def _():
            exchange()

        @pl.when(k == groups + 3)
        def _():
            spread()

        return 0

    lax.fori_loop(0, max(line.count, groups + 4), tick, 0)

    def then(part, grad):
        through = grad * gain_own[...] - x_own[part, :].astype(F32) * inv[part, :] * (
            dot_sum[:, part].T[:, :1] / features
        )
        out_o[part, :] = (grad_own[part, :] + inv[part, :] * through).astype(BF)

    line.finish(total, then)
    for i in range(replicas - 1):
        world_copy(i).wait()
    everything = world[0]
    for j in range(1, replicas):
        everything = everything + world[j]
    sum_o[...] = everything


def input_gradient(
    axes, grads, inv, gain, keep, attn_square, gain_rows, ffn_square, gain_own, x_own, grad_own,
    w_query, w_key_t, w_value_t, x, chunk, after,
):
    size, replicas = axes["tensor"], axes["dp"] * axes["context"]
    rows, features = x.shape
    width = features // size
    anywhere, vmem = pl.BlockSpec(memory_space=pl.ANY), pl.BlockSpec(memory_space=pltpu.VMEM)
    shape, dma = jax.ShapeDtypeStruct, pltpu.SemaphoreType.DMA

    def kernel(*refs):
        input_kernel(axes, chunk, *refs[:14], *refs[14 + len(after) :])

    return pl.pallas_call(
        kernel,
        in_specs=[vmem] * 10 + [anywhere] * (4 + len(after)),
        out_specs=[vmem] * 2,
        out_shape=[
            shape((rows, width), BF),
            shape((8, width), F32),
        ],
        scratch_shapes=scatter_scratch(size, rows, width, chunk)
        + [
            pltpu.VMEM((2, chunk, features), BF),
            pltpu.VMEM((chunk, features), F32),
            pltpu.VMEM(w_query.shape, BF),
            pltpu.VMEM(w_key_t.shape, BF),
            pltpu.VMEM(w_value_t.shape, BF),
            pltpu.VMEM((size, 8, rows), F32),
            pltpu.VMEM((8, rows), F32),
            pltpu.VMEM((size, 8, width), F32),
            pltpu.VMEM((size, 8, width), F32),
            pltpu.VMEM((replicas, 8, width), F32),
            pltpu.VMEM((1, features), F32),
            dma((size - 1,)),
            dma((size - 1,)),
            dma((size - 1,)),
            dma((size - 1,)),
            dma((replicas - 1,)),
            dma((replicas - 1,)),
            dma((3,)),
            dma((2,)),
        ],
        compiler_params=pltpu.CompilerParams(
            collective_id=4, has_side_effects=True, vmem_limit_bytes=VMEM_LIMIT
        ),
        cost_estimate=pl.CostEstimate(
            flops=2 * rows * features * grads.shape[0],
            bytes_accessed=20 << 20,
            transcendentals=rows,
        ),
        name="input_gradient",
    )(
        grads, inv, gain, keep, attn_square, gain_rows, ffn_square, gain_own, x_own, grad_own,
        w_query, w_key_t, w_value_t, x, *after,
    )


def local(
    axes,
    layer_input_hidden,
    cotangent,
    valid_mask,
    span_starts,
    gain_attn,
    w_query,
    w_key,
    w_value,
    w_out,
    gain_mlp,
    w_gate,
    w_up,
    w_down,
):
    _, rows, width = layer_input_hidden.shape
    size = axes["tensor"]
    features = width * size
    kvs = w_key.shape[1] // HD
    heads = w_query.shape[1] // HD
    position = lax.axis_index("context") * rows + jnp.arange(rows, dtype=jnp.int32)
    inverse_freq = rope_base ** (-2.0 * jnp.arange(HD // 2, dtype=F32) / HD)
    angles = inverse_freq[:, None] * position.astype(F32)[None, :]
    cos_tab, sin_tab = jnp.cos(angles), jnp.sin(angles)
    x_own = layer_input_hidden[0]
    w_key_t, w_value_t = w_key.T, w_value.T

    def shard(grad):
        return lax.psum_scatter(grad, ("dp", "context"), scatter_dimension=0, tiled=True)

    (
        x_low,
        normed_a,
        inv_a,
        gains,
        query_t,
        both,
        kend,
        keep,
        cot,
        mixed,
        lse,
    ) = attend_forward(
        axes,
        x_own,
        cotangent[0],
        jnp.stack([gain_attn, gain_mlp]),
        cos_tab,
        sin_tab,
        valid_mask,
        span_starts,
        w_query,
        w_key_t,
        w_value_t,
        GROUP_ROWS,
    )
    normed_m, act, ggu, down_part, back_part, middle, middle_own, attn_square = feed_forward(
        size,
        mixed.reshape(heads * HD, rows),
        keep,
        gains,
        w_out,
        w_gate,
        w_up,
        w_down,
        x_low,
        cot,
        GROUP_ROWS,
        HOP_ROWS,
    )
    grad_ggu = ein("sd,sf->df", normed_m, ggu).astype(BF)
    ggu_sum = shard(grad_ggu)

    grad_own, grad_attn, grad_mixed, gain_m_rows, grad_down = norm_back(
        size, back_part, keep, gains, w_out, middle, cot, act, GROUP_ROWS, HOP_ROWS, (grad_ggu,)
    )
    down_sum = shard(grad_down)
    grads, layer_out, ffn_square, grad_rest = attend_backward(
        axes,
        down_part,
        query_t,
        both,
        kend,
        grad_mixed.reshape(heads, HD, rows),
        mixed,
        lse,
        cos_tab,
        sin_tab,
        middle_own,
        grad_attn,
        normed_a,
        GROUP_ROWS,
        (ggu_sum,),
    )
    rest_sum = shard(grad_rest)

    input_grad, sums = input_gradient(
        axes,
        grads.reshape(-1, rows),
        inv_a,
        gains,
        keep,
        attn_square,
        gain_m_rows,
        ffn_square,
        gain_attn[None],
        x_own,
        grad_own,
        w_query,
        w_key_t,
        w_value_t,
        x_low,
        GROUP_ROWS,
        (grad_rest, down_sum),
    )
    rest_sum = jnp.where(sums[1, 3] >= 0.0, rest_sum.astype(F32), 0.0)
    gate_sum, up_sum = jnp.split(ggu_sum.astype(F32), 2, 1)
    down_sum = down_sum.astype(F32).T
    cut = [heads * HD, 2 * heads * HD, (2 * heads + kvs) * HD]
    out_sum, query_sum, key_sum, value_sum = jnp.split(rest_sum, cut, 1)
    rms = jnp.sqrt(sums[1, :3] / (sums[1, 3] * features))
    return (
        layer_out[None],
        input_grad[None],
        sums[0],
        query_sum,
        key_sum,
        value_sum,
        out_sum.T,
        sums[2],
        gate_sum,
        up_sum,
        down_sum,
        rms[0],
        rms[1],
        rms[2],
    )


def solution(mesh):
    token = P("dp", "context", "tensor")
    by_rows = P(("dp", "context"), "tensor")
    by_columns = P("tensor", ("dp", "context"))
    cols, rows, vec = P(None, "tensor"), P("tensor", None), P("tensor")
    return jax.shard_map(
        functools.partial(local, dict(mesh.shape)),
        mesh=mesh,
        in_specs=(
            token,
            token,
            P("dp", None),
            P("dp", None),
            vec,
            cols,
            cols,
            cols,
            rows,
            vec,
            cols,
            cols,
            rows,
        ),
        out_specs=(
            token,
            token,
            vec,
            by_rows,
            by_rows,
            by_rows,
            by_columns,
            vec,
            by_rows,
            by_rows,
            by_columns,
            P(),
            P(),
            P(),
        ),
        check_vma=False,
    )
```

```python
import functools
import math

import jax
import jax.numpy as jnp
from jax import lax
from jax.experimental import pallas as pl
from jax.experimental.pallas import tpu as pltpu
from jax.sharding import PartitionSpec as P

HD = 80
PIC = 256
LEAST_VALID = 1536
F32 = jnp.float32
BF = jnp.bfloat16
SCALE = HD**-0.5
SCALE2 = SCALE * math.log2(math.e)
LOWEST = -1e30
GROUP_ROWS = 256
HOP_ROWS = 64
VMEM_LIMIT = 60 << 20
KEY_ROWS_FWD = 512
KEY_ROWS_BWD = 512

epsilon = 1e-05
rope_base = 1000000.0


def dot(a, b):
    return jnp.dot(a, b, preferred_element_type=F32)


def dot_nt(a, b):
    return lax.dot_general(a, b, (((1,), (1,)), ((), ())), preferred_element_type=F32)


def ein(spec, a, b):
    return jnp.einsum(spec, a, b, preferred_element_type=F32)


MESH_ID = pl.DeviceIdType.MESH
SENT = 4


def ring_of(size):
    return size + 4


def add_low(a, b):
    return (a.astype(F32) + b.astype(F32)).astype(BF)


class Sums:
    def __init__(self, size, count, part, low, high, sent, sems):
        self.size, self.count, self.part = size, count, part
        self.low, self.high, self.sent = low, high, sent
        self.low_send, self.low_recv, self.high_send, self.high_recv = sems
        self.here = lax.axis_index("tensor")

    def barrier(self):
        here, size = self.here, self.size
        barrier = pltpu.get_barrier_semaphore()

        @pl.when(here > 0)
        def _():
            pl.semaphore_signal(
                barrier, inc=1, device_id={"tensor": here - 1}, device_id_type=MESH_ID
            )

        @pl.when(here < size - 1)
        def _():
            pl.semaphore_signal(
                barrier, inc=1, device_id={"tensor": here + 1}, device_id_type=MESH_ID
            )

        @pl.when((here > 0) & (here < size - 1))
        def _():
            pl.semaphore_wait(barrier, 2)

        @pl.when((here == 0) | (here == size - 1))
        def _():
            pl.semaphore_wait(barrier, 1)

    def up(self, c):
        slot = lax.rem(c, ring_of(self.size))
        return pltpu.make_async_remote_copy(
            src_ref=self.low.at[slot],
            dst_ref=self.low.at[slot],
            send_sem=self.low_send.at[slot],
            recv_sem=self.low_recv.at[slot],
            device_id={"tensor": self.here + 1},
            device_id_type=MESH_ID,
        )

    def down(self, c):
        slot, mine = lax.rem(c, ring_of(self.size)), lax.rem(c, SENT)
        return pltpu.make_async_remote_copy(
            src_ref=self.sent.at[mine],
            dst_ref=self.high.at[slot],
            send_sem=self.high_send.at[mine],
            recv_sem=self.high_recv.at[slot],
            device_id={"tensor": self.here - 1},
            device_id_type=MESH_ID,
        )

    def tick(self, k):
        here, size, count = self.here, self.size, self.count
        bottom, top = here == 0, here == size - 1
        c = k - here

        @pl.when((c >= 0) & (c < count))
        def _():
            slot = lax.rem(c, ring_of(self.size))

            @pl.when(bottom)
            def _():
                self.low[slot] = self.part(c)

            @pl.when(jnp.logical_not(bottom))
            def _():
                self.up(c).wait_recv()
                self.low[slot] = add_low(self.low[slot], self.part(c))

            @pl.when(jnp.logical_not(top))
            def _():
                self.up(c).start()

        d = k - (size - 1 - here)

        @pl.when((d >= 0) & (d < count))
        def _():
            slot, mine = lax.rem(d, ring_of(self.size)), lax.rem(d, SENT)

            @pl.when(top)
            def _():
                self.sent[mine] = self.part(d)

            @pl.when(jnp.logical_not(top))
            def _():
                self.down(d).wait_recv()

                @pl.when(jnp.logical_not(bottom))
                def _():
                    self.sent[mine] = add_low(self.high[slot], self.part(d))

            @pl.when(jnp.logical_not(bottom))
            def _():
                self.down(d).start()

        @pl.when((c >= 2) & (c < count + 2) & jnp.logical_not(top))
        def _():
            self.up(c - 2).wait_send()

        @pl.when((d >= 2) & (d < count + 2) & jnp.logical_not(bottom))
        def _():
            self.down(d - 2).wait_send()

    def total(self, c):
        slot = lax.rem(c, ring_of(self.size))
        high = jnp.where(self.here == self.size - 1, 0.0, self.high[slot].astype(F32))
        return self.low[slot].astype(F32) + high


def sum_scratch(size, hop, features):
    ring, dma = ring_of(size), pltpu.SemaphoreType.DMA
    return [
        pltpu.VMEM((ring, hop, features), BF),
        pltpu.VMEM((ring, hop, features), BF),
        pltpu.VMEM((SENT, hop, features), BF),
        dma((ring,)),
        dma((ring,)),
        dma((SENT,)),
        dma((ring,)),
    ]


def own_columns(size, a, then):
    width = a.shape[1] // size
    for j in range(size):

        @pl.when(lax.axis_index("tensor") == j)
        def _():
            then(a[:, j * width : (j + 1) * width])


def tile_of(n, most):
    for tile in range(most, 0, -128):
        if n % tile == 0:
            return tile
    return n


def ffn_kernel(
    size, hop, chunk,
    mixed, keep, gain, w_out, w_gate, w_up, w_down, x, cot,
    normed_o, act_o, ggu_o, ffn_o, back_o, middle_o, own_o, square_o,
    low, high, sent, low_send, low_recv, high_send, high_recv,
    wo, wg, wu, wd, parts, normed, xs, cots, mids, owns, act, ggu, ffn, back, split,
    w_sem, x_sem, cot_sem, normed_sem, mid_sem, own_sem, act_sem, ffn_sem,
):
    rows, features = x.shape
    hidden = w_gate.shape[1]
    count, per, groups = rows // hop, chunk // hop, rows // chunk
    tile_f, tile_d = tile_of(hidden, 256), tile_of(features, 256)
    tiles_f, tiles_d = hidden // tile_f, features // tile_d
    half_f, half_d = -(-tiles_f // 2), -(-tiles_d // 2)
    lag = size - 1 + per - 1
    ahead, part_slots = 3 * per // 4, parts.shape[0]
    ticks = max(per * groups + lag, count + size)

    def part(c):
        slot = lax.rem(lax.div(c, per), part_slots)
        return parts[slot, pl.ds(pl.multiple_of(lax.rem(c, per) * hop, hop), hop), :]

    sums = Sums(size, count, part, low, high, sent, (low_send, low_recv, high_send, high_recv))
    loads = [
        pltpu.make_async_copy(a, b, w_sem.at[i])
        for i, (a, b) in enumerate(((w_out, wo), (w_gate, wg), (w_up, wu), (w_down, wd)))
    ]
    for load in loads:
        load.start()

    def load_x(c):
        slot = lax.rem(c, 2)
        return pltpu.make_async_copy(x.at[pl.ds(c * hop, hop)], xs.at[slot], x_sem.at[slot])

    def load_cot(g):
        return pltpu.make_async_copy(cot.at[pl.ds(g * chunk, chunk)], cots, cot_sem)

    def save_normed(c):
        at, q = lax.rem(lax.div(c, per), 2), lax.rem(c, per)
        return pltpu.make_async_copy(
            normed.at[at, pl.ds(q * hop, hop)], normed_o.at[pl.ds(c * hop, hop)], normed_sem.at[at, q]
        )

    def save_mid(c):
        slot = lax.rem(c, 2)
        return pltpu.make_async_copy(mids.at[slot], middle_o.at[pl.ds(c * hop, hop)], mid_sem.at[slot])

    def save_own(c):
        slot = lax.rem(c, 2)
        return pltpu.make_async_copy(owns.at[slot], own_o.at[pl.ds(c * hop, hop)], own_sem.at[slot])

    def save_act(g):
        return [
            pltpu.make_async_copy(a, b.at[pl.ds(g * chunk, chunk)], act_sem.at[i])
            for i, (a, b) in enumerate(((act, act_o), (ggu, ggu_o)))
        ]

    def save_ffn(g):
        part = pl.ds(g * chunk, chunk)
        return [
            pltpu.make_async_copy(split, ffn_o.at[:, part], ffn_sem.at[0]),
            pltpu.make_async_copy(back, back_o.at[part], ffn_sem.at[1]),
        ]

    def project(g):
        at = lax.rem(g, part_slots)
        lhs = mixed[:, pl.ds(pl.multiple_of(g * chunk, chunk), chunk)]

        def one(j, _):
            cols = pl.ds(pl.multiple_of(j * tile_d, tile_d), tile_d)
            parts[at, :, cols] = lax.dot_general(
                lhs, wo[:, cols], (((0,), (0,)), ((), ())), preferred_element_type=F32
            ).astype(BF)
            return 0

        lax.fori_loop(0, tiles_d, one, 0)

    load_x(0).start()
    load_cot(0).start()
    square_o[...] = jnp.zeros_like(square_o)
    loads[0].wait()
    project(0)
    sums.barrier()

    def finish(c):
        slot = lax.rem(c, 2)
        load_x(c).wait()

        @pl.when(c + 1 < count)
        def _():
            load_x(c + 1).start()

        @pl.when(c >= 2)
        def _():
            save_mid(c - 2).wait()
            save_own(c - 2).wait()

        @pl.when(c >= 2 * per)
        def _():
            save_normed(c - 2 * per).wait()

        kept = keep[pl.ds(pl.multiple_of(c * hop, hop), hop), :]

        out = kept * sums.total(c)
        square_o[...] += jnp.sum(out * out, 0, keepdims=True)
        mids[slot] = xs[slot].astype(F32) + out
        mid = mids[slot]
        own_columns(size, mid, lambda piece: owns.__setitem__(slot, piece))
        save_own(c).start()
        inv = lax.rsqrt(jnp.sum(mid * mid, 1, keepdims=True) / features + epsilon)
        at = lax.rem(lax.div(c, per), 2)
        normed[at, pl.ds(pl.multiple_of(lax.rem(c, per) * hop, hop), hop), :] = (
            mid * inv * gain[1:2, :]
        ).astype(BF)
        save_mid(c).start()
        save_normed(c).start()

    def inner(g, lo, hi):
        at = lax.rem(g, 2)
        kept = keep[pl.ds(pl.multiple_of(g * chunk, chunk), chunk), :]

        def one(j, _):
            cols = pl.ds(pl.multiple_of(j * tile_f, tile_f), tile_f)
            gate = dot(normed[at], wg[:, cols])
            up = dot(normed[at], wu[:, cols])
            grad = dot_nt(cots[...], wd[cols, :]) * kept
            sig = jax.nn.sigmoid(gate)
            silu = gate * sig
            act[:, cols] = (silu * up * kept).astype(BF)
            ggu[:, cols] = (grad * up * (sig + silu * (1.0 - sig))).astype(BF)
            cols = pl.ds(pl.multiple_of(hidden + j * tile_f, tile_f), tile_f)
            ggu[:, cols] = (grad * silu).astype(BF)
            return 0

        lax.fori_loop(lo, hi, one, 0)

    def outer(g, lo, hi):
        def one(j, _):
            cols = pl.ds(pl.multiple_of(j * tile_d, tile_d), tile_d)
            ffn[:, cols] = dot(act[...], wd[:, cols]).astype(BF)
            back[:, cols] = (
                dot_nt(ggu[:, :hidden], wg[cols, :]) + dot_nt(ggu[:, hidden:], wu[cols, :])
            ).astype(BF)
            return 0

        lax.fori_loop(lo, hi, one, 0)

    def tick(k, _):
        sums.tick(k)
        c = k - (size - 1)

        @pl.when((c >= 0) & (c < count))
        def _():
            finish(c)

        later = k + ahead

        @pl.when((lax.rem(later, per) == 0) & (later < count))
        def _():
            project(lax.div(later, per))

        s = k - lag
        g, stage = lax.div(s, per), lax.rem(s, per)
        going = (s >= 0) & (g < groups)

        first, second, third, fourth = (stage == i * per // 4 for i in range(4))

        @pl.when(going & first)
        def _():
            @pl.when(g == 0)
            def _():
                for load in loads[1:]:
                    load.wait()

            load_cot(g).wait()

            @pl.when(g > 0)
            def _():
                for copy in save_act(g - 1):
                    copy.wait()

        @pl.when(going & (first | second))
        def _():
            inner(g, jnp.where(first, 0, half_f), jnp.where(first, half_f, tiles_f))

        @pl.when(going & second)
        def _():
            for copy in save_act(g):
                copy.start()

            @pl.when(g + 1 < groups)
            def _():
                load_cot(g + 1).start()

        @pl.when(going & third & (g > 0))
        def _():
            for copy in save_ffn(g - 1):
                copy.wait()

        @pl.when(going & (third | fourth))
        def _():
            outer(g, jnp.where(third, 0, half_d), jnp.where(third, half_d, tiles_d))

        @pl.when(going & fourth)
        def _():
            for j in range(size):
                split[j] = ffn[:, j * (features // size) : (j + 1) * (features // size)]
            for copy in save_ffn(g):
                copy.start()

        return 0

    lax.fori_loop(0, ticks, tick, 0)
    for copy in save_act(groups - 1) + save_ffn(groups - 1):
        copy.wait()
    for c in range(count - 2, count):
        save_mid(c).wait()
        save_own(c).wait()
    for c in range(count - 2 * per, count):
        save_normed(c).wait()


def feed_forward(size, mixed, keep, gain, w_out, w_gate, w_up, w_down, x, cot, chunk, hop):
    rows, features = x.shape
    hidden = w_gate.shape[1]
    per = chunk // hop
    anywhere, vmem = pl.BlockSpec(memory_space=pl.ANY), pl.BlockSpec(memory_space=pltpu.VMEM)
    shape = jax.ShapeDtypeStruct
    return pl.pallas_call(
        functools.partial(ffn_kernel, size, hop, chunk),
        in_specs=[vmem] * 3 + [anywhere] * 6,
        out_specs=[anywhere] * 7 + [vmem],
        out_shape=[
            shape((rows, features), BF),
            shape((rows, hidden), BF),
            shape((rows, 2 * hidden), BF),
            shape((size, rows, features // size), BF),
            shape((rows, features), BF),
            shape((rows, features), F32),
            shape((rows, features // size), F32),
            shape((1, features), F32),
        ],
        scratch_shapes=sum_scratch(size, hop, features)
        + [
            pltpu.VMEM(w_out.shape, BF),
            pltpu.VMEM(w_gate.shape, BF),
            pltpu.VMEM(w_up.shape, BF),
            pltpu.VMEM(w_down.shape, BF),
            pltpu.VMEM((-(-(per + size - 2 + 3 * per // 4) // per), chunk, features), BF),
            pltpu.VMEM((2, chunk, features), BF),
            pltpu.VMEM((2, hop, features), BF),
            pltpu.VMEM((chunk, features), BF),
            pltpu.VMEM((2, hop, features), F32),
            pltpu.VMEM((2, hop, features // size), F32),
            pltpu.VMEM((chunk, hidden), BF),
            pltpu.VMEM((chunk, 2 * hidden), BF),
            pltpu.VMEM((chunk, features), BF),
            pltpu.VMEM((chunk, features), BF),
            pltpu.VMEM((size, chunk, features // size), BF),
            pltpu.SemaphoreType.DMA((4,)),
            pltpu.SemaphoreType.DMA((2,)),
            pltpu.SemaphoreType.DMA,
            pltpu.SemaphoreType.DMA((2, per)),
            pltpu.SemaphoreType.DMA((2,)),
            pltpu.SemaphoreType.DMA((2,)),
            pltpu.SemaphoreType.DMA((2,)),
            pltpu.SemaphoreType.DMA((2,)),
        ],
        compiler_params=pltpu.CompilerParams(
            collective_id=1, has_side_effects=True, vmem_limit_bytes=VMEM_LIMIT
        ),
        cost_estimate=pl.CostEstimate(
            flops=2 * rows * features * (6 * hidden + w_out.shape[0]),
            bytes_accessed=80 << 20,
            transcendentals=rows * hidden,
        ),
        name="feed_forward",
    )(mixed, keep, gain, w_out, w_gate, w_up, w_down, x, cot)


def back_kernel(
    size, hop, chunk,
    parts, keep, gain, w_out, middle, cot, act,
    own_o, grad_low_o, mixed_o, gain_o, down_o,
    low, high, sent, low_send, low_recv, high_send, high_recv,
    wo, mids, cots, acts, owns, grads_low, tiles,
    load_sem, mid_sem, own_sem, grad_low_sem, tile_sem,
):
    rows, features = middle.shape
    count, per, groups = rows // hop, chunk // hop, rows // chunk
    tile = tile_of(features, 256)
    tile_count = features // tile
    ticks = max(count + size, per * (groups - 1) + size - 1 + per, tile_count + 1)

    def part(c):
        return parts[pl.ds(pl.multiple_of(c * hop, hop), hop), :]

    sums = Sums(size, count, part, low, high, sent, (low_send, low_recv, high_send, high_recv))
    loads = [
        pltpu.make_async_copy(a, b, load_sem.at[i])
        for i, (a, b) in enumerate(((cot, cots), (w_out, wo), (act, acts)))
    ]

    def load_mid(c):
        slot = lax.rem(c, 2)
        return pltpu.make_async_copy(
            middle.at[pl.ds(c * hop, hop)], mids.at[slot], mid_sem.at[slot]
        )

    def save_own(c):
        slot = lax.rem(c, 2)
        return pltpu.make_async_copy(owns.at[slot], own_o.at[pl.ds(c * hop, hop)], own_sem.at[slot])

    def save_low(c):
        q = lax.rem(c, per)
        return pltpu.make_async_copy(
            grads_low.at[pl.ds(q * hop, hop)], grad_low_o.at[pl.ds(c * hop, hop)], grad_low_sem.at[q]
        )

    def save_tile(j):
        slot = lax.rem(j, 2)
        return pltpu.make_async_copy(
            tiles.at[slot], down_o.at[pl.ds(j * tile, tile)], tile_sem.at[slot]
        )

    load_mid(0).start()
    for load in loads:
        load.start()
    gain_o[...] = jnp.zeros_like(gain_o)
    sums.barrier()

    def finish(c):
        slot = lax.rem(c, 2)
        load_mid(c).wait()

        @pl.when(c + 1 < count)
        def _():
            load_mid(c + 1).start()

        @pl.when(c >= 2)
        def _():
            save_own(c - 2).wait()

        @pl.when(c >= per)
        def _():
            save_low(c - per).wait()

        chunk_rows = pl.ds(pl.multiple_of(c * hop, hop), hop)
        kept = keep[chunk_rows, :]
        mid = mids[slot]
        inv = lax.rsqrt(jnp.sum(mid * mid, 1, keepdims=True) / features + epsilon)
        hat = mid * inv

        total = sums.total(c)
        gain_o[...] += jnp.sum(total * hat, 0, keepdims=True)
        weighted = total * gain[1:2, :]
        mean = jnp.sum(weighted * hat, 1, keepdims=True) / features
        mids[slot] = cots[chunk_rows, :].astype(F32) + inv * (weighted - hat * mean)
        grad = mids[slot]
        own_columns(size, grad, lambda piece: owns.__setitem__(slot, piece))
        grads_low[pl.ds(pl.multiple_of(lax.rem(c, per) * hop, hop), hop), :] = (kept * grad).astype(
            BF
        )
        save_own(c).start()
        save_low(c).start()

    def weight_tile(j):
        slot = lax.rem(j, 2)

        @pl.when(j >= 2)
        def _():
            save_tile(j - 2).wait()

        cols = pl.ds(pl.multiple_of(j * tile, tile), tile)
        tiles[slot] = dot(flip(cots[:, cols]).astype(BF), acts[...]).astype(BF)
        save_tile(j).start()

    def tick(k, _):
        sums.tick(k)
        c = k - (size - 1)

        @pl.when(k == 1)
        def _():
            for load in loads:
                load.wait()

        @pl.when((c >= 0) & (c < count))
        def _():
            finish(c)

            @pl.when(lax.rem(c, per) == per - 1)
            def _():
                g = lax.div(c, per)
                mixed_o[:, pl.ds(pl.multiple_of(g * chunk, chunk), chunk)] = dot_nt(
                    wo[...], grads_low[...]
                ).astype(BF)

        @pl.when((k >= 1) & (k <= tile_count))
        def _():
            weight_tile(k - 1)

        return 0

    lax.fori_loop(0, ticks, tick, 0)
    for c in range(count - 2, count):
        save_own(c).wait()
    for c in range(count - per, count):
        save_low(c).wait()
    for j in range(max(tile_count - 2, 0), tile_count):
        save_tile(j).wait()


def norm_back(size, parts, keep, gain, w_out, middle, cot, act, chunk, hop, after):
    rows, features = middle.shape
    per = chunk // hop
    anywhere, vmem = pl.BlockSpec(memory_space=pl.ANY), pl.BlockSpec(memory_space=pltpu.VMEM)
    shape, dma = jax.ShapeDtypeStruct, pltpu.SemaphoreType.DMA

    def kernel(*refs):
        back_kernel(size, hop, chunk, *refs[:7], *refs[7 + len(after) :])

    return pl.pallas_call(
        kernel,
        in_specs=[vmem] * 3 + [anywhere] * (4 + len(after)),
        out_specs=[anywhere] * 2 + [vmem] * 2 + [anywhere],
        out_shape=[
            shape((rows, features // size), F32),
            shape((rows, features), BF),
            shape((w_out.shape[0], rows), BF),
            shape((1, features), F32),
            shape((features, act.shape[1]), BF),
        ],
        scratch_shapes=sum_scratch(size, hop, features)
        + [
            pltpu.VMEM(w_out.shape, BF),
            pltpu.VMEM((2, hop, features), F32),
            pltpu.VMEM(cot.shape, BF),
            pltpu.VMEM(act.shape, BF),
            pltpu.VMEM((2, hop, features // size), F32),
            pltpu.VMEM((chunk, features), BF),
            pltpu.VMEM((2, tile_of(features, 256), act.shape[1]), BF),
            dma((3,)),
            dma((2,)),
            dma((2,)),
            dma((per,)),
            dma((2,)),
        ],
        compiler_params=pltpu.CompilerParams(
            collective_id=2, has_side_effects=True, vmem_limit_bytes=VMEM_LIMIT
        ),
        cost_estimate=pl.CostEstimate(
            flops=2 * rows * features * (w_out.shape[0] + act.shape[1]),
            bytes_accessed=40 << 20,
            transcendentals=rows,
        ),
        name="norm_back",
    )(parts, keep, gain, w_out, middle, cot, act, *after)


def greet(peers):
    barrier = pltpu.get_barrier_semaphore()
    for peer in peers:
        pl.semaphore_signal(barrier, inc=1, device_id=peer, device_id_type=MESH_ID)
    pl.semaphore_wait(barrier, len(peers))


def others(axis, size):
    here = lax.axis_index(axis)
    return [{axis: lax.rem(here + i, size)} for i in range(1, size)]


class Gather:
    def __init__(self, size, groups, chunk, own, blocks, sems):
        self.size, self.groups, self.chunk = size, groups, chunk
        self.own, self.blocks = own, blocks
        self.up_send, self.up_recv, self.down_send, self.down_recv, self.own_sem = sems
        self.steps = size - 1
        self.ticks = groups * self.steps + 1
        self.here = lax.axis_index("tensor")

    def load(self, g):
        part = pl.ds(g * self.chunk, self.chunk)
        return pltpu.make_async_copy(
            self.own.at[part], self.blocks.at[self.here, part], self.own_sem.at[g]
        )

    def load_all(self):
        for g in range(self.groups):
            self.load(g).start()

    def move(self, g, s, owner, peer, send, recv):
        block = self.blocks.at[jnp.clip(owner, 0, self.size - 1), pl.ds(g * self.chunk, self.chunk)]
        return pltpu.make_async_remote_copy(
            src_ref=block,
            dst_ref=block,
            send_sem=send.at[g, s],
            recv_sem=recv.at[g, s],
            device_id={"tensor": peer},
            device_id_type=MESH_ID,
        )

    def up(self, g, s):
        return self.move(g, s, self.here - s, self.here + 1, self.up_send, self.up_recv)

    def down(self, g, s):
        return self.move(g, s, self.here + s, self.here - 1, self.down_send, self.down_recv)

    def each(self, g, s, act):
        @pl.when((self.here >= s) & (self.here < self.size - 1))
        def _():
            act(self.up(g, s))

        @pl.when((self.here + s < self.size) & (self.here > 0))
        def _():
            act(self.down(g, s))

    def send(self, g, s):
        self.each(g, s, lambda copy: copy.start())

    def receive(self, g, s):
        @pl.when(self.here - 1 - s >= 0)
        def _():
            self.up(g, s).wait_recv()

        @pl.when(self.here + 1 + s < self.size)
        def _():
            self.down(g, s).wait_recv()

    def begin(self):
        self.load(0).wait()
        self.send(0, 0)

    def tick(self, k, then):
        g, s = lax.div(k, self.steps), lax.rem(k, self.steps)

        @pl.when((s > 0) & (g < self.groups))
        def _():
            self.receive(g, s - 1)
            self.send(g, s)

        @pl.when((s == self.steps - 1) & (g + 1 < self.groups))
        def _():
            self.load(g + 1).wait()
            self.send(g + 1, 0)

        @pl.when((s == 0) & (g > 0) & (g <= self.groups))
        def _():
            self.receive(g - 1, self.steps - 1)
            then(g - 1)

    def drain(self):
        for g in range(self.groups):
            for s in range(self.steps):
                self.each(g, s, lambda copy: copy.wait_send())


def gather_scratch(size, rows, width, chunk):
    dma, groups = pltpu.SemaphoreType.DMA, rows // chunk
    return [pltpu.VMEM((size, rows, width), BF)] + [dma((groups, size - 1))] * 4 + [dma((groups,))]


class Scatter:
    def __init__(self, size, groups, chunk, parts, ups, downs, sems):
        self.size, self.groups, self.chunk = size, groups, chunk
        self.parts, self.ups, self.downs = parts, ups, downs
        self.up_send, self.up_recv, self.down_send, self.down_recv = sems
        self.count = (size - 1) * groups
        self.here = lax.axis_index("tensor")

    def rows(self, m):
        return pl.ds(pl.multiple_of(lax.rem(m, self.groups) * self.chunk, self.chunk), self.chunk)

    def up(self, m, first):
        owner = self.size - 1 - lax.div(m, self.groups)
        return pltpu.make_async_remote_copy(
            src_ref=self.parts.at[owner, self.rows(m)] if first else self.ups.at[m],
            dst_ref=self.ups.at[m],
            send_sem=self.up_send.at[m],
            recv_sem=self.up_recv.at[m],
            device_id={"tensor": self.here + 1},
            device_id_type=MESH_ID,
        )

    def down(self, m, first):
        owner = lax.div(m, self.groups)
        return pltpu.make_async_remote_copy(
            src_ref=self.parts.at[owner, self.rows(m)] if first else self.downs.at[m],
            dst_ref=self.downs.at[m],
            send_sem=self.down_send.at[m],
            recv_sem=self.down_recv.at[m],
            device_id={"tensor": self.here - 1},
            device_id_type=MESH_ID,
        )

    def tick(self, k):
        bottom, top = self.here == 0, self.here == self.size - 1
        m = k - self.here
        owner = self.size - 1 - lax.div(m, self.groups)

        @pl.when((m >= 0) & (owner > self.here))
        def _():
            @pl.when(bottom)
            def _():
                self.up(m, True).start()

            @pl.when(jnp.logical_not(bottom))
            def _():
                self.up(m, False).wait_recv()
                self.ups[m] = add_low(self.ups[m], self.parts[owner, self.rows(m), :])
                self.up(m, False).start()

        n = k - (self.size - 1 - self.here)
        below = lax.div(n, self.groups)

        @pl.when((n >= 0) & (below < self.here))
        def _():
            @pl.when(top)
            def _():
                self.down(n, True).start()

            @pl.when(jnp.logical_not(top))
            def _():
                self.down(n, False).wait_recv()
                self.downs[n] = add_low(self.downs[n], self.parts[below, self.rows(n), :])
                self.down(n, False).start()

    def finish(self, total, then):
        here = self.here

        def last(c, _):
            part = self.rows(c)
            m, n = (self.size - 1 - here) * self.groups + c, here * self.groups + c
            total[...] = self.parts[here, part, :].astype(F32)

            @pl.when(here > 0)
            def _():
                self.up(m, False).wait_recv()
                total[...] += self.ups[m].astype(F32)

            @pl.when(here < self.size - 1)
            def _():
                self.down(n, False).wait_recv()
                total[...] += self.downs[n].astype(F32)

            then(part, total[...])
            return 0

        lax.fori_loop(0, self.groups, last, 0)

        def drain(m, _):
            @pl.when(self.size - 1 - lax.div(m, self.groups) > here)
            def _():
                self.up(m, False).wait_send()

            @pl.when(lax.div(m, self.groups) < here)
            def _():
                self.down(m, False).wait_send()

            return 0

        lax.fori_loop(0, self.count, drain, 0)


def scatter_scratch(size, rows, width, chunk):
    count = (size - 1) * (rows // chunk)
    return [
        pltpu.VMEM((size, rows, width), BF),
        pltpu.VMEM((count, chunk, width), BF),
        pltpu.VMEM((count, chunk, width), BF),
        pltpu.VMEM((chunk, width), F32),
    ] + [pltpu.SemaphoreType.DMA((count,))] * 4


def turn(u, cos_t, sin_t):
    lower, upper = u[: HD // 2], u[HD // 2 :]
    return jnp.concatenate([lower * cos_t - upper * sin_t, upper * cos_t + lower * sin_t], 0)


def flip(a):
    return a.astype(F32).T


def key_blocks(g, chunk, rows, keys, key_rows):
    start = lax.axis_index("context") * rows + g * chunk
    free = jnp.minimum(start + 1, min(LEAST_VALID, keys))
    last = jnp.minimum(start + chunk + PIC - 1, keys)
    return lax.div(free, key_rows), lax.div(last + key_rows - 1, key_rows)


def attend_kernel(
    size, contexts, chunk, key_rows,
    own, own_cot, gain_pair, cos_tab, sin_tab, mask, starts, w_query, w_key_t, w_value_t,
    x_o, normed_o, inv_o, gain_o, q, kv_o, kend, keep_o, cot_o, mixed_o, lse_o,
    xs, up_send, up_recv, down_send, down_recv, own_sem,
    blocks, up_send_c, up_recv_c, down_send_c, down_recv_c, own_sem_c,
    gains, full, normed, full_c, kv, wq, wk, wv, keys_in_rows, acc, mx, sm,
    gain_send, gain_recv, kv_send, kv_recv, w_sem, out_sem, kv_sem, cot_sem,
):
    here, place = lax.axis_index("tensor"), lax.axis_index("context")
    rows, width = own.shape
    features = size * width
    groups = rows // chunk
    heads, kvs = w_query.shape[1] // HD, w_key_t.shape[0] // HD
    keys, group = contexts * rows, heads // kvs
    units = kvs * groups
    line = Gather(
        size, groups, chunk, own, xs, (up_send, up_recv, down_send, down_recv, own_sem)
    )
    line_c = Gather(
        size, groups, chunk, own_cot, blocks,
        (up_send_c, up_recv_c, down_send_c, down_recv_c, own_sem_c),
    )
    loads = [
        pltpu.make_async_copy(a, b, w_sem.at[i])
        for i, (a, b) in enumerate(((w_query, wq), (w_key_t, wk), (w_value_t, wv)))
    ]
    line.load_all()
    for load in loads:
        load.start()
    gains[here] = jnp.zeros_like(gains[here])
    gains[here, 0:2] = gain_pair[...]
    tensor_peers, context_peers = others("tensor", size), others("context", contexts)
    greet(tensor_peers + context_peers)

    def gain_copy(i):
        return pltpu.make_async_remote_copy(
            src_ref=gains.at[here],
            dst_ref=gains.at[here],
            send_sem=gain_send.at[i],
            recv_sem=gain_recv.at[i],
            device_id=tensor_peers[i],
            device_id_type=MESH_ID,
        )

    def kv_copy(g, i):
        part = kv.at[:, :, pl.ds(pl.multiple_of(place * rows + g * chunk, chunk), chunk)]
        return pltpu.make_async_remote_copy(
            src_ref=part,
            dst_ref=part,
            send_sem=kv_send.at[g, i],
            recv_sem=kv_recv.at[g, i],
            device_id=context_peers[i],
            device_id_type=MESH_ID,
        )

    line.begin()
    line_c.load_all()
    for i in range(size - 1):
        gain_copy(i).start()

    length = jnp.sum(mask[...].astype(F32), 1, keepdims=True).astype(jnp.int32)
    position = lax.broadcasted_iota(jnp.int32, (1, rows), 1) + place * rows
    last = position
    for k in range(starts.shape[1]):
        start = starts[:, k : k + 1]
        inside = (position >= start) & (position < start + PIC)
        last = jnp.maximum(last, jnp.where(inside, start + PIC - 1, 0))
    kend[...] = jnp.minimum(last + 1, length)
    down_rows = lax.broadcasted_iota(jnp.int32, (rows, 1), 0) + place * rows
    keep_o[...] = jnp.where(down_rows < length, 1.0, 0.0)

    def save(g):
        part = pl.ds(g * chunk, chunk)
        return [
            pltpu.make_async_copy(full, x_o.at[part], out_sem.at[0]),
            pltpu.make_async_copy(normed, normed_o.at[part], out_sem.at[1]),
        ]

    def project(g):
        part = pl.ds(pl.multiple_of(g * chunk, chunk), chunk)

        @pl.when(g == 0)
        def _():
            for load in loads:
                load.wait()
            for i in range(size - 1):
                gain_copy(i).wait_recv()
            gain_o[...] = jnp.concatenate([gains[j] for j in range(size)], 1)

        @pl.when(g > 0)
        def _():
            for copy in save(g - 1):
                copy.wait()

        full[...] = jnp.concatenate([xs[j, part, :] for j in range(size)], 1)
        stream = full[...].astype(F32)
        inv = lax.rsqrt(jnp.sum(stream * stream, 1, keepdims=True) / features + epsilon)
        inv_o[part, :] = inv
        normed[...] = (stream * inv * gain_o[0:1, :]).astype(BF)
        for copy in save(g):
            copy.start()
        cos_t, sin_t = cos_tab[:, part], sin_tab[:, part]
        mine = pl.ds(pl.multiple_of(place * rows + g * chunk, chunk), chunk)
        key = dot_nt(wk[...], normed[...])
        value = dot_nt(wv[...], normed[...])
        for h in range(kvs):
            kv[h, :, mine] = turn(key[h * HD : (h + 1) * HD], cos_t, sin_t).astype(BF)
            kv[kvs + h, :, mine] = value[h * HD : (h + 1) * HD].astype(BF)
        for i in range(contexts - 1):
            kv_copy(g, i).start()
        query = dot(normed[...], wq[...]).T
        for h in range(heads):
            q[h, :, part] = turn(query[h * HD : (h + 1) * HD], cos_t, sin_t).astype(BF)

    def save_cot(g):
        return pltpu.make_async_copy(full_c, cot_o.at[pl.ds(g * chunk, chunk)], cot_sem)

    def join(g):
        @pl.when(g > 0)
        def _():
            save_cot(g - 1).wait()

        part = pl.ds(pl.multiple_of(g * chunk, chunk), chunk)
        full_c[...] = jnp.concatenate([blocks[j, part, :] for j in range(size)], 1)
        save_cot(g).start()

    save_kv = pltpu.make_async_copy(kv, kv_o, kv_sem)

    def meet():
        for g in range(groups):
            for i in range(contexts - 1):
                kv_copy(g, i).wait_recv()
        save_kv.start()
        for h in range(kvs):
            keys_in_rows[h] = flip(kv[h]).astype(BF)

    def unit(u):
        pair, g = lax.div(u, groups), lax.rem(u, groups)
        part = pl.ds(pl.multiple_of(g * chunk, chunk), chunk)
        free, last = key_blocks(g, chunk, rows, keys, key_rows)
        acc[...] = jnp.zeros_like(acc)
        sm[...] = jnp.zeros_like(sm)
        mx[...] = jnp.full_like(mx, LOWEST)
        limit = kend[:, part]

        def step(masked, i, _):
            at = pl.multiple_of(i * key_rows, key_rows)
            k_blk = keys_in_rows[pair, pl.ds(at, key_rows), :]
            v_blk = kv[kvs + pair, :, pl.ds(at, key_rows)]
            if masked:
                keep = (lax.broadcasted_iota(jnp.int32, (key_rows, chunk), 0) + at) < limit
            for h in range(group):
                s = dot(k_blk, q[pair * group + h, :, part])
                if masked:
                    s = jnp.where(keep, s, LOWEST)
                old = mx[h]
                new = jnp.maximum(old, jnp.max(s, 0, keepdims=True))
                p = jnp.exp2(s * SCALE2 - new * SCALE2)
                alpha = jnp.exp2((old - new) * SCALE2)
                mx[h] = new
                sm[h] = sm[h] * alpha + jnp.sum(p, 0, keepdims=True)
                acc[h] = acc[h] * alpha + dot(v_blk, p.astype(BF))
            return 0

        lax.fori_loop(0, free, functools.partial(step, False), 0)
        lax.fori_loop(free, last, functools.partial(step, True), 0)
        for h in range(group):
            mixed_o[pair * group + h, :, part] = (acc[h] / sm[h]).astype(BF)
            lse_o[pair * group + h, :, part] = mx[h] * SCALE2 + jnp.log2(sm[h])

    turnover = line.ticks - 1

    def tick(k, _):
        @pl.when(k == turnover)
        def _():
            line_c.begin()

        line.tick(k, project)

        @pl.when(k >= turnover)
        def _():
            line_c.tick(k - turnover, join)

        u = k - line.ticks

        @pl.when(u == 0)
        def _():
            meet()

        @pl.when((u >= 0) & (u < units))
        def _():
            unit(u)

        return 0

    lax.fori_loop(0, max(turnover + line_c.ticks, line.ticks + units), tick, 0)
    for copy in [*save(groups - 1), save_cot(groups - 1), save_kv]:
        copy.wait()
    for i in range(size - 1):
        gain_copy(i).wait_send()
    line.drain()
    line_c.drain()
    for g in range(groups):
        for i in range(contexts - 1):
            kv_copy(g, i).wait_send()


def attend_forward(
    axes, own, own_cot, gain_pair, cos_tab, sin_tab, mask, starts, w_query, w_key_t, w_value_t, chunk
):
    size, contexts = axes["tensor"], axes["context"]
    rows, width = own.shape
    features, groups = size * width, rows // chunk
    heads, kvs = w_query.shape[1] // HD, w_key_t.shape[0] // HD
    keys, group = contexts * rows, heads // kvs
    key_rows = min(KEY_ROWS_FWD, keys)
    anywhere, vmem = pl.BlockSpec(memory_space=pl.ANY), pl.BlockSpec(memory_space=pltpu.VMEM)
    shape, dma = jax.ShapeDtypeStruct, pltpu.SemaphoreType.DMA
    return pl.pallas_call(
        functools.partial(attend_kernel, size, contexts, chunk, key_rows),
        in_specs=[anywhere] * 2 + [vmem] * 5 + [anywhere] * 3,
        out_specs=[anywhere] * 2 + [vmem] * 3 + [anywhere] + [vmem] * 2 + [anywhere] + [vmem] * 2,
        out_shape=[
            shape((rows, features), BF),
            shape((rows, features), BF),
            shape((rows, 1), F32),
            shape((8, features), F32),
            shape((heads, HD, rows), BF),
            shape((2 * kvs, HD, keys), BF),
            shape((1, rows), jnp.int32),
            shape((rows, 1), F32),
            shape((rows, features), BF),
            shape((heads, HD, rows), BF),
            shape((heads, 1, rows), F32),
        ],
        scratch_shapes=gather_scratch(size, rows, width, chunk)
        + gather_scratch(size, rows, width, chunk)
        + [
            pltpu.VMEM((size, 8, width), F32),
            pltpu.VMEM((chunk, features), BF),
            pltpu.VMEM((chunk, features), BF),
            pltpu.VMEM((chunk, features), BF),
            pltpu.VMEM((2 * kvs, HD, keys), BF),
            pltpu.VMEM(w_query.shape, BF),
            pltpu.VMEM(w_key_t.shape, BF),
            pltpu.VMEM(w_value_t.shape, BF),
            pltpu.VMEM((kvs, keys, HD), BF),
            pltpu.VMEM((group, HD, chunk), F32),
            pltpu.VMEM((group, 1, chunk), F32),
            pltpu.VMEM((group, 1, chunk), F32),
            dma((size - 1,)),
            dma((size - 1,)),
            dma((groups, max(contexts - 1, 1))),
            dma((groups, max(contexts - 1, 1))),
            dma((3,)),
            dma((2,)),
            dma,
            dma,
        ],
        compiler_params=pltpu.CompilerParams(
            collective_id=3, has_side_effects=True, vmem_limit_bytes=VMEM_LIMIT
        ),
        cost_estimate=pl.CostEstimate(
            flops=2 * rows * features * (heads + 2 * kvs) * HD + 10 * heads * rows * keys * HD,
            bytes_accessed=40 << 20,
            transcendentals=heads * rows * keys,
        ),
        name="attend_forward",
    )(own, own_cot, gain_pair, cos_tab, sin_tab, mask, starts, w_query, w_key_t, w_value_t)


def attend_back_kernel(
    size, contexts, chunk, key_rows,
    ffn, q, kv, kend, do, o, lse, cos_tab, sin_tab, middle, grad_attn, normed,
    grads_o, layer_o, square_o, weights_o,
    parts, ups, downs, total, up_send, up_recv, down_send, down_recv,
    keys_in_rows, values_in_rows, dq, dk, dv, ds_all, p_all, q_all, do_all, mine, out_kv, in_kv,
    grads_in, normed_in, tiles,
    kv_send, kv_recv, part_sem, tile_sem,
):
    heads, _, rows = q.shape
    kvs, keys = kv.shape[0] // 2, kv.shape[2]
    groups, group = rows // chunk, heads // kvs
    units = kvs * groups
    place = lax.axis_index("context")
    line = Scatter(
        size, groups, chunk, parts, ups, downs, (up_send, up_recv, down_send, down_recv)
    )
    loads = [
        pltpu.make_async_copy(a, b, part_sem.at[i])
        for i, (a, b) in enumerate(((ffn, parts), (grad_attn, grads_in), (normed, normed_in)))
    ]
    for load in loads:
        load.start()
    square_o[...] = jnp.zeros_like(square_o)
    peers = others("context", contexts)
    greet(others("tensor", size) + peers)
    loads[0].wait()

    def half(of):
        at = pl.ds(pl.multiple_of(of * rows, rows), rows)
        return dk[at, :].T, dv[at, :].T

    def kv_copy(pair, i):
        return pltpu.make_async_remote_copy(
            src_ref=out_kv.at[pair, i],
            dst_ref=in_kv.at[pair, i],
            send_sem=kv_send.at[pair, i],
            recv_sem=kv_recv.at[pair, i],
            device_id=peers[i],
            device_id_type=MESH_ID,
        )

    def unit(u):
        pair, g = lax.div(u, groups), lax.rem(u, groups)
        part = pl.ds(pl.multiple_of(g * chunk, chunk), chunk)
        free, last = key_blocks(g, chunk, rows, keys, key_rows)
        limit = kend[:, part]

        @pl.when(g == 0)
        def _():
            dk[...] = jnp.zeros_like(dk)
            dv[...] = jnp.zeros_like(dv)

        dq[...] = jnp.zeros_like(dq)
        delta = []
        for h in range(group):
            head = pair * group + h
            cols = slice(h * chunk, (h + 1) * chunk)
            q_all[:, cols] = q[head, :, part]
            do_all[:, cols] = do[head, :, part]
            delta.append(
                jnp.sum(do_all[:, cols].astype(F32) * o[head, :, part].astype(F32), 0, keepdims=True)
            )

        def step(masked, i, _):
            at = pl.multiple_of(i * key_rows, key_rows)
            k_blk = keys_in_rows[pair, pl.ds(at, key_rows), :]
            v_blk = values_in_rows[pair, pl.ds(at, key_rows), :]
            kt_blk = kv[pair, :, pl.ds(at, key_rows)]
            if masked:
                keep = (lax.broadcasted_iota(jnp.int32, (key_rows, chunk), 0) + at) < limit
            for h in range(group):
                cols = slice(h * chunk, (h + 1) * chunk)
                s = dot(k_blk, q_all[:, cols])
                p = jnp.exp2(s * SCALE2 - lse[pair * group + h, :, part])
                if masked:
                    p = jnp.where(keep, p, 0.0)
                dp = dot(v_blk, do_all[:, cols])
                ds = (p * (dp - delta[h])).astype(BF)
                p_all[:, cols] = p.astype(BF)
                ds_all[:, cols] = ds
                dq[h] += dot(kt_blk, ds)
            dk[pl.ds(at, key_rows), :] += dot_nt(ds_all[...], q_all[...])
            dv[pl.ds(at, key_rows), :] += dot_nt(p_all[...], do_all[...])
            return 0

        lax.fori_loop(0, free, functools.partial(step, False), 0)
        lax.fori_loop(free, last, functools.partial(step, True), 0)
        for h in range(group):
            grads_o[pair * group + h, :, part] = turn(
                dq[h] * SCALE, cos_tab[:, part], -sin_tab[:, part]
            ).astype(BF)

        @pl.when(g == groups - 1)
        def _():
            for i in range(contexts - 1):
                key, value = half(peers[i]["context"])
                out_kv[pair, i, 0] = key.astype(BF)
                out_kv[pair, i, 1] = value.astype(BF)
                kv_copy(pair, i).start()
            mine[pair, 0], mine[pair, 1] = half(place)

    def join():
        for pair in range(kvs):
            key, value = mine[pair, 0], mine[pair, 1]
            for i in range(contexts - 1):
                kv_copy(pair, i).wait()
                key = key + in_kv[pair, i, 0].astype(F32)
                value = value + in_kv[pair, i, 1].astype(F32)
            grads_o[heads + pair] = turn(key * SCALE, cos_tab[...], -sin_tab[...]).astype(BF)
            grads_o[heads + kvs + pair] = value.astype(BF)

    features = normed.shape[1]
    tile = tile_of(features, 256)
    tile_count, each = features // tile, 4

    def save_tile(j):
        slot = lax.rem(j, 2)
        return pltpu.make_async_copy(
            tiles.at[slot], weights_o.at[pl.ds(j * tile, tile)], tile_sem.at[slot]
        )

    def weight_tile(j):
        slot = lax.rem(j, 2)

        @pl.when(j >= 2)
        def _():
            save_tile(j - 2).wait()

        cols = pl.ds(pl.multiple_of(j * tile, tile), tile)
        out = dot_nt(flip(grads_in[:, cols]).astype(BF), o[...].reshape(heads * HD, rows))
        into = dot_nt(
            flip(normed_in[:, cols]).astype(BF), grads_o[...].reshape((heads + 2 * kvs) * HD, rows)
        )
        tiles[slot] = jnp.concatenate([out, into], 1).astype(BF)
        save_tile(j).start()

    def tick(k, _):
        line.tick(k)

        @pl.when(k == 0)
        def _():
            for h in range(kvs):
                keys_in_rows[h] = flip(kv[h]).astype(BF)
                values_in_rows[h] = flip(kv[kvs + h]).astype(BF)

        @pl.when(k < units)
        def _():
            unit(k)

        @pl.when(k == units)
        def _():
            join()
            for load in loads[1:]:
                load.wait()

        first = (k - units - 1) * each
        for j in range(each):

            @pl.when((first >= 0) & (first + j < tile_count))
            def _():
                weight_tile(first + j)

        return 0

    lax.fori_loop(0, max(line.count, units + 1 + -(-tile_count // each)), tick, 0)

    def then(part, ffn_out):
        square_o[...] += jnp.sum(ffn_out * ffn_out, 0, keepdims=True)
        layer_o[part, :] = (middle[part, :] + ffn_out).astype(BF)

    line.finish(total, then)
    for j in range(max(tile_count - 2, 0), tile_count):
        save_tile(j).wait()


def attend_backward(
    axes, ffn, q, kv, kend, do, o, lse, cos_tab, sin_tab, middle, grad_attn, normed, chunk, after
):
    size, contexts = axes["tensor"], axes["context"]
    heads, _, rows = q.shape
    kvs, keys = kv.shape[0] // 2, kv.shape[2]
    group, width = heads // kvs, ffn.shape[2]
    key_rows = min(KEY_ROWS_BWD, keys)
    anywhere, vmem = pl.BlockSpec(memory_space=pl.ANY), pl.BlockSpec(memory_space=pltpu.VMEM)
    shape, dma = jax.ShapeDtypeStruct, pltpu.SemaphoreType.DMA
    slots = max(contexts - 1, 1)

    def kernel(*refs):
        attend_back_kernel(size, contexts, chunk, key_rows, *refs[:12], *refs[12 + len(after) :])

    return pl.pallas_call(
        kernel,
        in_specs=[anywhere] + [vmem] * 9 + [anywhere] * (2 + len(after)),
        out_specs=[vmem] * 3 + [anywhere],
        out_shape=[
            shape((heads + 2 * kvs, HD, rows), BF),
            shape((rows, width), BF),
            shape((1, width), F32),
            shape((size * width, (2 * heads + 2 * kvs) * HD), BF),
        ],
        scratch_shapes=scatter_scratch(size, rows, width, chunk)
        + [
            pltpu.VMEM((kvs, keys, HD), BF),
            pltpu.VMEM((kvs, keys, HD), BF),
            pltpu.VMEM((group, HD, chunk), F32),
            pltpu.VMEM((keys, HD), F32),
            pltpu.VMEM((keys, HD), F32),
            pltpu.VMEM((key_rows, group * chunk), BF),
            pltpu.VMEM((key_rows, group * chunk), BF),
            pltpu.VMEM((HD, group * chunk), BF),
            pltpu.VMEM((HD, group * chunk), BF),
            pltpu.VMEM((kvs, 2, HD, rows), F32),
            pltpu.VMEM((kvs, slots, 2, HD, rows), BF),
            pltpu.VMEM((kvs, slots, 2, HD, rows), BF),
            pltpu.VMEM(grad_attn.shape, BF),
            pltpu.VMEM(normed.shape, BF),
            pltpu.VMEM((2, tile_of(size * width, 256), (2 * heads + 2 * kvs) * HD), BF),
            dma((kvs, slots)),
            dma((kvs, slots)),
            dma((3,)),
            dma((2,)),
        ],
        compiler_params=pltpu.CompilerParams(
            collective_id=6, has_side_effects=True, vmem_limit_bytes=VMEM_LIMIT
        ),
        cost_estimate=pl.CostEstimate(
            flops=16 * heads * rows * keys * HD,
            bytes_accessed=16 << 20,
            transcendentals=heads * rows * keys,
        ),
        name="attend_backward",
    )(ffn, q, kv, kend, do, o, lse, cos_tab, sin_tab, middle, grad_attn, normed, *after)


def input_kernel(
    axes, chunk,
    grads, inv, gain, keep, attn_square, gain_rows, ffn_square, gain_own, x_own, grad_own,
    w_query, w_key_t, w_value_t, x,
    out_o, sum_o,
    parts, ups, downs, total, up_send, up_recv, down_send, down_recv,
    xs, whole, wq, wk, wv, dots, dot_sum, cols, cols_in, world, square,
    dot_send, dot_recv, col_send, col_recv, world_send, world_recv, w_sem, x_sem,
):
    size = axes["tensor"]
    here = lax.axis_index("tensor")
    rows, features = x.shape
    width, groups = features // size, rows // chunk
    nq, nk = w_query.shape[1], w_key_t.shape[0]
    line = Scatter(
        size, groups, chunk, parts, ups, downs, (up_send, up_recv, down_send, down_recv)
    )
    loads = [
        pltpu.make_async_copy(a, b, w_sem.at[i])
        for i, (a, b) in enumerate(((w_query, wq), (w_key_t, wk), (w_value_t, wv)))
    ]

    def load_x(c):
        slot = lax.rem(c, 2)
        return pltpu.make_async_copy(x.at[pl.ds(c * chunk, chunk)], xs.at[slot], x_sem.at[slot])

    for load in loads:
        load.start()
    load_x(0).start()
    contexts, replicas = axes["context"], axes["dp"] * axes["context"]
    spot = lax.axis_index("dp") * contexts + lax.axis_index("context")
    peers = others("tensor", size)
    far = [lax.rem(spot + i, replicas) for i in range(1, replicas)]
    far = [{"dp": lax.div(i, contexts), "context": lax.rem(i, contexts)} for i in far]
    greet(peers + far)
    for load in loads:
        load.wait()
    square[...] = jnp.zeros_like(square)
    row = lax.broadcasted_iota(jnp.int32, (8, width), 0)
    lane = lax.broadcasted_iota(jnp.int32, (8, width), 1)

    def compute(c):
        slot = lax.rem(c, 2)
        part = pl.ds(pl.multiple_of(c * chunk, chunk), chunk)
        load_x(c).wait()

        @pl.when(c + 1 < groups)
        def _():
            load_x(c + 1).start()

        g = flip(grads[:, part]).astype(BF)
        whole[...] = (
            dot_nt(g[:, :nq], wq[...])
            + dot(g[:, nq : nq + nk], wk[...])
            + dot(g[:, nq + nk :], wv[...])
        )
        for j in range(size):
            parts[j, part, :] = whole[:, j * width : (j + 1) * width].astype(BF)

    def add_up(c):
        slot = lax.rem(c, 2)
        part = pl.ds(pl.multiple_of(c * chunk, chunk), chunk)
        stream = xs[slot].astype(F32)
        square[...] += jnp.sum(stream * stream * keep[part, :], 0, keepdims=True)
        moved = whole[...] * (stream * inv[part, :])
        rowsum = jnp.sum(moved * gain[0:1, :], 1, keepdims=True)
        dots[here, :, part] = jnp.broadcast_to(rowsum, (chunk, 128)).T[:8]
        colsum = jnp.sum(moved, 0, keepdims=True)
        for j in range(size):
            piece = jnp.where(row == 0, colsum[:, j * width : (j + 1) * width], 0.0)

            @pl.when(c == 0)
            def _():
                cols[j] = piece

            @pl.when(c > 0)
            def _():
                cols[j] += piece

    def copy_to(src, dst, send, recv, peer):
        return pltpu.make_async_remote_copy(
            src_ref=src,
            dst_ref=dst,
            send_sem=send,
            recv_sem=recv,
            device_id=peer,
            device_id_type=MESH_ID,
        )

    def dot_copy(i):
        mine = dots.at[here]
        return copy_to(mine, mine, dot_send.at[i], dot_recv.at[i], peers[i])

    def col_copy(i):
        src = cols.at[peers[i]["tensor"]]
        return copy_to(src, cols_in.at[here], col_send.at[i], col_recv.at[i], peers[i])

    def world_copy(i):
        mine = world.at[spot]
        return copy_to(mine, mine, world_send.at[i], world_recv.at[i], far[i])

    def exchange():
        numbers = jnp.zeros((8, width), F32)
        for i, a in enumerate((square[...], attn_square[...], ffn_square[...], keep[...])):
            a = jnp.sum(jnp.sum(a, 0, keepdims=True), 1, keepdims=True)
            share = 1.0 if i == 2 else 1.0 / size
            numbers += jnp.where((row == 1) & (lane == i), a * share, 0.0)
        for j in range(size):
            cols[j] += numbers
        cols_in[here] = cols[here]
        for i in range(size - 1):
            dot_copy(i).start()
            col_copy(i).start()

    def spread():
        for i in range(size - 1):
            dot_copy(i).wait()
            col_copy(i).wait()
        dot_total, column = dots[0], cols_in[0]
        for j in range(1, size):
            dot_total = dot_total + dots[j]
            column = column + cols_in[j]
        dot_sum[...] = dot_total
        world[spot] = column

        def put(piece):
            world[spot, 2:3] = piece

        own_columns(size, gain_rows[...], put)
        for i in range(replicas - 1):
            world_copy(i).start()

    def tick(k, _):
        @pl.when(k < groups)
        def _():
            compute(k)

        line.tick(k)

        @pl.when(k < groups)
        def _():
            add_up(k)

        @pl.when(k == groups)
        def _():
            exchange()

        @pl.when(k == groups + 3)
        def _():
            spread()

        return 0

    lax.fori_loop(0, max(line.count, groups + 4), tick, 0)

    def then(part, grad):
        through = grad * gain_own[...] - x_own[part, :].astype(F32) * inv[part, :] * (
            dot_sum[:, part].T[:, :1] / features
        )
        out_o[part, :] = (grad_own[part, :] + inv[part, :] * through).astype(BF)

    line.finish(total, then)
    for i in range(replicas - 1):
        world_copy(i).wait()
    everything = world[0]
    for j in range(1, replicas):
        everything = everything + world[j]
    sum_o[...] = everything


def input_gradient(
    axes, grads, inv, gain, keep, attn_square, gain_rows, ffn_square, gain_own, x_own, grad_own,
    w_query, w_key_t, w_value_t, x, chunk, after,
):
    size, replicas = axes["tensor"], axes["dp"] * axes["context"]
    rows, features = x.shape
    width = features // size
    anywhere, vmem = pl.BlockSpec(memory_space=pl.ANY), pl.BlockSpec(memory_space=pltpu.VMEM)
    shape, dma = jax.ShapeDtypeStruct, pltpu.SemaphoreType.DMA

    def kernel(*refs):
        input_kernel(axes, chunk, *refs[:14], *refs[14 + len(after) :])

    return pl.pallas_call(
        kernel,
        in_specs=[vmem] * 10 + [anywhere] * (4 + len(after)),
        out_specs=[vmem] * 2,
        out_shape=[
            shape((rows, width), BF),
            shape((8, width), F32),
        ],
        scratch_shapes=scatter_scratch(size, rows, width, chunk)
        + [
            pltpu.VMEM((2, chunk, features), BF),
            pltpu.VMEM((chunk, features), F32),
            pltpu.VMEM(w_query.shape, BF),
            pltpu.VMEM(w_key_t.shape, BF),
            pltpu.VMEM(w_value_t.shape, BF),
            pltpu.VMEM((size, 8, rows), F32),
            pltpu.VMEM((8, rows), F32),
            pltpu.VMEM((size, 8, width), F32),
            pltpu.VMEM((size, 8, width), F32),
            pltpu.VMEM((replicas, 8, width), F32),
            pltpu.VMEM((1, features), F32),
            dma((size - 1,)),
            dma((size - 1,)),
            dma((size - 1,)),
            dma((size - 1,)),
            dma((replicas - 1,)),
            dma((replicas - 1,)),
            dma((3,)),
            dma((2,)),
        ],
        compiler_params=pltpu.CompilerParams(
            collective_id=4, has_side_effects=True, vmem_limit_bytes=VMEM_LIMIT
        ),
        cost_estimate=pl.CostEstimate(
            flops=2 * rows * features * grads.shape[0],
            bytes_accessed=20 << 20,
            transcendentals=rows,
        ),
        name="input_gradient",
    )(
        grads, inv, gain, keep, attn_square, gain_rows, ffn_square, gain_own, x_own, grad_own,
        w_query, w_key_t, w_value_t, x, *after,
    )


def local(
    axes,
    layer_input_hidden,
    cotangent,
    valid_mask,
    span_starts,
    gain_attn,
    w_query,
    w_key,
    w_value,
    w_out,
    gain_mlp,
    w_gate,
    w_up,
    w_down,
):
    _, rows, width = layer_input_hidden.shape
    size = axes["tensor"]
    features = width * size
    kvs = w_key.shape[1] // HD
    heads = w_query.shape[1] // HD
    position = lax.axis_index("context") * rows + jnp.arange(rows, dtype=jnp.int32)
    inverse_freq = rope_base ** (-2.0 * jnp.arange(HD // 2, dtype=F32) / HD)
    angles = inverse_freq[:, None] * position.astype(F32)[None, :]
    cos_tab, sin_tab = jnp.cos(angles), jnp.sin(angles)
    x_own = layer_input_hidden[0]
    w_key_t, w_value_t = w_key.T, w_value.T

    def shard(grad):
        return lax.psum_scatter(grad, ("dp", "context"), scatter_dimension=0, tiled=True)

    (
        x_low,
        normed_a,
        inv_a,
        gains,
        query_t,
        both,
        kend,
        keep,
        cot,
        mixed,
        lse,
    ) = attend_forward(
        axes,
        x_own,
        cotangent[0],
        jnp.stack([gain_attn, gain_mlp]),
        cos_tab,
        sin_tab,
        valid_mask,
        span_starts,
        w_query,
        w_key_t,
        w_value_t,
        GROUP_ROWS,
    )
    normed_m, act, ggu, down_part, back_part, middle, middle_own, attn_square = feed_forward(
        size,
        mixed.reshape(heads * HD, rows),
        keep,
        gains,
        w_out,
        w_gate,
        w_up,
        w_down,
        x_low,
        cot,
        GROUP_ROWS,
        HOP_ROWS,
    )
    grad_ggu = ein("sd,sf->df", normed_m, ggu).astype(BF)
    ggu_sum = shard(grad_ggu)

    grad_own, grad_attn, grad_mixed, gain_m_rows, grad_down = norm_back(
        size, back_part, keep, gains, w_out, middle, cot, act, GROUP_ROWS, HOP_ROWS, (grad_ggu,)
    )
    down_sum = shard(grad_down)
    grads, layer_out, ffn_square, grad_rest = attend_backward(
        axes,
        down_part,
        query_t,
        both,
        kend,
        grad_mixed.reshape(heads, HD, rows),
        mixed,
        lse,
        cos_tab,
        sin_tab,
        middle_own,
        grad_attn,
        normed_a,
        GROUP_ROWS,
        (ggu_sum,),
    )
    rest_sum = shard(grad_rest)

    input_grad, sums = input_gradient(
        axes,
        grads.reshape(-1, rows),
        inv_a,
        gains,
        keep,
        attn_square,
        gain_m_rows,
        ffn_square,
        gain_attn[None],
        x_own,
        grad_own,
        w_query,
        w_key_t,
        w_value_t,
        x_low,
        GROUP_ROWS,
        (grad_rest, down_sum),
    )
    rest_sum = jnp.where(sums[1, 3] >= 0.0, rest_sum.astype(F32), 0.0)
    gate_sum, up_sum = jnp.split(ggu_sum.astype(F32), 2, 1)
    down_sum = down_sum.astype(F32).T
    cut = [heads * HD, 2 * heads * HD, (2 * heads + kvs) * HD]
    out_sum, query_sum, key_sum, value_sum = jnp.split(rest_sum, cut, 1)
    rms = jnp.sqrt(sums[1, :3] / (sums[1, 3] * features))
    return (
        layer_out[None],
        input_grad[None],
        sums[0],
        query_sum,
        key_sum,
        value_sum,
        out_sum.T,
        sums[2],
        gate_sum,
        up_sum,
        down_sum,
        rms[0],
        rms[1],
        rms[2],
    )


def solution(mesh):
    token = P("dp", "context", "tensor")
    by_rows = P(("dp", "context"), "tensor")
    by_columns = P("tensor", ("dp", "context"))
    cols, rows, vec = P(None, "tensor"), P("tensor", None), P("tensor")
    return jax.shard_map(
        functools.partial(local, dict(mesh.shape)),
        mesh=mesh,
        in_specs=(
            token,
            token,
            P("dp", None),
            P("dp", None),
            vec,
            cols,
            cols,
            cols,
            rows,
            vec,
            cols,
            cols,
            rows,
        ),
        out_specs=(
            token,
            token,
            vec,
            by_rows,
            by_rows,
            by_rows,
            by_columns,
            vec,
            by_rows,
            by_rows,
            by_columns,
            P(),
            P(),
            P(),
        ),
        check_vma=False,
    )
```
